128 devices in a mesh: rows: 16 (over x_hi, y, core), ctx: 8 (over x_lo, z).
Axes of the slice: x: 4 (x_hi: 2, x_lo: 2; x = x_hi * 2 + x_lo), y: 4, z: 4, core: 2. Of those that a mesh axis runs over, the one named last changes fastest.
Arguments:
- tokens: bfloat16 [2, 16, 1024, 1024], P(None, 'rows', 'ctx'), may hold values from -6 to 6
- cotangent: bfloat16 [2, 16, 1024, 1024], P(None, 'rows', 'ctx'), may hold values from -6 to 6
- bounds: int32 [2, 16, 5], P(None, 'rows'), may hold values from 0 to 1024, as said below
- positions: int32 [2, 16, 1024], P(None, 'rows', 'ctx'), may hold values from 0 to 1023, as said below
- norm_gain_attn: float32 [1024], replicated, may hold values from 0.5 to 1.5
- w_qkv: bfloat16 [1024, 2048], replicated, may hold values from -0.1875 to 0.1875
- qk_gain: float32 [128], replicated, may hold values from 0.5 to 1.5
- w_out: bfloat16 [1024, 1024], replicated, may hold values from -0.75 to 0.75
- norm_gain_ffn: float32 [1024], replicated, may hold values from 0.5 to 1.5
- w_gate_up: bfloat16 [1024, 9216], replicated, may hold values from -0.1875 to 0.1875
- w_down: bfloat16 [4608, 1024], replicated, may hold values from -0.09375 to 0.09375
Outputs:
- layer_out: bfloat16 [2, 16, 1024, 1024], P(None, 'rows', 'ctx')
- grad_tokens: float32 [2, 16, 1024, 1024], P(None, 'rows', 'ctx')
- grad_norm_attn: float32 [1024], P(('rows', 'ctx'))
- grad_qkv: float32 [1024, 2048], P(('rows', 'ctx'))
- grad_qk_gain: float32 [128], P(('rows', 'ctx'))
- grad_out: float32 [1024, 1024], P(('rows', 'ctx'))
- grad_norm_ffn: float32 [1024], P(('rows', 'ctx'))
- grad_gate_up: float32 [1024, 9216], P(('rows', 'ctx'))
- grad_down: float32 [4608, 1024], P(('rows', 'ctx'))
The draws below stay inside these ranges and needn't reach their ends.
Inputs may be any that keep to these rules, and one draw needn't show every extreme that they name: `bounds`: in each row the offsets rise strictly; the first is 0 and the last is 1024; document k holds the tokens from offset k up to offset k + 1. `positions`: within a document the position rises by one from token to token.
All inputs are finite; a program needn't handle non-finite values.
Results may differ from the reference program's by a relative error of at most 0.035.
Values may be sent and summed in bfloat16 or wider, within the bound.
A program may use at most 256 MiB of HBM per device.

```python
import jax
import jax.numpy as jnp
from jax import lax

D = 1024
H = 16
HD = 64
FF = 4608
DOCS = 4
MICRO = 2
ROW = 1024
ROW_DEV = 128
NROWS = 16
QKV = 2048


def shuffled(subkey):
    return jax.random.permutation(subkey, ROW_DEV - 1)


def document_layout(key):
    count = MICRO * NROWS
    pick_key, head_key, tail_key, base_key = jax.random.split(key, 4)
    long_doc = jax.random.randint(pick_key, (count,), 0, DOCS)
    head_perm = jax.vmap(shuffled)(jax.random.split(head_key, count))
    tail_perm = jax.vmap(shuffled)(jax.random.split(tail_key, count))
    head_cuts = jnp.sort(head_perm[:, :DOCS - 1], axis=1) + 1
    tail_cuts = jnp.sort(tail_perm[:, :DOCS - 1], axis=1) + ROW - ROW_DEV + 1
    slots = jnp.arange(DOCS - 1)
    from_tail = jnp.take_along_axis(tail_cuts, jnp.clip(slots[None, :] - long_doc[:, None], 0, DOCS - 2), axis=1)
    cuts = jnp.where(slots[None, :] < long_doc[:, None], head_cuts, from_tail)
    first = jnp.zeros((count, 1), jnp.int32)
    last = jnp.full((count, 1), ROW, jnp.int32)
    bounds = jnp.concatenate([first, cuts.astype(jnp.int32), last], axis=1)
    lengths = bounds[:, 1:] - bounds[:, :-1]
    docs = jnp.arange(DOCS)[None, :]
    partner = (long_doc + 1) % DOCS
    random_base = jax.random.randint(base_key, (count, DOCS), 0, ROW - lengths + 1)
    base = jnp.where(docs == long_doc[:, None], 0, jnp.where(docs == partner[:, None], ROW - lengths, random_base))
    index = jnp.arange(ROW)
    doc_ids = jnp.sum((index[None, :, None] >= bounds[:, None, 1:DOCS]).astype(jnp.int32), axis=2)
    start = jnp.take_along_axis(bounds, doc_ids, axis=1)
    offset = jnp.take_along_axis(base, doc_ids, axis=1)
    positions = (offset + index[None, :] - start).astype(jnp.int32)
    return (bounds.reshape(MICRO, NROWS, DOCS + 1), positions.reshape(MICRO, NROWS, ROW))


def draw_bounds(key, part):
    return document_layout(key)[0]


def draw_positions(key, part):
    return document_layout(key)[1]


def spiked(result, rng, source, target, shards_of, factor):
    def block_of(axis_at):
        return (jnp.arange(result.shape[axis_at]) // (result.shape[axis_at] // shards_of)).reshape((-1,) + (1,) * (result.ndim - 1 - axis_at))

    one_side = jax.random.permutation(rng, shards_of)[block_of(target)]
    far = (block_of(target) + shards_of // 2) % shards_of
    return jnp.where((block_of(source) == one_side) | (block_of(source) == far), factor * result, result)


def block_scale(stream_key, extent, cuts, least, top_value):
    gain = 1.0
    for axis_at, blocks in cuts:
        heights = jax.random.uniform(jax.random.fold_in(jax.random.fold_in(stream_key, 6), axis_at), (blocks,), jnp.float32, least / len(cuts), top_value / len(cuts))
        gain = gain * jnp.repeat(jnp.exp(heights), extent[axis_at] // blocks).reshape((-1,) + (1,) * (len(extent) - 1 - axis_at))
    return gain


def normal_values(own_key, shape, spread, limit, cuts=(), held_as=jnp.bfloat16):
    entries = jax.random.normal(own_key, shape, jnp.float32) * spread
    if len(cuts) > 0:
        entries = block_scale(own_key, shape, cuts, -0.22, 0.18) * entries
    return jnp.clip(entries, min=-limit, max=limit).astype(held_as)


def bell_draw_with(own_key, dims, spread, most, cuts, heavy, kind=jnp.bfloat16):
    entries = spread * jax.random.normal(own_key, dims, jnp.float32)
    if cuts:
        entries = entries * block_scale(own_key, dims, cuts, -0.22, 0.18)
    return jnp.clip(spiked(entries, jax.random.fold_in(own_key, 3), *heavy), -most, most).astype(kind)


def setup_inputs(seed: int = 0) -> dict:
    splits = jax.random.split(jax.random.key(seed), 12)
    tokens = bell_draw_with(splits[0], (MICRO, NROWS, ROW, D), 1.0, 6.0, ((1, 16), (2, 8)), (2, 3, 8, 2.0))
    cotangent = normal_values(splits[1], (MICRO, NROWS, ROW, D), 1.0, 6.0, ((1, 16), (2, 8)))
    bounds = draw_bounds(jax.random.fold_in(splits[11], 71), 0)
    positions = draw_positions(jax.random.fold_in(splits[11], 71), 0)
    norm_gain_attn = jnp.clip(jax.random.uniform(splits[4], (D,), jnp.float32, 0.5, 1.5), 0.5, 1.5)
    w_qkv = normal_values(splits[5], (D, QKV), D ** -0.5, 0.1875)
    qk_gain = jnp.clip(jax.random.uniform(splits[6], (2 * HD,), jnp.float32, 0.5, 1.5), 0.5, 1.5)
    w_out = normal_values(splits[7], (H * HD, D), (H * HD // 16) ** -0.5, 0.75)
    norm_gain_ffn = jnp.clip(jax.random.uniform(splits[8], (D,), jnp.float32, 0.5, 1.5), 0.5, 1.5)
    w_gate_up = normal_values(splits[9], (D, 2 * FF), D ** -0.5, 0.1875)
    w_down = normal_values(splits[10], (FF, D), FF ** -0.5, 0.09375)
    return {"tokens": tokens, "cotangent": cotangent, "bounds": bounds, "positions": positions, "norm_gain_attn": norm_gain_attn, "w_qkv": w_qkv, "qk_gain": qk_gain, "w_out": w_out, "norm_gain_ffn": norm_gain_ffn, "w_gate_up": w_gate_up, "w_down": w_down}


norm_eps = 1e-05
rope_theta = 1000000.0
masked_score = -1e+30
highest = lax.Precision.HIGHEST

@jax.custom_vjp
def low(v):
    return lax.optimization_barrier(v.astype(jnp.bfloat16)).astype(jnp.float32)

@jax.custom_vjp
def low_back(v):
    return v

def low_keep(v):
    return (low(v), None)

def low_pass(kept, grad):
    return (grad,)

def back_keep(v):
    return (v, None)

def back_low(kept, grad):
    return (low(grad),)
low.defvjp(low_keep, low_pass)
low_back.defvjp(back_keep, back_low)

def rms(values):
    return values * lax.rsqrt(lax.optimization_barrier(jnp.mean(values * values, axis=-1, keepdims=True)) + norm_eps)

def rotary_tables(positions, width):
    half = width // 2
    freqs = rope_theta ** (-2.0 * jnp.arange(half, dtype=jnp.float32) / width)
    angles = positions.astype(jnp.float32)[:, None] * freqs[None, :]
    cosine = jnp.cos(angles)
    sine = jnp.sin(angles)
    return (jnp.concatenate([cosine, cosine], -1), jnp.concatenate([sine, sine], -1))

def rotate(values, cosine, sine):
    half = values.shape[-1] // 2
    turned = jnp.concatenate([-values[..., half:], values[..., :half]], -1)
    return values * cosine[:, None, :] + turned * sine[:, None, :]

def document_of(index, bounds_row):
    cuts = bounds_row[1:-1]
    return lax.optimization_barrier(jnp.sum((index[:, None] >= cuts[None, :]).astype(jnp.int32), axis=1))

def row_layer(params, x_row, bounds_row, pos_row):
    gain_attn, weight_qkv, gain_qk, weight_out, gain_ffn, weight_gu, weight_down = params
    seq = x_row.shape[0]
    head_dim = gain_qk.shape[0] // 2
    heads = weight_out.shape[0] // head_dim
    kv_heads = (weight_qkv.shape[1] - heads * head_dim) // (2 * head_dim)
    group = heads // kv_heads
    hidden_units = weight_down.shape[0]
    normed = low(rms(x_row) * gain_attn)
    projected = low_back(jnp.dot(normed, weight_qkv, precision=highest))
    proj_q = projected[:, :heads * head_dim].reshape(seq, heads, head_dim)
    proj_k = projected[:, heads * head_dim:(heads + kv_heads) * head_dim].reshape(seq, kv_heads, head_dim)
    proj_v = projected[:, (heads + kv_heads) * head_dim:].reshape(seq, kv_heads, head_dim)
    cosine, sine = rotary_tables(pos_row, head_dim)
    queries = low(rotate(rms(proj_q) * gain_qk[:head_dim], cosine, sine))
    keys = low(rotate(rms(proj_k) * gain_qk[head_dim:], cosine, sine))
    values = low(proj_v)
    index = jnp.arange(seq, dtype=jnp.int32)
    docs = document_of(index, bounds_row)
    block = 512 if seq % 512 == 0 else seq
    query_blocks = queries.reshape(seq // block, block, kv_heads, group, head_dim)

    def attend(pieces):
        query_block, index_block, doc_block = pieces
        scores = low_back(jnp.einsum('qkgd,nkd->kgqn', query_block, keys, precision=highest) * head_dim ** (-0.5))
        keep = (index[None, :] <= index_block[:, None]) & (docs[None, :] == doc_block[:, None])
        probs = low(jax.nn.softmax(jnp.where(keep, scores, masked_score), axis=-1))
        return jnp.einsum('kgqn,nkd->qkgd', probs, values, precision=highest)
    attended = lax.map(jax.checkpoint(attend), (query_blocks, index.reshape(-1, block), docs.reshape(-1, block)))
    attended = low(low_back(attended.reshape(seq, heads * head_dim)))
    mid = x_row + low_back(jnp.dot(attended, weight_out, precision=highest))
    normed_ffn = low(rms(mid) * gain_ffn)
    gate_up = low_back(jnp.dot(normed_ffn, weight_gu, precision=highest))
    hidden = low(jax.nn.silu(gate_up[:, :hidden_units]) * gate_up[:, hidden_units:])
    return mid + low_back(jnp.dot(hidden, weight_down, precision=highest))

def reference(tokens, cotangent, bounds, positions, norm_gain_attn, w_qkv, qk_gain, w_out, norm_gain_ffn, w_gate_up, w_down):
    width = tokens.shape[-1]
    seq = tokens.shape[2]
    inputs = tokens.astype(jnp.float32).reshape(-1, seq, width)
    row_bounds = bounds.reshape(-1, bounds.shape[-1])
    row_positions = positions.reshape(-1, seq)
    params = (norm_gain_attn.astype(jnp.float32), w_qkv.astype(jnp.float32), qk_gain.astype(jnp.float32), w_out.astype(jnp.float32), norm_gain_ffn.astype(jnp.float32), w_gate_up.astype(jnp.float32), w_down.astype(jnp.float32))

    def whole(inputs, params):

        def one_row(carry, pieces):
            return (carry, jax.checkpoint(row_layer)(params, pieces[0], pieces[1], pieces[2]))
        unused, outputs = lax.scan(one_row, jnp.zeros((), jnp.float32), (inputs, row_bounds, row_positions))
        return outputs
    outputs, pullback = jax.vjp(whole, inputs, params)
    grad_inputs, grad_params = pullback(cotangent.astype(jnp.float32).reshape(inputs.shape))
    return (outputs.astype(jnp.bfloat16).reshape(tokens.shape), grad_inputs.reshape(tokens.shape), grad_params[0], grad_params[1], grad_params[2], grad_params[3], grad_params[4], grad_params[5], grad_params[6])
```

```python
import functools

import jax
import jax.numpy as jnp
from jax import lax
from jax.experimental import pallas as pl
from jax.experimental.pallas import tpu as pltpu
from jax.sharding import PartitionSpec as P

MESH = pl.DeviceIdType.MESH
norm_eps = 1e-05
rope_theta = 1000000.0
masked_score = -1e30
f32 = jnp.float32
bf16 = jnp.bfloat16
VMEM_LIMIT = 64 * 2**20 - 2**18


class Place:
    def __init__(self):
        r = lax.axis_index("rows")
        k = lax.axis_index("ctx")
        self.x_hi = lax.div(r, 8)
        self.y = lax.rem(lax.div(r, 2), 4)
        self.core = lax.rem(r, 2)
        self.x_lo = lax.div(k, 4)
        self.z = lax.rem(k, 4)
        self.rows = r
        self.ctx = k
        self.bits = [
            self.x_hi,
            lax.rem(self.x_hi + self.x_lo, 2),
            lax.div(self.y, 2),
            lax.rem(lax.div(self.y, 2) + lax.rem(self.y, 2), 2),
            lax.div(self.z, 2),
            lax.rem(lax.div(self.z, 2) + lax.rem(self.z, 2), 2),
        ]

    def at(self, x_hi=None, x_lo=None, y=None, z=None, core=None):
        x_hi = self.x_hi if x_hi is None else x_hi
        x_lo = self.x_lo if x_lo is None else x_lo
        y = self.y if y is None else y
        z = self.z if z is None else z
        core = self.core if core is None else core
        return (x_hi * 8 + y * 2 + core, x_lo * 4 + z)

    def partner(self):
        return self.at(core=1 - self.core)

    def neighbour(self, dim):
        if dim == 0:
            return self.at(x_hi=1 - self.x_hi, x_lo=1 - self.x_lo)
        if dim == 1:
            return self.at(x_lo=1 - self.x_lo)
        if dim == 2:
            return self.at(y=3 - self.y)
        if dim == 3:
            return self.at(y=self.y + 1 - 2 * lax.rem(self.y, 2))
        if dim == 4:
            return self.at(z=3 - self.z)
        return self.at(z=self.z + 1 - 2 * lax.rem(self.z, 2))


def gray(v):
    return v ^ (v >> 1)


def chip_number(x_hi, x_lo, y, z):
    return gray(2 * x_hi + x_lo) * 16 + gray(y) * 4 + gray(z)


def slot_of(number, s):
    turned = number << s
    return (turned & 63) | (turned >> 6)


HELD_AT = [64 - (64 >> t) for t in range(7)]


class Scatter:
    def __init__(self, place, first, held, send_sems, recv_sems, per):
        self.place = place
        self.first = first
        self.held = held
        self.send_sems = send_sems
        self.recv_sems = recv_sems
        self.per = per

    def part(self, s, t, which):
        half = 32 >> t
        if t == 0:
            return self.first, which * half
        return self.held, HELD_AT[t - 1] + which * half

    def copy(self, s, t):
        half = 32 >> t
        dim = (s + t) % 6
        ref, start = self.part(s, t, 1 - self.place.bits[dim])
        return pltpu.make_async_remote_copy(
            src_ref=ref.at[s, pl.ds(start, half)],
            dst_ref=self.held.at[s, pl.ds(HELD_AT[t], half)],
            send_sem=self.send_sems.at[s, t],
            recv_sem=self.recv_sems.at[s, t],
            device_id=self.place.neighbour(dim),
            device_id_type=MESH,
        )

    def send(self, s, t):
        self.copy(s, t).start()

    def take(self, s, t):
        self.copy(s, t).wait_recv()
        half = 32 >> t
        ref, start = self.part(s, t, self.place.bits[(s + t) % 6])
        per = min(self.per, half)

        def body(i, carry):
            for j in range(per):
                at = i * per + j
                self.held[s, HELD_AT[t] + at] = (
                    self.held[s, HELD_AT[t] + at].astype(f32) + ref[s, start + at].astype(f32)
                ).astype(bf16)
            return carry

        lax.fori_loop(0, half // per, body, 0)
        self.send(s, t + 1)

    def last(self, s):
        self.copy(s, 5).wait_recv()
        ref, start = self.part(s, 5, self.place.bits[(s + 5) % 6])
        return self.held[s, HELD_AT[5]].astype(f32) + ref[s, start].astype(f32)

    def sent(self):
        for s in range(6):
            for t in range(6):
                self.copy(s, t).wait_send()


def greet(devices):
    barrier = pltpu.get_barrier_semaphore()
    for device in devices:
        pl.semaphore_signal(barrier, inc=1, device_id=device, device_id_type=MESH)
    pl.semaphore_wait(barrier, len(devices))


def greet_all(place, devices):
    barrier = pltpu.get_barrier_semaphore()
    targets = down_targets(place)
    for device in devices + targets[1:]:
        pl.semaphore_signal(barrier, inc=1, device_id=device, device_id_type=MESH)
    swapped = place.x_hi != place.core
    count = len(devices) + 3

    @pl.when(swapped)
    def _():
        pl.semaphore_signal(barrier, inc=1, device_id=targets[0], device_id_type=MESH)
        pl.semaphore_wait(barrier, count + 1)

    @pl.when(jnp.logical_not(swapped))
    def _():
        pl.semaphore_wait(barrier, count)


def push(place, src, dst, send_sem, recv_sem, device):
    return pltpu.make_async_remote_copy(
        src_ref=src,
        dst_ref=dst,
        send_sem=send_sem,
        recv_sem=recv_sem,
        device_id=device,
        device_id_type=MESH,
    )


def down_targets(place):
    return [
        place.at(x_hi=place.core, core=place.x_hi, z=lax.rem(place.z + off, 4)) for off in range(4)
    ]


def dot(left, right):
    return jnp.dot(left, right, preferred_element_type=f32)


def dot_cols(left, right):
    return lax.dot_general(left, right, (((1,), (1,)), ((), ())), preferred_element_type=f32)


FF_HALF = 2304


def ffn_kernel(
    mid_ref,
    cot_ref,
    gain_ref,
    wgu_hbm,
    wd_hbm,
    out_ref,
    dmid_ref,
    ggain_ref,
    ggu_ref,
    gdn_ref,
    wgu,
    wd,
    nf,
    nft,
    dyb,
    h,
    ht,
    dgu,
    sum_own,
    sum_send,
    sum_recv,
    g_first,
    g_held,
    d_first,
    d_held,
    g_fin,
    g_in,
    d_acc,
    d_stage,
    d_in,
    w_sems,
    x_send,
    x_recv,
    g_send,
    g_recv,
    d_send,
    d_recv,
    f_send,
    f_recv,
):
    place = Place()
    core = place.core
    loads = []
    for i in range(3):
        at = pl.multiple_of(core * FF_HALF + 768 * i, 256)
        loads.append(
            [
                pltpu.make_async_copy(
                    wgu_hbm.at[:, pl.ds(at, 768)], wgu.at[:, pl.ds(768 * i, 768)], w_sems.at[3 * i]
                ),
                pltpu.make_async_copy(
                    wgu_hbm.at[:, pl.ds(pl.multiple_of(4608 + at, 256), 768)],
                    wgu.at[:, pl.ds(FF_HALF + 768 * i, 768)],
                    w_sems.at[3 * i + 1],
                ),
                pltpu.make_async_copy(
                    wd_hbm.at[pl.ds(at, 768)], wd.at[pl.ds(768 * i, 768)], w_sems.at[3 * i + 2]
                ),
            ]
        )
        for copy in loads[-1]:
            copy.start()

    greet_all(place, [place.partner()] + [place.neighbour(dim) for dim in range(6)])

    partner = place.partner()
    to_dy = push(place, cot_ref, dyb.at[pl.ds(256, 256)], x_send.at[0], x_recv.at[0], partner)
    to_dy.start()
    mid = mid_ref[...]
    scale = lax.rsqrt(jnp.mean(mid * mid, axis=-1, keepdims=True) + norm_eps)
    nf[pl.ds(0, 256), :] = (mid * scale * gain_ref[...]).astype(bf16)
    dyb[pl.ds(0, 256), :] = cot_ref[...]
    to_nf = push(
        place,
        nf.at[pl.ds(0, 256)],
        nf.at[pl.ds(256, 256)],
        x_send.at[1],
        x_recv.at[1],
        partner,
    )
    to_nf.start()
    to_dy.wait_recv()
    to_nf.wait_recv()
    for i in range(2):
        nft[:, pl.ds(256 * i, 256)] = nf[pl.ds(256 * i, 256), :].T

    for i in range(3):
        for copy in loads[i]:
            copy.wait()

        def units(j, carry, i=i):
            at = pl.multiple_of(768 * i + 256 * j, 256)
            gate = dot(nf[...], wgu[:, pl.ds(at, 256)])
            upward = dot(nf[...], wgu[:, pl.ds(pl.multiple_of(FF_HALF + at, 256), 256)])
            grad_hidden = dot_cols(dyb[...], wd[pl.ds(at, 256), :])
            sigma = 1.0 / (1.0 + jnp.exp(-gate))
            silu = gate * sigma
            hidden = (silu * upward).astype(bf16)
            h[:, pl.ds(at, 256)] = hidden
            ht[pl.ds(at, 256), :] = hidden.T
            dgu[:, pl.ds(at, 256)] = (
                grad_hidden * upward * (sigma + silu * (1.0 - sigma))
            ).astype(bf16)
            dgu[:, pl.ds(pl.multiple_of(FF_HALF + at, 256), 256)] = (grad_hidden * silu).astype(bf16)
            return carry

        lax.fori_loop(0, 3, units, 0)

    down = Scatter(place, d_first, d_held, d_send, d_recv, 4)
    for block in range(3):

        def down_cols(z, carry, block=block):
            part = dot(
                ht[pl.ds(768 * block, 768), :], dyb[:, pl.ds(pl.multiple_of(256 * z, 256), 256)]
            )
            z_number = 2 * lax.div(z, 2) + lax.rem(lax.div(z, 2) + lax.rem(z, 2), 2)
            for i in range(16):
                q = 16 * block + i
                y, core_to, x_lo, rg = q // 12, (q // 6) % 2, (q // 3) % 2, q % 3
                number = chip_number(core_to, x_lo, y, 0) + z_number
                for ch in range(2):
                    s = 2 * rg + ch
                    turned = number * (1 << s)
                    slot = lax.rem(turned, 64) + lax.div(turned, 64)
                    d_first[s, slot] = part[48 * i : 48 * i + 48, 128 * ch : 128 * ch + 128].astype(
                        bf16
                    )
            return carry

        lax.fori_loop(0, 4, down_cols, 0)
    for s in range(6):
        down.send(s, 0)

    both = Scatter(place, g_first, g_held, g_send, g_recv, 2)
    for s in range(6):

        def gate_cols(j, carry, s=s):
            cols = dgu[:, pl.ds(pl.multiple_of(768 * s + 256 * j, 256), 256)]
            for x_hi in range(2):
                part = dot(nft[pl.ds(512 * x_hi, 512), :], cols)
                part = part.reshape(4, 2, 8, 8, 256)
                for y in range(4):
                    for x_lo in range(2):
                        for z in range(4):
                            slot = slot_of(chip_number(x_hi, x_lo, y, z), s)
                            piece = part[y, :, 4 * x_lo + z].reshape(16, 256)
                            g_first[s, slot, :, pl.ds(pl.multiple_of(256 * j, 256), 256)] = piece.astype(
                                bf16
                            )
            return carry

        lax.fori_loop(0, 3, gate_cols, 0)
        both.send(s, 0)

    def out_cols(j, carry):
        at = pl.ds(pl.multiple_of(256 * j, 256), 256)
        part = dot(h[...], wd[:, at])
        sum_own[:, at] = part[:256]
        sum_send[0, :, at] = part[256:].astype(bf16)
        return carry

    lax.fori_loop(0, 4, out_cols, 0)
    to_out = push(place, sum_send.at[0], sum_recv.at[0], x_send.at[2], x_recv.at[2], partner)
    to_out.start()

    def back_cols(j, carry):
        at = pl.ds(pl.multiple_of(256 * j, 256), 256)
        part = dot_cols(dgu[...], wgu[at, :])
        dmid_ref[:, at] = part[:256]
        sum_send[1, :, at] = part[256:].astype(bf16)
        return carry

    lax.fori_loop(0, 4, back_cols, 0)
    to_back = push(place, sum_send.at[1], sum_recv.at[1], x_send.at[3], x_recv.at[3], partner)
    to_back.start()
    to_out.wait_recv()
    out_ref[...] = (mid_ref[...] + sum_own[...] + sum_recv[0].astype(f32)).astype(bf16)
    to_back.wait_recv()
    mid = mid_ref[...]
    scale = lax.rsqrt(jnp.mean(mid * mid, axis=-1, keepdims=True) + norm_eps)
    normed = mid * scale
    grad_nffn = dmid_ref[...] + sum_recv[1].astype(f32)
    ggain_ref[...] = jnp.sum(grad_nffn * normed, axis=0, keepdims=True)
    grad_e = grad_nffn * gain_ref[...]
    dmid_ref[...] = cot_ref[...].astype(f32) + scale * (
        grad_e - normed * jnp.mean(grad_e * normed, axis=-1, keepdims=True)
    )

    for t in range(5):
        for s in range(6):
            down.take(s, t)
        for s in range(6):
            both.take(s, t)
    finish_down(place, down, d_acc, d_stage, d_in, f_send, f_recv, gdn_ref)
    for s in range(6):
        total = both.last(s)
        g_fin[0, s] = total[:8]
        g_fin[1, s] = total[8:]
    swap = push(place, g_fin.at[1 - core], g_in, x_send.at[4], x_recv.at[4], partner)
    swap.start()
    for s in range(6):
        base = (s // 3) * 4608 + (s % 3) * 768
        at = pl.multiple_of(base + core * FF_HALF, 256)
        ggu_ref[:, pl.ds(at, 768)] = g_fin[core, s]
    swap.wait_recv()
    for s in range(6):
        base = (s // 3) * 4608 + (s % 3) * 768
        at = pl.multiple_of(base + (1 - core) * FF_HALF, 256)
        ggu_ref[:, pl.ds(at, 768)] = g_in[s]
    to_dy.wait_send()
    to_nf.wait_send()
    to_out.wait_send()
    to_back.wait_send()
    swap.wait_send()
    down.sent()
    both.sent()


def finish_down(place, down, d_acc, d_stage, d_in, f_send, f_recv, gdn_ref):
    for s in range(6):
        d_acc[pl.ds(48 * (s // 2), 48), pl.ds(128 * (s % 2), 128)] = down.last(s)
    for z in range(4):
        d_stage[z, pl.ds(0, 36), :] = d_acc[pl.ds(36 * z, 36), :]
        d_stage[z, pl.ds(36, 4), :] = jnp.zeros((4, 256), f32)
    targets = down_targets(place)
    swapped = place.x_hi != place.core
    moves = []
    for off in range(4):
        moves.append(
            push(
                place,
                d_stage.at[lax.rem(place.z + off, 4)],
                d_in.at[place.z],
                f_send.at[off],
                f_recv.at[off],
                targets[off],
            )
        )
    for off in range(1, 4):
        moves[off].start()

    @pl.when(swapped)
    def _():
        moves[0].start()
        moves[0].wait_recv()

    @pl.when(jnp.logical_not(swapped))
    def _():
        d_in[place.z] = d_stage[place.z]

    for off in range(1, 4):
        moves[off].wait_recv()
    for z in range(4):
        gdn_ref[:, pl.ds(256 * z, 256)] = d_in[z, pl.ds(0, 36), :]
    for off in range(1, 4):
        moves[off].wait_send()

    @pl.when(swapped)
    def _():
        moves[0].wait_send()


def ffn(mid, cot, gain, w_gate_up, w_down):
    vmem = pl.BlockSpec(memory_space=pltpu.VMEM)
    hbm = pl.BlockSpec(memory_space=pl.ANY)
    dma = pltpu.SemaphoreType.DMA
    return pl.pallas_call(
        ffn_kernel,
        out_shape=(
            jax.ShapeDtypeStruct((256, 1024), bf16),
            jax.ShapeDtypeStruct((256, 1024), f32),
            jax.ShapeDtypeStruct((1, 1024), f32),
            jax.ShapeDtypeStruct((8, 9216), f32),
            jax.ShapeDtypeStruct((36, 1024), f32),
        ),
        in_specs=[vmem, vmem, vmem, hbm, hbm],
        out_specs=(vmem, vmem, vmem, vmem, vmem),
        scratch_shapes=[
            pltpu.VMEM((1024, 4608), bf16),
            pltpu.VMEM((FF_HALF, 1024), bf16),
            pltpu.VMEM((512, 1024), bf16),
            pltpu.VMEM((1024, 512), bf16),
            pltpu.VMEM((512, 1024), bf16),
            pltpu.VMEM((512, FF_HALF), bf16),
            pltpu.VMEM((FF_HALF, 512), bf16),
            pltpu.VMEM((512, 4608), bf16),
            pltpu.VMEM((256, 1024), f32),
            pltpu.VMEM((2, 256, 1024), bf16),
            pltpu.VMEM((2, 256, 1024), bf16),
            pltpu.VMEM((6, 64, 16, 768), bf16),
            pltpu.VMEM((6, 63, 16, 768), bf16),
            pltpu.VMEM((6, 64, 48, 128), bf16),
            pltpu.VMEM((6, 63, 48, 128), bf16),
            pltpu.VMEM((2, 6, 8, 768), f32),
            pltpu.VMEM((6, 8, 768), f32),
            pltpu.VMEM((144, 256), f32),
            pltpu.VMEM((4, 40, 256), f32),
            pltpu.VMEM((4, 40, 256), f32),
            dma((9,)),
            dma((5,)),
            dma((5,)),
            dma((6, 6)),
            dma((6, 6)),
            dma((6, 6)),
            dma((6, 6)),
            dma((4,)),
            dma((4,)),
        ],
        compiler_params=pltpu.CompilerParams(
            collective_id=0, has_side_effects=True, vmem_limit_bytes=VMEM_LIMIT
        ),
        name="feed_forward",
    )(mid, cot, gain, w_gate_up, w_down)


def reorder_store(part, first, s, x_hi, at, width):
    part = part.reshape(4, 2, 8, 8, width)
    for y in range(4):
        for x_lo in range(2):
            for z in range(4):
                slot = slot_of(chip_number(x_hi, x_lo, y, z), s)
                first[s, slot, :, at] = part[y, :, 4 * x_lo + z].reshape(16, width).astype(bf16)


def last_kernel(
    x_ref,
    dmid_ref,
    na_ref,
    dp_ref,
    att_ref,
    gain_ref,
    vec_ref,
    w_qkv,
    gtok_ref,
    gqkv_ref,
    gout_ref,
    vec_out,
    xin,
    dpin,
    dmin,
    dm_own,
    nat,
    attt,
    cols,
    q_first,
    q_held,
    q_fin,
    q_in,
    vec,
    vec_in,
    x_send,
    x_recv,
    q_send,
    q_recv,
    v_send,
    v_recv,
):
    place = Place()
    core = place.core
    partner = place.partner()
    greet([partner] + [place.neighbour(dim) for dim in range(6)])
    for half in range(2):
        dm_own[half] = dmid_ref[:, pl.ds(512 * half, 512)].astype(bf16)
    moves = [
        push(place, na_ref, xin.at[0], x_send.at[0], x_recv.at[0], partner),
        push(place, att_ref, xin.at[1], x_send.at[1], x_recv.at[1], partner),
        push(place, dp_ref.at[1 - core], dpin, x_send.at[2], x_recv.at[2], partner),
        push(place, dm_own.at[1 - core], dmin, x_send.at[3], x_recv.at[3], partner),
    ]
    for move in moves:
        move.start()
    nat[:, pl.ds(0, 256)] = na_ref[...].T
    attt[:, pl.ds(0, 256)] = att_ref[...].T
    cols[pl.ds(0, 256), pl.ds(0, 1024)] = dp_ref[core]
    cols[pl.ds(0, 256), pl.ds(1024, 512)] = dm_own[core]
    for move in moves:
        move.wait_recv()
    nat[:, pl.ds(256, 256)] = xin[0].T
    attt[:, pl.ds(256, 256)] = xin[1].T
    cols[pl.ds(256, 256), pl.ds(0, 1024)] = dpin[...]
    cols[pl.ds(256, 256), pl.ds(1024, 512)] = dmin[...]
    quad = Scatter(place, q_first, q_held, q_send, q_recv, 4)
    for s in range(6):
        left = nat if s < 4 else attt
        for x_hi in range(2):
            part = dot(left[pl.ds(512 * x_hi, 512), :], cols[:, pl.ds(256 * s, 256)])
            reorder_store(part, q_first, s, x_hi, slice(None), 256)
        quad.send(s, 0)

    inputs = x_ref[...].astype(f32)
    scale = lax.rsqrt(jnp.mean(inputs * inputs, axis=-1, keepdims=True) + norm_eps)
    normed = inputs * scale
    grad_n = dot_cols(dp_ref[0], w_qkv[:, pl.ds(0, 1024)]) + dot_cols(
        dp_ref[1], w_qkv[:, pl.ds(1024, 1024)]
    )
    gain_grad = jnp.sum(grad_n * normed, axis=0, keepdims=True)
    grad_e = grad_n * gain_ref[...]
    gtok_ref[...] = dmid_ref[...] + scale * (
        grad_e - normed * jnp.mean(grad_e * normed, axis=-1, keepdims=True)
    )
    vec[0, pl.ds(8, 16), :] = vec_ref[pl.ds(8, 16), :]
    for i in range(8):
        vec[0, pl.ds(i, 1), :] = gain_grad[:, 128 * i : 128 * i + 128]

    def vec_move(step):
        device = place.neighbour(step) if step < 6 else partner
        return push(place, vec.at[step], vec_in.at[step], v_send.at[step], v_recv.at[step], device)

    vec_move(0).start()
    for t in range(5):
        for s in range(6):
            quad.take(s, t)
        vec_move(t).wait_recv()
        vec[t + 1] = vec[t] + vec_in[t]
        vec_move(t + 1).start()
    for s in range(6):
        total = quad.last(s)
        q_fin[0, s] = total[:8]
        q_fin[1, s] = total[8:]
    swap = push(place, q_fin.at[1 - core], q_in, x_send.at[4], x_recv.at[4], partner)
    swap.start()
    vec_move(5).wait_recv()
    vec[6] = vec[5] + vec_in[5]
    vec_move(6).start()
    for s in range(4):
        gqkv_ref[:, pl.ds(pl.multiple_of(core * 1024 + 256 * s, 256), 256)] = q_fin[core, s]
    for s in range(4, 6):
        gout_ref[:, pl.ds(pl.multiple_of(core * 512 + 256 * (s - 4), 256), 256)] = q_fin[core, s]
    swap.wait_recv()
    for s in range(4):
        gqkv_ref[:, pl.ds(pl.multiple_of((1 - core) * 1024 + 256 * s, 256), 256)] = q_in[s]
    for s in range(4, 6):
        gout_ref[:, pl.ds(pl.multiple_of((1 - core) * 512 + 256 * (s - 4), 256), 256)] = q_in[s]
    vec_move(6).wait_recv()
    vec_out[...] = vec[6] + vec_in[6]
    for move in moves:
        move.wait_send()
    swap.wait_send()
    for step in range(7):
        vec_move(step).wait_send()
    quad.sent()


def last_part(x, dmid, na, dp, att, gain, vec, w_qkv):
    vmem = pl.BlockSpec(memory_space=pltpu.VMEM)
    dma = pltpu.SemaphoreType.DMA
    return pl.pallas_call(
        last_kernel,
        out_shape=(
            jax.ShapeDtypeStruct((256, 1024), f32),
            jax.ShapeDtypeStruct((8, 2048), f32),
            jax.ShapeDtypeStruct((8, 1024), f32),
            jax.ShapeDtypeStruct((24, 128), f32),
        ),
        in_specs=[vmem] * 8,
        out_specs=(vmem,) * 4,
        scratch_shapes=[
            pltpu.VMEM((2, 256, 1024), bf16),
            pltpu.VMEM((256, 1024), bf16),
            pltpu.VMEM((256, 512), bf16),
            pltpu.VMEM((2, 256, 512), bf16),
            pltpu.VMEM((1024, 512), bf16),
            pltpu.VMEM((1024, 512), bf16),
            pltpu.VMEM((512, 1536), bf16),
            pltpu.VMEM((6, 64, 16, 256), bf16),
            pltpu.VMEM((6, 63, 16, 256), bf16),
            pltpu.VMEM((2, 6, 8, 256), f32),
            pltpu.VMEM((6, 8, 256), f32),
            pltpu.VMEM((7, 24, 128), f32),
            pltpu.VMEM((7, 24, 128), f32),
            dma((5,)),
            dma((5,)),
            dma((6, 6)),
            dma((6, 6)),
            dma((7,)),
            dma((7,)),
        ],
        compiler_params=pltpu.CompilerParams(
            collective_id=1, has_side_effects=True, vmem_limit_bytes=VMEM_LIMIT
        ),
        name="projection_gradients",
    )(x, dmid, na, dp, att, gain, vec, w_qkv)


def rms_scale(values):
    return lax.rsqrt(jnp.mean(values * values, axis=-1, keepdims=True) + norm_eps)


def rms_back(grad_normed, values, scale):
    normed = values * scale
    return scale * (grad_normed - normed * jnp.mean(grad_normed * normed, axis=-1, keepdims=True))


def rotary_tables(positions, width):
    half = width // 2
    freqs = rope_theta ** (-2.0 * jnp.arange(half, dtype=jnp.float32) / width)
    angles = positions.astype(jnp.float32)[:, None] * freqs[None, :]
    cosine = jnp.cos(angles)
    sine = jnp.sin(angles)
    return (jnp.concatenate([cosine, cosine], -1), jnp.concatenate([sine, sine], -1))


def rotate(values, cosine, sine):
    half = values.shape[-1] // 2
    turned = jnp.concatenate([-values[..., half:], values[..., :half]], -1)
    return values * cosine[:, None, :] + turned * sine[:, None, :]


def rotate_back(grads, cosine, sine):
    half = grads.shape[-1] // 2
    scaled = grads * sine[:, None, :]
    turned = jnp.concatenate([scaled[..., half:], -scaled[..., :half]], -1)
    return grads * cosine[:, None, :] + turned


def document_of(index, bounds_row):
    cuts = bounds_row[1:-1]
    return jnp.sum((index[:, None] >= cuts[None, :]).astype(jnp.int32), axis=1)


def contract_rows(left, right):
    return lax.dot_general(
        left, right, (((0,), (0,)), ((), ())), preferred_element_type=jnp.float32
    )


def contract_cols(left, right):
    return lax.dot_general(
        left, right, (((1,), (1,)), ((), ())), preferred_element_type=jnp.float32
    )


def local(
    tokens,
    cotangent,
    bounds,
    positions,
    norm_gain_attn,
    w_qkv,
    qk_gain,
    w_out,
    norm_gain_ffn,
    w_gate_up,
    w_down,
):
    micro = tokens.shape[0]
    rows_dev = tokens.shape[2]
    width = tokens.shape[3]
    cycle = lax.axis_size("ctx")
    seq = rows_dev * cycle
    head_dim = qk_gain.shape[0] // 2
    heads = w_out.shape[0] // head_dim
    kv_heads = (w_qkv.shape[1] - heads * head_dim) // (2 * head_dim)
    group = heads // kv_heads
    hidden_units = w_down.shape[0]
    q_width = heads * head_dim
    k_width = kv_heads * head_dim
    scale = head_dim ** (-0.5)
    block = 512
    blocks = seq // block
    all_rows = micro * rows_dev
    query_index = lax.axis_index("ctx") * rows_dev + jnp.arange(rows_dev, dtype=jnp.int32)
    key_index = jnp.arange(seq, dtype=jnp.int32)
    index_blocks = key_index.reshape(blocks, block)
    gain_query = qk_gain[:head_dim]
    gain_key = qk_gain[head_dim:]
    inputs = tokens[:, 0].reshape(all_rows, width).astype(jnp.float32)
    cosine, sine = rotary_tables(positions[:, 0].reshape(all_rows), head_dim)
    scale_attn = rms_scale(inputs)
    normed_attn = (inputs * scale_attn * norm_gain_attn).astype(jnp.bfloat16)
    projected = jnp.dot(normed_attn, w_qkv, preferred_element_type=jnp.float32)
    proj_query = projected[:, :q_width].reshape(all_rows, heads, head_dim)
    proj_key = projected[:, q_width : q_width + k_width].reshape(all_rows, kv_heads, head_dim)
    proj_value = projected[:, q_width + k_width :]
    scale_query = rms_scale(proj_query)
    scale_key = rms_scale(proj_key)
    queries = rotate(proj_query * scale_query * gain_query, cosine, sine).astype(jnp.bfloat16)
    keys_local = (
        rotate(proj_key * scale_key * gain_key, cosine, sine)
        .astype(jnp.bfloat16)
        .reshape(all_rows, k_width)
    )
    values_local = proj_value.astype(jnp.bfloat16)

    def masked_scores(query_four, query_doc, key_block, index_block, doc_block):
        scores = (
            jnp.einsum("kgqd,nkd->kgqn", query_four, key_block, preferred_element_type=jnp.float32)
            * scale
        )
        keep = (index_block[None, :] <= query_index[:, None]) & (
            doc_block[None, :] == query_doc[:, None]
        )
        return (jnp.where(keep, scores, masked_score), keep)

    query_fours = []
    query_docs = []
    doc_tables = []
    log_totals = []
    out_fours = []
    kept_pairs = []
    for step in range(micro):
        lower = step * rows_dev
        bounds_row = bounds[step, 0]
        query_doc = document_of(query_index, bounds_row)
        doc_blocks = document_of(key_index, bounds_row).reshape(blocks, block)
        query_four = (
            queries[lower : lower + rows_dev]
            .reshape(rows_dev, kv_heads, group, head_dim)
            .transpose(1, 2, 0, 3)
        )
        keys_all, values_all = (
            lax.all_gather(keys_local[lower : lower + rows_dev], "ctx", axis=0, tiled=True),
            lax.all_gather(values_local[lower : lower + rows_dev], "ctx", axis=0, tiled=True),
        )
        key_blocks = keys_all.reshape(blocks, block, kv_heads, head_dim)
        value_blocks = values_all.reshape(blocks, block, kv_heads, head_dim)

        def stats_step(carry, pieces):
            top, total = carry
            scores, keep = masked_scores(query_four, query_doc, pieces[0], pieces[1], pieces[2])
            new_top = jnp.maximum(top, jnp.max(scores, axis=-1))
            weights = jnp.where(keep, jnp.exp(scores - new_top[..., None]), 0.0)
            total = total * jnp.exp(top - new_top) + jnp.sum(weights, axis=-1)
            return ((new_top, total), None)

        start_top = jnp.full((kv_heads, group, rows_dev), masked_score, jnp.float32)
        start_total = jnp.zeros((kv_heads, group, rows_dev), jnp.float32)
        (top, total), unused = lax.scan(
            stats_step, (start_top, start_total), (key_blocks, index_blocks, doc_blocks)
        )
        log_total = top + jnp.log(total)

        def output_step(carry, pieces):
            scores, keep = masked_scores(query_four, query_doc, pieces[0], pieces[1], pieces[2])
            probs = jnp.where(keep, jnp.exp(scores - log_total[..., None]), 0.0).astype(
                jnp.bfloat16
            )
            carry = carry + jnp.einsum(
                "kgqn,nkd->kgqd", probs, pieces[3], preferred_element_type=jnp.float32
            )
            return (carry, None)

        start_out = jnp.zeros((kv_heads, group, rows_dev, head_dim), jnp.float32)
        out_four, unused = lax.scan(
            output_step, start_out, (key_blocks, index_blocks, doc_blocks, value_blocks)
        )
        query_fours.append(query_four)
        query_docs.append(query_doc)
        doc_tables.append(doc_blocks)
        log_totals.append(log_total)
        out_fours.append(out_four)
        kept_pairs.append((keys_all, values_all))
    attended_low = jnp.concatenate(
        [piece.transpose(2, 0, 1, 3).reshape(rows_dev, q_width) for piece in out_fours], 0
    ).astype(jnp.bfloat16)
    mid = inputs + jnp.dot(attended_low, w_out, preferred_element_type=jnp.float32)
    cot = cotangent[:, 0].reshape(all_rows, width)
    layer_out, grad_mid, grad_gain_ffn, sum_gate_up, sum_down = ffn(
        mid, cot, norm_gain_ffn[None], w_gate_up, w_down
    )
    grad_mid_low = grad_mid.astype(jnp.bfloat16)
    grad_attended = contract_cols(grad_mid_low, w_out).astype(jnp.bfloat16)
    query_grads = []
    key_grads = []
    value_grads = []
    for step in range(micro):
        lower = step * rows_dev
        query_four = query_fours[step]
        query_doc = query_docs[step]
        doc_blocks = doc_tables[step]
        log_total = log_totals[step]
        grad_four = (
            grad_attended[lower : lower + rows_dev]
            .reshape(rows_dev, kv_heads, group, head_dim)
            .transpose(1, 2, 0, 3)
        )
        delta = jnp.sum(grad_four.astype(jnp.float32) * out_fours[step], axis=-1)
        back_keys, back_values = (
            lax.all_gather(keys_local[lower : lower + rows_dev], "ctx", axis=0, tiled=True),
            lax.all_gather(values_local[lower : lower + rows_dev], "ctx", axis=0, tiled=True),
        )
        back_key_blocks = back_keys.reshape(blocks, block, kv_heads, head_dim)
        back_value_blocks = back_values.reshape(blocks, block, kv_heads, head_dim)

        def grad_step(carry, pieces):
            key_block, index_block, doc_block, value_block = pieces
            scores, keep = masked_scores(query_four, query_doc, key_block, index_block, doc_block)
            probs = jnp.where(keep, jnp.exp(scores - log_total[..., None]), 0.0)
            probs_low = probs.astype(jnp.bfloat16)
            grad_probs = jnp.einsum(
                "kgqd,nkd->kgqn", grad_four, value_block, preferred_element_type=jnp.float32
            )
            grad_scores = (probs * (grad_probs - delta[..., None])).astype(jnp.bfloat16)
            carry = (
                carry
                + jnp.einsum(
                    "kgqn,nkd->kgqd", grad_scores, key_block, preferred_element_type=jnp.float32
                )
                * scale
            )
            grad_key_block = (
                jnp.einsum(
                    "kgqn,kgqd->nkd", grad_scores, query_four, preferred_element_type=jnp.float32
                )
                * scale
            )
            grad_value_block = jnp.einsum(
                "kgqn,kgqd->nkd", probs_low, grad_four, preferred_element_type=jnp.float32
            )
            return (carry, (grad_key_block, grad_value_block))

        start_grad = jnp.zeros((kv_heads, group, rows_dev, head_dim), jnp.float32)
        grad_query_four, (grad_key_blocks, grad_value_blocks) = lax.scan(
            grad_step, start_grad, (back_key_blocks, index_blocks, doc_blocks, back_value_blocks)
        )
        grad_keys, grad_values = (
            lax.psum_scatter(
                grad_key_blocks.reshape(seq, k_width).astype(jnp.bfloat16),
                "ctx",
                scatter_dimension=0,
                tiled=True,
            ).astype(jnp.float32),
            lax.psum_scatter(
                grad_value_blocks.reshape(seq, k_width).astype(jnp.bfloat16),
                "ctx",
                scatter_dimension=0,
                tiled=True,
            ).astype(jnp.float32),
        )
        query_grads.append(grad_query_four.transpose(2, 0, 1, 3).reshape(rows_dev, heads, head_dim))
        key_grads.append(grad_keys)
        value_grads.append(grad_values)
    grad_query = jnp.concatenate(query_grads, 0)
    grad_keys = jnp.concatenate(key_grads, 0).reshape(all_rows, kv_heads, head_dim)
    grad_values = jnp.concatenate(value_grads, 0)
    grad_turn_query = rotate_back(grad_query, cosine, sine)
    grad_turn_key = rotate_back(grad_keys, cosine, sine)
    grad_gain_query = jnp.sum(grad_turn_query * proj_query * scale_query, axis=(0, 1))
    grad_gain_key = jnp.sum(grad_turn_key * proj_key * scale_key, axis=(0, 1))
    grad_proj_query = rms_back(grad_turn_query * gain_query, proj_query, scale_query).reshape(
        all_rows, q_width
    )
    grad_proj_key = rms_back(grad_turn_key * gain_key, proj_key, scale_key).reshape(
        all_rows, k_width
    )
    grad_projected = jnp.concatenate([grad_proj_query, grad_proj_key, grad_values], -1).astype(
        jnp.bfloat16
    )
    vec = jnp.concatenate(
        [
            jnp.zeros((8, 128), f32),
            grad_gain_ffn.reshape(8, 128),
            jnp.concatenate([grad_gain_query, grad_gain_key], 0)[None],
            jnp.zeros((7, 128), f32),
        ],
        0,
    )
    grad_inputs, sum_qkv, sum_out, vec = last_part(
        tokens[:, 0].reshape(all_rows, width),
        grad_mid,
        normed_attn,
        jnp.stack([grad_projected[:, :1024], grad_projected[:, 1024:]]),
        attended_low,
        norm_gain_attn[None],
        vec,
        w_qkv,
    )
    own = lax.axis_index("rows") * 8 + lax.axis_index("ctx")
    results = (
        lax.dynamic_slice(vec[:8].reshape(1024), (own * 8,), (8,)),
        sum_qkv,
        lax.dynamic_slice(vec[16], (own,), (1,)),
        sum_out,
        lax.dynamic_slice(vec[8:16].reshape(1024), (own * 8,), (8,)),
        sum_gate_up,
        sum_down,
    )
    layer_shard = layer_out.astype(jnp.bfloat16).reshape(micro, 1, rows_dev, width)
    input_shard = grad_inputs.reshape(micro, 1, rows_dev, width)
    return (
        layer_shard,
        input_shard,
        results[0],
        results[1],
        results[2],
        results[3],
        results[4],
        results[5],
        results[6],
    )


def solution(mesh):
    placed = (
        P(None, "rows", "ctx", None),
        P(None, "rows", "ctx", None),
        P(None, "rows", None),
        P(None, "rows", "ctx"),
        P(),
        P(),
        P(),
        P(),
        P(),
        P(),
        P(),
    )
    return jax.shard_map(
        local,
        mesh=mesh,
        in_specs=placed,
        out_specs=(
            P(None, "rows", "ctx", None),
            P(None, "rows", "ctx", None),
            P(("rows", "ctx")),
            P(("rows", "ctx"), None),
            P(("rows", "ctx")),
            P(("rows", "ctx"), None),
            P(("rows", "ctx")),
            P(("rows", "ctx"), None),
            P(("rows", "ctx"), None),
        ),
        check_vma=False,
    )
```

```python
import functools

import jax
import jax.numpy as jnp
from jax import lax
from jax.experimental import pallas as pl
from jax.experimental.pallas import tpu as pltpu
from jax.sharding import PartitionSpec as P

MESH = pl.DeviceIdType.MESH
norm_eps = 1e-05
rope_theta = 1000000.0
f32 = jnp.float32
bf16 = jnp.bfloat16
VMEM_LIMIT = 64 * 2**20 - 2**18


class Place:
    def __init__(self):
        r = lax.axis_index("rows")
        k = lax.axis_index("ctx")
        self.x_hi = lax.div(r, 8)
        self.y = lax.rem(lax.div(r, 2), 4)
        self.core = lax.rem(r, 2)
        self.x_lo = lax.div(k, 4)
        self.z = lax.rem(k, 4)
        self.rows = r
        self.ctx = k
        self.bits = [
            self.x_hi,
            lax.rem(self.x_hi + self.x_lo, 2),
            lax.div(self.y, 2),
            lax.rem(lax.div(self.y, 2) + lax.rem(self.y, 2), 2),
            lax.div(self.z, 2),
            lax.rem(lax.div(self.z, 2) + lax.rem(self.z, 2), 2),
        ]

    def at(self, x_hi=None, x_lo=None, y=None, z=None, core=None):
        x_hi = self.x_hi if x_hi is None else x_hi
        x_lo = self.x_lo if x_lo is None else x_lo
        y = self.y if y is None else y
        z = self.z if z is None else z
        core = self.core if core is None else core
        return (x_hi * 8 + y * 2 + core, x_lo * 4 + z)

    def partner(self):
        return self.at(core=1 - self.core)

    def neighbour(self, dim):
        if dim == 0:
            return self.at(x_hi=1 - self.x_hi, x_lo=1 - self.x_lo)
        if dim == 1:
            return self.at(x_lo=1 - self.x_lo)
        if dim == 2:
            return self.at(y=3 - self.y)
        if dim == 3:
            return self.at(y=self.y + 1 - 2 * lax.rem(self.y, 2))
        if dim == 4:
            return self.at(z=3 - self.z)
        return self.at(z=self.z + 1 - 2 * lax.rem(self.z, 2))


def gray(v):
    return v ^ (v >> 1)


def chip_number(x_hi, x_lo, y, z):
    return gray(2 * x_hi + x_lo) * 16 + gray(y) * 4 + gray(z)


def slot_of(number, s):
    turned = number << s
    return (turned & 63) | (turned >> 6)


HELD_AT = [64 - (64 >> t) for t in range(7)]


class Scatter:
    def __init__(self, place, first, held, send_sems, recv_sems, per):
        self.place = place
        self.first = first
        self.held = held
        self.send_sems = send_sems
        self.recv_sems = recv_sems
        self.per = per

    def part(self, s, t, which):
        half = 32 >> t
        if t == 0:
            return self.first, which * half
        return self.held, HELD_AT[t - 1] + which * half

    def copy(self, s, t):
        half = 32 >> t
        dim = (s + t) % 6
        ref, start = self.part(s, t, 1 - self.place.bits[dim])
        return pltpu.make_async_remote_copy(
            src_ref=ref.at[s, pl.ds(start, half)],
            dst_ref=self.held.at[s, pl.ds(HELD_AT[t], half)],
            send_sem=self.send_sems.at[s, t],
            recv_sem=self.recv_sems.at[s, t],
            device_id=self.place.neighbour(dim),
            device_id_type=MESH,
        )

    def send(self, s, t):
        self.copy(s, t).start()

    def take(self, s, t):
        self.copy(s, t).wait_recv()
        half = 32 >> t
        ref, start = self.part(s, t, self.place.bits[(s + t) % 6])
        per = min(self.per, half)

        def body(i, carry):
            for j in range(per):
                at = i * per + j
                self.held[s, HELD_AT[t] + at] = (
                    self.held[s, HELD_AT[t] + at].astype(f32) + ref[s, start + at].astype(f32)
                ).astype(bf16)
            return carry

        lax.fori_loop(0, half // per, body, 0)
        self.send(s, t + 1)

    def last(self, s):
        self.copy(s, 5).wait_recv()
        ref, start = self.part(s, 5, self.place.bits[(s + 5) % 6])
        return self.held[s, HELD_AT[5]].astype(f32) + ref[s, start].astype(f32)

    def sent(self):
        for s in range(6):
            for t in range(6):
                self.copy(s, t).wait_send()


def greet(devices):
    barrier = pltpu.get_barrier_semaphore()
    for device in devices:
        pl.semaphore_signal(barrier, inc=1, device_id=device, device_id_type=MESH)
    pl.semaphore_wait(barrier, len(devices))


def greet_all(place, devices):
    barrier = pltpu.get_barrier_semaphore()
    targets = down_targets(place)
    for device in devices + targets[1:]:
        pl.semaphore_signal(barrier, inc=1, device_id=device, device_id_type=MESH)
    swapped = place.x_hi != place.core
    count = len(devices) + 3

    @pl.when(swapped)
    def _():
        pl.semaphore_signal(barrier, inc=1, device_id=targets[0], device_id_type=MESH)
        pl.semaphore_wait(barrier, count + 1)

    @pl.when(jnp.logical_not(swapped))
    def _():
        pl.semaphore_wait(barrier, count)


def push(place, src, dst, send_sem, recv_sem, device):
    return pltpu.make_async_remote_copy(
        src_ref=src,
        dst_ref=dst,
        send_sem=send_sem,
        recv_sem=recv_sem,
        device_id=device,
        device_id_type=MESH,
    )


def down_targets(place):
    return [
        place.at(x_hi=place.core, core=place.x_hi, z=lax.rem(place.z + off, 4)) for off in range(4)
    ]


def dot(left, right):
    return jnp.dot(left, right, preferred_element_type=f32)


def dot_cols(left, right):
    return lax.dot_general(left, right, (((1,), (1,)), ((), ())), preferred_element_type=f32)


FF_HALF = 2304


def ffn_kernel(
    mid_ref,
    cot_ref,
    gain_ref,
    wgu_hbm,
    wd_hbm,
    out_ref,
    dmid_ref,
    ggain_ref,
    ggu_ref,
    gdn_ref,
    wgu,
    wd,
    nf,
    nft,
    dyb,
    h,
    ht,
    dgu,
    sum_own,
    sum_send,
    sum_recv,
    g_first,
    g_held,
    d_first,
    d_held,
    g_fin,
    g_in,
    d_acc,
    d_stage,
    d_in,
    w_sems,
    x_send,
    x_recv,
    g_send,
    g_recv,
    d_send,
    d_recv,
    f_send,
    f_recv,
):
    place = Place()
    core = place.core
    loads = []
    for i in range(3):
        at = pl.multiple_of(core * FF_HALF + 768 * i, 256)
        loads.append(
            [
                pltpu.make_async_copy(
                    wgu_hbm.at[:, pl.ds(at, 768)], wgu.at[:, pl.ds(768 * i, 768)], w_sems.at[3 * i]
                ),
                pltpu.make_async_copy(
                    wgu_hbm.at[:, pl.ds(pl.multiple_of(4608 + at, 256), 768)],
                    wgu.at[:, pl.ds(FF_HALF + 768 * i, 768)],
                    w_sems.at[3 * i + 1],
                ),
                pltpu.make_async_copy(
                    wd_hbm.at[pl.ds(at, 768)], wd.at[pl.ds(768 * i, 768)], w_sems.at[3 * i + 2]
                ),
            ]
        )
        for copy in loads[-1]:
            copy.start()

    greet_all(place, [place.partner()] + [place.neighbour(dim) for dim in range(6)])

    partner = place.partner()
    to_dy = push(place, cot_ref, dyb.at[pl.ds(256, 256)], x_send.at[0], x_recv.at[0], partner)
    to_dy.start()
    mid = mid_ref[...]
    scale = lax.rsqrt(jnp.mean(mid * mid, axis=-1, keepdims=True) + norm_eps)
    nf[pl.ds(0, 256), :] = (mid * scale * gain_ref[...]).astype(bf16)
    dyb[pl.ds(0, 256), :] = cot_ref[...]
    to_nf = push(
        place,
        nf.at[pl.ds(0, 256)],
        nf.at[pl.ds(256, 256)],
        x_send.at[1],
        x_recv.at[1],
        partner,
    )
    to_nf.start()
    to_dy.wait_recv()
    to_nf.wait_recv()
    for i in range(2):
        nft[:, pl.ds(256 * i, 256)] = nf[pl.ds(256 * i, 256), :].T

    for i in range(3):
        for copy in loads[i]:
            copy.wait()

        def units(j, carry, i=i):
            at = pl.multiple_of(768 * i + 256 * j, 256)
            gate = dot(nf[...], wgu[:, pl.ds(at, 256)])
            upward = dot(nf[...], wgu[:, pl.ds(pl.multiple_of(FF_HALF + at, 256), 256)])
            grad_hidden = dot_cols(dyb[...], wd[pl.ds(at, 256), :])
            sigma = 1.0 / (1.0 + jnp.exp(-gate))
            silu = gate * sigma
            hidden = (silu * upward).astype(bf16)
            h[:, pl.ds(at, 256)] = hidden
            ht[pl.ds(at, 256), :] = hidden.T
            dgu[:, pl.ds(at, 256)] = (
                grad_hidden * upward * (sigma + silu * (1.0 - sigma))
            ).astype(bf16)
            dgu[:, pl.ds(pl.multiple_of(FF_HALF + at, 256), 256)] = (grad_hidden * silu).astype(bf16)
            return carry

        lax.fori_loop(0, 3, units, 0)

    down = Scatter(place, d_first, d_held, d_send, d_recv, 4)
    for block in range(3):

        def down_cols(z, carry, block=block):
            part = dot(
                ht[pl.ds(768 * block, 768), :], dyb[:, pl.ds(pl.multiple_of(256 * z, 256), 256)]
            )
            z_number = 2 * lax.div(z, 2) + lax.rem(lax.div(z, 2) + lax.rem(z, 2), 2)
            for i in range(16):
                q = 16 * block + i
                y, core_to, x_lo, rg = q // 12, (q // 6) % 2, (q // 3) % 2, q % 3
                number = chip_number(core_to, x_lo, y, 0) + z_number
                for ch in range(2):
                    s = 2 * rg + ch
                    turned = number * (1 << s)
                    slot = lax.rem(turned, 64) + lax.div(turned, 64)
                    d_first[s, slot] = part[48 * i : 48 * i + 48, 128 * ch : 128 * ch + 128].astype(
                        bf16
                    )
            return carry

        lax.fori_loop(0, 4, down_cols, 0)
    for s in range(6):
        down.send(s, 0)

    both = Scatter(place, g_first, g_held, g_send, g_recv, 2)
    for s in range(6):

        def gate_cols(j, carry, s=s):
            cols = dgu[:, pl.ds(pl.multiple_of(768 * s + 256 * j, 256), 256)]
            for x_hi in range(2):
                part = dot(nft[pl.ds(512 * x_hi, 512), :], cols)
                part = part.reshape(4, 2, 8, 8, 256)
                for y in range(4):
                    for x_lo in range(2):
                        for z in range(4):
                            slot = slot_of(chip_number(x_hi, x_lo, y, z), s)
                            piece = part[y, :, 4 * x_lo + z].reshape(16, 256)
                            g_first[s, slot, :, pl.ds(pl.multiple_of(256 * j, 256), 256)] = piece.astype(
                                bf16
                            )
            return carry

        lax.fori_loop(0, 3, gate_cols, 0)
        both.send(s, 0)

    def out_cols(j, carry):
        at = pl.ds(pl.multiple_of(256 * j, 256), 256)
        part = dot(h[...], wd[:, at])
        sum_own[:, at] = part[:256]
        sum_send[0, :, at] = part[256:].astype(bf16)
        return carry

    lax.fori_loop(0, 4, out_cols, 0)
    to_out = push(place, sum_send.at[0], sum_recv.at[0], x_send.at[2], x_recv.at[2], partner)
    to_out.start()

    def back_cols(j, carry):
        at = pl.ds(pl.multiple_of(256 * j, 256), 256)
        part = dot_cols(dgu[...], wgu[at, :])
        dmid_ref[:, at] = part[:256]
        sum_send[1, :, at] = part[256:].astype(bf16)
        return carry

    lax.fori_loop(0, 4, back_cols, 0)
    to_back = push(place, sum_send.at[1], sum_recv.at[1], x_send.at[3], x_recv.at[3], partner)
    to_back.start()
    to_out.wait_recv()
    out_ref[...] = (mid_ref[...] + sum_own[...] + sum_recv[0].astype(f32)).astype(bf16)
    to_back.wait_recv()
    mid = mid_ref[...]
    scale = lax.rsqrt(jnp.mean(mid * mid, axis=-1, keepdims=True) + norm_eps)
    normed = mid * scale
    grad_nffn = dmid_ref[...] + sum_recv[1].astype(f32)
    ggain_ref[...] = jnp.sum(grad_nffn * normed, axis=0, keepdims=True)
    grad_e = grad_nffn * gain_ref[...]
    dmid_ref[...] = cot_ref[...].astype(f32) + scale * (
        grad_e - normed * jnp.mean(grad_e * normed, axis=-1, keepdims=True)
    )

    for t in range(5):
        for s in range(6):
            down.take(s, t)
        for s in range(6):
            both.take(s, t)
    finish_down(place, down, d_acc, d_stage, d_in, f_send, f_recv, gdn_ref)
    for s in range(6):
        total = both.last(s)
        g_fin[0, s] = total[:8]
        g_fin[1, s] = total[8:]
    swap = push(place, g_fin.at[1 - core], g_in, x_send.at[4], x_recv.at[4], partner)
    swap.start()
    for s in range(6):
        base = (s // 3) * 4608 + (s % 3) * 768
        at = pl.multiple_of(base + core * FF_HALF, 256)
        ggu_ref[:, pl.ds(at, 768)] = g_fin[core, s]
    swap.wait_recv()
    for s in range(6):
        base = (s // 3) * 4608 + (s % 3) * 768
        at = pl.multiple_of(base + (1 - core) * FF_HALF, 256)
        ggu_ref[:, pl.ds(at, 768)] = g_in[s]
    to_dy.wait_send()
    to_nf.wait_send()
    to_out.wait_send()
    to_back.wait_send()
    swap.wait_send()
    down.sent()
    both.sent()


def finish_down(place, down, d_acc, d_stage, d_in, f_send, f_recv, gdn_ref):
    for s in range(6):
        d_acc[pl.ds(48 * (s // 2), 48), pl.ds(128 * (s % 2), 128)] = down.last(s)
    for z in range(4):
        d_stage[z, pl.ds(0, 36), :] = d_acc[pl.ds(36 * z, 36), :]
        d_stage[z, pl.ds(36, 4), :] = jnp.zeros((4, 256), f32)
    targets = down_targets(place)
    swapped = place.x_hi != place.core
    moves = []
    for off in range(4):
        moves.append(
            push(
                place,
                d_stage.at[lax.rem(place.z + off, 4)],
                d_in.at[place.z],
                f_send.at[off],
                f_recv.at[off],
                targets[off],
            )
        )
    for off in range(1, 4):
        moves[off].start()

    @pl.when(swapped)
    def _():
        moves[0].start()
        moves[0].wait_recv()

    @pl.when(jnp.logical_not(swapped))
    def _():
        d_in[place.z] = d_stage[place.z]

    for off in range(1, 4):
        moves[off].wait_recv()
    for z in range(4):
        gdn_ref[:, pl.ds(256 * z, 256)] = d_in[z, pl.ds(0, 36), :]
    for off in range(1, 4):
        moves[off].wait_send()

    @pl.when(swapped)
    def _():
        moves[0].wait_send()


def ffn(mid, cot, gain, w_gate_up, w_down):
    vmem = pl.BlockSpec(memory_space=pltpu.VMEM)
    hbm = pl.BlockSpec(memory_space=pl.ANY)
    dma = pltpu.SemaphoreType.DMA
    return pl.pallas_call(
        ffn_kernel,
        out_shape=(
            jax.ShapeDtypeStruct((256, 1024), bf16),
            jax.ShapeDtypeStruct((256, 1024), f32),
            jax.ShapeDtypeStruct((1, 1024), f32),
            jax.ShapeDtypeStruct((8, 9216), f32),
            jax.ShapeDtypeStruct((36, 1024), f32),
        ),
        in_specs=[vmem, vmem, vmem, hbm, hbm],
        out_specs=(vmem, vmem, vmem, vmem, vmem),
        scratch_shapes=[
            pltpu.VMEM((1024, 4608), bf16),
            pltpu.VMEM((FF_HALF, 1024), bf16),
            pltpu.VMEM((512, 1024), bf16),
            pltpu.VMEM((1024, 512), bf16),
            pltpu.VMEM((512, 1024), bf16),
            pltpu.VMEM((512, FF_HALF), bf16),
            pltpu.VMEM((FF_HALF, 512), bf16),
            pltpu.VMEM((512, 4608), bf16),
            pltpu.VMEM((256, 1024), f32),
            pltpu.VMEM((2, 256, 1024), bf16),
            pltpu.VMEM((2, 256, 1024), bf16),
            pltpu.VMEM((6, 64, 16, 768), bf16),
            pltpu.VMEM((6, 63, 16, 768), bf16),
            pltpu.VMEM((6, 64, 48, 128), bf16),
            pltpu.VMEM((6, 63, 48, 128), bf16),
            pltpu.VMEM((2, 6, 8, 768), f32),
            pltpu.VMEM((6, 8, 768), f32),
            pltpu.VMEM((144, 256), f32),
            pltpu.VMEM((4, 40, 256), f32),
            pltpu.VMEM((4, 40, 256), f32),
            dma((9,)),
            dma((5,)),
            dma((5,)),
            dma((6, 6)),
            dma((6, 6)),
            dma((6, 6)),
            dma((6, 6)),
            dma((4,)),
            dma((4,)),
        ],
        compiler_params=pltpu.CompilerParams(
            collective_id=0, has_side_effects=True, vmem_limit_bytes=VMEM_LIMIT
        ),
        name="feed_forward",
    )(mid, cot, gain, w_gate_up, w_down)


def lanes(rows):
    return lax.broadcasted_iota(jnp.int32, (rows, 128), 1)


def turn_heads(values):
    low = lax.rem(lanes(values.shape[0]), 64) < 32
    return jnp.where(low, pltpu.roll(values, 96, 1), pltpu.roll(values, 32, 1))


def head_mean(values):
    i = lax.broadcasted_iota(jnp.int32, (128, 128), 0)
    j = lax.broadcasted_iota(jnp.int32, (128, 128), 1)
    ones = jnp.where(lax.div(i, 64) == lax.div(j, 64), 1.0 / 64, 0.0).astype(bf16)
    high = values.astype(bf16)
    rest = (values - high.astype(f32)).astype(bf16)
    return dot(high, ones) + dot(rest, ones)


def gain_tiles(qk_gain):
    swapped = pltpu.roll(qk_gain, 64, 1)
    low = lax.broadcasted_iota(jnp.int32, (1, 128), 1) < 64
    return jnp.where(low, qk_gain, swapped), jnp.where(low, swapped, qk_gain)


def head_rows(values):
    low = lanes(values.shape[0]) < 64
    zero = jnp.zeros_like(values)
    return jnp.concatenate([jnp.where(low, values, zero), jnp.where(low, zero, values)], 0)


class Exchange:
    def __init__(self, place, out, into, send_sems, recv_sems):
        self.place = place
        self.out = out
        self.into = into
        self.send_sems = send_sems
        self.recv_sems = recv_sems

    def copy(self, m, off):
        j = lax.rem(self.place.ctx + off, 8)
        return push(
            self.place,
            self.out.at[m, j],
            self.into.at[m, self.place.ctx],
            self.send_sems.at[m, off - 1],
            self.recv_sems.at[m, off - 1],
            (self.place.rows, j),
        )

    def send(self, m):
        for off in range(1, 8):
            self.copy(m, off).start()
        self.into[m, self.place.ctx] = self.out[m, self.place.ctx]

    def arrived(self, m):
        for off in range(1, 8):
            self.copy(m, off).wait_recv()

    def sent(self):
        for m in range(2):
            for off in range(1, 8):
                self.copy(m, off).wait_send()


def ctx_peers(place):
    return [(place.rows, lax.rem(place.ctx + off, 8)) for off in range(1, 8)]


def document_edges(bounds_ref, m):
    index = lax.broadcasted_iota(jnp.int32, (1, 1024), 1)
    start = jnp.zeros((1, 1024), jnp.int32)
    end = jnp.full((1, 1024), 1024, jnp.int32)
    for k in range(1, 4):
        cut = bounds_ref[m, 0, k]
        start = jnp.where(index >= cut, cut, start)
        end = jnp.where(index < bounds_ref[m, 0, 4 - k], bounds_ref[m, 0, 4 - k], end)
    return start, end


def attention_kernel(
    bounds_ref,
    x_ref,
    cos_ref,
    sin_ref,
    gain_ref,
    qk_gain_ref,
    w_qkv_hbm,
    w_out_hbm,
    mid_ref,
    na_ref,
    att_ref,
    proj_ref,
    qkv_ref,
    o_ref,
    l_ref,
    w_qkv,
    w_out,
    q_out,
    a_out,
    a_in,
    q2,
    kk,
    vo,
    w_sems,
    q_send,
    q_recv,
    a_send,
    a_recv,
):
    place = Place()
    loads = [
        pltpu.make_async_copy(w_qkv_hbm, w_qkv, w_sems.at[0]),
        pltpu.make_async_copy(w_out_hbm, w_out, w_sems.at[1]),
    ]
    for load in loads:
        load.start()
    greet(ctx_peers(place))
    heads_out = Exchange(place, q_out, qkv_ref, q_send, q_recv)
    heads_back = Exchange(place, a_out, a_in, a_send, a_recv)

    inputs = x_ref[...].astype(f32)
    scale = lax.rsqrt(jnp.mean(inputs * inputs, axis=-1, keepdims=True) + norm_eps)
    na_ref[...] = (inputs * scale * gain_ref[...]).astype(bf16)
    loads[0].wait()
    gain_q, gain_k = gain_tiles(qk_gain_ref[...])
    low = lanes(256) < 64

    def turned(tile, gain):
        u = tile * lax.rsqrt(head_mean(tile * tile) + norm_eps) * gain
        return u * cos_ref[...] + turn_heads(u) * sin_ref[...]

    for i in range(4):
        pair = dot(na_ref[...], w_qkv[:, pl.ds(256 * i, 256)])
        proj_ref[:, pl.ds(256 * i, 256)] = pair
        for j in range(2):
            tile = turned(pair[:, 128 * j : 128 * j + 128], gain_q) * 0.125
            for m in range(2):
                q_out[m, 2 * i + j, :, pl.ds(0, 128)] = tile[128 * m : 128 * m + 128].astype(bf16)
    for i in range(2):
        key_pair = dot(na_ref[...], w_qkv[:, pl.ds(1024 + 256 * i, 256)])
        value_pair = dot(na_ref[...], w_qkv[:, pl.ds(1536 + 256 * i, 256)])
        proj_ref[:, pl.ds(1024 + 256 * i, 256)] = key_pair
        for j in range(2):
            key = turned(key_pair[:, 128 * j : 128 * j + 128], gain_k)
            value = value_pair[:, 128 * j : 128 * j + 128]
            first = jnp.where(low, key, pltpu.roll(value, 64, 1)).astype(bf16)
            second = jnp.where(low, pltpu.roll(key, 64, 1), value).astype(bf16)
            for m in range(2):
                rows = slice(128 * m, 128 * m + 128)
                q_out[m, 4 * i + 2 * j, :, pl.ds(128, 128)] = first[rows]
                q_out[m, 4 * i + 2 * j + 1, :, pl.ds(128, 128)] = second[rows]
    for m in range(2):
        heads_out.send(m)

    for m in range(2):
        heads_out.arrived(m)
        ends = document_edges(bounds_ref, m)[1]
        for b in range(4):
            query = qkv_ref[m, pl.ds(2 * b, 2), :, pl.ds(0, 128)].reshape(256, 128)
            both = qkv_ref[m, pl.ds(2 * b, 2), :, pl.ds(128, 128)].reshape(256, 128).astype(f32)
            swapped = pltpu.roll(both, 64, 1)
            q2[b] = head_rows(query)
            kk[b] = jnp.where(low, both, swapped).astype(bf16)
            vo[b] = jnp.where(low, swapped, 1.0).astype(bf16)
        for qb in range(4):
            acc = jnp.zeros((512, 128), f32)
            for kb in range(qb + 1):
                scores = dot_cols(q2[qb], kk[kb])
                t = 256 * qb + lax.rem(lax.broadcasted_iota(jnp.int32, (512, 256), 0), 256)
                keep = t < ends[:, 256 * kb : 256 * kb + 256]
                if kb == qb:
                    s = 256 * kb + lax.broadcasted_iota(jnp.int32, (512, 256), 1)
                    keep = keep & (s <= t)
                weights = jnp.where(keep, jnp.exp(scores), 0.0).astype(bf16)
                acc = acc + dot(weights, vo[kb])
            total = pltpu.roll(acc, 64, 1)
            head0 = acc[:256]
            head1 = pltpu.roll(acc[256:], 64, 1)
            denominator = jnp.where(low, total[:256], acc[256:])
            out = jnp.where(low, head0, head1) / denominator
            o_ref[m, pl.ds(256 * qb, 256), :] = out
            log_total = jnp.log(denominator).T
            l_ref[m, pl.ds(0, 1), pl.ds(256 * qb, 256)] = log_total[0:1]
            l_ref[m, pl.ds(1, 1), pl.ds(256 * qb, 256)] = log_total[64:65]
            for half in range(2):
                a_out[m, 2 * qb + half] = out[128 * half : 128 * half + 128].astype(bf16)
        heads_back.send(m)
    loads[1].wait()
    for m in range(2):
        heads_back.arrived(m)
        for j in range(8):
            att_ref[pl.ds(128 * m, 128), pl.ds(128 * j, 128)] = a_in[m, j]
    mid_ref[...] = x_ref[...].astype(f32) + dot(att_ref[...], w_out[...])
    heads_out.sent()
    heads_back.sent()


def attention(bounds, x, cosine, sine, gain, qk_gain, w_qkv, w_out):
    vmem = pl.BlockSpec(memory_space=pltpu.VMEM)
    hbm = pl.BlockSpec(memory_space=pl.ANY)
    smem = pl.BlockSpec(memory_space=pltpu.SMEM)
    dma = pltpu.SemaphoreType.DMA
    return pl.pallas_call(
        attention_kernel,
        out_shape=(
            jax.ShapeDtypeStruct((256, 1024), f32),
            jax.ShapeDtypeStruct((256, 1024), bf16),
            jax.ShapeDtypeStruct((256, 1024), bf16),
            jax.ShapeDtypeStruct((256, 1536), f32),
            jax.ShapeDtypeStruct((2, 8, 128, 256), bf16),
            jax.ShapeDtypeStruct((2, 1024, 128), f32),
            jax.ShapeDtypeStruct((2, 2, 1024), f32),
        ),
        in_specs=[smem] + [vmem] * 5 + [hbm] * 2,
        out_specs=(vmem,) * 7,
        scratch_shapes=[
            pltpu.VMEM((1024, 2048), bf16),
            pltpu.VMEM((1024, 1024), bf16),
            pltpu.VMEM((2, 8, 128, 256), bf16),
            pltpu.VMEM((2, 8, 128, 128), bf16),
            pltpu.VMEM((2, 8, 128, 128), bf16),
            pltpu.VMEM((4, 512, 128), bf16),
            pltpu.VMEM((4, 256, 128), bf16),
            pltpu.VMEM((4, 256, 128), bf16),
            dma((2,)),
            dma((2, 7)),
            dma((2, 7)),
            dma((2, 7)),
            dma((2, 7)),
        ],
        compiler_params=pltpu.CompilerParams(
            collective_id=2, has_side_effects=True, vmem_limit_bytes=VMEM_LIMIT
        ),
        name="attention_forward",
    )(bounds, x, cosine, sine, gain, qk_gain, w_qkv, w_out)


def reorder_store(part, first, s, x_hi, at, width):
    part = part.reshape(4, 2, 8, 8, width)
    for y in range(4):
        for x_lo in range(2):
            for z in range(4):
                slot = slot_of(chip_number(x_hi, x_lo, y, z), s)
                first[s, slot, :, at] = part[y, :, 4 * x_lo + z].reshape(16, width).astype(bf16)


def backward_kernel(
    bounds_ref,
    x_ref,
    cos_ref,
    sin_ref,
    gain_ref,
    qk_gain_ref,
    dmid_ref,
    na_ref,
    att_ref,
    proj_ref,
    qkv_ref,
    o_ref,
    l_ref,
    vec_ref,
    w_qkv_hbm,
    w_out_hbm,
    gtok_ref,
    gqkv_ref,
    gout_ref,
    vec_out,
    w_qkv,
    w_out,
    do_out,
    do_in,
    g_out,
    g_in,
    q2,
    do2,
    kk,
    vv,
    kt,
    delta,
    dq,
    dp,
    xin,
    dpin,
    dmin,
    dm_own,
    nat,
    attt,
    cols,
    q_first,
    q_held,
    q_fin,
    q_in,
    vec,
    vec_in,
    w_sems,
    do_send,
    do_recv,
    g_send,
    g_recv,
    x_send,
    x_recv,
    q_send,
    q_recv,
    v_send,
    v_recv,
):
    place = Place()
    core = place.core
    partner = place.partner()
    loads = [
        pltpu.make_async_copy(w_out_hbm, w_out, w_sems.at[0]),
        pltpu.make_async_copy(w_qkv_hbm, w_qkv, w_sems.at[1]),
    ]
    for load in loads:
        load.start()
    greet([partner] + [place.neighbour(dim) for dim in range(6)] + ctx_peers(place))
    for half in range(2):
        dm_own[half] = dmid_ref[:, pl.ds(512 * half, 512)].astype(bf16)
    moves = [
        push(place, na_ref, xin.at[0], x_send.at[0], x_recv.at[0], partner),
        push(place, att_ref, xin.at[1], x_send.at[1], x_recv.at[1], partner),
        push(place, dm_own.at[1 - core], dmin, x_send.at[2], x_recv.at[2], partner),
    ]
    for move in moves:
        move.start()

    grads_out = Exchange(place, do_out, do_in, do_send, do_recv)
    grads_back = Exchange(place, g_out, g_in, g_send, g_recv)
    loads[0].wait()
    for i in range(4):
        pair = dot_cols(dm_own[0], w_out[pl.ds(256 * i, 256), pl.ds(0, 512)]) + dot_cols(
            dm_own[1], w_out[pl.ds(256 * i, 256), pl.ds(512, 512)]
        )
        for j in range(2):
            for m in range(2):
                do_out[m, 2 * i + j] = pair[
                    128 * m : 128 * m + 128, 128 * j : 128 * j + 128
                ].astype(bf16)
    for m in range(2):
        grads_out.send(m)

    low = lanes(256) < 64
    for m in range(2):
        grads_out.arrived(m)
        starts = document_edges(bounds_ref, m)[0]
        for b in range(4):
            query = qkv_ref[m, pl.ds(2 * b, 2), :, pl.ds(0, 128)].reshape(256, 128)
            both = qkv_ref[m, pl.ds(2 * b, 2), :, pl.ds(128, 128)].reshape(256, 128).astype(f32)
            grad = do_in[m, pl.ds(2 * b, 2)].reshape(256, 128)
            swapped = pltpu.roll(both, 64, 1)
            key_pair = jnp.where(low, both, swapped)
            q2[b] = head_rows(query)
            do2[b] = head_rows(grad)
            kk[b] = key_pair.astype(bf16)
            vv[b] = jnp.where(low, swapped, both).astype(bf16)
            kt[b] = key_pair.T.astype(bf16)
            inner = (grad.astype(f32) * o_ref[m, pl.ds(256 * b, 256), :]).T
            delta[b, :, pl.ds(0, 256)] = jnp.sum(inner[:64], axis=0, keepdims=True)
            delta[b, :, pl.ds(256, 256)] = jnp.sum(inner[64:], axis=0, keepdims=True)
        for kb in range(4):
            grad_key = jnp.zeros((256, 128), f32)
            grad_value = jnp.zeros((256, 128), f32)
            for qb in range(kb, 4):
                scores = dot_cols(kk[kb], q2[qb])
                log_total = jnp.concatenate(
                    [l_ref[m, pl.ds(i, 1), pl.ds(256 * qb, 256)] for i in range(2)], 1
                )
                start = starts[:, 256 * qb : 256 * qb + 256]
                s = 256 * kb + lax.broadcasted_iota(jnp.int32, (256, 512), 0)
                keep = s >= jnp.concatenate([start, start], 1)
                if kb == qb:
                    t = 256 * qb + lax.rem(lax.broadcasted_iota(jnp.int32, (256, 512), 1), 256)
                    keep = keep & (s <= t)
                probs = jnp.where(keep, jnp.exp(scores - log_total), 0.0)
                grad_probs = dot_cols(vv[kb], do2[qb])
                grad_scores = (probs * (grad_probs - delta[qb])).astype(bf16)
                grad_value = grad_value + dot(probs.astype(bf16), do2[qb])
                grad_key = grad_key + dot(grad_scores, q2[qb])
                grad_query = dot(kt[kb], grad_scores)
                if kb == 0:
                    dq[qb] = grad_query[:64]
                else:
                    dq[qb] = dq[qb] + grad_query[:64]
            grad_key = grad_key + pltpu.roll(grad_key, 64, 1)
            grad_value = grad_value + pltpu.roll(grad_value, 64, 1)
            tile = jnp.where(low, grad_key, grad_value).astype(bf16)
            for half in range(2):
                g_out[m, 2 * kb + half, :, pl.ds(128, 128)] = tile[128 * half : 128 * half + 128]
        for qb in range(4):
            tile = (
                (jnp.concatenate([dq[qb, :, pl.ds(0, 256)], dq[qb, :, pl.ds(256, 256)]], 0) * 0.125)
                .T.astype(bf16)
            )
            for half in range(2):
                g_out[m, 2 * qb + half, :, pl.ds(0, 128)] = tile[128 * half : 128 * half + 128]
        grads_back.send(m)

    nat[:, pl.ds(0, 256)] = na_ref[...].T
    attt[:, pl.ds(0, 256)] = att_ref[...].T
    cols[pl.ds(0, 256), pl.ds(1024, 512)] = dm_own[core]
    for move in moves:
        move.wait_recv()
    nat[:, pl.ds(256, 256)] = xin[0].T
    attt[:, pl.ds(256, 256)] = xin[1].T
    cols[pl.ds(256, 256), pl.ds(1024, 512)] = dmin[...]
    quad = Scatter(place, q_first, q_held, q_send, q_recv, 4)

    def projection_cols(s):
        left = nat if s < 4 else attt
        for x_hi in range(2):
            part = dot(left[pl.ds(512 * x_hi, 512), :], cols[:, pl.ds(256 * s, 256)])
            reorder_store(part, q_first, s, x_hi, slice(None), 256)
        quad.send(s, 0)

    for s in range(4, 6):
        projection_cols(s)

    gain_q, gain_k = gain_tiles(qk_gain_ref[...])
    for m in range(2):
        grads_back.arrived(m)

    def both_rows(j, at):
        return jnp.concatenate([g_in[m, j, :, pl.ds(at, 128)] for m in range(2)], 0).astype(f32)

    def head_back(grad, value, gain):
        grad = grad * cos_ref[...] + turn_heads(grad * sin_ref[...])
        scale = lax.rsqrt(head_mean(value * value) + norm_eps)
        normed = value * scale
        grad_e = grad * gain
        gain_grad = jnp.sum(grad * normed, axis=0, keepdims=True)
        return scale * (grad_e - normed * head_mean(grad_e * normed)), gain_grad

    sum_q = jnp.zeros((1, 128), f32)
    sum_k = jnp.zeros((1, 128), f32)
    for j in range(8):
        back, part = head_back(both_rows(j, 0), proj_ref[:, pl.ds(128 * j, 128)], gain_q)
        dp[0, :, pl.ds(128 * j, 128)] = back.astype(bf16)
        sum_q = sum_q + part
    for i in range(4):
        first = both_rows(2 * i, 128)
        second = both_rows(2 * i + 1, 128)
        grad_key = jnp.where(low, first, pltpu.roll(second, 64, 1))
        grad_value = jnp.where(low, pltpu.roll(first, 64, 1), second)
        back, part = head_back(grad_key, proj_ref[:, pl.ds(1024 + 128 * i, 128)], gain_k)
        dp[1, :, pl.ds(128 * i, 128)] = back.astype(bf16)
        dp[1, :, pl.ds(512 + 128 * i, 128)] = grad_value.astype(bf16)
        sum_k = sum_k + part
    move = push(place, dp.at[1 - core], dpin, x_send.at[3], x_recv.at[3], partner)
    move.start()
    moves.append(move)
    sum_q = sum_q + pltpu.roll(sum_q, 64, 1)
    sum_k = sum_k + pltpu.roll(sum_k, 64, 1)
    vec[0, pl.ds(8, 8), :] = vec_ref[...]
    vec[0, pl.ds(16, 8), :] = jnp.zeros((8, 128), f32)
    vec[0, pl.ds(16, 1), :] = jnp.where(
        lax.broadcasted_iota(jnp.int32, (1, 128), 1) < 64, sum_q, sum_k
    )
    cols[pl.ds(0, 256), pl.ds(0, 1024)] = dp[core]
    move.wait_recv()
    cols[pl.ds(256, 256), pl.ds(0, 1024)] = dpin[...]
    for s in range(4):
        projection_cols(s)

    loads[1].wait()
    inputs = x_ref[...].astype(f32)
    scale = lax.rsqrt(jnp.mean(inputs * inputs, axis=-1, keepdims=True) + norm_eps)
    normed = inputs * scale
    grad_n = dot_cols(dp[0], w_qkv[:, pl.ds(0, 1024)]) + dot_cols(dp[1], w_qkv[:, pl.ds(1024, 1024)])
    gain_grad = jnp.sum(grad_n * normed, axis=0, keepdims=True)
    grad_e = grad_n * gain_ref[...]
    gtok_ref[...] = dmid_ref[...] + scale * (
        grad_e - normed * jnp.mean(grad_e * normed, axis=-1, keepdims=True)
    )
    for i in range(8):
        vec[0, pl.ds(i, 1), :] = gain_grad[:, 128 * i : 128 * i + 128]

    def vec_move(step):
        device = place.neighbour(step) if step < 6 else partner
        return push(place, vec.at[step], vec_in.at[step], v_send.at[step], v_recv.at[step], device)

    vec_move(0).start()
    for t in range(5):
        for s in range(6):
            quad.take(s, t)
        vec_move(t).wait_recv()
        vec[t + 1] = vec[t] + vec_in[t]
        vec_move(t + 1).start()
    for s in range(6):
        total = quad.last(s)
        q_fin[0, s] = total[:8]
        q_fin[1, s] = total[8:]
    swap = push(place, q_fin.at[1 - core], q_in, x_send.at[4], x_recv.at[4], partner)
    swap.start()
    vec_move(5).wait_recv()
    vec[6] = vec[5] + vec_in[5]
    vec_move(6).start()
    for s in range(4):
        gqkv_ref[:, pl.ds(pl.multiple_of(core * 1024 + 256 * s, 256), 256)] = q_fin[core, s]
    for s in range(4, 6):
        gout_ref[:, pl.ds(pl.multiple_of(core * 512 + 256 * (s - 4), 256), 256)] = q_fin[core, s]
    swap.wait_recv()
    for s in range(4):
        gqkv_ref[:, pl.ds(pl.multiple_of((1 - core) * 1024 + 256 * s, 256), 256)] = q_in[s]
    for s in range(4, 6):
        gout_ref[:, pl.ds(pl.multiple_of((1 - core) * 512 + 256 * (s - 4), 256), 256)] = q_in[s]
    vec_move(6).wait_recv()
    vec_out[...] = vec[6] + vec_in[6]
    for move in moves:
        move.wait_send()
    swap.wait_send()
    for step in range(7):
        vec_move(step).wait_send()
    quad.sent()
    grads_out.sent()
    grads_back.sent()


def backward(bounds, x, cosine, sine, gain, qk_gain, dmid, na, att, proj, qkv, o, l, vec, w_qkv, w_out):
    vmem = pl.BlockSpec(memory_space=pltpu.VMEM)
    hbm = pl.BlockSpec(memory_space=pl.ANY)
    smem = pl.BlockSpec(memory_space=pltpu.SMEM)
    dma = pltpu.SemaphoreType.DMA
    return pl.pallas_call(
        backward_kernel,
        out_shape=(
            jax.ShapeDtypeStruct((256, 1024), f32),
            jax.ShapeDtypeStruct((8, 2048), f32),
            jax.ShapeDtypeStruct((8, 1024), f32),
            jax.ShapeDtypeStruct((24, 128), f32),
        ),
        in_specs=[smem] + [vmem] * 13 + [hbm] * 2,
        out_specs=(vmem,) * 4,
        scratch_shapes=[
            pltpu.VMEM((1024, 2048), bf16),
            pltpu.VMEM((1024, 1024), bf16),
            pltpu.VMEM((2, 8, 128, 128), bf16),
            pltpu.VMEM((2, 8, 128, 128), bf16),
            pltpu.VMEM((2, 8, 128, 256), bf16),
            pltpu.VMEM((2, 8, 128, 256), bf16),
            pltpu.VMEM((4, 512, 128), bf16),
            pltpu.VMEM((4, 512, 128), bf16),
            pltpu.VMEM((4, 256, 128), bf16),
            pltpu.VMEM((4, 256, 128), bf16),
            pltpu.VMEM((4, 128, 256), bf16),
            pltpu.VMEM((4, 1, 512), f32),
            pltpu.VMEM((4, 64, 512), f32),
            pltpu.VMEM((2, 256, 1024), bf16),
            pltpu.VMEM((2, 256, 1024), bf16),
            pltpu.VMEM((256, 1024), bf16),
            pltpu.VMEM((256, 512), bf16),
            pltpu.VMEM((2, 256, 512), bf16),
            pltpu.VMEM((1024, 512), bf16),
            pltpu.VMEM((1024, 512), bf16),
            pltpu.VMEM((512, 1536), bf16),
            pltpu.VMEM((6, 64, 16, 256), bf16),
            pltpu.VMEM((6, 63, 16, 256), bf16),
            pltpu.VMEM((2, 6, 8, 256), f32),
            pltpu.VMEM((6, 8, 256), f32),
            pltpu.VMEM((7, 24, 128), f32),
            pltpu.VMEM((7, 24, 128), f32),
            dma((2,)),
            dma((2, 7)),
            dma((2, 7)),
            dma((2, 7)),
            dma((2, 7)),
            dma((5,)),
            dma((5,)),
            dma((6, 6)),
            dma((6, 6)),
            dma((7,)),
            dma((7,)),
        ],
        compiler_params=pltpu.CompilerParams(
            collective_id=1, has_side_effects=True, vmem_limit_bytes=VMEM_LIMIT
        ),
        name="attention_backward",
    )(bounds, x, cosine, sine, gain, qk_gain, dmid, na, att, proj, qkv, o, l, vec, w_qkv, w_out)


def tables(positions):
    lane = jnp.arange(128, dtype=jnp.int32)
    freqs = rope_theta ** (-2.0 * (lane % 32).astype(f32) / 64)
    angles = positions.astype(f32)[:, None] * freqs[None, :]
    return jnp.cos(angles), jnp.sin(angles) * jnp.where(lane % 64 < 32, -1.0, 1.0)


def local(
    tokens,
    cotangent,
    bounds,
    positions,
    norm_gain_attn,
    w_qkv,
    qk_gain,
    w_out,
    norm_gain_ffn,
    w_gate_up,
    w_down,
):
    x = tokens.reshape(256, 1024)
    cot = cotangent.reshape(256, 1024)
    cosine, sine = tables(positions.reshape(256))
    mid, na, att, proj, qkv, o, l = attention(
        bounds, x, cosine, sine, norm_gain_attn[None], qk_gain[None], w_qkv, w_out
    )
    layer_out, dmid, gain_ffn, sum_gate_up, sum_down = ffn(
        mid, cot, norm_gain_ffn[None], w_gate_up, w_down
    )
    grad_tokens, sum_qkv, sum_out, vec = backward(
        bounds,
        x,
        cosine,
        sine,
        norm_gain_attn[None],
        qk_gain[None],
        dmid,
        na,
        att,
        proj,
        qkv,
        o,
        l,
        gain_ffn.reshape(8, 128),
        w_qkv,
        w_out,
    )
    own = lax.axis_index("rows") * 8 + lax.axis_index("ctx")
    return (
        layer_out.reshape(tokens.shape),
        grad_tokens.reshape(tokens.shape),
        lax.dynamic_slice(vec[:8].reshape(1024), (own * 8,), (8,)),
        sum_qkv,
        lax.dynamic_slice(vec[16], (own,), (1,)),
        sum_out,
        lax.dynamic_slice(vec[8:16].reshape(1024), (own * 8,), (8,)),
        sum_gate_up,
        sum_down,
    )


def solution(mesh):
    placed = (
        P(None, "rows", "ctx", None),
        P(None, "rows", "ctx", None),
        P(None, "rows", None),
        P(None, "rows", "ctx"),
        P(),
        P(),
        P(),
        P(),
        P(),
        P(),
        P(),
    )
    return jax.shard_map(
        local,
        mesh=mesh,
        in_specs=placed,
        out_specs=(
            P(None, "rows", "ctx", None),
            P(None, "rows", "ctx", None),
            P(("rows", "ctx")),
            P(("rows", "ctx"), None),
            P(("rows", "ctx")),
            P(("rows", "ctx"), None),
            P(("rows", "ctx")),
            P(("rows", "ctx"), None),
            P(("rows", "ctx"), None),
        ),
        check_vma=False,
    )
```

```python
import functools

import jax
import jax.numpy as jnp
from jax import lax
from jax.experimental import pallas as pl
from jax.experimental.pallas import tpu as pltpu
from jax.sharding import PartitionSpec as P

MESH = pl.DeviceIdType.MESH
norm_eps = 1e-05
rope_theta = 1000000.0
f32 = jnp.float32
bf16 = jnp.bfloat16
VMEM_LIMIT = 64 * 2**20 - 2**18


class Place:
    def __init__(self):
        r = lax.axis_index("rows")
        k = lax.axis_index("ctx")
        self.x_hi = lax.div(r, 8)
        self.y = lax.rem(lax.div(r, 2), 4)
        self.core = lax.rem(r, 2)
        self.x_lo = lax.div(k, 4)
        self.z = lax.rem(k, 4)
        self.rows = r
        self.ctx = k
        self.bits = [
            self.x_hi,
            lax.rem(self.x_hi + self.x_lo, 2),
            lax.div(self.y, 2),
            lax.rem(lax.div(self.y, 2) + lax.rem(self.y, 2), 2),
            lax.div(self.z, 2),
            lax.rem(lax.div(self.z, 2) + lax.rem(self.z, 2), 2),
        ]

    def at(self, x_hi=None, x_lo=None, y=None, z=None, core=None):
        x_hi = self.x_hi if x_hi is None else x_hi
        x_lo = self.x_lo if x_lo is None else x_lo
        y = self.y if y is None else y
        z = self.z if z is None else z
        core = self.core if core is None else core
        return (x_hi * 8 + y * 2 + core, x_lo * 4 + z)

    def partner(self):
        return self.at(core=1 - self.core)

    def neighbour(self, dim):
        if dim == 0:
            return self.at(x_hi=1 - self.x_hi, x_lo=1 - self.x_lo)
        if dim == 1:
            return self.at(x_lo=1 - self.x_lo)
        if dim == 2:
            return self.at(y=3 - self.y)
        if dim == 3:
            return self.at(y=self.y + 1 - 2 * lax.rem(self.y, 2))
        if dim == 4:
            return self.at(z=3 - self.z)
        return self.at(z=self.z + 1 - 2 * lax.rem(self.z, 2))


def gray(v):
    return v ^ (v >> 1)


def chip_number(x_hi, x_lo, y, z):
    return gray(2 * x_hi + x_lo) * 16 + gray(y) * 4 + gray(z)


def slot_of(number, s):
    turned = number << s
    return (turned & 63) | (turned >> 6)


HELD_AT = [64 - (64 >> t) for t in range(7)]


class Scatter:
    def __init__(self, place, first, held, send_sems, recv_sems, per):
        self.place = place
        self.first, self.first_cols = first
        self.held, self.held_cols = held
        self.send_sems = send_sems
        self.recv_sems = recv_sems
        self.per = per

    def part(self, s, t, which):
        half = 32 >> t
        if t == 0:
            return self.first, which * half, self.first_cols
        return self.held, HELD_AT[t - 1] + which * half, self.held_cols

    def copy(self, s, t):
        half = 32 >> t
        dim = (s + t) % 6
        ref, start, cols = self.part(s, t, 1 - self.place.bits[dim])
        return pltpu.make_async_remote_copy(
            src_ref=ref.at[s, pl.ds(start, half), :, cols],
            dst_ref=self.held.at[s, pl.ds(HELD_AT[t], half), :, self.held_cols],
            send_sem=self.send_sems.at[s, t],
            recv_sem=self.recv_sems.at[s, t],
            device_id=self.place.neighbour(dim),
            device_id_type=MESH,
        )

    def send(self, s, t):
        self.copy(s, t).start()

    def take(self, s, t):
        self.copy(s, t).wait_recv()
        half = 32 >> t
        ref, start, cols = self.part(s, t, self.place.bits[(s + t) % 6])
        per = min(self.per, half)

        def body(i, carry):
            for j in range(per):
                at = i * per + j
                self.held[s, HELD_AT[t] + at, :, self.held_cols] = (
                    self.held[s, HELD_AT[t] + at, :, self.held_cols].astype(f32)
                    + ref[s, start + at, :, cols].astype(f32)
                ).astype(bf16)
            return carry

        lax.fori_loop(0, half // per, body, 0)
        self.send(s, t + 1)

    def takes(self, t):
        for s in range(6):
            self.take(s, t)

    def last(self, s):
        self.copy(s, 5).wait_recv()
        ref, start, cols = self.part(s, 5, self.place.bits[(s + 5) % 6])
        return self.held[s, HELD_AT[5], :, self.held_cols].astype(f32) + ref[
            s, start, :, cols
        ].astype(f32)

    def sent(self, steps=range(6)):
        for s in range(6):
            for t in steps:
                self.copy(s, t).wait_send()


def greet(devices):
    barrier = pltpu.get_barrier_semaphore()
    for device in devices:
        pl.semaphore_signal(barrier, inc=1, device_id=device, device_id_type=MESH)
    pl.semaphore_wait(barrier, len(devices))


def greet_all(place, devices):
    barrier = pltpu.get_barrier_semaphore()
    targets = down_targets(place)
    for device in devices + targets[1:]:
        pl.semaphore_signal(barrier, inc=1, device_id=device, device_id_type=MESH)
    swapped = place.x_hi != place.core
    count = len(devices) + 3

    @pl.when(swapped)
    def _():
        pl.semaphore_signal(barrier, inc=1, device_id=targets[0], device_id_type=MESH)
        pl.semaphore_wait(barrier, count + 1)

    @pl.when(jnp.logical_not(swapped))
    def _():
        pl.semaphore_wait(barrier, count)


def push(place, src, dst, send_sem, recv_sem, device):
    return pltpu.make_async_remote_copy(
        src_ref=src,
        dst_ref=dst,
        send_sem=send_sem,
        recv_sem=recv_sem,
        device_id=device,
        device_id_type=MESH,
    )


def down_targets(place):
    return [
        place.at(x_hi=place.core, core=place.x_hi, z=lax.rem(place.z + off, 4)) for off in range(4)
    ]


def dot(left, right):
    return jnp.dot(left, right, preferred_element_type=f32)


def dot_cols(left, right):
    return lax.dot_general(left, right, (((1,), (1,)), ((), ())), preferred_element_type=f32)


FF_HALF = 2304


def finish_down(place, down, d_acc, d_stage, d_in, f_send, f_recv, gdn_ref):
    for s in range(6):
        d_acc[pl.ds(48 * (s // 2), 48), pl.ds(128 * (s % 2), 128)] = down.last(s)
    for z in range(4):
        d_stage[z, pl.ds(0, 36), :] = d_acc[pl.ds(36 * z, 36), :]
        d_stage[z, pl.ds(36, 4), :] = jnp.zeros((4, 256), f32)
    targets = down_targets(place)
    swapped = place.x_hi != place.core
    moves = []
    for off in range(4):
        moves.append(
            push(
                place,
                d_stage.at[lax.rem(place.z + off, 4)],
                d_in.at[place.z],
                f_send.at[off],
                f_recv.at[off],
                targets[off],
            )
        )
    for off in range(1, 4):
        moves[off].start()

    @pl.when(swapped)
    def _():
        moves[0].start()
        moves[0].wait_recv()

    @pl.when(jnp.logical_not(swapped))
    def _():
        d_in[place.z] = d_stage[place.z]

    for off in range(1, 4):
        moves[off].wait_recv()
    for z in range(4):
        gdn_ref[:, pl.ds(256 * z, 256)] = d_in[z, pl.ds(0, 36), :]
    for off in range(1, 4):
        moves[off].wait_send()

    @pl.when(swapped)
    def _():
        moves[0].wait_send()


def lanes(rows):
    return lax.broadcasted_iota(jnp.int32, (rows, 128), 1)


def turn_heads(values):
    low = lax.rem(lanes(values.shape[0]), 64) < 32
    return jnp.where(low, pltpu.roll(values, 96, 1), pltpu.roll(values, 32, 1))


def head_mean(values):
    i = lax.broadcasted_iota(jnp.int32, (128, 128), 0)
    j = lax.broadcasted_iota(jnp.int32, (128, 128), 1)
    ones = jnp.where(lax.div(i, 64) == lax.div(j, 64), 1.0 / 64, 0.0).astype(bf16)
    high = values.astype(bf16)
    rest = (values - high.astype(f32)).astype(bf16)
    return dot(high, ones) + dot(rest, ones)


def gain_tiles(qk_gain):
    swapped = pltpu.roll(qk_gain, 64, 1)
    low = lax.broadcasted_iota(jnp.int32, (1, 128), 1) < 64
    return jnp.where(low, qk_gain, swapped), jnp.where(low, swapped, qk_gain)


def head_rows(values):
    low = lanes(values.shape[0]) < 64
    zero = jnp.zeros_like(values)
    return jnp.concatenate([jnp.where(low, values, zero), jnp.where(low, zero, values)], 0)


class Exchange:
    def __init__(self, place, out, into_at, send_sems, recv_sems):
        self.place = place
        self.out = out
        self.into_at = into_at
        self.send_sems = send_sems
        self.recv_sems = recv_sems

    def copy(self, m, off):
        j = lax.rem(self.place.ctx + off, 8)
        return push(
            self.place,
            self.out.at[m, j],
            self.into_at(m, self.place.ctx),
            self.send_sems.at[m, off - 1],
            self.recv_sems.at[m, off - 1],
            (self.place.rows, j),
        )

    def send(self, m):
        for off in range(1, 8):
            self.copy(m, off).start()
        self.into_at(m, self.place.ctx)[...] = self.out[m, self.place.ctx]

    def arrived(self, m):
        for off in range(1, 8):
            self.copy(m, off).wait_recv()

    def sent(self):
        for m in range(2):
            for off in range(1, 8):
                self.copy(m, off).wait_send()


def ctx_peers(place):
    return [(place.rows, lax.rem(place.ctx + off, 8)) for off in range(1, 8)]


def document_edges(bounds_ref, m):
    index = lax.broadcasted_iota(jnp.int32, (1, 1024), 1)
    start = jnp.zeros((1, 1024), jnp.int32)
    end = jnp.full((1, 1024), 1024, jnp.int32)
    for k in range(1, 4):
        cut = bounds_ref[m, 0, k]
        start = jnp.where(index >= cut, cut, start)
        end = jnp.where(index < bounds_ref[m, 0, 4 - k], bounds_ref[m, 0, 4 - k], end)
    return start, end


def attention_kernel(
    bounds_ref,
    x_ref,
    cos_ref,
    sin_ref,
    gain_ref,
    qk_gain_ref,
    w_qkv_hbm,
    w_out_hbm,
    mid_ref,
    na_ref,
    att_ref,
    proj_ref,
    qkv_ref,
    o_ref,
    l_ref,
    w_qkv,
    w_out,
    q_out,
    a_out,
    a_in,
    q2,
    kk,
    vo,
    w_sems,
    q_send,
    q_recv,
    a_send,
    a_recv,
):
    place = Place()
    loads = [
        pltpu.make_async_copy(w_qkv_hbm, w_qkv, w_sems.at[0]),
        pltpu.make_async_copy(w_out_hbm, w_out, w_sems.at[1]),
    ]
    for load in loads:
        load.start()
    greet(ctx_peers(place))
    heads_out = Exchange(place, q_out, lambda m, j: qkv_ref.at[m, j], q_send, q_recv)
    heads_back = Exchange(place, a_out, lambda m, j: a_in.at[m, j], a_send, a_recv)

    inputs = x_ref[...].astype(f32)
    scale = lax.rsqrt(jnp.mean(inputs * inputs, axis=-1, keepdims=True) + norm_eps)
    na_ref[...] = (inputs * scale * gain_ref[...]).astype(bf16)
    loads[0].wait()
    gain_q, gain_k = gain_tiles(qk_gain_ref[...])
    low = lanes(256) < 64

    def turned(tile, gain):
        u = tile * lax.rsqrt(head_mean(tile * tile) + norm_eps) * gain
        return u * cos_ref[...] + turn_heads(u) * sin_ref[...]

    for i in range(4):
        pair = dot(na_ref[...], w_qkv[:, pl.ds(256 * i, 256)])
        proj_ref[:, pl.ds(256 * i, 256)] = pair
        for j in range(2):
            tile = turned(pair[:, 128 * j : 128 * j + 128], gain_q) * 0.125
            for m in range(2):
                q_out[m, 2 * i + j, :, pl.ds(0, 128)] = tile[128 * m : 128 * m + 128].astype(bf16)
    for i in range(2):
        key_pair = dot(na_ref[...], w_qkv[:, pl.ds(1024 + 256 * i, 256)])
        value_pair = dot(na_ref[...], w_qkv[:, pl.ds(1536 + 256 * i, 256)])
        proj_ref[:, pl.ds(1024 + 256 * i, 256)] = key_pair
        for j in range(2):
            key = turned(key_pair[:, 128 * j : 128 * j + 128], gain_k)
            value = value_pair[:, 128 * j : 128 * j + 128]
            first = jnp.where(low, key, pltpu.roll(value, 64, 1)).astype(bf16)
            second = jnp.where(low, pltpu.roll(key, 64, 1), value).astype(bf16)
            for m in range(2):
                rows = slice(128 * m, 128 * m + 128)
                q_out[m, 4 * i + 2 * j, :, pl.ds(128, 128)] = first[rows]
                q_out[m, 4 * i + 2 * j + 1, :, pl.ds(128, 128)] = second[rows]
    for m in range(2):
        heads_out.send(m)

    for m in range(2):
        heads_out.arrived(m)
        ends = document_edges(bounds_ref, m)[1]
        for b in range(4):
            query = qkv_ref[m, pl.ds(2 * b, 2), :, pl.ds(0, 128)].reshape(256, 128)
            both = qkv_ref[m, pl.ds(2 * b, 2), :, pl.ds(128, 128)].reshape(256, 128).astype(f32)
            swapped = pltpu.roll(both, 64, 1)
            q2[b] = head_rows(query)
            kk[b] = jnp.where(low, both, swapped).astype(bf16)
            vo[b] = jnp.where(low, swapped, 1.0).astype(bf16)
        for qb in range(4):
            acc = jnp.zeros((512, 128), f32)
            for kb in range(qb + 1):
                scores = dot_cols(q2[qb], kk[kb])
                t = 256 * qb + lax.rem(lax.broadcasted_iota(jnp.int32, (512, 256), 0), 256)
                keep = t < ends[:, 256 * kb : 256 * kb + 256]
                if kb == qb:
                    s = 256 * kb + lax.broadcasted_iota(jnp.int32, (512, 256), 1)
                    keep = keep & (s <= t)
                weights = jnp.where(keep, jnp.exp(scores), 0.0).astype(bf16)
                acc = acc + dot(weights, vo[kb])
            total = pltpu.roll(acc, 64, 1)
            head0 = acc[:256]
            head1 = pltpu.roll(acc[256:], 64, 1)
            denominator = jnp.where(low, total[:256], acc[256:])
            out = jnp.where(low, head0, head1) / denominator
            o_ref[m, pl.ds(256 * qb, 256), :] = out
            log_total = jnp.log(denominator).T
            l_ref[m, pl.ds(0, 1), pl.ds(256 * qb, 256)] = log_total[0:1]
            l_ref[m, pl.ds(1, 1), pl.ds(256 * qb, 256)] = log_total[64:65]
            for half in range(2):
                a_out[m, 2 * qb + half] = out[128 * half : 128 * half + 128].astype(bf16)
        heads_back.send(m)
    loads[1].wait()
    for m in range(2):
        heads_back.arrived(m)
        for j in range(8):
            att_ref[pl.ds(128 * m, 128), pl.ds(128 * j, 128)] = a_in[m, j]
    mid_ref[...] = x_ref[...].astype(f32) + dot(att_ref[...], w_out[...])
    heads_out.sent()
    heads_back.sent()


def attention(bounds, x, cosine, sine, gain, qk_gain, w_qkv, w_out):
    vmem = pl.BlockSpec(memory_space=pltpu.VMEM)
    hbm = pl.BlockSpec(memory_space=pl.ANY)
    smem = pl.BlockSpec(memory_space=pltpu.SMEM)
    dma = pltpu.SemaphoreType.DMA
    return pl.pallas_call(
        attention_kernel,
        out_shape=(
            jax.ShapeDtypeStruct((256, 1024), f32),
            jax.ShapeDtypeStruct((256, 1024), bf16),
            jax.ShapeDtypeStruct((256, 1024), bf16),
            jax.ShapeDtypeStruct((256, 1536), f32),
            jax.ShapeDtypeStruct((2, 8, 128, 256), bf16),
            jax.ShapeDtypeStruct((2, 1024, 128), f32),
            jax.ShapeDtypeStruct((2, 2, 1024), f32),
        ),
        in_specs=[smem] + [vmem] * 5 + [hbm] * 2,
        out_specs=(vmem,) * 7,
        scratch_shapes=[
            pltpu.VMEM((1024, 2048), bf16),
            pltpu.VMEM((1024, 1024), bf16),
            pltpu.VMEM((2, 8, 128, 256), bf16),
            pltpu.VMEM((2, 8, 128, 128), bf16),
            pltpu.VMEM((2, 8, 128, 128), bf16),
            pltpu.VMEM((4, 512, 128), bf16),
            pltpu.VMEM((4, 256, 128), bf16),
            pltpu.VMEM((4, 256, 128), bf16),
            dma((2,)),
            dma((2, 7)),
            dma((2, 7)),
            dma((2, 7)),
            dma((2, 7)),
        ],
        compiler_params=pltpu.CompilerParams(
            collective_id=2, has_side_effects=True, vmem_limit_bytes=VMEM_LIMIT
        ),
        name="attention_forward",
    )(bounds, x, cosine, sine, gain, qk_gain, w_qkv, w_out)


def reorder_store(part, first, s, x_hi, at, width):
    part = part.reshape(4, 2, 8, 8, width)
    for y in range(4):
        for x_lo in range(2):
            for z in range(4):
                slot = slot_of(chip_number(x_hi, x_lo, y, z), s)
                first[s, slot, :, at] = part[y, :, 4 * x_lo + z].reshape(16, width).astype(bf16)


def main_kernel(
    bounds_ref,
    mid_ref,
    gain_ffn_ref,
    gain_ref,
    qk_gain_ref,
    cot_hbm,
    x_hbm,
    cos_hbm,
    sin_hbm,
    na_hbm,
    att_hbm,
    proj_hbm,
    qkv_hbm,
    o_hbm,
    l_hbm,
    wgu_hbm,
    wd_hbm,
    w_qkv_hbm,
    w_out_hbm,
    out_hbm,
    gtok_hbm,
    ggu_ref,
    gdn_ref,
    gqkv_ref,
    gout_ref,
    vec_out,
    g_first,
    g_held,
    d_first,
    d_held,
    nf,
    dyb,
    sum_send,
    sum_recv,
    xboth,
    dmid,
    do_out,
    do_in,
    dpin,
    dmin,
    dm_own,
    g_fin,
    g_in,
    d_acc,
    d_stage,
    d_in,
    q_fin,
    q_in,
    vec,
    vec_in,
    w_sems,
    l_sems,
    x_send,
    x_recv,
    g_send,
    g_recv,
    d_send,
    d_recv,
    q_send,
    q_recv,
    f_send,
    f_recv,
    do_send,
    do_recv,
    t_send,
    t_recv,
    v_send,
    v_recv,
    free_sem,
):
    place = Place()
    core = place.core
    partner = place.partner()
    every = slice(None)
    down = Scatter(place, (d_first, every), (d_held, every), d_send, d_recv, 4)
    both = Scatter(place, (g_first, every), (g_held, every), g_send, g_recv, 2)
    quad = Scatter(
        place, (g_first, pl.ds(0, 256)), (g_first, pl.ds(256, 256)), q_send, q_recv, 4
    )
    def t_at(m, j):
        return nf.at[
            pl.ds(pl.multiple_of(256 * m + 128 * lax.div(j, 4), 128), 128),
            pl.ds(pl.multiple_of(256 * lax.rem(j, 4), 256), 256),
        ]

    grads_out = Exchange(place, do_out, lambda m, j: do_in.at[m, j], do_send, do_recv)
    own_rows = pl.ds(0, 256)
    other_rows = pl.ds(256, 256)
    to_dy = push(place, cot_hbm, dyb.at[other_rows], x_send.at[0], x_recv.at[0], partner)
    to_nf = push(place, nf.at[own_rows], nf.at[other_rows], x_send.at[1], x_recv.at[1], partner)
    to_out = push(place, sum_send, sum_recv.at[0], x_send.at[2], x_recv.at[2], partner)
    to_back = push(place, sum_send, sum_recv.at[1], x_send.at[3], x_recv.at[3], partner)
    to_na = push(place, na_hbm, xboth.at[0], x_send.at[4], x_recv.at[4], partner)
    to_att = push(place, att_hbm, xboth.at[1], x_send.at[5], x_recv.at[5], partner)
    to_dm = push(place, dm_own.at[1 - core], dmin, x_send.at[6], x_recv.at[6], partner)
    out_copy = pltpu.make_async_copy(sum_send, out_hbm, l_sems.at[0])

    def feed_forward(wgu, wd, nft, h, ht, dgu, sum_own):
        loads = []
        for i in range(3):
            at = pl.multiple_of(core * FF_HALF + 768 * i, 256)
            up_at = pl.multiple_of(4608 + core * FF_HALF + 768 * i, 256)
            loads.append(
                [
                    pltpu.make_async_copy(
                        wgu_hbm.at[:, pl.ds(at, 768)],
                        wgu.at[:, pl.ds(768 * i, 768)],
                        w_sems.at[3 * i],
                    ),
                    pltpu.make_async_copy(
                        wgu_hbm.at[:, pl.ds(up_at, 768)],
                        wgu.at[:, pl.ds(FF_HALF + 768 * i, 768)],
                        w_sems.at[3 * i + 1],
                    ),
                    pltpu.make_async_copy(
                        wd_hbm.at[pl.ds(at, 768)], wd.at[pl.ds(768 * i, 768)], w_sems.at[3 * i + 2]
                    ),
                ]
            )
        cot_load = pltpu.make_async_copy(cot_hbm, dyb.at[own_rows], l_sems.at[1])
        cot_load.start()
        for copies in loads:
            for copy in copies:
                copy.start()
        greet_all(
            place,
            [partner] + [place.neighbour(dim) for dim in range(6)] + ctx_peers(place),
        )
        to_dy.start()
        mid = mid_ref[...]
        scale = lax.rsqrt(jnp.mean(mid * mid, axis=-1, keepdims=True) + norm_eps)
        nf[own_rows, :] = (mid * scale * gain_ffn_ref[...]).astype(bf16)
        to_nf.start()
        nft[:, own_rows] = nf[own_rows, :].T
        to_na.start()
        to_att.start()
        cot_load.wait()
        to_dy.wait_recv()
        to_nf.wait_recv()
        nft[:, other_rows] = nf[other_rows, :].T

        for i in range(3):
            for copy in loads[i]:
                copy.wait()

            def units(j, carry, i=i):
                at = pl.multiple_of(768 * i + 256 * j, 256)
                up_at = pl.multiple_of(FF_HALF + 768 * i + 256 * j, 256)
                gate = dot(nf[...], wgu[:, pl.ds(at, 256)])
                upward = dot(nf[...], wgu[:, pl.ds(up_at, 256)])
                grad_hidden = dot_cols(dyb[...], wd[pl.ds(at, 256), :])
                sigma = 1.0 / (1.0 + jnp.exp(-gate))
                silu = gate * sigma
                h[:, pl.ds(at, 256)] = (silu * upward).astype(bf16)
                dgu[:, pl.ds(at, 256)] = (
                    grad_hidden * upward * (sigma + silu * (1.0 - sigma))
                ).astype(bf16)
                dgu[:, pl.ds(up_at, 256)] = (grad_hidden * silu).astype(bf16)
                return carry

            lax.fori_loop(0, 3, units, 0)

        for block in range(3):
            ht[...] = h[:, pl.ds(768 * block, 768)].T

            def down_cols(z, carry, block=block):
                part = dot(ht[...], dyb[:, pl.ds(pl.multiple_of(256 * z, 256), 256)])
                z_number = 2 * lax.div(z, 2) + lax.rem(lax.div(z, 2) + lax.rem(z, 2), 2)
                for i in range(16):
                    q = 16 * block + i
                    y, core_to, x_lo, rg = q // 12, (q // 6) % 2, (q // 3) % 2, q % 3
                    number = chip_number(core_to, x_lo, y, 0) + z_number
                    for ch in range(2):
                        s = 2 * rg + ch
                        turned = number * (1 << s)
                        slot = lax.rem(turned, 64) + lax.div(turned, 64)
                        d_first[s, slot] = part[
                            48 * i : 48 * i + 48, 128 * ch : 128 * ch + 128
                        ].astype(bf16)
                return carry

            lax.fori_loop(0, 4, down_cols, 0)
        for s in range(6):
            down.send(s, 0)

        def back_cols(j, carry):
            at = pl.ds(pl.multiple_of(256 * j, 256), 256)
            part = dot_cols(dgu[...], wgu[at, :])
            dmid[:, at] = part[:256]
            sum_send[:, at] = part[256:].astype(bf16)
            return carry

        lax.fori_loop(0, 4, back_cols, 0)
        to_back.start()

        def gate_up(s):
            def gate_cols(j, carry):
                at = pl.ds(pl.multiple_of(256 * j, 256), 256)
                cols = dgu[:, pl.ds(pl.multiple_of(768 * s + 256 * j, 256), 256)]
                for x_hi in range(2):
                    part = dot(nft[pl.ds(512 * x_hi, 512), :], cols)
                    reorder_store(part, g_first, s, x_hi, at, 256)
                return carry

            lax.fori_loop(0, 3, gate_cols, 0)
            both.send(s, 0)

        for s in range(2):
            gate_up(s)

        to_back.wait_send()

        def out_cols(j, carry):
            at = pl.ds(pl.multiple_of(256 * j, 256), 256)
            part = dot(h[...], wd[:, at])
            sum_own[:, at] = part[:256]
            sum_send[:, at] = part[256:].astype(bf16)
            return carry

        lax.fori_loop(0, 4, out_cols, 0)
        to_out.start()
        w_out = wd.at[pl.ds(0, 1024)]
        w_out_load = pltpu.make_async_copy(w_out_hbm, w_out, l_sems.at[4])
        w_out_load.start()

        to_back.wait_recv()
        mid = mid_ref[...]
        scale = lax.rsqrt(jnp.mean(mid * mid, axis=-1, keepdims=True) + norm_eps)
        normed = mid * scale
        grad_nffn = dmid[...] + sum_recv[1].astype(f32)
        gain_grad = jnp.sum(grad_nffn * normed, axis=0, keepdims=True)
        for i in range(8):
            vec[0, pl.ds(8 + i, 1), :] = gain_grad[:, 128 * i : 128 * i + 128]
        grad_e = grad_nffn * gain_ffn_ref[...]
        dmid[...] = dyb[own_rows, :].astype(f32) + scale * (
            grad_e - normed * jnp.mean(grad_e * normed, axis=-1, keepdims=True)
        )
        for half in range(2):
            dm_own[half] = dmid[:, pl.ds(512 * half, 512)].astype(bf16)
        to_dm.start()

        to_nf.wait_send()
        w_out_load.wait()
        for i in range(4):
            pair = dot_cols(dm_own[0], wd[pl.ds(256 * i, 256), pl.ds(0, 512)]) + dot_cols(
                dm_own[1], wd[pl.ds(256 * i, 256), pl.ds(512, 512)]
            )
            for j in range(2):
                for m in range(2):
                    do_out[m, 2 * i + j] = pair[
                        128 * m : 128 * m + 128, 128 * j : 128 * j + 128
                    ].astype(bf16)
        for m in range(2):
            grads_out.send(m)
        for s in range(2, 6):
            gate_up(s)
        to_out.wait()
        sum_send[...] = (mid_ref[...] + sum_own[...] + sum_recv[0].astype(f32)).astype(bf16)
        out_copy.start()

    pl.run_scoped(
        feed_forward,
        pltpu.VMEM((1024, 4608), bf16),
        pltpu.VMEM((FF_HALF, 1024), bf16),
        pltpu.VMEM((1024, 512), bf16),
        pltpu.VMEM((512, FF_HALF), bf16),
        pltpu.VMEM((768, 512), bf16),
        pltpu.VMEM((512, 4608), bf16),
        pltpu.VMEM((256, 1024), f32),
    )

    def attention_back(
        w_qkv, x_ref, gtok, cos_ref, sin_ref, proj_ref, qkv_ref, o_ref, l_ref,
        q2, do2, kk, vv, kt, delta, dq, dp, own, nat, attt, cols, t_out,
    ):
        sources = [qkv_hbm, o_hbm, l_hbm, cos_hbm, sin_hbm, proj_hbm, x_hbm, w_qkv_hbm]
        loads = [
            pltpu.make_async_copy(source, target, w_sems.at[i])
            for i, (source, target) in enumerate(
                zip(
                    sources,
                    [qkv_ref, o_ref, l_ref, cos_ref, sin_ref, proj_ref, x_ref, w_qkv],
                    strict=True,
                )
            )
        ]
        for load in loads:
            load.start()
        grads_back = Exchange(place, t_out, t_at, t_send, t_recv)
        down.takes(0)
        for load in loads[:3]:
            load.wait()
        low = lanes(256) < 64

        def heads_back(m):
            grads_out.arrived(m)
            starts = document_edges(bounds_ref, m)[0]
            for b in range(4):
                query = qkv_ref[m, pl.ds(2 * b, 2), :, pl.ds(0, 128)].reshape(256, 128)
                pair = qkv_ref[m, pl.ds(2 * b, 2), :, pl.ds(128, 128)].reshape(256, 128)
                pair = pair.astype(f32)
                grad = do_in[m, pl.ds(2 * b, 2)].reshape(256, 128)
                swapped = pltpu.roll(pair, 64, 1)
                key_pair = jnp.where(low, pair, swapped)
                q2[b] = head_rows(query)
                do2[b] = head_rows(grad)
                kk[b] = key_pair.astype(bf16)
                vv[b] = jnp.where(low, swapped, pair).astype(bf16)
                kt[b] = key_pair.T.astype(bf16)
                inner = (grad.astype(f32) * o_ref[m, pl.ds(256 * b, 256), :]).T
                delta[b, :, pl.ds(0, 256)] = jnp.sum(inner[:64], axis=0, keepdims=True)
                delta[b, :, pl.ds(256, 256)] = jnp.sum(inner[64:], axis=0, keepdims=True)
            for kb in range(4):
                grad_key = jnp.zeros((256, 128), f32)
                grad_value = jnp.zeros((256, 128), f32)
                for qb in range(kb, 4):
                    scores = dot_cols(kk[kb], q2[qb])
                    log_total = jnp.concatenate(
                        [l_ref[m, pl.ds(i, 1), pl.ds(256 * qb, 256)] for i in range(2)], 1
                    )
                    start = starts[:, 256 * qb : 256 * qb + 256]
                    s = 256 * kb + lax.broadcasted_iota(jnp.int32, (256, 512), 0)
                    keep = s >= jnp.concatenate([start, start], 1)
                    if kb == qb:
                        t = lax.broadcasted_iota(jnp.int32, (256, 512), 1)
                        keep = keep & (s <= 256 * qb + lax.rem(t, 256))
                    probs = jnp.where(keep, jnp.exp(scores - log_total), 0.0)
                    grad_probs = dot_cols(vv[kb], do2[qb])
                    grad_scores = (probs * (grad_probs - delta[qb])).astype(bf16)
                    grad_value = grad_value + dot(probs.astype(bf16), do2[qb])
                    grad_key = grad_key + dot(grad_scores, q2[qb])
                    grad_query = dot(kt[kb], grad_scores)
                    if kb == 0:
                        dq[qb] = grad_query[:64]
                    else:
                        dq[qb] = dq[qb] + grad_query[:64]
                grad_key = grad_key + pltpu.roll(grad_key, 64, 1)
                grad_value = grad_value + pltpu.roll(grad_value, 64, 1)
                tile = jnp.where(low, grad_key, grad_value).astype(bf16)
                for half in range(2):
                    rows = slice(128 * half, 128 * half + 128)
                    t_out[m, 2 * kb + half, :, pl.ds(128, 128)] = tile[rows]
            for qb in range(4):
                stacked = jnp.concatenate([dq[qb, :, pl.ds(0, 256)], dq[qb, :, pl.ds(256, 256)]], 0)
                tile = (stacked * 0.125).T.astype(bf16)
                for half in range(2):
                    rows = slice(128 * half, 128 * half + 128)
                    t_out[m, 2 * qb + half, :, pl.ds(0, 128)] = tile[rows]
            grads_back.send(m)

        heads_back(0)
        both.takes(0)
        down.takes(1)
        both.sent([0])
        for dim in range(6):
            pl.semaphore_signal(
                free_sem, inc=1, device_id=place.neighbour(dim), device_id_type=MESH
            )
        heads_back(1)

        own_loads = [
            pltpu.make_async_copy(na_hbm, own.at[0], l_sems.at[2]),
            pltpu.make_async_copy(att_hbm, own.at[1], l_sems.at[3]),
        ]
        for load in own_loads:
            load.start()
        to_na.wait_recv()
        nat[:, other_rows] = xboth[0].T
        to_att.wait_recv()
        attt[:, other_rows] = xboth[1].T
        for load in own_loads:
            load.wait()
        nat[:, own_rows] = own[0].T
        attt[:, own_rows] = own[1].T
        to_dm.wait_recv()
        cols[own_rows, pl.ds(1024, 512)] = dm_own[core]
        cols[other_rows, pl.ds(1024, 512)] = dmin[...]
        pl.semaphore_wait(free_sem, 6)

        def projection_cols(s):
            left = nat if s < 4 else attt
            for x_hi in range(2):
                part = dot(left[pl.ds(512 * x_hi, 512), :], cols[:, pl.ds(256 * s, 256)])
                reorder_store(part, g_first, s, x_hi, pl.ds(0, 256), 256)
            quad.send(s, 0)

        for s in range(4, 6):
            projection_cols(s)
        both.takes(1)
        down.takes(2)

        for load in loads[3:6]:
            load.wait()
        gain_q, gain_k = gain_tiles(qk_gain_ref[...])
        for m in range(2):
            grads_back.arrived(m)

        def both_rows(j, at):
            return jnp.concatenate([t_at(m, j)[:, pl.ds(at, 128)] for m in range(2)], 0).astype(f32)

        def head_back(grad, value, gain):
            grad = grad * cos_ref[...] + turn_heads(grad * sin_ref[...])
            scale = lax.rsqrt(head_mean(value * value) + norm_eps)
            normed = value * scale
            grad_e = grad * gain
            gain_grad = jnp.sum(grad * normed, axis=0, keepdims=True)
            return scale * (grad_e - normed * head_mean(grad_e * normed)), gain_grad

        sum_q = jnp.zeros((1, 128), f32)
        sum_k = jnp.zeros((1, 128), f32)
        for j in range(8):
            back, part = head_back(both_rows(j, 0), proj_ref[:, pl.ds(128 * j, 128)], gain_q)
            dp[0, :, pl.ds(128 * j, 128)] = back.astype(bf16)
            sum_q = sum_q + part
        for i in range(4):
            first = both_rows(2 * i, 128)
            second = both_rows(2 * i + 1, 128)
            grad_key = jnp.where(low, first, pltpu.roll(second, 64, 1))
            grad_value = jnp.where(low, pltpu.roll(first, 64, 1), second)
            back, part = head_back(grad_key, proj_ref[:, pl.ds(1024 + 128 * i, 128)], gain_k)
            dp[1, :, pl.ds(128 * i, 128)] = back.astype(bf16)
            dp[1, :, pl.ds(512 + 128 * i, 128)] = grad_value.astype(bf16)
            sum_k = sum_k + part
        to_dp = push(place, dp.at[1 - core], dpin, x_send.at[7], x_recv.at[7], partner)
        to_dp.start()
        sum_q = sum_q + pltpu.roll(sum_q, 64, 1)
        sum_k = sum_k + pltpu.roll(sum_k, 64, 1)
        vec[0, pl.ds(16, 8), :] = jnp.zeros((8, 128), f32)
        vec[0, pl.ds(16, 1), :] = jnp.where(
            lax.broadcasted_iota(jnp.int32, (1, 128), 1) < 64, sum_q, sum_k
        )
        cols[own_rows, pl.ds(0, 1024)] = dp[core]
        to_dp.wait_recv()
        cols[other_rows, pl.ds(0, 1024)] = dpin[...]
        for s in range(4):
            projection_cols(s)

        loads[6].wait()
        loads[7].wait()
        inputs = x_ref[...].astype(f32)
        scale = lax.rsqrt(jnp.mean(inputs * inputs, axis=-1, keepdims=True) + norm_eps)
        normed = inputs * scale
        grad_n = dot_cols(dp[0], w_qkv[:, pl.ds(0, 1024)]) + dot_cols(
            dp[1], w_qkv[:, pl.ds(1024, 1024)]
        )
        gain_grad = jnp.sum(grad_n * normed, axis=0, keepdims=True)
        grad_e = grad_n * gain_ref[...]
        gtok[...] = dmid[...] + scale * (
            grad_e - normed * jnp.mean(grad_e * normed, axis=-1, keepdims=True)
        )
        gtok_copy = pltpu.make_async_copy(gtok, gtok_hbm, l_sems.at[1])
        gtok_copy.start()
        for i in range(8):
            vec[0, pl.ds(i, 1), :] = gain_grad[:, 128 * i : 128 * i + 128]
        gtok_copy.wait()
        to_dp.wait_send()
        grads_back.sent()

    pl.run_scoped(
        attention_back,
        pltpu.VMEM((1024, 2048), bf16),
        pltpu.VMEM((256, 1024), bf16),
        pltpu.VMEM((256, 1024), f32),
        pltpu.VMEM((256, 128), f32),
        pltpu.VMEM((256, 128), f32),
        pltpu.VMEM((256, 1536), f32),
        pltpu.VMEM((2, 8, 128, 256), bf16),
        pltpu.VMEM((2, 1024, 128), f32),
        pltpu.VMEM((2, 2, 1024), f32),
        pltpu.VMEM((4, 512, 128), bf16),
        pltpu.VMEM((4, 512, 128), bf16),
        pltpu.VMEM((4, 256, 128), bf16),
        pltpu.VMEM((4, 256, 128), bf16),
        pltpu.VMEM((4, 128, 256), bf16),
        pltpu.VMEM((4, 1, 512), f32),
        pltpu.VMEM((4, 64, 512), f32),
        pltpu.VMEM((2, 256, 1024), bf16),
        pltpu.VMEM((2, 256, 1024), bf16),
        pltpu.VMEM((1024, 512), bf16),
        pltpu.VMEM((1024, 512), bf16),
        pltpu.VMEM((512, 1536), bf16),
        pltpu.VMEM((2, 8, 128, 256), bf16),
    )

    def vec_move(step):
        device = place.neighbour(step) if step < 6 else partner
        return push(place, vec.at[step], vec_in.at[step], v_send.at[step], v_recv.at[step], device)

    vec_move(0).start()

    def vec_take(step):
        vec_move(step).wait_recv()
        vec[step + 1] = vec[step] + vec_in[step]
        vec_move(step + 1).start()

    both.takes(2)
    down.takes(3)
    quad.takes(0)
    vec_take(0)
    both.takes(3)
    down.takes(4)
    quad.takes(1)
    vec_take(1)
    both.takes(4)
    finish_down(place, down, d_acc, d_stage, d_in, f_send, f_recv, gdn_ref)
    quad.takes(2)
    vec_take(2)
    for s in range(6):
        total = both.last(s)
        g_fin[0, s] = total[:8]
        g_fin[1, s] = total[8:]
    swap = push(place, g_fin.at[1 - core], g_in, x_send.at[8], x_recv.at[8], partner)
    swap.start()
    quad.takes(3)
    vec_take(3)
    for s in range(6):
        base = (s // 3) * 4608 + (s % 3) * 768
        ggu_ref[:, pl.ds(pl.multiple_of(base + core * FF_HALF, 256), 768)] = g_fin[core, s]
    quad.takes(4)
    vec_take(4)
    swap.wait_recv()
    for s in range(6):
        base = (s // 3) * 4608 + (s % 3) * 768
        ggu_ref[:, pl.ds(pl.multiple_of(base + (1 - core) * FF_HALF, 256), 768)] = g_in[s]
    for s in range(6):
        total = quad.last(s)
        q_fin[0, s] = total[:8]
        q_fin[1, s] = total[8:]
    swap_q = push(place, q_fin.at[1 - core], q_in, x_send.at[9], x_recv.at[9], partner)
    swap_q.start()
    vec_take(5)
    for s in range(4):
        gqkv_ref[:, pl.ds(pl.multiple_of(core * 1024 + 256 * s, 256), 256)] = q_fin[core, s]
    for s in range(4, 6):
        gout_ref[:, pl.ds(pl.multiple_of(core * 512 + 256 * (s - 4), 256), 256)] = q_fin[core, s]
    swap_q.wait_recv()
    for s in range(4):
        gqkv_ref[:, pl.ds(pl.multiple_of((1 - core) * 1024 + 256 * s, 256), 256)] = q_in[s]
    for s in range(4, 6):
        gout_ref[:, pl.ds(pl.multiple_of((1 - core) * 512 + 256 * (s - 4), 256), 256)] = q_in[s]
    vec_move(6).wait_recv()
    vec_out[...] = vec[6] + vec_in[6]

    for move in (to_dy, to_na, to_att, to_dm, swap, swap_q):
        move.wait_send()
    out_copy.wait()
    for step in range(7):
        vec_move(step).wait_send()
    down.sent()
    both.sent(range(1, 6))
    quad.sent()
    grads_out.sent()


def main_part(bounds, *arrays):
    vmem = pl.BlockSpec(memory_space=pltpu.VMEM)
    hbm = pl.BlockSpec(memory_space=pl.ANY)
    smem = pl.BlockSpec(memory_space=pltpu.SMEM)
    dma = pltpu.SemaphoreType.DMA
    return pl.pallas_call(
        main_kernel,
        out_shape=(
            jax.ShapeDtypeStruct((256, 1024), bf16),
            jax.ShapeDtypeStruct((256, 1024), f32),
            jax.ShapeDtypeStruct((8, 9216), f32),
            jax.ShapeDtypeStruct((36, 1024), f32),
            jax.ShapeDtypeStruct((8, 2048), f32),
            jax.ShapeDtypeStruct((8, 1024), f32),
            jax.ShapeDtypeStruct((24, 128), f32),
        ),
        in_specs=[smem] + [vmem] * 4 + [hbm] * 14,
        out_specs=(hbm, hbm) + (vmem,) * 5,
        scratch_shapes=[
            pltpu.VMEM((6, 64, 16, 768), bf16),
            pltpu.VMEM((6, 63, 16, 768), bf16),
            pltpu.VMEM((6, 64, 48, 128), bf16),
            pltpu.VMEM((6, 63, 48, 128), bf16),
            pltpu.VMEM((512, 1024), bf16),
            pltpu.VMEM((512, 1024), bf16),
            pltpu.VMEM((256, 1024), bf16),
            pltpu.VMEM((2, 256, 1024), bf16),
            pltpu.VMEM((2, 256, 1024), bf16),
            pltpu.VMEM((256, 1024), f32),
            pltpu.VMEM((2, 8, 128, 128), bf16),
            pltpu.VMEM((2, 8, 128, 128), bf16),
            pltpu.VMEM((256, 1024), bf16),
            pltpu.VMEM((256, 512), bf16),
            pltpu.VMEM((2, 256, 512), bf16),
            pltpu.VMEM((2, 6, 8, 768), f32),
            pltpu.VMEM((6, 8, 768), f32),
            pltpu.VMEM((144, 256), f32),
            pltpu.VMEM((4, 40, 256), f32),
            pltpu.VMEM((4, 40, 256), f32),
            pltpu.VMEM((2, 6, 8, 256), f32),
            pltpu.VMEM((6, 8, 256), f32),
            pltpu.VMEM((7, 24, 128), f32),
            pltpu.VMEM((7, 24, 128), f32),
            dma((9,)),
            dma((5,)),
            dma((10,)),
            dma((10,)),
            dma((6, 6)),
            dma((6, 6)),
            dma((6, 6)),
            dma((6, 6)),
            dma((6, 6)),
            dma((6, 6)),
            dma((4,)),
            dma((4,)),
            dma((2, 7)),
            dma((2, 7)),
            dma((2, 7)),
            dma((2, 7)),
            dma((7,)),
            dma((7,)),
            pltpu.SemaphoreType.REGULAR,
        ],
        compiler_params=pltpu.CompilerParams(
            collective_id=0, has_side_effects=True, vmem_limit_bytes=VMEM_LIMIT
        ),
        name="feed_forward_and_backward",
    )(bounds, *arrays)


def tables(positions):
    lane = jnp.arange(128, dtype=jnp.int32)
    freqs = rope_theta ** (-2.0 * (lane % 32).astype(f32) / 64)
    angles = positions.astype(f32)[:, None] * freqs[None, :]
    return jnp.cos(angles), jnp.sin(angles) * jnp.where(lane % 64 < 32, -1.0, 1.0)


def local(
    tokens,
    cotangent,
    bounds,
    positions,
    norm_gain_attn,
    w_qkv,
    qk_gain,
    w_out,
    norm_gain_ffn,
    w_gate_up,
    w_down,
):
    x = tokens.reshape(256, 1024)
    cot = cotangent.reshape(256, 1024)
    cosine, sine = tables(positions.reshape(256))
    mid, na, att, proj, qkv, o, l = attention(
        bounds, x, cosine, sine, norm_gain_attn[None], qk_gain[None], w_qkv, w_out
    )
    layer_out, grad_tokens, sum_gate_up, sum_down, sum_qkv, sum_out, vec = main_part(
        bounds,
        mid,
        norm_gain_ffn[None],
        norm_gain_attn[None],
        qk_gain[None],
        cot,
        x,
        cosine,
        sine,
        na,
        att,
        proj,
        qkv,
        o,
        l,
        w_gate_up,
        w_down,
        w_qkv,
        w_out,
    )
    own = lax.axis_index("rows") * 8 + lax.axis_index("ctx")
    return (
        layer_out.reshape(tokens.shape),
        grad_tokens.reshape(tokens.shape),
        lax.dynamic_slice(vec[:8].reshape(1024), (own * 8,), (8,)),
        sum_qkv,
        lax.dynamic_slice(vec[16], (own,), (1,)),
        sum_out,
        lax.dynamic_slice(vec[8:16].reshape(1024), (own * 8,), (8,)),
        sum_gate_up,
        sum_down,
    )


def solution(mesh):
    placed = (
        P(None, "rows", "ctx", None),
        P(None, "rows", "ctx", None),
        P(None, "rows", None),
        P(None, "rows", "ctx"),
        P(),
        P(),
        P(),
        P(),
        P(),
        P(),
        P(),
    )
    return jax.shard_map(
        local,
        mesh=mesh,
        in_specs=placed,
        out_specs=(
            P(None, "rows", "ctx", None),
            P(None, "rows", "ctx", None),
            P(("rows", "ctx")),
            P(("rows", "ctx"), None),
            P(("rows", "ctx")),
            P(("rows", "ctx"), None),
            P(("rows", "ctx")),
            P(("rows", "ctx"), None),
            P(("rows", "ctx"), None),
        ),
        check_vma=False,
    )
```

```python
import functools

import jax
import jax.numpy as jnp
from jax import lax
from jax.experimental import pallas as pl
from jax.experimental.pallas import tpu as pltpu
from jax.sharding import PartitionSpec as P

MESH = pl.DeviceIdType.MESH
norm_eps = 1e-05
rope_theta = 1000000.0
f32 = jnp.float32
bf16 = jnp.bfloat16
VMEM_LIMIT = 64 * 2**20 - 2**18


class Place:
    def __init__(self):
        r = lax.axis_index("rows")
        k = lax.axis_index("ctx")
        self.x_hi = lax.div(r, 8)
        self.y = lax.rem(lax.div(r, 2), 4)
        self.core = lax.rem(r, 2)
        self.x_lo = lax.div(k, 4)
        self.z = lax.rem(k, 4)
        self.rows = r
        self.ctx = k
        self.bits = [
            self.x_hi,
            lax.rem(self.x_hi + self.x_lo, 2),
            lax.div(self.y, 2),
            lax.rem(lax.div(self.y, 2) + lax.rem(self.y, 2), 2),
            lax.div(self.z, 2),
            lax.rem(lax.div(self.z, 2) + lax.rem(self.z, 2), 2),
        ]

    def at(self, x_hi=None, x_lo=None, y=None, z=None, core=None):
        x_hi = self.x_hi if x_hi is None else x_hi
        x_lo = self.x_lo if x_lo is None else x_lo
        y = self.y if y is None else y
        z = self.z if z is None else z
        core = self.core if core is None else core
        return (x_hi * 8 + y * 2 + core, x_lo * 4 + z)

    def partner(self):
        return self.at(core=1 - self.core)

    def neighbour(self, dim):
        if dim == 0:
            return self.at(x_hi=1 - self.x_hi, x_lo=1 - self.x_lo)
        if dim == 1:
            return self.at(x_lo=1 - self.x_lo)
        if dim == 2:
            return self.at(y=3 - self.y)
        if dim == 3:
            return self.at(y=self.y + 1 - 2 * lax.rem(self.y, 2))
        if dim == 4:
            return self.at(z=3 - self.z)
        return self.at(z=self.z + 1 - 2 * lax.rem(self.z, 2))


def gray(v):
    return v ^ (v >> 1)


def chip_number(x_hi, x_lo, y, z):
    return gray(2 * x_hi + x_lo) * 16 + gray(y) * 4 + gray(z)


def slot_of(number, order):
    return sum(((number >> (5 - dim)) & 1) << (5 - t) for t, dim in enumerate(order))


HELD_AT = [64 - (64 >> t) for t in range(7)]


class Scatter:
    def __init__(self, place, orders, first, held, send_sems, recv_sems):
        self.place = place
        self.orders = orders
        self.first, self.first_cols = first
        self.held, self.held_cols = held
        self.send_sems = send_sems
        self.recv_sems = recv_sems

    def part(self, s, t, which):
        half = 32 >> t
        if t == 0:
            return self.first, which * half, self.first_cols
        return self.held, HELD_AT[t - 1] + which * half, self.held_cols

    def copy(self, s, t):
        half = 32 >> t
        dim = self.orders[s][t]
        ref, start, cols = self.part(s, t, 1 - self.place.bits[dim])
        return pltpu.make_async_remote_copy(
            src_ref=ref.at[s, pl.ds(start, half), :, cols],
            dst_ref=self.held.at[s, pl.ds(HELD_AT[t], half), :, self.held_cols],
            send_sem=self.send_sems.at[s, t],
            recv_sem=self.recv_sems.at[s, t],
            device_id=self.place.neighbour(dim),
            device_id_type=MESH,
        )

    def send(self, s, t):
        self.copy(s, t).start()

    def take(self, s, t):
        self.copy(s, t).wait_recv()
        half = 32 >> t
        ref, start, cols = self.part(s, t, self.place.bits[self.orders[s][t]])
        per = min(8, half)

        def body(i, carry):
            for j in range(per):
                at = i * per + j
                self.held[s, HELD_AT[t] + at, :, self.held_cols] = (
                    self.held[s, HELD_AT[t] + at, :, self.held_cols].astype(f32)
                    + ref[s, start + at, :, cols].astype(f32)
                ).astype(bf16)
            return carry

        lax.fori_loop(0, half // per, body, 0)
        self.send(s, t + 1)

    def last(self, s):
        self.copy(s, 5).wait_recv()
        ref, start, cols = self.part(s, 5, self.place.bits[self.orders[s][5]])
        return self.held[s, HELD_AT[5], :, self.held_cols].astype(f32) + ref[
            s, start, :, cols
        ].astype(f32)

    def sent(self, steps=range(6)):
        for s in range(6):
            for t in steps:
                self.copy(s, t).wait_send()


def greet(devices):
    barrier = pltpu.get_barrier_semaphore()
    for device in devices:
        pl.semaphore_signal(barrier, inc=1, device_id=device, device_id_type=MESH)
    pl.semaphore_wait(barrier, len(devices))


def greet_all(place, devices):
    barrier = pltpu.get_barrier_semaphore()
    targets = down_targets(place)
    for device in devices + targets[1:]:
        pl.semaphore_signal(barrier, inc=1, device_id=device, device_id_type=MESH)
    swapped = place.x_hi != place.core
    count = len(devices) + 3

    @pl.when(swapped)
    def _():
        pl.semaphore_signal(barrier, inc=1, device_id=targets[0], device_id_type=MESH)
        pl.semaphore_wait(barrier, count + 1)

    @pl.when(jnp.logical_not(swapped))
    def _():
        pl.semaphore_wait(barrier, count)


def push(place, src, dst, send_sem, recv_sem, device):
    return pltpu.make_async_remote_copy(
        src_ref=src,
        dst_ref=dst,
        send_sem=send_sem,
        recv_sem=recv_sem,
        device_id=device,
        device_id_type=MESH,
    )


def down_targets(place):
    return [
        place.at(x_hi=place.core, core=place.x_hi, z=lax.rem(place.z + off, 4)) for off in range(4)
    ]


def dot(left, right):
    return jnp.dot(left, right, preferred_element_type=f32)


def dot_cols(left, right):
    return lax.dot_general(left, right, (((1,), (1,)), ((), ())), preferred_element_type=f32)


FF_HALF = 2304
DOWN_ORDERS = (
    (1, 3, 5, 2, 0, 4),
    (4, 0, 1, 3, 5, 2),
    (0, 1, 3, 2, 4, 5),
    (5, 3, 0, 1, 2, 4),
    (3, 2, 4, 5, 1, 0),
    (2, 3, 5, 0, 4, 1),
)
GATE_ORDERS = (
    (0, 5, 4, 1, 3, 2),
    (1, 5, 0, 4, 3, 2),
    (2, 4, 5, 3, 1, 0),
    (3, 0, 5, 4, 2, 1),
    (2, 5, 0, 3, 1, 4),
    (0, 1, 3, 4, 5, 2),
)
UP_ORDERS = (
    (2, 0, 3, 5, 1, 4),
    (5, 2, 0, 3, 4, 1),
    (3, 1, 5, 2, 0, 4),
    (4, 2, 5, 0, 1, 3),
    (3, 0, 2, 5, 4, 1),
    (4, 1, 5, 0, 2, 3),
)
QUAD_ORDERS = (
    (1, 2, 0, 5, 4, 3),
    (0, 4, 1, 2, 3, 5),
    (3, 1, 5, 0, 2, 4),
    (2, 0, 3, 4, 1, 5),
    (2, 4, 3, 5, 0, 1),
    (4, 0, 2, 3, 5, 1),
)
STEPS = (
    "Bmm0", "Amm0", "Bmm2", "dn", "Amm2", "down", "lo", "Amm1", "B40", "datt",
    "A10", "A40", "A50", "B50", "B10", "out", "Bmm1", "split", "heads0", "D30",
    "B00", "nat", "A30", "D40", "D50", "heads1", "A20", "A11", "B51", "A00",
    "D20", "B20", "D10", "D00", "B11", "B30", "A51", "A41", "free", "Qmm4",
    "Qmm5", "headb", "B52", "B01", "D31", "lastnorm", "B31", "Qmm0", "D41", "D51",
    "Qmm2", "Qmm3", "D21", "B41", "Qmm1", "D01", "A21", "A31", "v0", "D11",
    "Q40", "A01", "A42", "D02", "Q50", "v1", "Q00", "Q20", "Q10", "Q30",
    "B21", "D52", "Q41", "A12", "D32", "B02", "D22", "A22", "B32", "D12",
    "A43", "A02", "Q51", "v2", "B12", "A52", "B53", "D42", "Q21", "Q11",
    "A32", "Q31", "Q01", "B22", "B42", "D03", "Q42", "D13", "B03", "D23",
    "D43", "D53", "A53", "A13", "D33", "A23", "v3", "Q52", "B13", "Q22",
    "B33", "A03", "Q12", "A33", "Q32", "Q02", "B54", "B43", "B23", "D54",
    "Q43", "A44", "A14", "D14", "D34", "B14", "v4", "Q53", "Q23", "Q13",
    "A04", "D44", "Q33", "Q03", "D24", "D04", "A24", "B44", "A54", "B24",
    "B34", "A34", "B04", "Q24", "v5", "Q54", "Q14", "Q44", "Q34", "Q04",
    "Dfin", "Afin", "Qfin", "end",
)


def finish_down(place, down, d_acc, d_stage, d_in, f_send, f_recv, gdn_ref):
    for s in range(6):
        d_acc[pl.ds(48 * (s // 2), 48), pl.ds(128 * (s % 2), 128)] = down.last(s)
    for z in range(4):
        d_stage[z, pl.ds(0, 36), :] = d_acc[pl.ds(36 * z, 36), :]
        d_stage[z, pl.ds(36, 4), :] = jnp.zeros((4, 256), f32)
    targets = down_targets(place)
    swapped = place.x_hi != place.core
    moves = []
    for off in range(4):
        moves.append(
            push(
                place,
                d_stage.at[lax.rem(place.z + off, 4)],
                d_in.at[place.z],
                f_send.at[off],
                f_recv.at[off],
                targets[off],
            )
        )
    for off in range(1, 4):
        moves[off].start()

    @pl.when(swapped)
    def _():
        moves[0].start()
        moves[0].wait_recv()

    @pl.when(jnp.logical_not(swapped))
    def _():
        d_in[place.z] = d_stage[place.z]

    for off in range(1, 4):
        moves[off].wait_recv()
    for z in range(4):
        gdn_ref[:, pl.ds(256 * z, 256)] = d_in[z, pl.ds(0, 36), :]
    for off in range(1, 4):
        moves[off].wait_send()

    @pl.when(swapped)
    def _():
        moves[0].wait_send()


def lanes(rows):
    return lax.broadcasted_iota(jnp.int32, (rows, 128), 1)


def turn_heads(values):
    low = lax.rem(lanes(values.shape[0]), 64) < 32
    return jnp.where(low, pltpu.roll(values, 96, 1), pltpu.roll(values, 32, 1))


def head_mean(values):
    i = lax.broadcasted_iota(jnp.int32, (128, 128), 0)
    j = lax.broadcasted_iota(jnp.int32, (128, 128), 1)
    ones = jnp.where(lax.div(i, 64) == lax.div(j, 64), 1.0 / 64, 0.0).astype(bf16)
    high = values.astype(bf16)
    rest = (values - high.astype(f32)).astype(bf16)
    return dot(high, ones) + dot(rest, ones)


def gain_tiles(qk_gain):
    swapped = pltpu.roll(qk_gain, 64, 1)
    low = lax.broadcasted_iota(jnp.int32, (1, 128), 1) < 64
    return jnp.where(low, qk_gain, swapped), jnp.where(low, swapped, qk_gain)


def head_rows(values):
    low = lanes(values.shape[0]) < 64
    zero = jnp.zeros_like(values)
    return jnp.concatenate([jnp.where(low, values, zero), jnp.where(low, zero, values)], 0)


class Exchange:
    def __init__(self, place, out, into_at, send_sems, recv_sems):
        self.place = place
        self.out = out
        self.into_at = into_at
        self.send_sems = send_sems
        self.recv_sems = recv_sems

    def copy(self, m, off):
        j = lax.rem(self.place.ctx + off, 8)
        return push(
            self.place,
            self.out.at[m, j],
            self.into_at(m, self.place.ctx),
            self.send_sems.at[m, off - 1],
            self.recv_sems.at[m, off - 1],
            (self.place.rows, j),
        )

    def send(self, m):
        for off in range(1, 8):
            self.copy(m, off).start()
        self.into_at(m, self.place.ctx)[...] = self.out[m, self.place.ctx]

    def arrived(self, m):
        for off in range(1, 8):
            self.copy(m, off).wait_recv()

    def sent(self):
        for m in range(2):
            for off in range(1, 8):
                self.copy(m, off).wait_send()


def ctx_peers(place):
    return [(place.rows, lax.rem(place.ctx + off, 8)) for off in range(1, 8)]


def document_edges(bounds_ref, m):
    index = lax.broadcasted_iota(jnp.int32, (1, 1024), 1)
    start = jnp.zeros((1, 1024), jnp.int32)
    end = jnp.full((1, 1024), 1024, jnp.int32)
    for k in range(1, 4):
        cut = bounds_ref[m, 0, k]
        start = jnp.where(index >= cut, cut, start)
        end = jnp.where(index < bounds_ref[m, 0, 4 - k], bounds_ref[m, 0, 4 - k], end)
    return start, end


def attention_kernel(
    bounds_ref,
    x_ref,
    cos_ref,
    sin_ref,
    gain_ref,
    qk_gain_ref,
    w_qkv_hbm,
    w_out_hbm,
    mid_ref,
    na_ref,
    att_ref,
    proj_ref,
    qkv_ref,
    o_ref,
    l_ref,
    w_qkv,
    w_out,
    q_out,
    a_out,
    a_in,
    q2,
    kk,
    vo,
    w_sems,
    q_send,
    q_recv,
    a_send,
    a_recv,
):
    place = Place()
    loads = [
        pltpu.make_async_copy(w_qkv_hbm, w_qkv, w_sems.at[0]),
        pltpu.make_async_copy(w_out_hbm, w_out, w_sems.at[1]),
    ]
    for load in loads:
        load.start()
    greet(ctx_peers(place))
    heads_out = Exchange(place, q_out, lambda m, j: qkv_ref.at[m, j], q_send, q_recv)
    heads_back = Exchange(place, a_out, lambda m, j: a_in.at[m, j], a_send, a_recv)

    inputs = x_ref[...].astype(f32)
    scale = lax.rsqrt(jnp.mean(inputs * inputs, axis=-1, keepdims=True) + norm_eps)
    na_ref[...] = (inputs * scale * gain_ref[...]).astype(bf16)
    loads[0].wait()
    gain_q, gain_k = gain_tiles(qk_gain_ref[...])
    low = lanes(256) < 64

    def turned(tile, gain):
        u = tile * lax.rsqrt(head_mean(tile * tile) + norm_eps) * gain
        return u * cos_ref[...] + turn_heads(u) * sin_ref[...]

    for i in range(4):
        pair = dot(na_ref[...], w_qkv[:, pl.ds(256 * i, 256)])
        proj_ref[:, pl.ds(256 * i, 256)] = pair
        for j in range(2):
            tile = turned(pair[:, 128 * j : 128 * j + 128], gain_q) * 0.125
            for m in range(2):
                q_out[m, 2 * i + j, :, pl.ds(0, 128)] = tile[128 * m : 128 * m + 128].astype(bf16)
    for i in range(2):
        key_pair = dot(na_ref[...], w_qkv[:, pl.ds(1024 + 256 * i, 256)])
        value_pair = dot(na_ref[...], w_qkv[:, pl.ds(1536 + 256 * i, 256)])
        proj_ref[:, pl.ds(1024 + 256 * i, 256)] = key_pair
        for j in range(2):
            key = turned(key_pair[:, 128 * j : 128 * j + 128], gain_k)
            value = value_pair[:, 128 * j : 128 * j + 128]
            first = jnp.where(low, key, pltpu.roll(value, 64, 1)).astype(bf16)
            second = jnp.where(low, pltpu.roll(key, 64, 1), value).astype(bf16)
            for m in range(2):
                rows = slice(128 * m, 128 * m + 128)
                q_out[m, 4 * i + 2 * j, :, pl.ds(128, 128)] = first[rows]
                q_out[m, 4 * i + 2 * j + 1, :, pl.ds(128, 128)] = second[rows]
    for m in range(2):
        heads_out.send(m)

    for m in range(2):
        heads_out.arrived(m)
        ends = document_edges(bounds_ref, m)[1]
        for b in range(4):
            query = qkv_ref[m, pl.ds(2 * b, 2), :, pl.ds(0, 128)].reshape(256, 128)
            both = qkv_ref[m, pl.ds(2 * b, 2), :, pl.ds(128, 128)].reshape(256, 128).astype(f32)
            swapped = pltpu.roll(both, 64, 1)
            q2[b] = head_rows(query)
            kk[b] = jnp.where(low, both, swapped).astype(bf16)
            vo[b] = jnp.where(low, swapped, 1.0).astype(bf16)
        for qb in range(4):
            acc = jnp.zeros((512, 128), f32)
            for kb in range(qb + 1):
                scores = dot_cols(q2[qb], kk[kb])
                t = 256 * qb + lax.rem(lax.broadcasted_iota(jnp.int32, (512, 256), 0), 256)
                keep = t < ends[:, 256 * kb : 256 * kb + 256]
                if kb == qb:
                    s = 256 * kb + lax.broadcasted_iota(jnp.int32, (512, 256), 1)
                    keep = keep & (s <= t)
                weights = jnp.where(keep, jnp.exp(scores), 0.0).astype(bf16)
                acc = acc + dot(weights, vo[kb])
            total = pltpu.roll(acc, 64, 1)
            head0 = acc[:256]
            head1 = pltpu.roll(acc[256:], 64, 1)
            denominator = jnp.where(low, total[:256], acc[256:])
            out = jnp.where(low, head0, head1) / denominator
            o_ref[m, pl.ds(256 * qb, 256), :] = out
            log_total = jnp.log(denominator).T
            l_ref[m, pl.ds(0, 1), pl.ds(256 * qb, 256)] = log_total[0:1]
            l_ref[m, pl.ds(1, 1), pl.ds(256 * qb, 256)] = log_total[64:65]
            for half in range(2):
                a_out[m, 2 * qb + half] = out[128 * half : 128 * half + 128].astype(bf16)
        heads_back.send(m)
    loads[1].wait()
    for m in range(2):
        heads_back.arrived(m)
        for j in range(8):
            att_ref[pl.ds(128 * m, 128), pl.ds(128 * j, 128)] = a_in[m, j]
    mid_ref[...] = x_ref[...].astype(f32) + dot(att_ref[...], w_out[...])
    heads_out.sent()
    heads_back.sent()


def attention(bounds, x, cosine, sine, gain, qk_gain, w_qkv, w_out):
    vmem = pl.BlockSpec(memory_space=pltpu.VMEM)
    hbm = pl.BlockSpec(memory_space=pl.ANY)
    smem = pl.BlockSpec(memory_space=pltpu.SMEM)
    dma = pltpu.SemaphoreType.DMA
    return pl.pallas_call(
        attention_kernel,
        out_shape=(
            jax.ShapeDtypeStruct((256, 1024), f32),
            jax.ShapeDtypeStruct((256, 1024), bf16),
            jax.ShapeDtypeStruct((256, 1024), bf16),
            jax.ShapeDtypeStruct((256, 1536), f32),
            jax.ShapeDtypeStruct((2, 8, 128, 256), bf16),
            jax.ShapeDtypeStruct((2, 1024, 128), f32),
            jax.ShapeDtypeStruct((2, 2, 1024), f32),
        ),
        in_specs=[smem] + [vmem] * 5 + [hbm] * 2,
        out_specs=(vmem,) * 7,
        scratch_shapes=[
            pltpu.VMEM((1024, 2048), bf16),
            pltpu.VMEM((1024, 1024), bf16),
            pltpu.VMEM((2, 8, 128, 256), bf16),
            pltpu.VMEM((2, 8, 128, 128), bf16),
            pltpu.VMEM((2, 8, 128, 128), bf16),
            pltpu.VMEM((4, 512, 128), bf16),
            pltpu.VMEM((4, 256, 128), bf16),
            pltpu.VMEM((4, 256, 128), bf16),
            dma((2,)),
            dma((2, 7)),
            dma((2, 7)),
            dma((2, 7)),
            dma((2, 7)),
        ],
        compiler_params=pltpu.CompilerParams(
            collective_id=2, has_side_effects=True, vmem_limit_bytes=VMEM_LIMIT
        ),
        name="attention_forward",
    )(bounds, x, cosine, sine, gain, qk_gain, w_qkv, w_out)


def reorder_store(part, first, s, order, x_hi, at, width):
    part = part.reshape(4, 2, 8, 8, width)
    for y in range(4):
        for x_lo in range(2):
            for z in range(4):
                slot = slot_of(chip_number(x_hi, x_lo, y, z), order)
                first[s, slot, :, at] = part[y, :, 4 * x_lo + z].reshape(16, width).astype(bf16)


def main_kernel(
    bounds_ref,
    mid_ref,
    gain_ffn_ref,
    gain_ref,
    qk_gain_ref,
    cot_hbm,
    x_hbm,
    cos_hbm,
    sin_hbm,
    na_hbm,
    att_hbm,
    proj_hbm,
    qkv_hbm,
    o_hbm,
    l_hbm,
    wgu_hbm,
    wd_hbm,
    w_qkv_hbm,
    w_out_hbm,
    out_hbm,
    gtok_hbm,
    ggu_ref,
    gdn_ref,
    gqkv_ref,
    gout_ref,
    vec_out,
    a_first,
    a_held,
    b_first,
    b_held,
    d_first,
    d_held,
    nf,
    dyb,
    sum_send,
    sum_recv,
    xboth,
    dmid,
    do_out,
    do_in,
    dpin,
    dmin,
    dm_own,
    g_fin,
    g_in,
    d_acc,
    d_stage,
    d_in,
    q_fin,
    q_in,
    vec,
    vec_in,
    w_sems,
    l_sems,
    x_send,
    x_recv,
    a_send,
    a_recv,
    b_send,
    b_recv,
    d_send,
    d_recv,
    q_send,
    q_recv,
    f_send,
    f_recv,
    do_send,
    do_recv,
    t_send,
    t_recv,
    v_send,
    v_recv,
    free_sem,
):
    place = Place()
    core = place.core
    partner = place.partner()
    every = slice(None)
    down = Scatter(place, DOWN_ORDERS, (d_first, every), (d_held, every), d_send, d_recv)
    gate = Scatter(place, GATE_ORDERS, (a_first, every), (a_held, every), a_send, a_recv)
    up = Scatter(place, UP_ORDERS, (b_first, every), (b_held, every), b_send, b_recv)
    narrow = pl.ds(0, 256)
    quad = Scatter(place, QUAD_ORDERS, (a_first, narrow), (b_first, narrow), q_send, q_recv)
    sums = {"D": down, "A": gate, "B": up, "Q": quad}
    steps = iter(STEPS)

    def run(ops, until):
        for name in steps:
            if name == until:
                return
            if name in ops:
                ops[name]()
            else:
                sums[name[0]].take(int(name[1]), int(name[2]))
    def t_at(m, j):
        return nf.at[
            pl.ds(pl.multiple_of(256 * m + 128 * lax.div(j, 4), 128), 128),
            pl.ds(pl.multiple_of(256 * lax.rem(j, 4), 256), 256),
        ]

    grads_out = Exchange(place, do_out, lambda m, j: do_in.at[m, j], do_send, do_recv)
    own_rows = pl.ds(0, 256)
    other_rows = pl.ds(256, 256)
    to_dy = push(place, cot_hbm, dyb.at[other_rows], x_send.at[0], x_recv.at[0], partner)
    to_nf = push(place, nf.at[own_rows], nf.at[other_rows], x_send.at[1], x_recv.at[1], partner)
    to_out = push(place, sum_send, sum_recv.at[0], x_send.at[2], x_recv.at[2], partner)
    to_back = push(place, sum_send, sum_recv.at[1], x_send.at[3], x_recv.at[3], partner)
    to_na = push(place, na_hbm, xboth.at[0], x_send.at[4], x_recv.at[4], partner)
    to_att = push(place, att_hbm, xboth.at[1], x_send.at[5], x_recv.at[5], partner)
    to_dm = push(place, dm_own.at[1 - core], dmin, x_send.at[6], x_recv.at[6], partner)
    out_copy = pltpu.make_async_copy(sum_send, out_hbm, l_sems.at[0])

    def feed_forward(wgu, wd, nft, h, ht, dgu, sum_own):
        loads = []
        for i in range(3):
            at = pl.multiple_of(core * FF_HALF + 768 * i, 256)
            up_at = pl.multiple_of(4608 + core * FF_HALF + 768 * i, 256)
            loads.append(
                [
                    pltpu.make_async_copy(
                        wgu_hbm.at[:, pl.ds(at, 768)],
                        wgu.at[:, pl.ds(768 * i, 768)],
                        w_sems.at[3 * i],
                    ),
                    pltpu.make_async_copy(
                        wgu_hbm.at[:, pl.ds(up_at, 768)],
                        wgu.at[:, pl.ds(FF_HALF + 768 * i, 768)],
                        w_sems.at[3 * i + 1],
                    ),
                    pltpu.make_async_copy(
                        wd_hbm.at[pl.ds(at, 768)], wd.at[pl.ds(768 * i, 768)], w_sems.at[3 * i + 2]
                    ),
                ]
            )
        cot_load = pltpu.make_async_copy(cot_hbm, dyb.at[own_rows], l_sems.at[1])
        cot_load.start()
        for copies in loads:
            for copy in copies:
                copy.start()
        greet_all(
            place,
            [partner] + [place.neighbour(dim) for dim in range(6)] + ctx_peers(place),
        )
        to_dy.start()
        mid = mid_ref[...]
        scale = lax.rsqrt(jnp.mean(mid * mid, axis=-1, keepdims=True) + norm_eps)
        nf[own_rows, :] = (mid * scale * gain_ffn_ref[...]).astype(bf16)
        to_nf.start()
        nft[:, own_rows] = nf[own_rows, :].T
        to_na.start()
        to_att.start()
        cot_load.wait()
        to_dy.wait_recv()
        to_nf.wait_recv()
        nft[:, other_rows] = nf[other_rows, :].T

        for i in range(3):
            for copy in loads[i]:
                copy.wait()
            for j in range(3):
                at = 768 * i + 256 * j
                cols, up_cols = pl.ds(at, 256), pl.ds(FF_HALF + at, 256)
                gated = dot(nf[...], wgu[:, cols])
                upward = dot(nf[...], wgu[:, up_cols])
                grad_hidden = dot_cols(dyb[...], wd[cols, :])
                sigma = 1.0 / (1.0 + jnp.exp(-gated))
                silu = gated * sigma
                h[:, cols] = (silu * upward).astype(bf16)
                dgu[:, cols] = (grad_hidden * upward * (sigma + silu * (1.0 - sigma))).astype(bf16)
                dgu[:, up_cols] = (grad_hidden * silu).astype(bf16)

        def down_grads():
            for block in range(3):
                ht[...] = h[:, pl.ds(768 * block, 768)].T
                for z in range(4):
                    part = dot(ht[...], dyb[:, pl.ds(256 * z, 256)])
                    for i in range(16):
                        q = 16 * block + i
                        y, core_to, x_lo, rg = q // 12, (q // 6) % 2, (q // 3) % 2, q % 3
                        for ch in range(2):
                            s = 2 * rg + ch
                            slot = slot_of(chip_number(core_to, x_lo, y, z), DOWN_ORDERS[s])
                            d_first[s, slot] = part[
                                48 * i : 48 * i + 48, 128 * ch : 128 * ch + 128
                            ].astype(bf16)
            for s in range(6):
                down.send(s, 0)

        def back_to_norm():
            for j in range(4):
                at = pl.ds(256 * j, 256)
                part = dot_cols(dgu[...], wgu[at, :])
                dmid[:, at] = part[:256]
                sum_send[:, at] = part[256:].astype(bf16)
            to_back.start()

        def wide_grads(scatter, first, base, orders, p):
            for x_hi in range(2):
                rows = nft[pl.ds(512 * x_hi, 512), :]
                for j in range(3):
                    part = dot(rows, dgu[:, pl.ds(base + 768 * p + 256 * j, 256)])
                    for k in range(2):
                        tile = 2 * j + k
                        s = 2 * p + tile // 3
                        reorder_store(
                            part[:, 128 * k : 128 * k + 128],
                            first,
                            s,
                            orders[s],
                            x_hi,
                            pl.ds(128 * (tile % 3), 128),
                            128,
                        )
            for s in (2 * p, 2 * p + 1):
                scatter.send(s, 0)

        w_out_load = pltpu.make_async_copy(w_out_hbm, wd.at[pl.ds(0, 1024)], l_sems.at[4])

        def output():
            to_back.wait_send()
            for j in range(4):
                at = pl.ds(256 * j, 256)
                part = dot(h[...], wd[:, at])
                sum_own[:, at] = part[:256]
                sum_send[:, at] = part[256:].astype(bf16)
            to_out.start()
            w_out_load.start()

        def output_sum():
            to_out.wait()
            sum_send[...] = (mid_ref[...] + sum_own[...] + sum_recv[0].astype(f32)).astype(bf16)
            out_copy.start()

        def norm_back():
            to_back.wait_recv()
            mid = mid_ref[...]
            scale = lax.rsqrt(jnp.mean(mid * mid, axis=-1, keepdims=True) + norm_eps)
            normed = mid * scale
            grad_nffn = dmid[...] + sum_recv[1].astype(f32)
            gain_grad = jnp.sum(grad_nffn * normed, axis=0, keepdims=True)
            for i in range(8):
                vec[0, pl.ds(8 + i, 1), :] = gain_grad[:, 128 * i : 128 * i + 128]
            grad_e = grad_nffn * gain_ffn_ref[...]
            dmid[...] = dyb[own_rows, :].astype(f32) + scale * (
                grad_e - normed * jnp.mean(grad_e * normed, axis=-1, keepdims=True)
            )
            for half in range(2):
                dm_own[half] = dmid[:, pl.ds(512 * half, 512)].astype(bf16)
            to_dm.start()

            to_nf.wait_send()
            w_out_load.wait()
            for i in range(4):
                pair = dot_cols(dm_own[0], wd[pl.ds(256 * i, 256), pl.ds(0, 512)]) + dot_cols(
                    dm_own[1], wd[pl.ds(256 * i, 256), pl.ds(512, 512)]
                )
                for j in range(2):
                    for m in range(2):
                        do_out[m, 2 * i + j] = pair[
                            128 * m : 128 * m + 128, 128 * j : 128 * j + 128
                        ].astype(bf16)
            for m in range(2):
                grads_out.send(m)

        ops = {
            "down": down_grads,
            "dn": back_to_norm,
            "lo": output,
            "datt": norm_back,
            "out": output_sum,
        }
        for p in range(3):
            ops[f"Amm{p}"] = functools.partial(wide_grads, gate, a_first, 0, GATE_ORDERS, p)
            ops[f"Bmm{p}"] = functools.partial(wide_grads, up, b_first, FF_HALF, UP_ORDERS, p)
        run(ops, "split")

    pl.run_scoped(
        feed_forward,
        pltpu.VMEM((1024, 4608), bf16),
        pltpu.VMEM((FF_HALF, 1024), bf16),
        pltpu.VMEM((1024, 512), bf16),
        pltpu.VMEM((512, FF_HALF), bf16),
        pltpu.VMEM((768, 512), bf16),
        pltpu.VMEM((512, 4608), bf16),
        pltpu.VMEM((256, 1024), f32),
    )

    def vec_move(step):
        device = place.neighbour(step) if step < 6 else partner
        return push(place, vec.at[step], vec_in.at[step], v_send.at[step], v_recv.at[step], device)

    def vec_take(step):
        vec_move(step).wait_recv()
        vec[step + 1] = vec[step] + vec_in[step]
        vec_move(step + 1).start()

    def down_end():
        finish_down(place, down, d_acc, d_stage, d_in, f_send, f_recv, gdn_ref)

    swap = push(place, g_fin.at[1 - core], g_in, x_send.at[8], x_recv.at[8], partner)
    swap_q = push(place, q_fin.at[1 - core], q_in, x_send.at[9], x_recv.at[9], partner)

    def wide_end():
        for s in range(12):
            total = (gate if s < 6 else up).last(s % 6)
            g_fin[0, s] = total[:8]
            g_fin[1, s] = total[8:]
        swap.start()

    def quad_end():
        for s in range(6):
            total = quad.last(s)
            q_fin[0, s] = total[:8]
            q_fin[1, s] = total[8:]
        swap_q.start()

    def attention_back(
        w_qkv, x_ref, gtok, cos_ref, sin_ref, proj_ref, qkv_ref, o_ref, l_ref,
        q2, do2, kk, vv, kt, delta, dq, dp, own, nat, attt, cols, t_out,
    ):
        sources = [qkv_hbm, o_hbm, l_hbm, cos_hbm, sin_hbm, proj_hbm, x_hbm, w_qkv_hbm]
        loads = [
            pltpu.make_async_copy(source, target, w_sems.at[i])
            for i, (source, target) in enumerate(
                zip(
                    sources,
                    [qkv_ref, o_ref, l_ref, cos_ref, sin_ref, proj_ref, x_ref, w_qkv],
                    strict=True,
                )
            )
        ]
        for load in loads:
            load.start()
        grads_back = Exchange(place, t_out, t_at, t_send, t_recv)
        low = lanes(256) < 64

        def heads_back(m):
            if m == 0:
                for load in loads[:3]:
                    load.wait()
            grads_out.arrived(m)
            starts = document_edges(bounds_ref, m)[0]
            for b in range(4):
                query = qkv_ref[m, pl.ds(2 * b, 2), :, pl.ds(0, 128)].reshape(256, 128)
                pair = qkv_ref[m, pl.ds(2 * b, 2), :, pl.ds(128, 128)].reshape(256, 128)
                pair = pair.astype(f32)
                grad = do_in[m, pl.ds(2 * b, 2)].reshape(256, 128)
                swapped = pltpu.roll(pair, 64, 1)
                key_pair = jnp.where(low, pair, swapped)
                q2[b] = head_rows(query)
                do2[b] = head_rows(grad)
                kk[b] = key_pair.astype(bf16)
                vv[b] = jnp.where(low, swapped, pair).astype(bf16)
                kt[b] = key_pair.T.astype(bf16)
                inner = (grad.astype(f32) * o_ref[m, pl.ds(256 * b, 256), :]).T
                delta[b, :, pl.ds(0, 256)] = jnp.sum(inner[:64], axis=0, keepdims=True)
                delta[b, :, pl.ds(256, 256)] = jnp.sum(inner[64:], axis=0, keepdims=True)
            for kb in range(4):
                grad_key = jnp.zeros((256, 128), f32)
                grad_value = jnp.zeros((256, 128), f32)
                for qb in range(kb, 4):
                    scores = dot_cols(kk[kb], q2[qb])
                    log_total = jnp.concatenate(
                        [l_ref[m, pl.ds(i, 1), pl.ds(256 * qb, 256)] for i in range(2)], 1
                    )
                    start = starts[:, 256 * qb : 256 * qb + 256]
                    s = 256 * kb + lax.broadcasted_iota(jnp.int32, (256, 512), 0)
                    keep = s >= jnp.concatenate([start, start], 1)
                    if kb == qb:
                        t = lax.broadcasted_iota(jnp.int32, (256, 512), 1)
                        keep = keep & (s <= 256 * qb + lax.rem(t, 256))
                    probs = jnp.where(keep, jnp.exp(scores - log_total), 0.0)
                    grad_probs = dot_cols(vv[kb], do2[qb])
                    grad_scores = (probs * (grad_probs - delta[qb])).astype(bf16)
                    grad_value = grad_value + dot(probs.astype(bf16), do2[qb])
                    grad_key = grad_key + dot(grad_scores, q2[qb])
                    grad_query = dot(kt[kb], grad_scores)
                    if kb == 0:
                        dq[qb] = grad_query[:64]
                    else:
                        dq[qb] = dq[qb] + grad_query[:64]
                grad_key = grad_key + pltpu.roll(grad_key, 64, 1)
                grad_value = grad_value + pltpu.roll(grad_value, 64, 1)
                tile = jnp.where(low, grad_key, grad_value).astype(bf16)
                for half in range(2):
                    rows = slice(128 * half, 128 * half + 128)
                    t_out[m, 2 * kb + half, :, pl.ds(128, 128)] = tile[rows]
            for qb in range(4):
                stacked = jnp.concatenate([dq[qb, :, pl.ds(0, 256)], dq[qb, :, pl.ds(256, 256)]], 0)
                tile = (stacked * 0.125).T.astype(bf16)
                for half in range(2):
                    rows = slice(128 * half, 128 * half + 128)
                    t_out[m, 2 * qb + half, :, pl.ds(0, 128)] = tile[rows]
            grads_back.send(m)

        def sums_free():
            gate.sent([0])
            up.sent([0])
            for dim in range(6):
                pl.semaphore_signal(
                    free_sem, inc=1, device_id=place.neighbour(dim), device_id_type=MESH
                )

        own_loads = [
            pltpu.make_async_copy(na_hbm, own.at[0], l_sems.at[2]),
            pltpu.make_async_copy(att_hbm, own.at[1], l_sems.at[3]),
        ]
        for load in own_loads:
            load.start()

        def token_sides():
            to_na.wait_recv()
            nat[:, other_rows] = xboth[0].T
            to_att.wait_recv()
            attt[:, other_rows] = xboth[1].T
            for load in own_loads:
                load.wait()
            nat[:, own_rows] = own[0].T
            attt[:, own_rows] = own[1].T
            to_dm.wait_recv()
            cols[own_rows, pl.ds(1024, 512)] = dm_own[core]
            cols[other_rows, pl.ds(1024, 512)] = dmin[...]

        def projection_grads(s):
            left = nat if s < 4 else attt
            if s == 0:
                to_dp.wait_recv()
                cols[other_rows, pl.ds(0, 1024)] = dpin[...]
            for x_hi in range(2):
                part = dot(left[pl.ds(512 * x_hi, 512), :], cols[:, pl.ds(256 * s, 256)])
                reorder_store(part, a_first, s, QUAD_ORDERS[s], x_hi, narrow, 256)
            if s == 4:
                pl.semaphore_wait(free_sem, 6)
            quad.send(s, 0)

        gain_q, gain_k = gain_tiles(qk_gain_ref[...])

        def both_rows(j, at):
            return jnp.concatenate([t_at(m, j)[:, pl.ds(at, 128)] for m in range(2)], 0).astype(f32)

        def head_back(grad, value, gain):
            grad = grad * cos_ref[...] + turn_heads(grad * sin_ref[...])
            scale = lax.rsqrt(head_mean(value * value) + norm_eps)
            normed = value * scale
            grad_e = grad * gain
            gain_grad = jnp.sum(grad * normed, axis=0, keepdims=True)
            return scale * (grad_e - normed * head_mean(grad_e * normed)), gain_grad

        to_dp = push(place, dp.at[1 - core], dpin, x_send.at[7], x_recv.at[7], partner)
        gtok_copy = pltpu.make_async_copy(gtok, gtok_hbm, l_sems.at[1])

        def turn_back():
            for load in loads[3:6]:
                load.wait()
            for m in range(2):
                grads_back.arrived(m)
            sum_q = jnp.zeros((1, 128), f32)
            sum_k = jnp.zeros((1, 128), f32)
            for j in range(8):
                back, part = head_back(both_rows(j, 0), proj_ref[:, pl.ds(128 * j, 128)], gain_q)
                dp[0, :, pl.ds(128 * j, 128)] = back.astype(bf16)
                sum_q = sum_q + part
            for i in range(4):
                first = both_rows(2 * i, 128)
                second = both_rows(2 * i + 1, 128)
                grad_key = jnp.where(low, first, pltpu.roll(second, 64, 1))
                grad_value = jnp.where(low, pltpu.roll(first, 64, 1), second)
                back, part = head_back(grad_key, proj_ref[:, pl.ds(1024 + 128 * i, 128)], gain_k)
                dp[1, :, pl.ds(128 * i, 128)] = back.astype(bf16)
                dp[1, :, pl.ds(512 + 128 * i, 128)] = grad_value.astype(bf16)
                sum_k = sum_k + part
            to_dp.start()
            sum_q = sum_q + pltpu.roll(sum_q, 64, 1)
            sum_k = sum_k + pltpu.roll(sum_k, 64, 1)
            vec[0, pl.ds(16, 8), :] = jnp.zeros((8, 128), f32)
            vec[0, pl.ds(16, 1), :] = jnp.where(
                lax.broadcasted_iota(jnp.int32, (1, 128), 1) < 64, sum_q, sum_k
            )
            cols[own_rows, pl.ds(0, 1024)] = dp[core]

        def last_norm():
            loads[6].wait()
            loads[7].wait()
            inputs = x_ref[...].astype(f32)
            scale = lax.rsqrt(jnp.mean(inputs * inputs, axis=-1, keepdims=True) + norm_eps)
            normed = inputs * scale
            grad_n = dot_cols(dp[0], w_qkv[:, pl.ds(0, 1024)]) + dot_cols(
                dp[1], w_qkv[:, pl.ds(1024, 1024)]
            )
            gain_grad = jnp.sum(grad_n * normed, axis=0, keepdims=True)
            grad_e = grad_n * gain_ref[...]
            gtok[...] = dmid[...] + scale * (
                grad_e - normed * jnp.mean(grad_e * normed, axis=-1, keepdims=True)
            )
            gtok_copy.start()
            for i in range(8):
                vec[0, pl.ds(i, 1), :] = gain_grad[:, 128 * i : 128 * i + 128]
            vec_move(0).start()

        ops = {
            "heads0": functools.partial(heads_back, 0),
            "heads1": functools.partial(heads_back, 1),
            "free": sums_free,
            "nat": token_sides,
            "headb": turn_back,
            "lastnorm": last_norm,
            "Dfin": down_end,
            "Afin": wide_end,
            "Qfin": quad_end,
        }
        for s in range(6):
            ops[f"Qmm{s}"] = functools.partial(projection_grads, s)
            ops[f"v{s}"] = functools.partial(vec_take, s)
        run(ops, "end")
        gtok_copy.wait()
        to_dp.wait_send()
        grads_back.sent()

    pl.run_scoped(
        attention_back,
        pltpu.VMEM((1024, 2048), bf16),
        pltpu.VMEM((256, 1024), bf16),
        pltpu.VMEM((256, 1024), f32),
        pltpu.VMEM((256, 128), f32),
        pltpu.VMEM((256, 128), f32),
        pltpu.VMEM((256, 1536), f32),
        pltpu.VMEM((2, 8, 128, 256), bf16),
        pltpu.VMEM((2, 1024, 128), f32),
        pltpu.VMEM((2, 2, 1024), f32),
        pltpu.VMEM((4, 512, 128), bf16),
        pltpu.VMEM((4, 512, 128), bf16),
        pltpu.VMEM((4, 256, 128), bf16),
        pltpu.VMEM((4, 256, 128), bf16),
        pltpu.VMEM((4, 128, 256), bf16),
        pltpu.VMEM((4, 1, 512), f32),
        pltpu.VMEM((4, 64, 512), f32),
        pltpu.VMEM((2, 256, 1024), bf16),
        pltpu.VMEM((2, 256, 1024), bf16),
        pltpu.VMEM((1024, 512), bf16),
        pltpu.VMEM((1024, 512), bf16),
        pltpu.VMEM((512, 1536), bf16),
        pltpu.VMEM((2, 8, 128, 256), bf16),
    )

    def wide_cols(of, s):
        return pl.ds(pl.multiple_of((s // 6) * 4608 + of * FF_HALF + (s % 6) * 384, 128), 384)

    def quad_cols(of, s):
        if s < 4:
            return gqkv_ref, pl.ds(pl.multiple_of(of * 1024 + 256 * s, 256), 256)
        return gout_ref, pl.ds(pl.multiple_of(of * 512 + 256 * (s - 4), 256), 256)

    for s in range(12):
        ggu_ref[:, wide_cols(core, s)] = g_fin[core, s]
    swap.wait_recv()
    for s in range(12):
        ggu_ref[:, wide_cols(1 - core, s)] = g_in[s]
    for s in range(6):
        ref, at = quad_cols(core, s)
        ref[:, at] = q_fin[core, s]
    swap_q.wait_recv()
    for s in range(6):
        ref, at = quad_cols(1 - core, s)
        ref[:, at] = q_in[s]
    vec_move(6).wait_recv()
    vec_out[...] = vec[6] + vec_in[6]

    for move in (to_dy, to_na, to_att, to_dm, swap, swap_q):
        move.wait_send()
    out_copy.wait()
    for step in range(7):
        vec_move(step).wait_send()
    down.sent()
    gate.sent(range(1, 6))
    up.sent(range(1, 6))
    quad.sent()
    grads_out.sent()


def main_part(bounds, *arrays):
    vmem = pl.BlockSpec(memory_space=pltpu.VMEM)
    hbm = pl.BlockSpec(memory_space=pl.ANY)
    smem = pl.BlockSpec(memory_space=pltpu.SMEM)
    dma = pltpu.SemaphoreType.DMA
    return pl.pallas_call(
        main_kernel,
        out_shape=(
            jax.ShapeDtypeStruct((256, 1024), bf16),
            jax.ShapeDtypeStruct((256, 1024), f32),
            jax.ShapeDtypeStruct((8, 9216), f32),
            jax.ShapeDtypeStruct((36, 1024), f32),
            jax.ShapeDtypeStruct((8, 2048), f32),
            jax.ShapeDtypeStruct((8, 1024), f32),
            jax.ShapeDtypeStruct((24, 128), f32),
        ),
        in_specs=[smem] + [vmem] * 4 + [hbm] * 14,
        out_specs=(hbm, hbm) + (vmem,) * 5,
        scratch_shapes=[
            pltpu.VMEM((6, 64, 16, 384), bf16),
            pltpu.VMEM((6, 63, 16, 384), bf16),
            pltpu.VMEM((6, 64, 16, 384), bf16),
            pltpu.VMEM((6, 63, 16, 384), bf16),
            pltpu.VMEM((6, 64, 48, 128), bf16),
            pltpu.VMEM((6, 63, 48, 128), bf16),
            pltpu.VMEM((512, 1024), bf16),
            pltpu.VMEM((512, 1024), bf16),
            pltpu.VMEM((256, 1024), bf16),
            pltpu.VMEM((2, 256, 1024), bf16),
            pltpu.VMEM((2, 256, 1024), bf16),
            pltpu.VMEM((256, 1024), f32),
            pltpu.VMEM((2, 8, 128, 128), bf16),
            pltpu.VMEM((2, 8, 128, 128), bf16),
            pltpu.VMEM((256, 1024), bf16),
            pltpu.VMEM((256, 512), bf16),
            pltpu.VMEM((2, 256, 512), bf16),
            pltpu.VMEM((2, 12, 8, 384), f32),
            pltpu.VMEM((12, 8, 384), f32),
            pltpu.VMEM((144, 256), f32),
            pltpu.VMEM((4, 40, 256), f32),
            pltpu.VMEM((4, 40, 256), f32),
            pltpu.VMEM((2, 6, 8, 256), f32),
            pltpu.VMEM((6, 8, 256), f32),
            pltpu.VMEM((7, 24, 128), f32),
            pltpu.VMEM((7, 24, 128), f32),
            dma((9,)),
            dma((5,)),
            dma((10,)),
            dma((10,)),
            dma((6, 6)),
            dma((6, 6)),
            dma((6, 6)),
            dma((6, 6)),
            dma((6, 6)),
            dma((6, 6)),
            dma((6, 6)),
            dma((6, 6)),
            dma((4,)),
            dma((4,)),
            dma((2, 7)),
            dma((2, 7)),
            dma((2, 7)),
            dma((2, 7)),
            dma((7,)),
            dma((7,)),
            pltpu.SemaphoreType.REGULAR,
        ],
        compiler_params=pltpu.CompilerParams(
            collective_id=0, has_side_effects=True, vmem_limit_bytes=VMEM_LIMIT
        ),
        name="feed_forward_and_backward",
    )(bounds, *arrays)


def finish_kernel(*refs):
    arrays, vec = refs[:6], refs[6]
    targets, (gain_a, gain_f, gain_qk) = refs[7:13], refs[13:16]
    passing, (in_sems, out_sems) = refs[16:22], refs[22:]
    reads = [
        pltpu.make_async_copy(array, held, in_sems.at[i])
        for i, (array, held) in enumerate(zip(arrays, passing, strict=True))
    ]
    writes = [
        pltpu.make_async_copy(held, target, out_sems.at[i])
        for i, (held, target) in enumerate(zip(passing, targets, strict=True))
    ]
    for read in reads:
        read.start()
    own = lax.axis_index("rows") * 8 + lax.axis_index("ctx")
    row = lax.div(own, 16)
    at = lax.rem(own, 16)
    lane = lax.broadcasted_iota(jnp.int32, (8, 128), 1)
    tile = lax.broadcasted_iota(jnp.int32, (8, 128), 0)

    def pick(values, of_row, of_lane, count):
        kept = jnp.sum(jnp.where(tile == of_row, values, 0.0), axis=0, keepdims=True)
        place = lax.broadcasted_iota(jnp.int32, (128, count), 0)
        order = lax.broadcasted_iota(jnp.int32, (128, count), 1)
        rows = jnp.broadcast_to(kept, (8, 128)).T[:, :count]
        return jnp.sum(jnp.where(place == of_lane + order, rows, 0.0), axis=0, keepdims=True)

    gain_a[...] = pick(vec[pl.ds(0, 8), :], row, 8 * at, 8)
    gain_f[...] = pick(vec[pl.ds(8, 8), :], row, 8 * at, 8)
    gain_qk[...] = pick(vec[pl.ds(16, 8), :], 0, own, 1)
    for read, write in zip(reads, writes, strict=True):
        read.wait()
        write.start()
    for write in writes:
        write.wait()


def finish(out, gtok, ggu, gdn, gqkv, gout, vec):
    vmem = pl.BlockSpec(memory_space=pltpu.VMEM)
    hbm = pl.BlockSpec(memory_space=pl.ANY)
    same = [jax.ShapeDtypeStruct(a.shape, a.dtype) for a in (out, gtok, ggu, gdn, gqkv, gout)]
    return pl.pallas_call(
        finish_kernel,
        out_shape=(
            *same,
            jax.ShapeDtypeStruct((1, 8), f32),
            jax.ShapeDtypeStruct((1, 8), f32),
            jax.ShapeDtypeStruct((1, 1), f32),
        ),
        in_specs=[hbm] * 6 + [vmem],
        out_specs=(hbm,) * 6 + (vmem,) * 3,
        scratch_shapes=[pltpu.VMEM(a.shape, a.dtype) for a in same]
        + [pltpu.SemaphoreType.DMA((6,)), pltpu.SemaphoreType.DMA((6,))],
        name="results",
    )(out, gtok, ggu, gdn, gqkv, gout, vec)


def tables(positions):
    lane = jnp.arange(128, dtype=jnp.int32)
    freqs = rope_theta ** (-2.0 * (lane % 32).astype(f32) / 64)
    angles = positions.astype(f32)[:, None] * freqs[None, :]
    return jnp.cos(angles), jnp.sin(angles) * jnp.where(lane % 64 < 32, -1.0, 1.0)


def local(
    tokens,
    cotangent,
    bounds,
    positions,
    norm_gain_attn,
    w_qkv,
    qk_gain,
    w_out,
    norm_gain_ffn,
    w_gate_up,
    w_down,
):
    x = tokens.reshape(256, 1024)
    cot = cotangent.reshape(256, 1024)
    cosine, sine = tables(positions.reshape(256))
    mid, na, att, proj, qkv, o, l = attention(
        bounds, x, cosine, sine, norm_gain_attn[None], qk_gain[None], w_qkv, w_out
    )
    results = main_part(
        bounds,
        mid,
        norm_gain_ffn[None],
        norm_gain_attn[None],
        qk_gain[None],
        cot,
        x,
        cosine,
        sine,
        na,
        att,
        proj,
        qkv,
        o,
        l,
        w_gate_up,
        w_down,
        w_qkv,
        w_out,
    )
    layer_out, grad_tokens, sum_gate_up, sum_down, sum_qkv, sum_out, gain_a, gain_f, gain_qk = (
        finish(*results)
    )
    return (
        layer_out.reshape(tokens.shape),
        grad_tokens.reshape(tokens.shape),
        gain_a.reshape(8),
        sum_qkv,
        gain_qk.reshape(1),
        sum_out,
        gain_f.reshape(8),
        sum_gate_up,
        sum_down,
    )


def solution(mesh):
    placed = (
        P(None, "rows", "ctx", None),
        P(None, "rows", "ctx", None),
        P(None, "rows", None),
        P(None, "rows", "ctx"),
        P(),
        P(),
        P(),
        P(),
        P(),
        P(),
        P(),
    )
    return jax.shard_map(
        local,
        mesh=mesh,
        in_specs=placed,
        out_specs=(
            P(None, "rows", "ctx", None),
            P(None, "rows", "ctx", None),
            P(("rows", "ctx")),
            P(("rows", "ctx"), None),
            P(("rows", "ctx")),
            P(("rows", "ctx"), None),
            P(("rows", "ctx")),
            P(("rows", "ctx"), None),
            P(("rows", "ctx"), None),
        ),
        check_vma=False,
    )
```

```python
import functools

import jax
import jax.numpy as jnp
import numpy as np
from jax import lax
from jax.experimental import pallas as pl
from jax.experimental.pallas import tpu as pltpu
from jax.sharding import PartitionSpec as P

MESH = pl.DeviceIdType.MESH
norm_eps = 1e-05
rope_theta = 1000000.0
f32 = jnp.float32
bf16 = jnp.bfloat16
VMEM_LIMIT = 64 * 2**20 - 2**18


class Place:
    def __init__(self):
        r = lax.axis_index("rows")
        k = lax.axis_index("ctx")
        self.x_hi = lax.div(r, 8)
        self.y = lax.rem(lax.div(r, 2), 4)
        self.core = lax.rem(r, 2)
        self.x_lo = lax.div(k, 4)
        self.z = lax.rem(k, 4)
        self.rows = r
        self.ctx = k
        self.bits = [
            self.x_hi,
            lax.rem(self.x_hi + self.x_lo, 2),
            lax.div(self.y, 2),
            lax.rem(lax.div(self.y, 2) + lax.rem(self.y, 2), 2),
            lax.div(self.z, 2),
            lax.rem(lax.div(self.z, 2) + lax.rem(self.z, 2), 2),
        ]

    def at(self, x_hi=None, x_lo=None, y=None, z=None, core=None):
        x_hi = self.x_hi if x_hi is None else x_hi
        x_lo = self.x_lo if x_lo is None else x_lo
        y = self.y if y is None else y
        z = self.z if z is None else z
        core = self.core if core is None else core
        return (x_hi * 8 + y * 2 + core, x_lo * 4 + z)

    def partner(self):
        return self.at(core=1 - self.core)

    def neighbour(self, dim):
        if dim == 0:
            return self.at(x_hi=1 - self.x_hi, x_lo=1 - self.x_lo)
        if dim == 1:
            return self.at(x_lo=1 - self.x_lo)
        if dim == 2:
            return self.at(y=3 - self.y)
        if dim == 3:
            return self.at(y=self.y + 1 - 2 * lax.rem(self.y, 2))
        if dim == 4:
            return self.at(z=3 - self.z)
        return self.at(z=self.z + 1 - 2 * lax.rem(self.z, 2))


def gray(v):
    return v ^ (v >> 1)


def chip_number(x_hi, x_lo, y, z):
    return gray(2 * x_hi + x_lo) * 16 + gray(y) * 4 + gray(z)


def slot_of(number, order):
    return sum(((number >> (5 - dim)) & 1) << (5 - t) for t, dim in enumerate(order))


HELD_AT = [64 - (64 >> t) for t in range(7)]


class Scatter:
    def __init__(self, place, orders, first, held, send_sems, recv_sems):
        self.place = place
        self.orders = orders
        self.first, self.first_cols = first
        self.held, self.held_cols = held
        self.send_sems = send_sems
        self.recv_sems = recv_sems

    def part(self, s, t, which):
        half = 32 >> t
        if t == 0:
            return self.first, which * half, self.first_cols
        return self.held, HELD_AT[t - 1] + which * half, self.held_cols

    def copy(self, s, t):
        half = 32 >> t
        dim = self.orders[s][t]
        ref, start, cols = self.part(s, t, 1 - self.place.bits[dim])
        return pltpu.make_async_remote_copy(
            src_ref=ref.at[s, pl.ds(start, half), :, cols],
            dst_ref=self.held.at[s, pl.ds(HELD_AT[t], half), :, self.held_cols],
            send_sem=self.send_sems.at[s, t],
            recv_sem=self.recv_sems.at[s, t],
            device_id=self.place.neighbour(dim),
            device_id_type=MESH,
        )

    def send(self, s, t):
        self.copy(s, t).start()

    def take(self, s, t):
        self.copy(s, t).wait_recv()
        half = 32 >> t
        ref, start, cols = self.part(s, t, self.place.bits[self.orders[s][t]])
        per = min(8, half)

        def body(i, carry):
            for j in range(per):
                at = i * per + j
                self.held[s, HELD_AT[t] + at, :, self.held_cols] = (
                    self.held[s, HELD_AT[t] + at, :, self.held_cols].astype(f32)
                    + ref[s, start + at, :, cols].astype(f32)
                ).astype(bf16)
            return carry

        lax.fori_loop(0, half // per, body, 0)
        self.send(s, t + 1)

    def last(self, s):
        self.copy(s, 5).wait_recv()
        ref, start, cols = self.part(s, 5, self.place.bits[self.orders[s][5]])
        return self.held[s, HELD_AT[5], :, self.held_cols].astype(f32) + ref[
            s, start, :, cols
        ].astype(f32)

    def sent(self, steps=range(6)):
        for s in range(6):
            for t in steps:
                self.copy(s, t).wait_send()


def greet(devices):
    barrier = pltpu.get_barrier_semaphore()
    for device in devices:
        pl.semaphore_signal(barrier, inc=1, device_id=device, device_id_type=MESH)
    pl.semaphore_wait(barrier, len(devices))


def greet_all(place, devices):
    barrier = pltpu.get_barrier_semaphore()
    targets = down_targets(place)
    for device in devices + targets[1:]:
        pl.semaphore_signal(barrier, inc=1, device_id=device, device_id_type=MESH)
    swapped = place.x_hi != place.core
    count = len(devices) + 3

    @pl.when(swapped)
    def _():
        pl.semaphore_signal(barrier, inc=1, device_id=targets[0], device_id_type=MESH)
        pl.semaphore_wait(barrier, count + 1)

    @pl.when(jnp.logical_not(swapped))
    def _():
        pl.semaphore_wait(barrier, count)


def push(place, src, dst, send_sem, recv_sem, device):
    return pltpu.make_async_remote_copy(
        src_ref=src,
        dst_ref=dst,
        send_sem=send_sem,
        recv_sem=recv_sem,
        device_id=device,
        device_id_type=MESH,
    )


def down_targets(place):
    return [
        place.at(x_hi=place.core, core=place.x_hi, z=lax.rem(place.z + off, 4)) for off in range(4)
    ]


def dot(left, right):
    return jnp.dot(left, right, preferred_element_type=f32)


def dot_cols(left, right):
    return lax.dot_general(left, right, (((1,), (1,)), ((), ())), preferred_element_type=f32)


FF_HALF = 2304
DOWN_ORDERS = (
    (1, 3, 5, 2, 0, 4),
    (4, 0, 1, 3, 5, 2),
    (0, 1, 3, 2, 4, 5),
    (5, 3, 0, 1, 2, 4),
    (3, 2, 4, 5, 1, 0),
    (2, 3, 5, 0, 4, 1),
)
GATE_ORDERS = (
    (0, 5, 4, 1, 3, 2),
    (1, 5, 0, 4, 3, 2),
    (2, 4, 5, 3, 1, 0),
    (3, 0, 5, 4, 2, 1),
    (2, 5, 0, 3, 1, 4),
    (0, 1, 3, 4, 5, 2),
)
UP_ORDERS = (
    (2, 0, 3, 5, 1, 4),
    (5, 2, 0, 3, 4, 1),
    (3, 1, 5, 2, 0, 4),
    (4, 2, 5, 0, 1, 3),
    (3, 0, 2, 5, 4, 1),
    (4, 1, 5, 0, 2, 3),
)
QUAD_ORDERS = (
    (1, 2, 0, 5, 4, 3),
    (0, 4, 1, 2, 3, 5),
    (3, 1, 5, 0, 2, 4),
    (2, 0, 3, 4, 1, 5),
    (2, 4, 3, 5, 0, 1),
    (4, 0, 2, 3, 5, 1),
)
STEPS = (
    "Bmm0", "Amm0", "Bmm2", "dn", "Amm2", "down", "lo", "Amm1", "B40", "datt",
    "A10", "A40", "A50", "B50", "B10", "out", "Bmm1", "split", "heads0", "D30",
    "B00", "nat", "A30", "D40", "D50", "heads1", "A20", "A11", "B51", "A00",
    "D20", "B20", "D10", "D00", "B11", "B30", "A51", "A41", "free", "Qmm4",
    "Qmm5", "headb", "B52", "B01", "D31", "lastnorm", "B31", "Qmm0", "D41", "D51",
    "Qmm2", "Qmm3", "D21", "B41", "Qmm1", "D01", "A21", "A31", "v0", "D11",
    "Q40", "A01", "A42", "D02", "Q50", "v1", "Q00", "Q20", "Q10", "Q30",
    "B21", "D52", "Q41", "A12", "D32", "B02", "D22", "A22", "B32", "D12",
    "A43", "A02", "Q51", "v2", "B12", "A52", "B53", "D42", "Q21", "Q11",
    "A32", "Q31", "Q01", "B22", "B42", "D03", "Q42", "D13", "B03", "D23",
    "D43", "D53", "A53", "A13", "D33", "A23", "v3", "Q52", "B13", "Q22",
    "B33", "A03", "Q12", "A33", "Q32", "Q02", "B54", "B43", "B23", "D54",
    "Q43", "A44", "A14", "D14", "D34", "B14", "v4", "Q53", "Q23", "Q13",
    "A04", "D44", "Q33", "Q03", "D24", "D04", "A24", "B44", "A54", "B24",
    "B34", "A34", "B04", "Q24", "v5", "Q54", "Q14", "Q44", "Q34", "Q04",
    "Dfin", "Afin", "Qfin", "end",
)


def finish_down(place, down, d_acc, d_stage, d_in, f_send, f_recv, gdn_ref):
    for s in range(6):
        d_acc[pl.ds(48 * (s // 2), 48), pl.ds(128 * (s % 2), 128)] = down.last(s)
    for z in range(4):
        d_stage[z, pl.ds(0, 36), :] = d_acc[pl.ds(36 * z, 36), :]
        d_stage[z, pl.ds(36, 4), :] = jnp.zeros((4, 256), f32)
    targets = down_targets(place)
    swapped = place.x_hi != place.core
    moves = []
    for off in range(4):
        moves.append(
            push(
                place,
                d_stage.at[lax.rem(place.z + off, 4)],
                d_in.at[place.z],
                f_send.at[off],
                f_recv.at[off],
                targets[off],
            )
        )
    for off in range(1, 4):
        moves[off].start()

    @pl.when(swapped)
    def _():
        moves[0].start()
        moves[0].wait_recv()

    @pl.when(jnp.logical_not(swapped))
    def _():
        d_in[place.z] = d_stage[place.z]

    for off in range(1, 4):
        moves[off].wait_recv()
    for z in range(4):
        gdn_ref[:, pl.ds(256 * z, 256)] = d_in[z, pl.ds(0, 36), :]
    for off in range(1, 4):
        moves[off].wait_send()

    @pl.when(swapped)
    def _():
        moves[0].wait_send()


def lanes(rows):
    return lax.broadcasted_iota(jnp.int32, (rows, 128), 1)


def turn_heads(values):
    low = lax.rem(lanes(values.shape[0]), 64) < 32
    return jnp.where(low, pltpu.roll(values, 96, 1), pltpu.roll(values, 32, 1))


def head_mean(values):
    i = lax.broadcasted_iota(jnp.int32, (128, 128), 0)
    j = lax.broadcasted_iota(jnp.int32, (128, 128), 1)
    ones = jnp.where(lax.div(i, 64) == lax.div(j, 64), 1.0 / 64, 0.0).astype(bf16)
    high = values.astype(bf16)
    rest = (values - high.astype(f32)).astype(bf16)
    return dot(high, ones) + dot(rest, ones)


def gain_tiles(qk_gain):
    swapped = pltpu.roll(qk_gain, 64, 1)
    low = lax.broadcasted_iota(jnp.int32, (1, 128), 1) < 64
    return jnp.where(low, qk_gain, swapped), jnp.where(low, swapped, qk_gain)


def head_rows(values):
    low = lanes(values.shape[0]) < 64
    zero = jnp.zeros_like(values)
    return jnp.concatenate([jnp.where(low, values, zero), jnp.where(low, zero, values)], 0)


class Exchange:
    def __init__(self, place, out_at, into_at, send_sems, recv_sems):
        self.place = place
        self.out_at = out_at
        self.into_at = into_at
        self.send_sems = send_sems
        self.recv_sems = recv_sems

    def copy(self, m, off):
        j = lax.rem(self.place.ctx + off, 8)
        return push(
            self.place,
            self.out_at(m, j),
            self.into_at(m, self.place.ctx),
            self.send_sems.at[m, off - 1],
            self.recv_sems.at[m, off - 1],
            (self.place.rows, j),
        )

    def send(self, m):
        for off in range(1, 8):
            self.copy(m, off).start()
        self.into_at(m, self.place.ctx)[...] = self.out_at(m, self.place.ctx)[...]

    def arrived(self, m):
        for off in range(1, 8):
            self.copy(m, off).wait_recv()

    def sent(self):
        for m in range(2):
            for off in range(1, 8):
                self.copy(m, off).wait_send()


def ctx_peers(place):
    return [(place.rows, lax.rem(place.ctx + off, 8)) for off in range(1, 8)]


def document_edges(bounds_ref, m):
    index = lax.broadcasted_iota(jnp.int32, (1, 1024), 1)
    start = jnp.zeros((1, 1024), jnp.int32)
    end = jnp.full((1, 1024), 1024, jnp.int32)
    for k in range(1, 4):
        cut = bounds_ref[m, 0, k]
        start = jnp.where(index >= cut, cut, start)
        end = jnp.where(index < bounds_ref[m, 0, 4 - k], bounds_ref[m, 0, 4 - k], end)
    return start, end


def reorder_store(part, first, s, order, x_hi, at, width):
    part = part.reshape(4, 2, 8, 8, width)
    for y in range(4):
        for x_lo in range(2):
            for z in range(4):
                slot = slot_of(chip_number(x_hi, x_lo, y, z), order)
                first[s, slot, :, at] = part[y, :, 4 * x_lo + z].reshape(16, width).astype(bf16)


def block_kernel(
    bounds_ref,
    pos_ref,
    freq_ref,
    gain_ref,
    gain_ffn_ref,
    qk_gain_ref,
    x_hbm,
    cot_hbm,
    wgu_hbm,
    wd_hbm,
    w_qkv_hbm,
    w_out_hbm,
    out_hbm,
    gtok_hbm,
    ggu_ref,
    gdn_ref,
    gqkv_ref,
    gout_ref,
    vec_out,
    na_hbm,
    na_other_hbm,
    att_hbm,
    att_other_hbm,
    proj_hbm,
    qkv_hbm,
    o_hbm,
    a_first,
    a_held,
    b_first,
    b_held,
    d_first,
    d_held,
    nf,
    dyb,
    sum_send,
    sum_recv,
    mid_ref,
    dmid,
    cos_ref,
    sin_ref,
    l_ref,
    do_out,
    do_in,
    dpin,
    dmin,
    dm_own,
    g_fin,
    g_in,
    d_acc,
    d_stage,
    d_in,
    q_fin,
    q_in,
    vec,
    vec_in,
    w_sems,
    l_sems,
    x_send,
    x_recv,
    a_send,
    a_recv,
    b_send,
    b_recv,
    d_send,
    d_recv,
    q_send,
    q_recv,
    f_send,
    f_recv,
    k_send,
    k_recv,
    e_send,
    e_recv,
    do_send,
    do_recv,
    t_send,
    t_recv,
    v_send,
    v_recv,
    free_sem,
):
    place = Place()
    core = place.core
    partner = place.partner()
    every = slice(None)
    down = Scatter(place, DOWN_ORDERS, (d_first, every), (d_held, every), d_send, d_recv)
    gate = Scatter(place, GATE_ORDERS, (a_first, every), (a_held, every), a_send, a_recv)
    up = Scatter(place, UP_ORDERS, (b_first, every), (b_held, every), b_send, b_recv)
    narrow = pl.ds(0, 256)
    quad = Scatter(place, QUAD_ORDERS, (a_first, narrow), (b_first, narrow), q_send, q_recv)
    sums = {"D": down, "A": gate, "B": up, "Q": quad}
    steps = iter(STEPS)

    def run(ops, until):
        for name in steps:
            if name == until:
                return
            if name in ops:
                ops[name]()
            else:
                sums[name[0]].take(int(name[1]), int(name[2]))
    def t_at(m, j):
        return nf.at[
            pl.ds(pl.multiple_of(256 * m + 128 * lax.div(j, 4), 128), 128),
            pl.ds(pl.multiple_of(256 * lax.rem(j, 4), 256), 256),
        ]

    def tiles(ref, s, j, width):
        return ref.at[s, pl.ds(pl.multiple_of(8 * j, 8), 8), :, pl.ds(0, width)]

    heads_out = Exchange(
        place,
        lambda m, j: tiles(a_first, m, j, 256),
        lambda m, j: tiles(b_first, m, j, 256),
        k_send,
        k_recv,
    )
    heads_back = Exchange(
        place,
        lambda m, j: tiles(b_first, 4 + m, j, 128),
        lambda m, j: tiles(b_first, 2 + m, j, 128),
        e_send,
        e_recv,
    )
    grads_out = Exchange(
        place, lambda m, j: do_out.at[m, j], lambda m, j: do_in.at[m, j], do_send, do_recv
    )
    own_rows = pl.ds(0, 256)
    other_rows = pl.ds(256, 256)
    to_dy = push(place, cot_hbm, dyb.at[other_rows], x_send.at[0], x_recv.at[0], partner)
    to_nf = push(place, nf.at[own_rows], nf.at[other_rows], x_send.at[1], x_recv.at[1], partner)
    to_out = push(place, sum_send, sum_recv.at[0], x_send.at[2], x_recv.at[2], partner)
    to_back = push(place, sum_send, sum_recv.at[1], x_send.at[3], x_recv.at[3], partner)
    to_att = push(place, dm_own, att_other_hbm, x_send.at[5], x_recv.at[5], partner)
    att_copy = pltpu.make_async_copy(dm_own, att_hbm, l_sems.at[7])
    qkv_copy = pltpu.make_async_copy(
        b_first.at[pl.ds(0, 2), :, :, pl.ds(0, 256)], qkv_hbm, l_sems.at[8]
    )
    o_copy = pltpu.make_async_copy(
        b_first.at[pl.ds(4, 2), :, :, pl.ds(0, 128)], o_hbm, l_sems.at[9]
    )
    cot_load = pltpu.make_async_copy(cot_hbm, dyb.at[own_rows], l_sems.at[1])
    low = lanes(256) < 64
    gain_q, gain_k = gain_tiles(qk_gain_ref[...])

    def attend(w_qkv, x_ref, na, proj_ref, q2, kk, vo):
        x_load = pltpu.make_async_copy(x_hbm, x_ref, l_sems.at[2])
        w_load = pltpu.make_async_copy(w_qkv_hbm, w_qkv, l_sems.at[3])
        na_copy = pltpu.make_async_copy(na, na_hbm, l_sems.at[4])
        proj_copy = pltpu.make_async_copy(proj_ref, proj_hbm, l_sems.at[5])
        for load in (x_load, w_load, cot_load):
            load.start()
        greet_all(
            place,
            [partner] + [place.neighbour(dim) for dim in range(6)] + ctx_peers(place),
        )
        to_dy.start()
        columns = jnp.concatenate(
            [pos_ref[0].astype(f32), pos_ref[1].astype(f32), jnp.zeros((6, 128), f32)], 0
        ).T
        sign = jnp.where(lax.rem(lanes(128), 64) < 32, -1.0, 1.0)
        for m in range(2):
            angle = columns[:, m : m + 1] * freq_ref[...]
            cos_ref[pl.ds(128 * m, 128), :] = jnp.cos(angle)
            sin_ref[pl.ds(128 * m, 128), :] = jnp.sin(angle) * sign
        x_load.wait()
        inputs = x_ref[...].astype(f32)
        scale = lax.rsqrt(jnp.mean(inputs * inputs, axis=-1, keepdims=True) + norm_eps)
        na[...] = (inputs * scale * gain_ref[...]).astype(bf16)
        to_na = push(place, na, na_other_hbm, x_send.at[4], x_recv.at[4], partner)
        na_copy.start()
        w_load.wait()

        def turned(tile, gain):
            u = tile * lax.rsqrt(head_mean(tile * tile) + norm_eps) * gain
            return u * cos_ref[...] + turn_heads(u) * sin_ref[...]

        def store(at, j, tile):
            for m in range(2):
                rows = tile[128 * m : 128 * m + 128].astype(bf16)
                a_first[m, pl.ds(8 * j, 8), :, pl.ds(at, 128)] = rows.reshape(8, 16, 128)

        for i in range(4):
            pair = dot(na[...], w_qkv[:, pl.ds(256 * i, 256)])
            proj_ref[:, pl.ds(256 * i, 256)] = pair
            for j in range(2):
                store(0, 2 * i + j, turned(pair[:, 128 * j : 128 * j + 128], gain_q) * 0.125)
        for i in range(2):
            key_pair = dot(na[...], w_qkv[:, pl.ds(1024 + 256 * i, 256)])
            value_pair = dot(na[...], w_qkv[:, pl.ds(1536 + 256 * i, 256)])
            proj_ref[:, pl.ds(1024 + 256 * i, 256)] = key_pair
            for j in range(2):
                key = turned(key_pair[:, 128 * j : 128 * j + 128], gain_k)
                value = value_pair[:, 128 * j : 128 * j + 128]
                store(128, 4 * i + 2 * j, jnp.where(low, key, pltpu.roll(value, 64, 1)))
                store(128, 4 * i + 2 * j + 1, jnp.where(low, pltpu.roll(key, 64, 1), value))
        for m in range(2):
            heads_out.send(m)
        to_na.start()
        proj_copy.start()

        def heads(m, carry):
            heads_out.arrived(m)
            ends = document_edges(bounds_ref, m)[1]
            for b in range(4):
                query = b_first[m, pl.ds(16 * b, 16), :, pl.ds(0, 128)].reshape(256, 128)
                pair = b_first[m, pl.ds(16 * b, 16), :, pl.ds(128, 128)].reshape(256, 128)
                pair = pair.astype(f32)
                swapped = pltpu.roll(pair, 64, 1)
                q2[b] = head_rows(query)
                kk[b] = jnp.where(low, pair, swapped).astype(bf16)
                vo[b] = jnp.where(low, swapped, 1.0).astype(bf16)
            for qb in range(4):
                acc = jnp.zeros((512, 128), f32)
                for kb in range(qb + 1):
                    scores = dot_cols(q2[qb], kk[kb])
                    t = 256 * qb + lax.rem(lax.broadcasted_iota(jnp.int32, (512, 256), 0), 256)
                    keep = t < ends[:, 256 * kb : 256 * kb + 256]
                    if kb == qb:
                        s = 256 * kb + lax.broadcasted_iota(jnp.int32, (512, 256), 1)
                        keep = keep & (s <= t)
                    weights = jnp.where(keep, jnp.exp(scores), 0.0).astype(bf16)
                    acc = acc + dot(weights, vo[kb])
                total = pltpu.roll(acc, 64, 1)
                head0 = acc[:256]
                head1 = pltpu.roll(acc[256:], 64, 1)
                denominator = jnp.where(low, total[:256], acc[256:])
                out = jnp.where(low, head0, head1) / denominator
                log_total = jnp.log(denominator).T
                l_ref[m, pl.ds(0, 1), pl.ds(256 * qb, 256)] = log_total[0:1]
                l_ref[m, pl.ds(1, 1), pl.ds(256 * qb, 256)] = log_total[64:65]
                b_first[4 + m, pl.ds(16 * qb, 16), :, pl.ds(0, 128)] = out.astype(bf16).reshape(
                    16, 16, 128
                )
            heads_back.send(m)
            return carry

        lax.fori_loop(0, 2, heads, 0)
        qkv_copy.start()
        o_copy.start()
        na_copy.wait()
        proj_copy.wait()
        to_na.wait()

    pl.run_scoped(
        attend,
        pltpu.VMEM((1024, 2048), bf16),
        pltpu.VMEM((256, 1024), bf16),
        pltpu.VMEM((256, 1024), bf16),
        pltpu.VMEM((256, 1536), f32),
        pltpu.VMEM((4, 512, 128), bf16),
        pltpu.VMEM((4, 256, 128), bf16),
        pltpu.VMEM((4, 256, 128), bf16),
    )

    to_dm = push(place, dm_own.at[1 - core], dmin, x_send.at[6], x_recv.at[6], partner)
    out_copy = pltpu.make_async_copy(sum_send, out_hbm, l_sems.at[0])

    def feed_forward(wgu, wd, nft, h, ht, dgu, sum_own):
        def unit_loads(i):
            at = pl.multiple_of(core * FF_HALF + 768 * i, 256)
            up_at = pl.multiple_of(4608 + core * FF_HALF + 768 * i, 256)
            here = pl.ds(pl.multiple_of(768 * i, 256), 768)
            up_here = pl.ds(pl.multiple_of(FF_HALF + 768 * i, 256), 768)
            return [
                pltpu.make_async_copy(
                    wgu_hbm.at[:, pl.ds(at, 768)], wgu.at[:, here], w_sems.at[3 * i]
                ),
                pltpu.make_async_copy(
                    wgu_hbm.at[:, pl.ds(up_at, 768)], wgu.at[:, up_here], w_sems.at[3 * i + 1]
                ),
                pltpu.make_async_copy(
                    wd_hbm.at[pl.ds(at, 768)], wd.at[here], w_sems.at[3 * i + 2]
                ),
            ]

        w_out_loads = [
            pltpu.make_async_copy(
                w_out_hbm.at[pl.ds(512 * i, 512)], dgu.at[:, pl.ds(1024 * i, 1024)], l_sems.at[2 + i]
            )
            for i in range(2)
        ]
        x_load = pltpu.make_async_copy(x_hbm, sum_send, l_sems.at[4])
        for load in (x_load, *w_out_loads):
            load.start()
        for i in range(3):
            for copy in unit_loads(i):
                copy.start()
        for m in range(2):
            heads_back.arrived(m)
            for j in range(8):
                tile = b_first[2 + m, pl.ds(8 * j, 8), :, pl.ds(0, 128)].reshape(128, 128)
                dm_own[j // 4, pl.ds(128 * m, 128), pl.ds(128 * (j % 4), 128)] = tile
        to_att.start()
        att_copy.start()
        for load in (x_load, *w_out_loads):
            load.wait()
        mid = sum_send[...].astype(f32) + (
            dot(dm_own[0], dgu[:, pl.ds(0, 1024)]) + dot(dm_own[1], dgu[:, pl.ds(1024, 1024)])
        )
        mid_ref[...] = mid
        scale = lax.rsqrt(jnp.mean(mid * mid, axis=-1, keepdims=True) + norm_eps)
        nf[own_rows, :] = (mid * scale * gain_ffn_ref[...]).astype(bf16)
        to_nf.start()
        nft[:, own_rows] = nf[own_rows, :].T
        heads_out.sent()
        heads_back.sent()
        qkv_copy.wait()
        o_copy.wait()
        cot_load.wait()
        to_dy.wait_recv()
        to_nf.wait_recv()
        nft[:, other_rows] = nf[other_rows, :].T

        def units(i, carry):
            @pl.when(lax.rem(i, 3) == 0)
            def _():
                for copy in unit_loads(lax.div(i, 3)):
                    copy.wait()

            cols = pl.ds(pl.multiple_of(256 * i, 256), 256)
            up_cols = pl.ds(pl.multiple_of(FF_HALF + 256 * i, 256), 256)
            gated = dot(nf[...], wgu[:, cols])
            upward = dot(nf[...], wgu[:, up_cols])
            grad_hidden = dot_cols(dyb[...], wd[cols, :])
            sigma = 1.0 / (1.0 + jnp.exp(-gated))
            silu = gated * sigma
            h[:, cols] = (silu * upward).astype(bf16)
            dgu[:, cols] = (grad_hidden * upward * (sigma + silu * (1.0 - sigma))).astype(bf16)
            dgu[:, up_cols] = (grad_hidden * silu).astype(bf16)
            return carry

        lax.fori_loop(0, 9, units, 0)

        def down_grads():
            for block in range(3):
                ht[...] = h[:, pl.ds(768 * block, 768)].T
                for z in range(4):
                    part = dot(ht[...], dyb[:, pl.ds(256 * z, 256)])
                    for i in range(16):
                        q = 16 * block + i
                        y, core_to, x_lo, rg = q // 12, (q // 6) % 2, (q // 3) % 2, q % 3
                        for ch in range(2):
                            s = 2 * rg + ch
                            slot = slot_of(chip_number(core_to, x_lo, y, z), DOWN_ORDERS[s])
                            d_first[s, slot] = part[
                                48 * i : 48 * i + 48, 128 * ch : 128 * ch + 128
                            ].astype(bf16)
            for s in range(6):
                down.send(s, 0)

        def back_to_norm():
            def pair(i, carry):
                for j in range(2):
                    at = pl.ds(pl.multiple_of(512 * i + 256 * j, 256), 256)
                    part = dot_cols(dgu[...], wgu[at, :])
                    dmid[:, at] = part[:256]
                    sum_send[:, at] = part[256:].astype(bf16)
                return carry

            lax.fori_loop(0, 2, pair, 0)
            to_back.start()

        def wide_grads(scatter, first, base, orders, p):
            for x_hi in range(2):
                rows = nft[pl.ds(512 * x_hi, 512), :]
                for j in range(3):
                    part = dot(rows, dgu[:, pl.ds(base + 768 * p + 256 * j, 256)])
                    for k in range(2):
                        tile = 2 * j + k
                        s = 2 * p + tile // 3
                        reorder_store(
                            part[:, 128 * k : 128 * k + 128],
                            first,
                            s,
                            orders[s],
                            x_hi,
                            pl.ds(128 * (tile % 3), 128),
                            128,
                        )
            for s in (2 * p, 2 * p + 1):
                scatter.send(s, 0)

        w_out_load = pltpu.make_async_copy(w_out_hbm, wd.at[pl.ds(0, 1024)], l_sems.at[4])

        def output():
            to_back.wait_send()

            def pair(i, carry):
                for j in range(2):
                    at = pl.ds(pl.multiple_of(512 * i + 256 * j, 256), 256)
                    part = dot(h[...], wd[:, at])
                    sum_own[:, at] = part[:256]
                    sum_send[:, at] = part[256:].astype(bf16)
                return carry

            lax.fori_loop(0, 2, pair, 0)
            to_out.start()
            w_out_load.start()

        def output_sum():
            to_out.wait()
            sum_send[...] = (mid_ref[...] + sum_own[...] + sum_recv[0].astype(f32)).astype(bf16)
            out_copy.start()

        def norm_back():
            to_back.wait_recv()
            mid = mid_ref[...]
            scale = lax.rsqrt(jnp.mean(mid * mid, axis=-1, keepdims=True) + norm_eps)
            normed = mid * scale
            grad_nffn = dmid[...] + sum_recv[1].astype(f32)
            gain_grad = jnp.sum(grad_nffn * normed, axis=0, keepdims=True)
            for i in range(8):
                vec[0, pl.ds(8 + i, 1), :] = gain_grad[:, 128 * i : 128 * i + 128]
            grad_e = grad_nffn * gain_ffn_ref[...]
            dmid[...] = dyb[own_rows, :].astype(f32) + scale * (
                grad_e - normed * jnp.mean(grad_e * normed, axis=-1, keepdims=True)
            )
            to_att.wait_send()
            att_copy.wait()
            for half in range(2):
                dm_own[half] = dmid[:, pl.ds(512 * half, 512)].astype(bf16)
            to_dm.start()

            to_nf.wait_send()
            w_out_load.wait()
            for i in range(4):
                pair = dot_cols(dm_own[0], wd[pl.ds(256 * i, 256), pl.ds(0, 512)]) + dot_cols(
                    dm_own[1], wd[pl.ds(256 * i, 256), pl.ds(512, 512)]
                )
                for j in range(2):
                    for m in range(2):
                        do_out[m, 2 * i + j] = pair[
                            128 * m : 128 * m + 128, 128 * j : 128 * j + 128
                        ].astype(bf16)
            for m in range(2):
                grads_out.send(m)

        ops = {
            "down": down_grads,
            "dn": back_to_norm,
            "lo": output,
            "datt": norm_back,
            "out": output_sum,
        }
        for p in range(3):
            ops[f"Amm{p}"] = functools.partial(wide_grads, gate, a_first, 0, GATE_ORDERS, p)
            ops[f"Bmm{p}"] = functools.partial(wide_grads, up, b_first, FF_HALF, UP_ORDERS, p)
        run(ops, "split")

    pl.run_scoped(
        feed_forward,
        pltpu.VMEM((1024, 4608), bf16),
        pltpu.VMEM((FF_HALF, 1024), bf16),
        pltpu.VMEM((1024, 512), bf16),
        pltpu.VMEM((512, FF_HALF), bf16),
        pltpu.VMEM((768, 512), bf16),
        pltpu.VMEM((512, 4608), bf16),
        pltpu.VMEM((256, 1024), f32),
    )

    def vec_move(step):
        device = place.neighbour(step) if step < 6 else partner
        return push(place, vec.at[step], vec_in.at[step], v_send.at[step], v_recv.at[step], device)

    def vec_take(step):
        vec_move(step).wait_recv()
        vec[step + 1] = vec[step] + vec_in[step]
        vec_move(step + 1).start()

    def down_end():
        finish_down(place, down, d_acc, d_stage, d_in, f_send, f_recv, gdn_ref)

    swap = push(place, g_fin.at[1 - core], g_in, x_send.at[8], x_recv.at[8], partner)
    swap_q = push(place, q_fin.at[1 - core], q_in, x_send.at[9], x_recv.at[9], partner)

    def wide_end():
        for s in range(12):
            total = (gate if s < 6 else up).last(s % 6)
            g_fin[0, s] = total[:8]
            g_fin[1, s] = total[8:]
        swap.start()

    def quad_end():
        for s in range(6):
            total = quad.last(s)
            q_fin[0, s] = total[:8]
            q_fin[1, s] = total[8:]
        swap_q.start()

    def attention_back(
        w_qkv, x_ref, gtok, proj_ref, qkv_ref, o_ref, q2, do2, kk, vv, kt, delta, dq, dp,
        na_own, na_other, att_own, att_other, nat, attt, cols, t_out,
    ):
        sources = [qkv_hbm, o_hbm, proj_hbm, x_hbm, w_qkv_hbm]
        loads = [
            pltpu.make_async_copy(source, target, w_sems.at[i])
            for i, (source, target) in enumerate(
                zip(sources, [qkv_ref, o_ref, proj_ref, x_ref, w_qkv], strict=True)
            )
        ]
        for load in loads:
            load.start()
        grads_back = Exchange(place, lambda m, j: t_out.at[m, j], t_at, t_send, t_recv)

        def heads_grad(m):
            if m == 0:
                for load in loads[:2]:
                    load.wait()
            grads_out.arrived(m)
            starts = document_edges(bounds_ref, m)[0]
            for b in range(4):
                query = qkv_ref[m, pl.ds(16 * b, 16), :, pl.ds(0, 128)].reshape(256, 128)
                pair = qkv_ref[m, pl.ds(16 * b, 16), :, pl.ds(128, 128)].reshape(256, 128)
                pair = pair.astype(f32)
                grad = do_in[m, pl.ds(2 * b, 2)].reshape(256, 128)
                swapped = pltpu.roll(pair, 64, 1)
                key_pair = jnp.where(low, pair, swapped)
                q2[b] = head_rows(query)
                do2[b] = head_rows(grad)
                kk[b] = key_pair.astype(bf16)
                vv[b] = jnp.where(low, swapped, pair).astype(bf16)
                kt[b] = key_pair.T.astype(bf16)
                out = o_ref[m, pl.ds(16 * b, 16)].reshape(256, 128).astype(f32)
                inner = (grad.astype(f32) * out).T
                delta[b, :, pl.ds(0, 256)] = jnp.sum(inner[:64], axis=0, keepdims=True)
                delta[b, :, pl.ds(256, 256)] = jnp.sum(inner[64:], axis=0, keepdims=True)
            for kb in range(4):
                grad_key = jnp.zeros((256, 128), f32)
                grad_value = jnp.zeros((256, 128), f32)
                for qb in range(kb, 4):
                    scores = dot_cols(kk[kb], q2[qb])
                    log_total = jnp.concatenate(
                        [l_ref[m, pl.ds(i, 1), pl.ds(256 * qb, 256)] for i in range(2)], 1
                    )
                    start = starts[:, 256 * qb : 256 * qb + 256]
                    s = 256 * kb + lax.broadcasted_iota(jnp.int32, (256, 512), 0)
                    keep = s >= jnp.concatenate([start, start], 1)
                    if kb == qb:
                        t = lax.broadcasted_iota(jnp.int32, (256, 512), 1)
                        keep = keep & (s <= 256 * qb + lax.rem(t, 256))
                    probs = jnp.where(keep, jnp.exp(scores - log_total), 0.0)
                    grad_probs = dot_cols(vv[kb], do2[qb])
                    grad_scores = (probs * (grad_probs - delta[qb])).astype(bf16)
                    grad_value = grad_value + dot(probs.astype(bf16), do2[qb])
                    grad_key = grad_key + dot(grad_scores, q2[qb])
                    grad_query = dot(kt[kb], grad_scores)
                    if kb == 0:
                        dq[qb] = grad_query[:64]
                    else:
                        dq[qb] = dq[qb] + grad_query[:64]
                grad_key = grad_key + pltpu.roll(grad_key, 64, 1)
                grad_value = grad_value + pltpu.roll(grad_value, 64, 1)
                tile = jnp.where(low, grad_key, grad_value).astype(bf16)
                for half in range(2):
                    rows = slice(128 * half, 128 * half + 128)
                    t_out[m, 2 * kb + half, :, pl.ds(128, 128)] = tile[rows]
            for qb in range(4):
                stacked = jnp.concatenate([dq[qb, :, pl.ds(0, 256)], dq[qb, :, pl.ds(256, 256)]], 0)
                tile = (stacked * 0.125).T.astype(bf16)
                for half in range(2):
                    rows = slice(128 * half, 128 * half + 128)
                    t_out[m, 2 * qb + half, :, pl.ds(0, 128)] = tile[rows]
            grads_back.send(m)

        def sums_free():
            gate.sent([0])
            up.sent([0])
            for dim in range(6):
                pl.semaphore_signal(
                    free_sem, inc=1, device_id=place.neighbour(dim), device_id_type=MESH
                )

        sides = [
            pltpu.make_async_copy(source, target, l_sems.at[2 + i])
            for i, (source, target) in enumerate(
                zip(
                    [na_hbm, att_hbm, na_other_hbm, att_other_hbm],
                    [na_own, att_own, na_other, att_other],
                    strict=True,
                )
            )
        ]
        for load in sides[:3]:
            load.start()

        def token_sides():
            to_att.wait_recv()
            sides[3].start()
            for load in sides[:3]:
                load.wait()
            nat[:, own_rows] = na_own[...].T
            nat[:, other_rows] = na_other[...].T
            sides[3].wait()
            for i in range(2):
                attt[pl.ds(512 * i, 512), own_rows] = att_own[i].T
                attt[pl.ds(512 * i, 512), other_rows] = att_other[i].T
            to_dm.wait_recv()
            cols[own_rows, pl.ds(1024, 512)] = dm_own[core]
            cols[other_rows, pl.ds(1024, 512)] = dmin[...]

        def projection_grads(s):
            left = nat if s < 4 else attt
            if s == 0:
                to_dp.wait_recv()
                cols[other_rows, pl.ds(0, 1024)] = dpin[...]
            for x_hi in range(2):
                part = dot(left[pl.ds(512 * x_hi, 512), :], cols[:, pl.ds(256 * s, 256)])
                reorder_store(part, a_first, s, QUAD_ORDERS[s], x_hi, narrow, 256)
            if s == 4:
                pl.semaphore_wait(free_sem, 6)
            quad.send(s, 0)

        def both_rows(j, at):
            return jnp.concatenate([t_at(m, j)[:, pl.ds(at, 128)] for m in range(2)], 0).astype(f32)

        def head_back(grad, value, gain):
            grad = grad * cos_ref[...] + turn_heads(grad * sin_ref[...])
            scale = lax.rsqrt(head_mean(value * value) + norm_eps)
            normed = value * scale
            grad_e = grad * gain
            gain_grad = jnp.sum(grad * normed, axis=0, keepdims=True)
            return scale * (grad_e - normed * head_mean(grad_e * normed)), gain_grad

        to_dp = push(place, dp.at[1 - core], dpin, x_send.at[7], x_recv.at[7], partner)
        gtok_copy = pltpu.make_async_copy(gtok, gtok_hbm, l_sems.at[1])

        def turn_back():
            loads[2].wait()
            for m in range(2):
                grads_back.arrived(m)
            sum_k = jnp.zeros((1, 128), f32)

            def query_pair(i, total):
                for j in range(2):
                    at = pl.ds(pl.multiple_of(256 * i + 128 * j, 128), 128)
                    back, part = head_back(both_rows(2 * i + j, 0), proj_ref[:, at], gain_q)
                    dp[0, :, at] = back.astype(bf16)
                    total = total + part
                return total

            sum_q = lax.fori_loop(0, 4, query_pair, jnp.zeros((1, 128), f32))
            for i in range(4):
                first = both_rows(2 * i, 128)
                second = both_rows(2 * i + 1, 128)
                grad_key = jnp.where(low, first, pltpu.roll(second, 64, 1))
                grad_value = jnp.where(low, pltpu.roll(first, 64, 1), second)
                back, part = head_back(grad_key, proj_ref[:, pl.ds(1024 + 128 * i, 128)], gain_k)
                dp[1, :, pl.ds(128 * i, 128)] = back.astype(bf16)
                dp[1, :, pl.ds(512 + 128 * i, 128)] = grad_value.astype(bf16)
                sum_k = sum_k + part
            to_dp.start()
            sum_q = sum_q + pltpu.roll(sum_q, 64, 1)
            sum_k = sum_k + pltpu.roll(sum_k, 64, 1)
            vec[0, pl.ds(16, 8), :] = jnp.zeros((8, 128), f32)
            vec[0, pl.ds(16, 1), :] = jnp.where(
                lax.broadcasted_iota(jnp.int32, (1, 128), 1) < 64, sum_q, sum_k
            )
            cols[own_rows, pl.ds(0, 1024)] = dp[core]

        def last_norm():
            loads[3].wait()
            loads[4].wait()
            inputs = x_ref[...].astype(f32)
            scale = lax.rsqrt(jnp.mean(inputs * inputs, axis=-1, keepdims=True) + norm_eps)
            normed = inputs * scale
            grad_n = dot_cols(dp[0], w_qkv[:, pl.ds(0, 1024)]) + dot_cols(
                dp[1], w_qkv[:, pl.ds(1024, 1024)]
            )
            gain_grad = jnp.sum(grad_n * normed, axis=0, keepdims=True)
            grad_e = grad_n * gain_ref[...]
            gtok[...] = dmid[...] + scale * (
                grad_e - normed * jnp.mean(grad_e * normed, axis=-1, keepdims=True)
            )
            gtok_copy.start()
            for i in range(8):
                vec[0, pl.ds(i, 1), :] = gain_grad[:, 128 * i : 128 * i + 128]
            vec_move(0).start()

        ops = {
            "heads0": functools.partial(heads_grad, 0),
            "heads1": functools.partial(heads_grad, 1),
            "free": sums_free,
            "nat": token_sides,
            "headb": turn_back,
            "lastnorm": last_norm,
            "Dfin": down_end,
            "Afin": wide_end,
            "Qfin": quad_end,
        }
        for s in range(6):
            ops[f"Qmm{s}"] = functools.partial(projection_grads, s)
            ops[f"v{s}"] = functools.partial(vec_take, s)
        run(ops, "end")
        gtok_copy.wait()
        to_dp.wait_send()
        grads_back.sent()

    pl.run_scoped(
        attention_back,
        pltpu.VMEM((1024, 2048), bf16),
        pltpu.VMEM((256, 1024), bf16),
        pltpu.VMEM((256, 1024), f32),
        pltpu.VMEM((256, 1536), f32),
        pltpu.VMEM((2, 64, 16, 256), bf16),
        pltpu.VMEM((2, 64, 16, 128), bf16),
        pltpu.VMEM((4, 512, 128), bf16),
        pltpu.VMEM((4, 512, 128), bf16),
        pltpu.VMEM((4, 256, 128), bf16),
        pltpu.VMEM((4, 256, 128), bf16),
        pltpu.VMEM((4, 128, 256), bf16),
        pltpu.VMEM((4, 1, 512), f32),
        pltpu.VMEM((4, 64, 512), f32),
        pltpu.VMEM((2, 256, 1024), bf16),
        pltpu.VMEM((256, 1024), bf16),
        pltpu.VMEM((256, 1024), bf16),
        pltpu.VMEM((2, 256, 512), bf16),
        pltpu.VMEM((2, 256, 512), bf16),
        pltpu.VMEM((1024, 512), bf16),
        pltpu.VMEM((1024, 512), bf16),
        pltpu.VMEM((512, 1536), bf16),
        pltpu.VMEM((2, 8, 128, 256), bf16),
    )

    def wide_cols(of, s):
        return pl.ds(pl.multiple_of((s // 6) * 4608 + of * FF_HALF + (s % 6) * 384, 128), 384)

    def quad_cols(of, s):
        if s < 4:
            return gqkv_ref, pl.ds(pl.multiple_of(of * 1024 + 256 * s, 256), 256)
        return gout_ref, pl.ds(pl.multiple_of(of * 512 + 256 * (s - 4), 256), 256)

    for s in range(12):
        ggu_ref[:, wide_cols(core, s)] = g_fin[core, s]
    swap.wait_recv()
    for s in range(12):
        ggu_ref[:, wide_cols(1 - core, s)] = g_in[s]
    for s in range(6):
        ref, at = quad_cols(core, s)
        ref[:, at] = q_fin[core, s]
    swap_q.wait_recv()
    for s in range(6):
        ref, at = quad_cols(1 - core, s)
        ref[:, at] = q_in[s]
    vec_move(6).wait_recv()
    vec_out[...] = vec[6] + vec_in[6]

    for move in (to_dy, to_dm, swap, swap_q):
        move.wait_send()
    out_copy.wait()
    for step in range(7):
        vec_move(step).wait_send()
    down.sent()
    gate.sent(range(1, 6))
    up.sent(range(1, 6))
    quad.sent()
    grads_out.sent()


def block(bounds, *arrays):
    vmem = pl.BlockSpec(memory_space=pltpu.VMEM)
    hbm = pl.BlockSpec(memory_space=pl.ANY)
    smem = pl.BlockSpec(memory_space=pltpu.SMEM)
    dma = pltpu.SemaphoreType.DMA
    return pl.pallas_call(
        block_kernel,
        out_shape=(
            jax.ShapeDtypeStruct((256, 1024), bf16),
            jax.ShapeDtypeStruct((256, 1024), f32),
            jax.ShapeDtypeStruct((8, 9216), f32),
            jax.ShapeDtypeStruct((36, 1024), f32),
            jax.ShapeDtypeStruct((8, 2048), f32),
            jax.ShapeDtypeStruct((8, 1024), f32),
            jax.ShapeDtypeStruct((24, 128), f32),
            jax.ShapeDtypeStruct((256, 1024), bf16),
            jax.ShapeDtypeStruct((256, 1024), bf16),
            jax.ShapeDtypeStruct((2, 256, 512), bf16),
            jax.ShapeDtypeStruct((2, 256, 512), bf16),
            jax.ShapeDtypeStruct((256, 1536), f32),
            jax.ShapeDtypeStruct((2, 64, 16, 256), bf16),
            jax.ShapeDtypeStruct((2, 64, 16, 128), bf16),
        ),
        in_specs=[smem] + [vmem] * 5 + [hbm] * 6,
        out_specs=(hbm, hbm) + (vmem,) * 5 + (hbm,) * 7,
        scratch_shapes=[
            pltpu.VMEM((6, 64, 16, 384), bf16),
            pltpu.VMEM((6, 63, 16, 384), bf16),
            pltpu.VMEM((6, 64, 16, 384), bf16),
            pltpu.VMEM((6, 63, 16, 384), bf16),
            pltpu.VMEM((6, 64, 48, 128), bf16),
            pltpu.VMEM((6, 63, 48, 128), bf16),
            pltpu.VMEM((512, 1024), bf16),
            pltpu.VMEM((512, 1024), bf16),
            pltpu.VMEM((256, 1024), bf16),
            pltpu.VMEM((2, 256, 1024), bf16),
            pltpu.VMEM((256, 1024), f32),
            pltpu.VMEM((256, 1024), f32),
            pltpu.VMEM((256, 128), f32),
            pltpu.VMEM((256, 128), f32),
            pltpu.VMEM((2, 2, 1024), f32),
            pltpu.VMEM((2, 8, 128, 128), bf16),
            pltpu.VMEM((2, 8, 128, 128), bf16),
            pltpu.VMEM((256, 1024), bf16),
            pltpu.VMEM((256, 512), bf16),
            pltpu.VMEM((2, 256, 512), bf16),
            pltpu.VMEM((2, 12, 8, 384), f32),
            pltpu.VMEM((12, 8, 384), f32),
            pltpu.VMEM((144, 256), f32),
            pltpu.VMEM((4, 40, 256), f32),
            pltpu.VMEM((4, 40, 256), f32),
            pltpu.VMEM((2, 6, 8, 256), f32),
            pltpu.VMEM((6, 8, 256), f32),
            pltpu.VMEM((7, 24, 128), f32),
            pltpu.VMEM((7, 24, 128), f32),
            dma((9,)),
            dma((10,)),
            dma((10,)),
            dma((10,)),
            dma((6, 6)),
            dma((6, 6)),
            dma((6, 6)),
            dma((6, 6)),
            dma((6, 6)),
            dma((6, 6)),
            dma((6, 6)),
            dma((6, 6)),
            dma((4,)),
            dma((4,)),
            dma((2, 7)),
            dma((2, 7)),
            dma((2, 7)),
            dma((2, 7)),
            dma((2, 7)),
            dma((2, 7)),
            dma((2, 7)),
            dma((2, 7)),
            dma((7,)),
            dma((7,)),
            pltpu.SemaphoreType.REGULAR,
        ],
        compiler_params=pltpu.CompilerParams(
            collective_id=0, has_side_effects=True, vmem_limit_bytes=VMEM_LIMIT
        ),
        name="transformer_block",
    )(bounds, *arrays)


def finish_kernel(*refs):
    arrays, vec = refs[:6], refs[6]
    targets, (gain_a, gain_f, gain_qk) = refs[7:13], refs[13:16]
    passing, (in_sems, out_sems) = refs[16:22], refs[22:]
    reads = [
        pltpu.make_async_copy(array, held, in_sems.at[i])
        for i, (array, held) in enumerate(zip(arrays, passing, strict=True))
    ]
    writes = [
        pltpu.make_async_copy(held, target, out_sems.at[i])
        for i, (held, target) in enumerate(zip(passing, targets, strict=True))
    ]
    for read in reads:
        read.start()
    own = lax.axis_index("rows") * 8 + lax.axis_index("ctx")
    row = lax.div(own, 16)
    at = lax.rem(own, 16)
    lane = lax.broadcasted_iota(jnp.int32, (8, 128), 1)
    tile = lax.broadcasted_iota(jnp.int32, (8, 128), 0)

    def pick(values, of_row, of_lane, count):
        kept = jnp.sum(jnp.where(tile == of_row, values, 0.0), axis=0, keepdims=True)
        place = lax.broadcasted_iota(jnp.int32, (128, count), 0)
        order = lax.broadcasted_iota(jnp.int32, (128, count), 1)
        rows = jnp.broadcast_to(kept, (8, 128)).T[:, :count]
        return jnp.sum(jnp.where(place == of_lane + order, rows, 0.0), axis=0, keepdims=True)

    gain_a[...] = pick(vec[pl.ds(0, 8), :], row, 8 * at, 8)
    gain_f[...] = pick(vec[pl.ds(8, 8), :], row, 8 * at, 8)
    gain_qk[...] = pick(vec[pl.ds(16, 8), :], 0, own, 1)
    for read, write in zip(reads, writes, strict=True):
        read.wait()
        write.start()
    for write in writes:
        write.wait()


def finish(out, gtok, ggu, gdn, gqkv, gout, vec):
    vmem = pl.BlockSpec(memory_space=pltpu.VMEM)
    hbm = pl.BlockSpec(memory_space=pl.ANY)
    same = [jax.ShapeDtypeStruct(a.shape, a.dtype) for a in (out, gtok, ggu, gdn, gqkv, gout)]
    return pl.pallas_call(
        finish_kernel,
        out_shape=(
            *same,
            jax.ShapeDtypeStruct((1, 8), f32),
            jax.ShapeDtypeStruct((1, 8), f32),
            jax.ShapeDtypeStruct((1, 1), f32),
        ),
        in_specs=[hbm] * 6 + [vmem],
        out_specs=(hbm,) * 6 + (vmem,) * 3,
        scratch_shapes=[pltpu.VMEM(a.shape, a.dtype) for a in same]
        + [pltpu.SemaphoreType.DMA((6,)), pltpu.SemaphoreType.DMA((6,))],
        name="results",
    )(out, gtok, ggu, gdn, gqkv, gout, vec)


def local(
    tokens,
    cotangent,
    bounds,
    positions,
    norm_gain_attn,
    w_qkv,
    qk_gain,
    w_out,
    norm_gain_ffn,
    w_gate_up,
    w_down,
):
    lane = np.arange(128) % 32
    freqs = (rope_theta ** (-2.0 * lane / 64)).astype(np.float32)[None]
    results = block(
        bounds,
        positions,
        freqs,
        norm_gain_attn[None],
        norm_gain_ffn[None],
        qk_gain[None],
        tokens.reshape(256, 1024),
        cotangent.reshape(256, 1024),
        w_gate_up,
        w_down,
        w_qkv,
        w_out,
    )
    layer_out, grad_tokens, sum_gate_up, sum_down, sum_qkv, sum_out, gain_a, gain_f, gain_qk = (
        finish(*results[:7])
    )
    return (
        layer_out.reshape(tokens.shape),
        grad_tokens.reshape(tokens.shape),
        gain_a.reshape(8),
        sum_qkv,
        gain_qk.reshape(1),
        sum_out,
        gain_f.reshape(8),
        sum_gate_up,
        sum_down,
    )


def solution(mesh):
    placed = (
        P(None, "rows", "ctx", None),
        P(None, "rows", "ctx", None),
        P(None, "rows", None),
        P(None, "rows", "ctx"),
        P(),
        P(),
        P(),
        P(),
        P(),
        P(),
        P(),
    )
    return jax.shard_map(
        local,
        mesh=mesh,
        in_specs=placed,
        out_specs=(
            P(None, "rows", "ctx", None),
            P(None, "rows", "ctx", None),
            P(("rows", "ctx")),
            P(("rows", "ctx"), None),
            P(("rows", "ctx")),
            P(("rows", "ctx"), None),
            P(("rows", "ctx")),
            P(("rows", "ctx"), None),
            P(("rows", "ctx"), None),
        ),
        check_vma=False,
    )
```

```python
import functools

import jax
import jax.numpy as jnp
import numpy as np
from jax import lax
from jax.experimental import pallas as pl
from jax.experimental.pallas import tpu as pltpu
from jax.sharding import PartitionSpec as P

MESH = pl.DeviceIdType.MESH
norm_eps = 1e-05
rope_theta = 1000000.0
f32 = jnp.float32
bf16 = jnp.bfloat16
VMEM_LIMIT = 64 * 2**20 - 2**18


class Place:
    def __init__(self):
        r = lax.axis_index("rows")
        k = lax.axis_index("ctx")
        self.x_hi = lax.div(r, 8)
        self.y = lax.rem(lax.div(r, 2), 4)
        self.core = lax.rem(r, 2)
        self.x_lo = lax.div(k, 4)
        self.z = lax.rem(k, 4)
        self.rows = r
        self.ctx = k
        self.bits = [
            self.x_hi,
            lax.rem(self.x_hi + self.x_lo, 2),
            lax.div(self.y, 2),
            lax.rem(lax.div(self.y, 2) + lax.rem(self.y, 2), 2),
            lax.div(self.z, 2),
            lax.rem(lax.div(self.z, 2) + lax.rem(self.z, 2), 2),
        ]

    def at(self, x_hi=None, x_lo=None, y=None, z=None, core=None):
        x_hi = self.x_hi if x_hi is None else x_hi
        x_lo = self.x_lo if x_lo is None else x_lo
        y = self.y if y is None else y
        z = self.z if z is None else z
        core = self.core if core is None else core
        return (x_hi * 8 + y * 2 + core, x_lo * 4 + z)

    def partner(self):
        return self.at(core=1 - self.core)

    def neighbour(self, dim):
        if dim == 0:
            return self.at(x_hi=1 - self.x_hi, x_lo=1 - self.x_lo)
        if dim == 1:
            return self.at(x_lo=1 - self.x_lo)
        if dim == 2:
            return self.at(y=3 - self.y)
        if dim == 3:
            return self.at(y=self.y + 1 - 2 * lax.rem(self.y, 2))
        if dim == 4:
            return self.at(z=3 - self.z)
        return self.at(z=self.z + 1 - 2 * lax.rem(self.z, 2))


    def flipped(self, dims):
        if len(dims) == 1:
            return self.neighbour(dims[0])
        if 0 in dims:
            return self.at(x_hi=1 - self.x_hi)
        if 2 in dims:
            return self.at(y=lax.rem(self.y + 2, 4))
        return self.at(z=lax.rem(self.z + 2, 4))


def gray(v):
    return v ^ (v >> 1)


def chip_number(x_hi, x_lo, y, z):
    return gray(2 * x_hi + x_lo) * 16 + gray(y) * 4 + gray(z)


def slot_of(number, order):
    return sum(((number >> (5 - dim)) & 1) << (5 - t) for t, dim in enumerate(order))


ONES = (1, 1, 1, 1, 1, 1)
FLIPS = {1: ((1,),), 2: ((0, 1), (1, 0), (1, 1))}


class Scatter:
    def __init__(self, place, orders, shape, first, held, send_sems, recv_sems):
        self.place = place
        self.orders = orders
        self.first, self.first_cols = first
        self.held, self.held_cols = held
        self.send_sems = send_sems
        self.recv_sems = recv_sems
        self.stages = []
        at, slots, base = 0, 64, 0
        for width in shape:
            size = slots >> width
            self.stages.append((at, width, size, base))
            base += size * len(FLIPS[width])
            at += width
            slots = size

    def source(self, k):
        if k == 0:
            return self.first, 0, self.first_cols
        return self.held, self.stages[k - 1][3], self.held_cols

    def part(self, s, k, flips):
        at, width, size, _ = self.stages[k]
        which = 0
        for dim, flip in zip(self.orders[s][at : at + width], flips, strict=True):
            bit = self.place.bits[dim]
            which = 2 * which + (1 - bit if flip else bit)
        return which * size

    def copies(self, s, k):
        at, width, size, base = self.stages[k]
        ref, start, cols = self.source(k)
        dims = self.orders[s][at : at + width]
        return [
            pltpu.make_async_remote_copy(
                src_ref=ref.at[s, pl.ds(start + self.part(s, k, flips), size), :, cols],
                dst_ref=self.held.at[s, pl.ds(base + i * size, size), :, self.held_cols],
                send_sem=self.send_sems.at[min(k, 1)],
                recv_sem=self.recv_sems.at[s, k],
                device_id=self.place.flipped([d for d, f in zip(dims, flips, strict=True) if f]),
                device_id_type=MESH,
            )
            for i, flips in enumerate(FLIPS[width])
        ]

    def send(self, s, k):
        for copy in self.copies(s, k):
            copy.start()

    def arrived(self, s, k):
        _, width, size, base = self.stages[k]
        place = self.held.at[s, pl.ds(base, size * len(FLIPS[width])), :, self.held_cols]
        self.wait(place, 0, self.recv_sems.at[s, k]).wait_recv()
        ref, start, cols = self.source(k)
        own = start + self.part(s, k, (0,) * width)

        def total(at):
            value = ref[s, own + at, :, cols].astype(f32)
            for i in range(len(FLIPS[width])):
                value = value + self.held[s, base + i * size + at, :, self.held_cols].astype(f32)
            return value

        return total, size, base

    def take(self, s, k):
        total, size, base = self.arrived(s, k)
        per = min(8, size)

        def body(i, carry):
            for j in range(per):
                at = i * per + j
                self.held[s, base + at, :, self.held_cols] = total(at).astype(bf16)
            return carry

        lax.fori_loop(0, size // per, body, 0)
        self.send(s, k + 1)

    def last(self, s):
        return self.arrived(s, len(self.stages) - 1)[0](0)

    def wait(self, ref, part, recv_sem):
        return push(
            self.place, ref, ref, self.send_sems.at[part], recv_sem, self.place.partner()
        )

    def sent(self, part):
        slots = pl.ds(0, 32) if part == 0 else pl.ds(32, 31)
        self.wait(
            self.held.at[:, slots, :, self.held_cols], part, self.recv_sems.at[0, 0]
        ).wait_send()


def greet_signal(place, devices):
    barrier = pltpu.get_barrier_semaphore()
    targets = down_targets(place)
    for device in devices + targets[1:]:
        pl.semaphore_signal(barrier, inc=1, device_id=device, device_id_type=MESH)

    @pl.when(place.x_hi != place.core)
    def _():
        pl.semaphore_signal(barrier, inc=1, device_id=targets[0], device_id_type=MESH)


def greet_wait(place, devices):
    barrier = pltpu.get_barrier_semaphore()
    count = len(devices) + 3

    @pl.when(place.x_hi != place.core)
    def _():
        pl.semaphore_wait(barrier, count + 1)

    @pl.when(place.x_hi == place.core)
    def _():
        pl.semaphore_wait(barrier, count)


def push(place, src, dst, send_sem, recv_sem, device):
    return pltpu.make_async_remote_copy(
        src_ref=src,
        dst_ref=dst,
        send_sem=send_sem,
        recv_sem=recv_sem,
        device_id=device,
        device_id_type=MESH,
    )


def down_targets(place):
    return [
        place.at(x_hi=place.core, core=place.x_hi, z=lax.rem(place.z + off, 4)) for off in range(4)
    ]


def dot(left, right):
    return jnp.dot(left, right, preferred_element_type=f32)


def dot_cols(left, right):
    return lax.dot_general(left, right, (((1,), (1,)), ((), ())), preferred_element_type=f32)


FF_HALF = 2304
DOWN_ORDERS = (
    (1, 5, 4, 2, 3, 0),
    (0, 2, 5, 1, 3, 4),
    (4, 3, 1, 0, 2, 5),
    (0, 2, 1, 3, 5, 4),
    (5, 3, 2, 0, 1, 4),
    (2, 3, 1, 4, 5, 0),
)
GATE_ORDERS = (
    (4, 3, 5, 1, 2, 0),
    (1, 3, 0, 4, 2, 5),
    (4, 3, 1, 0, 2, 5),
    (5, 0, 3, 2, 4, 1),
    (2, 1, 4, 3, 0, 5),
    (3, 2, 0, 5, 1, 4),
)
UP_ORDERS = (
    (5, 4, 0, 1, 3, 2),
    (3, 0, 2, 4, 5, 1),
    (2, 3, 4, 5, 0, 1),
    (0, 3, 4, 5, 2, 1),
    (0, 2, 5, 3, 4, 1),
    (1, 2, 0, 3, 4, 5),
)
QUAD_ORDERS = (
    (4, 5, 0, 1, 3, 2),
    (0, 1, 2, 3, 5, 4),
    (5, 4, 3, 2, 1, 0),
    (1, 0, 4, 5, 3, 2),
    (2, 3, 1, 0, 4, 5),
    (3, 2, 5, 4, 1, 0),
)
QUAD_STAGES = (1, 1, 2, 2)
LINKED = ((0,), (1,), (2,), (3,), (4,), (5,), (0, 1), (2, 3), (4, 5))
STEPS = (
    "Amm0", "Bmm0", "Bmm1", "Amm1", "Bmm2", "Amm2", "dn", "A10", "down", "B30",
    "lo", "A50", "A20", "datt", "A00", "A40", "B40", "D20", "B00", "A30",
    "out", "B50", "D50", "D00", "D10", "B10", "A21", "B31", "split", "heads",
    "D21", "B01", "B20", "D51", "A31", "free", "B32", "D30", "nat", "A01",
    "D40", "A41", "A51", "B51", "A22", "Qmm4", "Qmm5", "B41", "B21", "A11",
    "D11", "headb", "D01", "B11", "D31", "A42", "B02", "lastnorm", "D52", "A02",
    "Qmm0", "Qmm2", "Qmm1", "Qmm3", "D32", "D41", "B42", "v0", "D02", "B22",
    "A52", "Q40", "A12", "D22", "A32", "D12", "B52", "D42", "B12", "Q50",
    "Q20", "Q00", "Q10", "A43", "Q30", "B23", "D33", "v1", "B03", "A13",
    "D23", "A03", "D43", "A53", "A23", "A33", "B43", "B33", "D13", "B13",
    "D53", "Q41", "D03", "Q51", "v2", "B53", "Q21", "Q11", "Q01", "A04",
    "Q31", "D34", "D24", "A44", "B14", "v3", "A14", "B44", "A34", "D14",
    "A54", "B34", "B24", "A24", "B04", "D04", "D44", "Q52", "B54", "Q42",
    "D54", "Q22", "Q02", "Q32", "Q12", "v4", "Afin", "Dfin", "Qfin", "v5",
    "end",
)


def finish_down(place, down, d_acc, d_stage, d_in, f_send, f_recv, gdn_ref):
    for s in range(6):
        d_acc[pl.ds(48 * (s // 2), 48), pl.ds(128 * (s % 2), 128)] = down.last(s)
    for z in range(4):
        d_stage[z, pl.ds(0, 36), :] = d_acc[pl.ds(36 * z, 36), :]
        d_stage[z, pl.ds(36, 4), :] = jnp.zeros((4, 256), f32)
    targets = down_targets(place)
    swapped = place.x_hi != place.core
    moves = []
    for off in range(4):
        moves.append(
            push(
                place,
                d_stage.at[lax.rem(place.z + off, 4)],
                d_in.at[place.z],
                f_send.at[min(off, 1)],
                f_recv.at[min(off, 1)],
                targets[off],
            )
        )
    three = d_in.at[pl.ds(0, 3)]
    others = push(place, three, three, f_send.at[1], f_recv.at[1], targets[1])
    for off in range(1, 4):
        moves[off].start()

    @pl.when(swapped)
    def _():
        moves[0].start()
        moves[0].wait_recv()

    @pl.when(jnp.logical_not(swapped))
    def _():
        d_in[place.z] = d_stage[place.z]

    others.wait_recv()
    for z in range(4):
        gdn_ref[:, pl.ds(256 * z, 256)] = d_in[z, pl.ds(0, 36), :]
    others.wait_send()

    @pl.when(swapped)
    def _():
        moves[0].wait_send()


def lanes(rows):
    return lax.broadcasted_iota(jnp.int32, (rows, 128), 1)


def turn_heads(values):
    low = lax.rem(lanes(values.shape[0]), 64) < 32
    return jnp.where(low, pltpu.roll(values, 96, 1), pltpu.roll(values, 32, 1))


def head_mean(values):
    i = lax.broadcasted_iota(jnp.int32, (128, 128), 0)
    j = lax.broadcasted_iota(jnp.int32, (128, 128), 1)
    ones = jnp.where(lax.div(i, 64) == lax.div(j, 64), 1.0 / 64, 0.0).astype(bf16)
    high = values.astype(bf16)
    rest = (values - high.astype(f32)).astype(bf16)
    return dot(high, ones) + dot(rest, ones)


def gain_tiles(qk_gain):
    swapped = pltpu.roll(qk_gain, 64, 1)
    low = lax.broadcasted_iota(jnp.int32, (1, 128), 1) < 64
    return jnp.where(low, qk_gain, swapped), jnp.where(low, swapped, qk_gain)


def head_rows(values):
    low = lanes(values.shape[0]) < 64
    zero = jnp.zeros_like(values)
    return jnp.concatenate([jnp.where(low, values, zero), jnp.where(low, zero, values)], 0)


class Exchange:
    def __init__(self, place, out_at, into_at, seven, send_sems, recv_sems):
        self.place = place
        self.seven = seven
        self.out_at = out_at
        self.into_at = into_at
        self.send_sems = send_sems
        self.recv_sems = recv_sems

    def copy(self, m, off):
        j = lax.rem(self.place.ctx + off, 8)
        return push(
            self.place,
            self.out_at(m, j),
            self.into_at(m, self.place.ctx),
            self.send_sems.at[m],
            self.recv_sems.at[m],
            (self.place.rows, j),
        )

    def send(self, m):
        for off in range(1, 8):
            self.copy(m, off).start()
        self.keep(m)

    def keep(self, m):
        self.into_at(m, self.place.ctx)[...] = self.out_at(m, self.place.ctx)[...]

    def all_seven(self, m):
        ref = self.seven(m)
        return push(
            self.place, ref, ref, self.send_sems.at[m], self.recv_sems.at[m], self.place.partner()
        )

    def arrived(self, m):
        self.all_seven(m).wait_recv()

    def sent(self):
        for m in range(2):
            self.all_seven(m).wait_send()


def ctx_peers(place):
    return [(place.rows, lax.rem(place.ctx + off, 8)) for off in range(1, 8)]


def document_edges(bounds_ref, m):
    index = lax.broadcasted_iota(jnp.int32, (1, 1024), 1)
    start = jnp.zeros((1, 1024), jnp.int32)
    end = jnp.full((1, 1024), 1024, jnp.int32)
    for k in range(1, 4):
        cut = bounds_ref[m, 0, k]
        start = jnp.where(index >= cut, cut, start)
        end = jnp.where(index < bounds_ref[m, 0, 4 - k], bounds_ref[m, 0, 4 - k], end)
    return start, end


def reorder_store(part, first, s, order, x_hi, at, width):
    part = part.reshape(4, 2, 8, 8, width)
    for y in range(4):
        for x_lo in range(2):
            for z in range(4):
                slot = slot_of(chip_number(x_hi, x_lo, y, z), order)
                first[s, slot, :, at] = part[y, :, 4 * x_lo + z].reshape(16, width).astype(bf16)


def block_kernel(
    bounds_ref,
    pos_ref,
    freq_ref,
    gain_ref,
    gain_ffn_ref,
    qk_gain_ref,
    x_hbm,
    cot_hbm,
    wgu_hbm,
    wd_hbm,
    w_qkv_hbm,
    w_out_hbm,
    out_hbm,
    gtok_hbm,
    ggu_hbm,
    gdn_hbm,
    gqkv_hbm,
    gout_hbm,
    vec_hbm,
    na_hbm,
    na_other_hbm,
    att_hbm,
    att_other_hbm,
    proj_hbm,
    qkv_hbm,
    o_hbm,
    a_first,
    a_held,
    b_first,
    b_held,
    d_first,
    d_held,
    nf,
    dyb,
    sum_send,
    sum_recv,
    mid_ref,
    dmid,
    cos_ref,
    sin_ref,
    l_ref,
    do_out,
    do_in,
    dpin,
    dmin,
    dm_own,
    g_fin,
    g_in,
    d_acc,
    d_stage,
    d_in,
    q_fin,
    q_in,
    vec,
    vec_in,
    ggu_ref,
    gdn_ref,
    gqkv_ref,
    gout_ref,
    w_sems,
    l_sems,
    r_sems,
    x_send,
    x_recv,
    a_send,
    a_recv,
    b_send,
    b_recv,
    d_send,
    d_recv,
    q_send,
    q_recv,
    f_send,
    f_recv,
    k_send,
    k_recv,
    e_send,
    e_recv,
    do_send,
    do_recv,
    t_send,
    t_recv,
    v_send,
    v_recv,
    free_sem,
):
    place = Place()
    core = place.core
    partner = place.partner()
    every = slice(None)
    down = Scatter(place, DOWN_ORDERS, ONES, (d_first, every), (d_held, every), d_send, d_recv)
    gate = Scatter(place, GATE_ORDERS, ONES, (a_first, every), (a_held, every), a_send, a_recv)
    up = Scatter(place, UP_ORDERS, ONES, (b_first, every), (b_held, every), b_send, b_recv)
    narrow = pl.ds(0, 256)
    quad = Scatter(
        place, QUAD_ORDERS, QUAD_STAGES, (a_first, narrow), (b_first, narrow), q_send, q_recv
    )
    sums = {"D": down, "A": gate, "B": up, "Q": quad}
    steps = iter(STEPS)

    def run(ops, until):
        for name in steps:
            if name == until:
                return
            if name in ops:
                ops[name]()
            else:
                sums[name[0]].take(int(name[1]), int(name[2]))
    def t_at(m, j):
        return nf.at[
            pl.ds(pl.multiple_of(256 * m + 128 * lax.div(j, 4), 128), 128),
            pl.ds(pl.multiple_of(256 * lax.rem(j, 4), 256), 256),
        ]

    def tiles(ref, s, j, width):
        return ref.at[s, pl.ds(pl.multiple_of(8 * j, 8), 8), :, pl.ds(0, width)]

    heads_out = Exchange(
        place,
        lambda m, j: tiles(a_first, m, j, 256),
        lambda m, j: tiles(b_first, m, j, 256),
        lambda m: b_first.at[m, pl.ds(0, 56), :, pl.ds(0, 256)],
        k_send,
        k_recv,
    )
    heads_back = Exchange(
        place,
        lambda m, j: tiles(b_first, 4 + m, j, 128),
        lambda m, j: tiles(b_first, 2 + m, j, 128),
        lambda m: b_first.at[2 + m, pl.ds(0, 56), :, pl.ds(0, 128)],
        e_send,
        e_recv,
    )
    grads_out = Exchange(
        place,
        lambda m, j: do_out.at[m, j],
        lambda m, j: do_in.at[m, j],
        lambda m: do_in.at[m, pl.ds(0, 7)],
        do_send,
        do_recv,
    )
    own_rows = pl.ds(0, 256)
    other_rows = pl.ds(256, 256)
    to_dy = push(place, cot_hbm, dyb.at[other_rows], x_send.at[0], x_recv.at[0], partner)
    to_nf = push(place, nf.at[own_rows], nf.at[other_rows], x_send.at[1], x_recv.at[1], partner)
    to_out = push(place, sum_send, sum_recv.at[0], x_send.at[2], x_recv.at[2], partner)
    to_back = push(place, sum_send, sum_recv.at[1], x_send.at[3], x_recv.at[3], partner)
    to_att = push(place, dm_own, att_other_hbm, x_send.at[5], x_recv.at[5], partner)
    att_copy = pltpu.make_async_copy(dm_own, att_hbm, l_sems.at[7])
    qkv_copy = pltpu.make_async_copy(
        b_first.at[pl.ds(0, 2), :, :, pl.ds(0, 256)], qkv_hbm, l_sems.at[8]
    )
    o_copy = pltpu.make_async_copy(
        b_first.at[pl.ds(4, 2), :, :, pl.ds(0, 128)], o_hbm, l_sems.at[9]
    )
    cot_load = pltpu.make_async_copy(cot_hbm, dyb.at[own_rows], l_sems.at[1])
    low = lanes(256) < 64
    gain_q, gain_k = gain_tiles(qk_gain_ref[...])

    def attend(w_qkv, x_ref, na, proj_ref, q2, kk, vo):
        x_load = pltpu.make_async_copy(x_hbm, x_ref, l_sems.at[2])
        w_loads = [
            pltpu.make_async_copy(w_qkv_hbm.at[:, cols], w_qkv.at[:, cols], sem)
            for cols, sem in (
                (pl.ds(1024, 1024), l_sems.at[3]),
                (pl.ds(0, 1024), l_sems.at[6]),
            )
        ]
        na_copy = pltpu.make_async_copy(na, na_hbm, l_sems.at[4])
        proj_copy = pltpu.make_async_copy(proj_ref, proj_hbm, l_sems.at[5])
        for load in (x_load, *w_loads, cot_load):
            load.start()
        peers = [partner] + [place.flipped(dims) for dims in LINKED] + ctx_peers(place)
        greet_signal(place, peers)
        columns = jnp.concatenate(
            [pos_ref[0].astype(f32), pos_ref[1].astype(f32), jnp.zeros((6, 128), f32)], 0
        ).T
        sign = jnp.where(lax.rem(lanes(128), 64) < 32, -1.0, 1.0)
        for m in range(2):
            angle = columns[:, m : m + 1] * freq_ref[...]
            cos_ref[pl.ds(128 * m, 128), :] = jnp.cos(angle)
            sin_ref[pl.ds(128 * m, 128), :] = jnp.sin(angle) * sign
        x_load.wait()
        inputs = x_ref[...].astype(f32)
        scale = lax.rsqrt(jnp.mean(inputs * inputs, axis=-1, keepdims=True) + norm_eps)
        na[...] = (inputs * scale * gain_ref[...]).astype(bf16)
        to_na = push(place, na, na_other_hbm, x_send.at[4], x_recv.at[4], partner)
        na_copy.start()
        w_loads[0].wait()

        def turned(tile, gain):
            u = tile * lax.rsqrt(head_mean(tile * tile) + norm_eps) * gain
            return u * cos_ref[...] + turn_heads(u) * sin_ref[...]

        def store(at, j, tile):
            for m in range(2):
                rows = tile[128 * m : 128 * m + 128].astype(bf16)
                a_first[m, pl.ds(8 * j, 8), :, pl.ds(at, 128)] = rows.reshape(8, 16, 128)

        for i in range(2):
            key_pair = dot(na[...], w_qkv[:, pl.ds(1024 + 256 * i, 256)])
            value_pair = dot(na[...], w_qkv[:, pl.ds(1536 + 256 * i, 256)])
            proj_ref[:, pl.ds(1024 + 256 * i, 256)] = key_pair
            for j in range(2):
                key = turned(key_pair[:, 128 * j : 128 * j + 128], gain_k)
                value = value_pair[:, 128 * j : 128 * j + 128]
                store(128, 4 * i + 2 * j, jnp.where(low, key, pltpu.roll(value, 64, 1)))
                store(128, 4 * i + 2 * j + 1, jnp.where(low, pltpu.roll(key, 64, 1), value))
        greet_wait(place, peers)
        to_dy.start()

        w_loads[1].wait()
        for i in range(4):
            p = lax.rem(lax.div(place.ctx, 2) + 1 + i, 4)
            at = pl.ds(pl.multiple_of(256 * p, 256), 256)
            pair = dot(na[...], w_qkv[:, at])
            proj_ref[:, at] = pair
            for j in range(2):
                store(0, 2 * p + j, turned(pair[:, 128 * j : 128 * j + 128], gain_q) * 0.125)
            for j in range(2):
                off = lax.rem(2 * p + j + 8 - place.ctx, 8)

                @pl.when(off > 0)
                def _(off=off):
                    heads_out.copy(0, off).start()

        heads_out.keep(0)
        heads_out.send(1)
        to_na.start()
        proj_copy.start()

        def heads(m, carry):
            heads_out.arrived(m)
            ends = document_edges(bounds_ref, m)[1]
            for b in range(4):
                query = b_first[m, pl.ds(16 * b, 16), :, pl.ds(0, 128)].reshape(256, 128)
                pair = b_first[m, pl.ds(16 * b, 16), :, pl.ds(128, 128)].reshape(256, 128)
                pair = pair.astype(f32)
                swapped = pltpu.roll(pair, 64, 1)
                q2[b] = head_rows(query)
                kk[b] = jnp.where(low, pair, swapped).astype(bf16)
                vo[b] = jnp.where(low, swapped, 1.0).astype(bf16)
            for qb in range(4):
                acc = jnp.zeros((512, 128), f32)
                for kb in range(qb + 1):
                    scores = dot_cols(q2[qb], kk[kb])
                    t = 256 * qb + lax.rem(lax.broadcasted_iota(jnp.int32, (512, 256), 0), 256)
                    keep = t < ends[:, 256 * kb : 256 * kb + 256]
                    if kb == qb:
                        s = 256 * kb + lax.broadcasted_iota(jnp.int32, (512, 256), 1)
                        keep = keep & (s <= t)
                    weights = jnp.where(keep, jnp.exp(scores), 0.0).astype(bf16)
                    acc = acc + dot(weights, vo[kb])
                total = pltpu.roll(acc, 64, 1)
                head0 = acc[:256]
                head1 = pltpu.roll(acc[256:], 64, 1)
                denominator = jnp.where(low, total[:256], acc[256:])
                out = jnp.where(low, head0, head1) / denominator
                log_total = jnp.log(denominator).T
                l_ref[m, pl.ds(0, 1), pl.ds(256 * qb, 256)] = log_total[0:1]
                l_ref[m, pl.ds(1, 1), pl.ds(256 * qb, 256)] = log_total[64:65]
                b_first[4 + m, pl.ds(16 * qb, 16), :, pl.ds(0, 128)] = out.astype(bf16).reshape(
                    16, 16, 128
                )
            heads_back.send(m)
            return carry

        lax.fori_loop(0, 2, heads, 0)
        qkv_copy.start()
        o_copy.start()
        na_copy.wait()
        proj_copy.wait()
        to_na.wait()

    pl.run_scoped(
        attend,
        pltpu.VMEM((1024, 2048), bf16),
        pltpu.VMEM((256, 1024), bf16),
        pltpu.VMEM((256, 1024), bf16),
        pltpu.VMEM((256, 1536), f32),
        pltpu.VMEM((4, 512, 128), bf16),
        pltpu.VMEM((4, 256, 128), bf16),
        pltpu.VMEM((4, 256, 128), bf16),
    )

    to_dm = push(place, dm_own.at[1 - core], dmin, x_send.at[6], x_recv.at[6], partner)
    out_copy = pltpu.make_async_copy(sum_send, out_hbm, l_sems.at[0])

    def feed_forward(wgu, wd, nft, h, ht, dgu, sum_own):
        def unit_loads(i):
            at = pl.multiple_of(core * FF_HALF + 768 * i, 256)
            up_at = pl.multiple_of(4608 + core * FF_HALF + 768 * i, 256)
            here = pl.ds(pl.multiple_of(768 * i, 256), 768)
            up_here = pl.ds(pl.multiple_of(FF_HALF + 768 * i, 256), 768)
            return [
                pltpu.make_async_copy(
                    wgu_hbm.at[:, pl.ds(at, 768)], wgu.at[:, here], w_sems.at[3 * i]
                ),
                pltpu.make_async_copy(
                    wgu_hbm.at[:, pl.ds(up_at, 768)], wgu.at[:, up_here], w_sems.at[3 * i + 1]
                ),
                pltpu.make_async_copy(
                    wd_hbm.at[pl.ds(at, 768)], wd.at[here], w_sems.at[3 * i + 2]
                ),
            ]

        w_out_loads = [
            pltpu.make_async_copy(
                w_out_hbm.at[pl.ds(512 * i, 512)], dgu.at[:, pl.ds(1024 * i, 1024)], l_sems.at[2 + i]
            )
            for i in range(2)
        ]
        x_load = pltpu.make_async_copy(x_hbm, sum_send, l_sems.at[4])
        for load in (x_load, *w_out_loads):
            load.start()
        for i in range(3):
            for copy in unit_loads(i):
                copy.start()
        for m in range(2):
            heads_back.arrived(m)
            for j in range(8):
                tile = b_first[2 + m, pl.ds(8 * j, 8), :, pl.ds(0, 128)].reshape(128, 128)
                dm_own[j // 4, pl.ds(128 * m, 128), pl.ds(128 * (j % 4), 128)] = tile
        to_att.start()
        att_copy.start()
        for load in (x_load, *w_out_loads):
            load.wait()
        mid = sum_send[...].astype(f32) + (
            dot(dm_own[0], dgu[:, pl.ds(0, 1024)]) + dot(dm_own[1], dgu[:, pl.ds(1024, 1024)])
        )
        mid_ref[...] = mid
        scale = lax.rsqrt(jnp.mean(mid * mid, axis=-1, keepdims=True) + norm_eps)
        nf[own_rows, :] = (mid * scale * gain_ffn_ref[...]).astype(bf16)
        to_nf.start()
        nft[:, own_rows] = nf[own_rows, :].T
        heads_out.sent()
        heads_back.sent()
        qkv_copy.wait()
        o_copy.wait()
        cot_load.wait()

        def token_half(half, carry):
            rows = pl.ds(pl.multiple_of(256 * half, 256), 256)

            @pl.when(half == 1)
            def _():
                to_dy.wait_recv()
                to_nf.wait_recv()

            def units(i, inner):
                @pl.when(half == 0)
                def _():
                    for copy in unit_loads(i):
                        copy.wait()

                cols = pl.ds(pl.multiple_of(768 * i, 256), 768)
                up_cols = pl.ds(pl.multiple_of(FF_HALF + 768 * i, 256), 768)
                gated = dot(nf[rows, :], wgu[:, cols])
                upward = dot(nf[rows, :], wgu[:, up_cols])
                grad_hidden = dot_cols(dyb[rows, :], wd[cols, :])
                sigma = 1.0 / (1.0 + jnp.exp(-gated))
                silu = gated * sigma
                h[rows, cols] = (silu * upward).astype(bf16)
                dgu[rows, cols] = (grad_hidden * upward * (sigma + silu * (1.0 - sigma))).astype(
                    bf16
                )
                dgu[rows, up_cols] = (grad_hidden * silu).astype(bf16)
                return inner

            return lax.fori_loop(0, 3, units, carry)

        lax.fori_loop(0, 2, token_half, 0)
        nft[:, other_rows] = nf[other_rows, :].T

        def down_grads():
            for block in range(3):
                ht[...] = h[:, pl.ds(768 * block, 768)].T
                for z in range(4):
                    part = dot(ht[...], dyb[:, pl.ds(256 * z, 256)])
                    for i in range(16):
                        q = 16 * block + i
                        y, core_to, x_lo, rg = q // 12, (q // 6) % 2, (q // 3) % 2, q % 3
                        for ch in range(2):
                            s = 2 * rg + ch
                            slot = slot_of(chip_number(core_to, x_lo, y, z), DOWN_ORDERS[s])
                            d_first[s, slot] = part[
                                48 * i : 48 * i + 48, 128 * ch : 128 * ch + 128
                            ].astype(bf16)
            for s in range(6):
                down.send(s, 0)

        def back_to_norm():
            def pair(i, carry):
                for j in range(2):
                    at = pl.ds(pl.multiple_of(512 * i + 256 * j, 256), 256)
                    part = dot_cols(dgu[...], wgu[at, :])
                    dmid[:, at] = part[:256]
                    sum_send[:, at] = part[256:].astype(bf16)
                return carry

            lax.fori_loop(0, 2, pair, 0)
            to_back.start()

        def wide_grads(scatter, first, base, orders, p):
            for x_hi in range(2):
                rows = nft[pl.ds(512 * x_hi, 512), :]
                for j in range(3):
                    part = dot(rows, dgu[:, pl.ds(base + 768 * p + 256 * j, 256)])
                    for k in range(2):
                        tile = 2 * j + k
                        s = 2 * p + tile // 3
                        reorder_store(
                            part[:, 128 * k : 128 * k + 128],
                            first,
                            s,
                            orders[s],
                            x_hi,
                            pl.ds(128 * (tile % 3), 128),
                            128,
                        )
            for s in (2 * p, 2 * p + 1):
                scatter.send(s, 0)

        w_out_load = pltpu.make_async_copy(w_out_hbm, wd.at[pl.ds(0, 1024)], l_sems.at[4])

        def output():
            to_back.wait_send()

            def pair(i, carry):
                for j in range(2):
                    at = pl.ds(pl.multiple_of(512 * i + 256 * j, 256), 256)
                    part = dot(h[...], wd[:, at])
                    sum_own[:, at] = part[:256]
                    sum_send[:, at] = part[256:].astype(bf16)
                return carry

            lax.fori_loop(0, 2, pair, 0)
            to_out.start()
            w_out_load.start()

        def output_sum():
            to_out.wait()
            sum_send[...] = (mid_ref[...] + sum_own[...] + sum_recv[0].astype(f32)).astype(bf16)
            out_copy.start()

        def norm_back():
            to_back.wait_recv()
            mid = mid_ref[...]
            scale = lax.rsqrt(jnp.mean(mid * mid, axis=-1, keepdims=True) + norm_eps)
            normed = mid * scale
            grad_nffn = dmid[...] + sum_recv[1].astype(f32)
            gain_grad = jnp.sum(grad_nffn * normed, axis=0, keepdims=True)
            for i in range(8):
                vec[0, pl.ds(8 + i, 1), :] = gain_grad[:, 128 * i : 128 * i + 128]
            grad_e = grad_nffn * gain_ffn_ref[...]
            dmid[...] = dyb[own_rows, :].astype(f32) + scale * (
                grad_e - normed * jnp.mean(grad_e * normed, axis=-1, keepdims=True)
            )
            to_att.wait_send()
            att_copy.wait()
            for half in range(2):
                dm_own[half] = dmid[:, pl.ds(512 * half, 512)].astype(bf16)
            to_dm.start()

            to_nf.wait_send()
            w_out_load.wait()
            for i in range(4):
                pair = dot_cols(dm_own[0], wd[pl.ds(256 * i, 256), pl.ds(0, 512)]) + dot_cols(
                    dm_own[1], wd[pl.ds(256 * i, 256), pl.ds(512, 512)]
                )
                for j in range(2):
                    for m in range(2):
                        do_out[m, 2 * i + j] = pair[
                            128 * m : 128 * m + 128, 128 * j : 128 * j + 128
                        ].astype(bf16)
            for m in range(2):
                grads_out.send(m)

        ops = {
            "down": down_grads,
            "dn": back_to_norm,
            "lo": output,
            "datt": norm_back,
            "out": output_sum,
        }
        for p in range(3):
            ops[f"Amm{p}"] = functools.partial(wide_grads, gate, a_first, 0, GATE_ORDERS, p)
            ops[f"Bmm{p}"] = functools.partial(wide_grads, up, b_first, FF_HALF, UP_ORDERS, p)
        run(ops, "split")

    pl.run_scoped(
        feed_forward,
        pltpu.VMEM((1024, 4608), bf16),
        pltpu.VMEM((FF_HALF, 1024), bf16),
        pltpu.VMEM((1024, 512), bf16),
        pltpu.VMEM((512, FF_HALF), bf16),
        pltpu.VMEM((768, 512), bf16),
        pltpu.VMEM((512, 4608), bf16),
        pltpu.VMEM((256, 1024), f32),
    )

    def vec_move(step):
        device = place.neighbour(step) if step < 6 else partner
        return push(place, vec.at[step], vec_in.at[step], v_send, v_recv.at[step], device)

    def vec_take(step):
        vec_move(step).wait_recv()
        vec[step + 1] = vec[step] + vec_in[step]
        vec_move(step + 1).start()

    def down_end():
        finish_down(place, down, d_acc, d_stage, d_in, f_send, f_recv, gdn_ref)

    swap = push(place, g_fin.at[1 - core], g_in, x_send.at[8], x_recv.at[8], partner)
    swap_q = push(place, q_fin.at[1 - core], q_in, x_send.at[9], x_recv.at[9], partner)

    def wide_end():
        for s in range(12):
            total = (gate if s < 6 else up).last(s % 6)
            g_fin[0, s] = total[:8]
            g_fin[1, s] = total[8:]
        swap.start()

    def quad_end():
        for s in range(6):
            total = quad.last(s)
            q_fin[0, s] = total[:8]
            q_fin[1, s] = total[8:]
        swap_q.start()

    def attention_back(
        w_qkv, x_ref, gtok, proj_ref, qkv_ref, o_ref, q2, do2, kk, vv, kt, delta, dq, dp,
        na_own, na_other, att_own, att_other, nat, attt, cols, t_out,
    ):
        sources = [qkv_hbm, o_hbm, proj_hbm, x_hbm, w_qkv_hbm]
        loads = [
            pltpu.make_async_copy(source, target, w_sems.at[i])
            for i, (source, target) in enumerate(
                zip(sources, [qkv_ref, o_ref, proj_ref, x_ref, w_qkv], strict=True)
            )
        ]
        for load in loads:
            load.start()
        grads_back = Exchange(
            place,
            lambda m, j: t_out.at[m, j],
            t_at,
            lambda m: t_out.at[m, pl.ds(0, 7)],
            t_send,
            t_recv,
        )

        def heads_grad(m, carry):
            grads_out.arrived(m)
            starts = document_edges(bounds_ref, m)[0]
            for b in range(4):
                query = qkv_ref[m, pl.ds(16 * b, 16), :, pl.ds(0, 128)].reshape(256, 128)
                pair = qkv_ref[m, pl.ds(16 * b, 16), :, pl.ds(128, 128)].reshape(256, 128)
                pair = pair.astype(f32)
                grad = do_in[m, pl.ds(2 * b, 2)].reshape(256, 128)
                swapped = pltpu.roll(pair, 64, 1)
                key_pair = jnp.where(low, pair, swapped)
                q2[b] = head_rows(query)
                do2[b] = head_rows(grad)
                kk[b] = key_pair.astype(bf16)
                vv[b] = jnp.where(low, swapped, pair).astype(bf16)
                kt[b] = key_pair.T.astype(bf16)
                out = o_ref[m, pl.ds(16 * b, 16)].reshape(256, 128).astype(f32)
                inner = (grad.astype(f32) * out).T
                delta[b, :, pl.ds(0, 256)] = jnp.sum(inner[:64], axis=0, keepdims=True)
                delta[b, :, pl.ds(256, 256)] = jnp.sum(inner[64:], axis=0, keepdims=True)
            for kb in range(4):
                grad_key = jnp.zeros((256, 128), f32)
                grad_value = jnp.zeros((256, 128), f32)
                for qb in range(kb, 4):
                    scores = dot_cols(kk[kb], q2[qb])
                    log_total = jnp.concatenate(
                        [l_ref[m, pl.ds(i, 1), pl.ds(256 * qb, 256)] for i in range(2)], 1
                    )
                    start = starts[:, 256 * qb : 256 * qb + 256]
                    s = 256 * kb + lax.broadcasted_iota(jnp.int32, (256, 512), 0)
                    keep = s >= jnp.concatenate([start, start], 1)
                    if kb == qb:
                        t = lax.broadcasted_iota(jnp.int32, (256, 512), 1)
                        keep = keep & (s <= 256 * qb + lax.rem(t, 256))
                    probs = jnp.where(keep, jnp.exp(scores - log_total), 0.0)
                    grad_probs = dot_cols(vv[kb], do2[qb])
                    grad_scores = (probs * (grad_probs - delta[qb])).astype(bf16)
                    grad_value = grad_value + dot(probs.astype(bf16), do2[qb])
                    grad_key = grad_key + dot(grad_scores, q2[qb])
                    grad_query = dot(kt[kb], grad_scores)
                    if kb == 0:
                        dq[qb] = grad_query[:64]
                    else:
                        dq[qb] = dq[qb] + grad_query[:64]
                grad_key = grad_key + pltpu.roll(grad_key, 64, 1)
                grad_value = grad_value + pltpu.roll(grad_value, 64, 1)
                tile = jnp.where(low, grad_key, grad_value).astype(bf16)
                for half in range(2):
                    rows = slice(128 * half, 128 * half + 128)
                    t_out[m, 2 * kb + half, :, pl.ds(128, 128)] = tile[rows]
            for qb in range(4):
                stacked = jnp.concatenate([dq[qb, :, pl.ds(0, 256)], dq[qb, :, pl.ds(256, 256)]], 0)
                tile = (stacked * 0.125).T.astype(bf16)
                for half in range(2):
                    rows = slice(128 * half, 128 * half + 128)
                    t_out[m, 2 * qb + half, :, pl.ds(0, 128)] = tile[rows]
            grads_back.send(m)
            return carry

        def heads_grads():
            for load in loads[:2]:
                load.wait()
            lax.fori_loop(0, 2, heads_grad, 0)

        def sums_free():
            gate.sent(0)
            up.sent(0)
            for dim in range(6):
                pl.semaphore_signal(
                    free_sem, inc=1, device_id=place.neighbour(dim), device_id_type=MESH
                )

        sides = [
            pltpu.make_async_copy(source, target, l_sems.at[2 + i])
            for i, (source, target) in enumerate(
                zip(
                    [na_hbm, att_hbm, na_other_hbm, att_other_hbm],
                    [na_own, att_own, na_other, att_other],
                    strict=True,
                )
            )
        ]
        for load in sides[:3]:
            load.start()

        def token_sides():
            to_att.wait_recv()
            sides[3].start()
            for load in sides[:3]:
                load.wait()
            nat[:, own_rows] = na_own[...].T
            nat[:, other_rows] = na_other[...].T
            sides[3].wait()
            for i in range(2):
                attt[pl.ds(512 * i, 512), own_rows] = att_own[i].T
                attt[pl.ds(512 * i, 512), other_rows] = att_other[i].T
            to_dm.wait_recv()
            cols[own_rows, pl.ds(1024, 512)] = dm_own[core]
            cols[other_rows, pl.ds(1024, 512)] = dmin[...]

        def projection_grads(s):
            left = nat if s < 4 else attt
            if s == 0:
                to_dp.wait_recv()
                cols[other_rows, pl.ds(0, 1024)] = dpin[...]
            for x_hi in range(2):
                part = dot(left[pl.ds(512 * x_hi, 512), :], cols[:, pl.ds(256 * s, 256)])
                reorder_store(part, a_first, s, QUAD_ORDERS[s], x_hi, narrow, 256)
            if s == 4:
                pl.semaphore_wait(free_sem, 6)
            quad.send(s, 0)

        def both_rows(j, at):
            return jnp.concatenate([t_at(m, j)[:, pl.ds(at, 128)] for m in range(2)], 0).astype(f32)

        def head_back(grad, value, gain):
            grad = grad * cos_ref[...] + turn_heads(grad * sin_ref[...])
            scale = lax.rsqrt(head_mean(value * value) + norm_eps)
            normed = value * scale
            grad_e = grad * gain
            gain_grad = jnp.sum(grad * normed, axis=0, keepdims=True)
            return scale * (grad_e - normed * head_mean(grad_e * normed)), gain_grad

        to_dp = push(place, dp.at[1 - core], dpin, x_send.at[7], x_recv.at[7], partner)
        gtok_copy = pltpu.make_async_copy(gtok, gtok_hbm, l_sems.at[1])

        def turn_back():
            loads[2].wait()
            for m in range(2):
                grads_back.arrived(m)
            sum_k = jnp.zeros((1, 128), f32)

            def query_pair(i, total):
                for j in range(2):
                    at = pl.ds(pl.multiple_of(256 * i + 128 * j, 128), 128)
                    back, part = head_back(both_rows(2 * i + j, 0), proj_ref[:, at], gain_q)
                    dp[0, :, at] = back.astype(bf16)
                    total = total + part
                return total

            sum_q = lax.fori_loop(0, 4, query_pair, jnp.zeros((1, 128), f32))
            for i in range(4):
                first = both_rows(2 * i, 128)
                second = both_rows(2 * i + 1, 128)
                grad_key = jnp.where(low, first, pltpu.roll(second, 64, 1))
                grad_value = jnp.where(low, pltpu.roll(first, 64, 1), second)
                back, part = head_back(grad_key, proj_ref[:, pl.ds(1024 + 128 * i, 128)], gain_k)
                dp[1, :, pl.ds(128 * i, 128)] = back.astype(bf16)
                dp[1, :, pl.ds(512 + 128 * i, 128)] = grad_value.astype(bf16)
                sum_k = sum_k + part
            to_dp.start()
            sum_q = sum_q + pltpu.roll(sum_q, 64, 1)
            sum_k = sum_k + pltpu.roll(sum_k, 64, 1)
            vec[0, pl.ds(16, 8), :] = jnp.zeros((8, 128), f32)
            vec[0, pl.ds(16, 1), :] = jnp.where(
                lax.broadcasted_iota(jnp.int32, (1, 128), 1) < 64, sum_q, sum_k
            )
            cols[own_rows, pl.ds(0, 1024)] = dp[core]

        def last_norm():
            loads[3].wait()
            loads[4].wait()
            inputs = x_ref[...].astype(f32)
            scale = lax.rsqrt(jnp.mean(inputs * inputs, axis=-1, keepdims=True) + norm_eps)
            normed = inputs * scale
            grad_n = dot_cols(dp[0], w_qkv[:, pl.ds(0, 1024)]) + dot_cols(
                dp[1], w_qkv[:, pl.ds(1024, 1024)]
            )
            gain_grad = jnp.sum(grad_n * normed, axis=0, keepdims=True)
            grad_e = grad_n * gain_ref[...]
            gtok[...] = dmid[...] + scale * (
                grad_e - normed * jnp.mean(grad_e * normed, axis=-1, keepdims=True)
            )
            gtok_copy.start()
            for i in range(8):
                vec[0, pl.ds(i, 1), :] = gain_grad[:, 128 * i : 128 * i + 128]
            vec_move(0).start()

        ops = {
            "heads": heads_grads,
            "free": sums_free,
            "nat": token_sides,
            "headb": turn_back,
            "lastnorm": last_norm,
            "Dfin": down_end,
            "Afin": wide_end,
            "Qfin": quad_end,
        }
        for s in range(6):
            ops[f"Qmm{s}"] = functools.partial(projection_grads, s)
            ops[f"v{s}"] = functools.partial(vec_take, s)
        run(ops, "end")
        gtok_copy.wait()
        to_dp.wait_send()
        grads_back.sent()

    pl.run_scoped(
        attention_back,
        pltpu.VMEM((1024, 2048), bf16),
        pltpu.VMEM((256, 1024), bf16),
        pltpu.VMEM((256, 1024), f32),
        pltpu.VMEM((256, 1536), f32),
        pltpu.VMEM((2, 64, 16, 256), bf16),
        pltpu.VMEM((2, 64, 16, 128), bf16),
        pltpu.VMEM((4, 512, 128), bf16),
        pltpu.VMEM((4, 512, 128), bf16),
        pltpu.VMEM((4, 256, 128), bf16),
        pltpu.VMEM((4, 256, 128), bf16),
        pltpu.VMEM((4, 128, 256), bf16),
        pltpu.VMEM((4, 1, 512), f32),
        pltpu.VMEM((4, 64, 512), f32),
        pltpu.VMEM((2, 256, 1024), bf16),
        pltpu.VMEM((256, 1024), bf16),
        pltpu.VMEM((256, 1024), bf16),
        pltpu.VMEM((2, 256, 512), bf16),
        pltpu.VMEM((2, 256, 512), bf16),
        pltpu.VMEM((1024, 512), bf16),
        pltpu.VMEM((1024, 512), bf16),
        pltpu.VMEM((512, 1536), bf16),
        pltpu.VMEM((2, 8, 128, 256), bf16),
    )

    def wide_cols(of, s):
        return pl.ds(pl.multiple_of((s // 6) * 4608 + of * FF_HALF + (s % 6) * 384, 128), 384)

    def quad_cols(of, s):
        if s < 4:
            return gqkv_ref, pl.ds(pl.multiple_of(of * 1024 + 256 * s, 256), 256)
        return gout_ref, pl.ds(pl.multiple_of(of * 512 + 256 * (s - 4), 256), 256)

    results = [
        pltpu.make_async_copy(source, target, r_sems.at[i])
        for i, (source, target) in enumerate(
            (
                (gdn_ref, gdn_hbm),
                (ggu_ref, ggu_hbm),
                (gqkv_ref, gqkv_hbm),
                (gout_ref, gout_hbm),
                (vec.at[7], vec_hbm),
            )
        )
    ]
    results[0].start()
    for s in range(12):
        ggu_ref[:, wide_cols(core, s)] = g_fin[core, s]
    swap.wait_recv()
    for s in range(12):
        ggu_ref[:, wide_cols(1 - core, s)] = g_in[s]
    results[1].start()
    vec_move(6).wait_recv()
    vec[7] = vec[6] + vec_in[6]
    results[4].start()
    for s in range(6):
        ref, at = quad_cols(core, s)
        ref[:, at] = q_fin[core, s]
    swap_q.wait_recv()
    for s in range(6):
        ref, at = quad_cols(1 - core, s)
        ref[:, at] = q_in[s]
    results[2].start()
    results[3].start()

    for move in (to_dy, to_dm, swap, swap_q):
        move.wait_send()
    out_copy.wait()
    push(place, vec_in, vec_in, v_send, v_recv.at[0], partner).wait_send()
    for scatter, parts in ((down, (0, 1)), (gate, (1,)), (up, (1,)), (quad, (0, 1))):
        for part in parts:
            scatter.sent(part)
    grads_out.sent()
    for copy in results:
        copy.wait()


def block(bounds, *arrays):
    vmem = pl.BlockSpec(memory_space=pltpu.VMEM)
    hbm = pl.BlockSpec(memory_space=pl.ANY)
    smem = pl.BlockSpec(memory_space=pltpu.SMEM)
    dma = pltpu.SemaphoreType.DMA
    return pl.pallas_call(
        block_kernel,
        out_shape=(
            jax.ShapeDtypeStruct((256, 1024), bf16),
            jax.ShapeDtypeStruct((256, 1024), f32),
            jax.ShapeDtypeStruct((8, 9216), f32),
            jax.ShapeDtypeStruct((36, 1024), f32),
            jax.ShapeDtypeStruct((8, 2048), f32),
            jax.ShapeDtypeStruct((8, 1024), f32),
            jax.ShapeDtypeStruct((24, 128), f32),
            jax.ShapeDtypeStruct((256, 1024), bf16),
            jax.ShapeDtypeStruct((256, 1024), bf16),
            jax.ShapeDtypeStruct((2, 256, 512), bf16),
            jax.ShapeDtypeStruct((2, 256, 512), bf16),
            jax.ShapeDtypeStruct((256, 1536), f32),
            jax.ShapeDtypeStruct((2, 64, 16, 256), bf16),
            jax.ShapeDtypeStruct((2, 64, 16, 128), bf16),
        ),
        in_specs=[smem] + [vmem] * 5 + [hbm] * 6,
        out_specs=(hbm,) * 14,
        scratch_shapes=[
            pltpu.VMEM((6, 64, 16, 384), bf16),
            pltpu.VMEM((6, 63, 16, 384), bf16),
            pltpu.VMEM((6, 64, 16, 384), bf16),
            pltpu.VMEM((6, 63, 16, 384), bf16),
            pltpu.VMEM((6, 64, 48, 128), bf16),
            pltpu.VMEM((6, 63, 48, 128), bf16),
            pltpu.VMEM((512, 1024), bf16),
            pltpu.VMEM((512, 1024), bf16),
            pltpu.VMEM((256, 1024), bf16),
            pltpu.VMEM((2, 256, 1024), bf16),
            pltpu.VMEM((256, 1024), f32),
            pltpu.VMEM((256, 1024), f32),
            pltpu.VMEM((256, 128), f32),
            pltpu.VMEM((256, 128), f32),
            pltpu.VMEM((2, 2, 1024), f32),
            pltpu.VMEM((2, 8, 128, 128), bf16),
            pltpu.VMEM((2, 8, 128, 128), bf16),
            pltpu.VMEM((256, 1024), bf16),
            pltpu.VMEM((256, 512), bf16),
            pltpu.VMEM((2, 256, 512), bf16),
            pltpu.VMEM((2, 12, 8, 384), f32),
            pltpu.VMEM((12, 8, 384), f32),
            pltpu.VMEM((144, 256), f32),
            pltpu.VMEM((4, 40, 256), f32),
            pltpu.VMEM((4, 40, 256), f32),
            pltpu.VMEM((2, 6, 8, 256), f32),
            pltpu.VMEM((6, 8, 256), f32),
            pltpu.VMEM((8, 24, 128), f32),
            pltpu.VMEM((7, 24, 128), f32),
            pltpu.VMEM((8, 9216), f32),
            pltpu.VMEM((36, 1024), f32),
            pltpu.VMEM((8, 2048), f32),
            pltpu.VMEM((8, 1024), f32),
            dma((9,)),
            dma((10,)),
            dma((5,)),
            dma((10,)),
            dma((10,)),
            dma((2,)),
            dma((6, 6)),
            dma((2,)),
            dma((6, 6)),
            dma((2,)),
            dma((6, 6)),
            dma((2,)),
            dma((6, 4)),
            dma((2,)),
            dma((2,)),
            dma((2,)),
            dma((2,)),
            dma((2,)),
            dma((2,)),
            dma((2,)),
            dma((2,)),
            dma((2,)),
            dma((2,)),
            dma,
            dma((7,)),
            pltpu.SemaphoreType.REGULAR,
        ],
        compiler_params=pltpu.CompilerParams(
            collective_id=0, has_side_effects=True, vmem_limit_bytes=VMEM_LIMIT
        ),
        name="transformer_block",
    )(bounds, *arrays)


def finish_kernel(*refs):
    arrays, vec = refs[:6], refs[6]
    targets, (gain_a, gain_f, gain_qk) = refs[7:13], refs[13:16]
    passing, (in_sems, out_sems) = refs[16:22], refs[22:]
    reads = [
        pltpu.make_async_copy(array, held, in_sems.at[i])
        for i, (array, held) in enumerate(zip(arrays, passing, strict=True))
    ]
    writes = [
        pltpu.make_async_copy(held, target, out_sems.at[i])
        for i, (held, target) in enumerate(zip(passing, targets, strict=True))
    ]
    for read in reads:
        read.start()
    own = lax.axis_index("rows") * 8 + lax.axis_index("ctx")
    row = lax.div(own, 16)
    at = lax.rem(own, 16)
    lane = lax.broadcasted_iota(jnp.int32, (8, 128), 1)
    tile = lax.broadcasted_iota(jnp.int32, (8, 128), 0)

    def pick(values, of_row, of_lane, count):
        kept = jnp.sum(jnp.where(tile == of_row, values, 0.0), axis=0, keepdims=True)
        place = lax.broadcasted_iota(jnp.int32, (128, count), 0)
        order = lax.broadcasted_iota(jnp.int32, (128, count), 1)
        rows = jnp.broadcast_to(kept, (8, 128)).T[:, :count]
        return jnp.sum(jnp.where(place == of_lane + order, rows, 0.0), axis=0, keepdims=True)

    gain_a[...] = pick(vec[pl.ds(0, 8), :], row, 8 * at, 8)
    gain_f[...] = pick(vec[pl.ds(8, 8), :], row, 8 * at, 8)
    gain_qk[...] = pick(vec[pl.ds(16, 8), :], 0, own, 1)
    for read, write in zip(reads, writes, strict=True):
        read.wait()
        write.start()
    for write in writes:
        write.wait()


def finish(out, gtok, ggu, gdn, gqkv, gout, vec):
    vmem = pl.BlockSpec(memory_space=pltpu.VMEM)
    hbm = pl.BlockSpec(memory_space=pl.ANY)
    same = [jax.ShapeDtypeStruct(a.shape, a.dtype) for a in (out, gtok, ggu, gdn, gqkv, gout)]
    return pl.pallas_call(
        finish_kernel,
        out_shape=(
            *same,
            jax.ShapeDtypeStruct((1, 8), f32),
            jax.ShapeDtypeStruct((1, 8), f32),
            jax.ShapeDtypeStruct((1, 1), f32),
        ),
        in_specs=[hbm] * 6 + [vmem],
        out_specs=(hbm,) * 6 + (vmem,) * 3,
        scratch_shapes=[pltpu.VMEM(a.shape, a.dtype) for a in same]
        + [pltpu.SemaphoreType.DMA((6,)), pltpu.SemaphoreType.DMA((6,))],
        name="results",
    )(out, gtok, ggu, gdn, gqkv, gout, vec)


def local(
    tokens,
    cotangent,
    bounds,
    positions,
    norm_gain_attn,
    w_qkv,
    qk_gain,
    w_out,
    norm_gain_ffn,
    w_gate_up,
    w_down,
):
    lane = np.arange(128) % 32
    freqs = (rope_theta ** (-2.0 * lane / 64)).astype(np.float32)[None]
    results = block(
        bounds,
        positions,
        freqs,
        norm_gain_attn[None],
        norm_gain_ffn[None],
        qk_gain[None],
        tokens.reshape(256, 1024),
        cotangent.reshape(256, 1024),
        w_gate_up,
        w_down,
        w_qkv,
        w_out,
    )
    layer_out, grad_tokens, sum_gate_up, sum_down, sum_qkv, sum_out, gain_a, gain_f, gain_qk = (
        finish(*results[:7])
    )
    return (
        layer_out.reshape(tokens.shape),
        grad_tokens.reshape(tokens.shape),
        gain_a.reshape(8),
        sum_qkv,
        gain_qk.reshape(1),
        sum_out,
        gain_f.reshape(8),
        sum_gate_up,
        sum_down,
    )


def solution(mesh):
    placed = (
        P(None, "rows", "ctx", None),
        P(None, "rows", "ctx", None),
        P(None, "rows", None),
        P(None, "rows", "ctx"),
        P(),
        P(),
        P(),
        P(),
        P(),
        P(),
        P(),
    )
    return jax.shard_map(
        local,
        mesh=mesh,
        in_specs=placed,
        out_specs=(
            P(None, "rows", "ctx", None),
            P(None, "rows", "ctx", None),
            P(("rows", "ctx")),
            P(("rows", "ctx"), None),
            P(("rows", "ctx")),
            P(("rows", "ctx"), None),
            P(("rows", "ctx")),
            P(("rows", "ctx"), None),
            P(("rows", "ctx"), None),
        ),
        check_vma=False,
    )
```

```python
import functools

import jax
import jax.numpy as jnp
import numpy as np
from jax import lax
from jax.experimental import pallas as pl
from jax.experimental.pallas import tpu as pltpu
from jax.sharding import PartitionSpec as P

MESH = pl.DeviceIdType.MESH
norm_eps = 1e-05
rope_theta = 1000000.0
f32 = jnp.float32
bf16 = jnp.bfloat16
VMEM_LIMIT = 64 * 2**20 - 2**18


class Place:
    def __init__(self):
        r = lax.axis_index("rows")
        k = lax.axis_index("ctx")
        self.x_hi = lax.div(r, 8)
        self.y = lax.rem(lax.div(r, 2), 4)
        self.core = lax.rem(r, 2)
        self.x_lo = lax.div(k, 4)
        self.z = lax.rem(k, 4)
        self.rows = r
        self.ctx = k
        self.bits = [
            self.x_hi,
            lax.rem(self.x_hi + self.x_lo, 2),
            lax.div(self.y, 2),
            lax.rem(lax.div(self.y, 2) + lax.rem(self.y, 2), 2),
            lax.div(self.z, 2),
            lax.rem(lax.div(self.z, 2) + lax.rem(self.z, 2), 2),
        ]

    def at(self, x_hi=None, x_lo=None, y=None, z=None, core=None):
        x_hi = self.x_hi if x_hi is None else x_hi
        x_lo = self.x_lo if x_lo is None else x_lo
        y = self.y if y is None else y
        z = self.z if z is None else z
        core = self.core if core is None else core
        return (x_hi * 8 + y * 2 + core, x_lo * 4 + z)

    def partner(self):
        return self.at(core=1 - self.core)

    def neighbour(self, dim):
        if dim == 0:
            return self.at(x_hi=1 - self.x_hi, x_lo=1 - self.x_lo)
        if dim == 1:
            return self.at(x_lo=1 - self.x_lo)
        if dim == 2:
            return self.at(y=3 - self.y)
        if dim == 3:
            return self.at(y=self.y + 1 - 2 * lax.rem(self.y, 2))
        if dim == 4:
            return self.at(z=3 - self.z)
        return self.at(z=self.z + 1 - 2 * lax.rem(self.z, 2))


    def flipped(self, dims):
        if len(dims) == 1:
            return self.neighbour(dims[0])
        if 0 in dims:
            return self.at(x_hi=1 - self.x_hi)
        if 2 in dims:
            return self.at(y=lax.rem(self.y + 2, 4))
        return self.at(z=lax.rem(self.z + 2, 4))


def gray(v):
    return v ^ (v >> 1)


def chip_number(x_hi, x_lo, y, z):
    return gray(2 * x_hi + x_lo) * 16 + gray(y) * 4 + gray(z)


def slot_of(number, order):
    return sum(((number >> (5 - dim)) & 1) << (5 - t) for t, dim in enumerate(order))


ONES = (1, 1, 1, 1, 1, 1)
FLIPS = {1: ((1,),), 2: ((0, 1), (1, 0), (1, 1))}


class Scatter:
    def __init__(self, place, orders, shape, first, held, send_sems, recv_sems):
        self.place = place
        self.orders = orders
        self.first, self.first_cols = first
        self.held, self.held_cols = held
        self.send_sems = send_sems
        self.recv_sems = recv_sems
        self.stages = []
        at, slots, base = 0, 64, 0
        for width in shape:
            size = slots >> width
            self.stages.append((at, width, size, base))
            base += size * len(FLIPS[width])
            at += width
            slots = size

    def source(self, k):
        if k == 0:
            return self.first, 0, self.first_cols
        return self.held, self.stages[k - 1][3], self.held_cols

    def part(self, s, k, flips):
        at, width, size, _ = self.stages[k]
        which = 0
        for dim, flip in zip(self.orders[s][at : at + width], flips, strict=True):
            bit = self.place.bits[dim]
            which = 2 * which + (1 - bit if flip else bit)
        return which * size

    def copies(self, s, k):
        at, width, size, base = self.stages[k]
        ref, start, cols = self.source(k)
        dims = self.orders[s][at : at + width]
        return [
            pltpu.make_async_remote_copy(
                src_ref=ref.at[s, pl.ds(start + self.part(s, k, flips), size), :, cols],
                dst_ref=self.held.at[s, pl.ds(base + i * size, size), :, self.held_cols],
                send_sem=self.send_sems.at[min(k, 1)],
                recv_sem=self.recv_sems.at[s, k],
                device_id=self.place.flipped([d for d, f in zip(dims, flips, strict=True) if f]),
                device_id_type=MESH,
            )
            for i, flips in enumerate(FLIPS[width])
        ]

    def send(self, s, k):
        for copy in self.copies(s, k):
            copy.start()

    def arrived(self, s, k):
        _, width, size, base = self.stages[k]
        place = self.held.at[s, pl.ds(base, size * len(FLIPS[width])), :, self.held_cols]
        self.wait(place, 0, self.recv_sems.at[s, k]).wait_recv()
        ref, start, cols = self.source(k)
        own = start + self.part(s, k, (0,) * width)

        def total(at):
            value = ref[s, own + at, :, cols].astype(f32)
            for i in range(len(FLIPS[width])):
                value = value + self.held[s, base + i * size + at, :, self.held_cols].astype(f32)
            return value

        return total, size, base

    def take(self, s, k):
        total, size, base = self.arrived(s, k)
        per = min(8, size)

        def body(i, carry):
            for j in range(per):
                at = i * per + j
                self.held[s, base + at, :, self.held_cols] = total(at).astype(bf16)
            return carry

        lax.fori_loop(0, size // per, body, 0)
        self.send(s, k + 1)

    def last(self, s):
        return self.arrived(s, len(self.stages) - 1)[0](0)

    def wait(self, ref, part, recv_sem):
        return push(
            self.place, ref, ref, self.send_sems.at[part], recv_sem, self.place.partner()
        )

    def sent(self, part):
        slots = pl.ds(0, 32) if part == 0 else pl.ds(32, 31)
        self.wait(
            self.held.at[:, slots, :, self.held_cols], part, self.recv_sems.at[0, 0]
        ).wait_send()


def greet_signal(place, devices):
    barrier = pltpu.get_barrier_semaphore()
    targets = down_targets(place)
    for device in devices + targets[1:]:
        pl.semaphore_signal(barrier, inc=1, device_id=device, device_id_type=MESH)

    @pl.when(place.x_hi != place.core)
    def _():
        pl.semaphore_signal(barrier, inc=1, device_id=targets[0], device_id_type=MESH)


def greet_wait(place, devices):
    barrier = pltpu.get_barrier_semaphore()
    count = len(devices) + 3

    @pl.when(place.x_hi != place.core)
    def _():
        pl.semaphore_wait(barrier, count + 1)

    @pl.when(place.x_hi == place.core)
    def _():
        pl.semaphore_wait(barrier, count)


def push(place, src, dst, send_sem, recv_sem, device):
    return pltpu.make_async_remote_copy(
        src_ref=src,
        dst_ref=dst,
        send_sem=send_sem,
        recv_sem=recv_sem,
        device_id=device,
        device_id_type=MESH,
    )


def down_targets(place):
    return [
        place.at(x_hi=place.core, core=place.x_hi, z=lax.rem(place.z + off, 4)) for off in range(4)
    ]


def dot(left, right):
    return jnp.dot(left, right, preferred_element_type=f32)


def dot_cols(left, right):
    return lax.dot_general(left, right, (((1,), (1,)), ((), ())), preferred_element_type=f32)


FF_HALF = 2304
DOWN_ORDERS = (
    (0, 3, 5, 2, 1, 4),
    (3, 5, 4, 2, 0, 1),
    (2, 3, 0, 4, 1, 5),
    (4, 2, 0, 1, 3, 5),
    (5, 2, 3, 4, 0, 1),
    (0, 3, 4, 1, 5, 2),
)
GATE_ORDERS = (
    (5, 2, 1, 3, 4, 0),
    (4, 0, 3, 5, 1, 2),
    (2, 1, 4, 3, 0, 5),
    (0, 3, 2, 5, 4, 1),
    (4, 0, 2, 3, 5, 1),
    (5, 3, 0, 2, 1, 4),
)
UP_ORDERS = (
    (2, 3, 1, 4, 0, 5),
    (3, 4, 5, 0, 2, 1),
    (0, 2, 5, 4, 3, 1),
    (1, 0, 2, 3, 5, 4),
    (1, 2, 5, 0, 4, 3),
    (3, 1, 2, 0, 4, 5),
)
QUAD_ORDERS = (
    (2, 3, 1, 0, 4, 5),
    (1, 0, 5, 4, 2, 3),
    (3, 2, 1, 0, 5, 4),
    (5, 4, 3, 2, 1, 0),
    (4, 5, 2, 3, 0, 1),
    (1, 0, 5, 4, 2, 3),
)
QUAD_STAGES = (1, 1, 2, 2)
LINKED = ((0,), (1,), (2,), (3,), (4,), (5,), (0, 1), (2, 3), (4, 5))
STEPS = (
    "Bmm0", "Amm0", "Bmm1", "Bmm2", "Amm2", "Amm1", "dn", "B00", "down", "lo",
    "B20", "A20", "A00", "A10", "B30", "datt", "B50", "A40", "B10", "B40",
    "A30", "D40", "D10", "out", "A21", "B01", "A50", "split", "D20", "B21",
    "heads", "A31", "nat", "D00", "B51", "B11", "free", "D11", "A11", "D21",
    "D30", "A01", "A22", "D50", "B41", "D41", "B02", "B22", "A51", "B31",
    "Qmm4", "B52", "Qmm5", "A12", "D01", "A32", "headb", "A41", "lastnorm", "A02",
    "D12", "B03", "B12", "D31", "D51", "B23", "B32", "Qmm0", "Qmm1", "Qmm3",
    "Qmm2", "D42", "B53", "A13", "v0", "D13", "B24", "A42", "A23", "A52",
    "B42", "Q50", "A33", "B13", "A03", "D02", "B04", "D22", "D32", "D14",
    "Q40", "A24", "D52", "B33", "B43", "D43", "Q00", "B54", "Q10", "Q30",
    "v1", "Q20", "A53", "A34", "Q51", "B14", "A04", "D23", "D33", "D03",
    "A43", "D53", "v2", "Q41", "B44", "A54", "Q01", "B34", "Q11", "A14",
    "Q31", "Q21", "D04", "D34", "v3", "Q52", "D54", "D24", "A44", "D44",
    "Q42", "Q02", "Q12", "Q32", "Q22", "v4", "Afin", "Dfin", "Qfin", "v5",
    "end",
)


class DownOwners:
    def __init__(self, place, stage, into, send_sems, recv_sems):
        self.swapped = place.x_hi != place.core
        self.place = place
        self.stage = stage
        self.into = into
        targets = down_targets(place)
        self.moves = [
            push(
                place,
                stage.at[lax.rem(place.z + off, 4)],
                into.at[place.z],
                send_sems.at[min(off, 1)],
                recv_sems.at[min(off, 1)],
                targets[off],
            )
            for off in range(4)
        ]
        three = into.at[pl.ds(0, 3)]
        self.others = push(place, three, three, send_sems.at[1], recv_sems.at[1], targets[1])

    def send(self, down, acc):
        for s in range(6):
            acc[pl.ds(48 * (s // 2), 48), pl.ds(128 * (s % 2), 128)] = down.last(s)
        for z in range(4):
            self.stage[z, pl.ds(0, 36), :] = acc[pl.ds(36 * z, 36), :]
            self.stage[z, pl.ds(36, 4), :] = jnp.zeros((4, 256), f32)
        for move in self.moves[1:]:
            move.start()

        @pl.when(self.swapped)
        def _():
            self.moves[0].start()

        @pl.when(jnp.logical_not(self.swapped))
        def _():
            self.into[self.place.z] = self.stage[self.place.z]

    def arrived(self, out):
        @pl.when(self.swapped)
        def _():
            self.moves[0].wait_recv()

        self.others.wait_recv()
        for z in range(4):
            out[:, pl.ds(256 * z, 256)] = self.into[z, pl.ds(0, 36), :]

    def sent(self):
        self.others.wait_send()

        @pl.when(self.swapped)
        def _():
            self.moves[0].wait_send()


def lanes(rows):
    return lax.broadcasted_iota(jnp.int32, (rows, 128), 1)


def turn_heads(values):
    low = lax.rem(lanes(values.shape[0]), 64) < 32
    return jnp.where(low, pltpu.roll(values, 96, 1), pltpu.roll(values, 32, 1))


def head_mean(values):
    i = lax.broadcasted_iota(jnp.int32, (128, 128), 0)
    j = lax.broadcasted_iota(jnp.int32, (128, 128), 1)
    ones = jnp.where(lax.div(i, 64) == lax.div(j, 64), 1.0 / 64, 0.0).astype(bf16)
    high = values.astype(bf16)
    rest = (values - high.astype(f32)).astype(bf16)
    return dot(high, ones) + dot(rest, ones)


def gain_tiles(qk_gain):
    swapped = pltpu.roll(qk_gain, 64, 1)
    low = lax.broadcasted_iota(jnp.int32, (1, 128), 1) < 64
    return jnp.where(low, qk_gain, swapped), jnp.where(low, swapped, qk_gain)


def head_rows(values):
    low = lanes(values.shape[0]) < 64
    zero = jnp.zeros_like(values)
    return jnp.concatenate([jnp.where(low, values, zero), jnp.where(low, zero, values)], 0)


class Exchange:
    def __init__(self, place, out_at, into_at, seven, send_sems, recv_sems):
        self.place = place
        self.seven = seven
        self.out_at = out_at
        self.into_at = into_at
        self.send_sems = send_sems
        self.recv_sems = recv_sems

    def copy(self, m, off):
        j = lax.rem(self.place.ctx + off, 8)
        return push(
            self.place,
            self.out_at(m, j),
            self.into_at(m, self.place.ctx),
            self.send_sems.at[m],
            self.recv_sems.at[m],
            (self.place.rows, j),
        )

    def send(self, m):
        for off in range(1, 8):
            self.copy(m, off).start()
        self.keep(m)

    def keep(self, m):
        self.into_at(m, self.place.ctx)[...] = self.out_at(m, self.place.ctx)[...]

    def all_seven(self, m):
        ref = self.seven(m)
        return push(
            self.place, ref, ref, self.send_sems.at[m], self.recv_sems.at[m], self.place.partner()
        )

    def arrived(self, m):
        self.all_seven(m).wait_recv()

    def sent(self):
        for m in range(2):
            self.all_seven(m).wait_send()


def ctx_peers(place):
    return [(place.rows, lax.rem(place.ctx + off, 8)) for off in range(1, 8)]


def document_edges(bounds_ref, m):
    index = lax.broadcasted_iota(jnp.int32, (1, 1024), 1)
    start = jnp.zeros((1, 1024), jnp.int32)
    end = jnp.full((1, 1024), 1024, jnp.int32)
    for k in range(1, 4):
        cut = bounds_ref[m, 0, k]
        start = jnp.where(index >= cut, cut, start)
        end = jnp.where(index < bounds_ref[m, 0, 4 - k], bounds_ref[m, 0, 4 - k], end)
    return start, end


def reorder_store(part, first, s, order, x_hi, at, width):
    part = part.reshape(4, 2, 8, 8, width)
    for y in range(4):
        for x_lo in range(2):
            for z in range(4):
                slot = slot_of(chip_number(x_hi, x_lo, y, z), order)
                first[s, slot, :, at] = part[y, :, 4 * x_lo + z].reshape(16, width).astype(bf16)


def block_kernel(
    bounds_ref,
    pos_ref,
    freq_ref,
    gain_ref,
    gain_ffn_ref,
    qk_gain_ref,
    x_hbm,
    cot_hbm,
    wgu_hbm,
    wd_hbm,
    w_qkv_hbm,
    w_out_hbm,
    out_hbm,
    gtok_hbm,
    ggu_hbm,
    gdn_hbm,
    gqkv_hbm,
    gout_hbm,
    vec_hbm,
    na_hbm,
    na_other_hbm,
    att_hbm,
    att_other_hbm,
    proj_hbm,
    qkv_hbm,
    o_hbm,
    a_first,
    a_held,
    b_first,
    b_held,
    d_first,
    d_held,
    nf,
    dyb,
    sum_send,
    sum_recv,
    mid_ref,
    dmid,
    cos_ref,
    sin_ref,
    l_ref,
    do_out,
    do_in,
    dpin,
    dmin,
    dm_own,
    g_fin,
    g_in,
    d_acc,
    d_stage,
    d_in,
    q_fin,
    q_in,
    vec,
    vec_in,
    ggu_ref,
    gdn_ref,
    gqkv_ref,
    gout_ref,
    w_sems,
    l_sems,
    r_sems,
    x_send,
    x_recv,
    a_send,
    a_recv,
    b_send,
    b_recv,
    d_send,
    d_recv,
    q_send,
    q_recv,
    f_send,
    f_recv,
    k_send,
    k_recv,
    e_send,
    e_recv,
    do_send,
    do_recv,
    t_send,
    t_recv,
    v_send,
    v_recv,
    free_sem,
):
    place = Place()
    core = place.core
    partner = place.partner()
    every = slice(None)
    down = Scatter(place, DOWN_ORDERS, ONES, (d_first, every), (d_held, every), d_send, d_recv)
    gate = Scatter(place, GATE_ORDERS, ONES, (a_first, every), (a_held, every), a_send, a_recv)
    up = Scatter(place, UP_ORDERS, ONES, (b_first, every), (b_held, every), b_send, b_recv)
    narrow = pl.ds(0, 256)
    quad = Scatter(
        place, QUAD_ORDERS, QUAD_STAGES, (a_first, narrow), (b_first, narrow), q_send, q_recv
    )
    sums = {"D": down, "A": gate, "B": up, "Q": quad}
    steps = iter(STEPS)

    def run(ops, until):
        for name in steps:
            if name == until:
                return
            if name in ops:
                ops[name]()
            else:
                sums[name[0]].take(int(name[1]), int(name[2]))
    def t_at(m, j):
        return nf.at[
            pl.ds(pl.multiple_of(256 * m + 128 * lax.div(j, 4), 128), 128),
            pl.ds(pl.multiple_of(256 * lax.rem(j, 4), 256), 256),
        ]

    def tiles(ref, s, j, width):
        return ref.at[s, pl.ds(pl.multiple_of(8 * j, 8), 8), :, pl.ds(0, width)]

    heads_out = Exchange(
        place,
        lambda m, j: tiles(a_first, m, j, 256),
        lambda m, j: tiles(b_first, m, j, 256),
        lambda m: b_first.at[m, pl.ds(0, 56), :, pl.ds(0, 256)],
        k_send,
        k_recv,
    )
    heads_back = Exchange(
        place,
        lambda m, j: tiles(b_first, 4 + m, j, 128),
        lambda m, j: tiles(b_first, 2 + m, j, 128),
        lambda m: b_first.at[2 + m, pl.ds(0, 56), :, pl.ds(0, 128)],
        e_send,
        e_recv,
    )
    grads_out = Exchange(
        place,
        lambda m, j: do_out.at[m, j],
        lambda m, j: do_in.at[m, j],
        lambda m: do_in.at[m, pl.ds(0, 7)],
        do_send,
        do_recv,
    )
    own_rows = pl.ds(0, 256)
    other_rows = pl.ds(256, 256)
    to_dy = push(place, cot_hbm, dyb.at[other_rows], x_send.at[0], x_recv.at[0], partner)
    to_nf = push(place, nf.at[own_rows], nf.at[other_rows], x_send.at[1], x_recv.at[1], partner)
    to_out = push(place, sum_send, sum_recv.at[0], x_send.at[2], x_recv.at[2], partner)
    to_back = push(place, sum_send, sum_recv.at[1], x_send.at[3], x_recv.at[3], partner)
    to_att = push(place, dm_own, att_other_hbm, x_send.at[5], x_recv.at[5], partner)
    att_copy = pltpu.make_async_copy(dm_own, att_hbm, l_sems.at[7])
    qkv_copy = pltpu.make_async_copy(
        b_first.at[pl.ds(0, 2), :, :, pl.ds(0, 256)], qkv_hbm, l_sems.at[8]
    )
    o_copy = pltpu.make_async_copy(
        b_first.at[pl.ds(4, 2), :, :, pl.ds(0, 128)], o_hbm, l_sems.at[9]
    )
    cot_load = pltpu.make_async_copy(cot_hbm, dyb.at[own_rows], l_sems.at[1])
    low = lanes(256) < 64
    gain_q, gain_k = gain_tiles(qk_gain_ref[...])

    def attend(w_qkv, x_ref, na, proj_ref, q2, kk, vo):
        x_load = pltpu.make_async_copy(x_hbm, x_ref, l_sems.at[2])
        w_loads = [
            pltpu.make_async_copy(w_qkv_hbm.at[:, cols], w_qkv.at[:, cols], sem)
            for cols, sem in (
                (pl.ds(1024, 1024), l_sems.at[3]),
                (pl.ds(0, 1024), l_sems.at[6]),
            )
        ]
        na_copy = pltpu.make_async_copy(na, na_hbm, l_sems.at[4])
        proj_copy = pltpu.make_async_copy(proj_ref, proj_hbm, l_sems.at[5])
        for load in (x_load, *w_loads, cot_load):
            load.start()
        peers = [partner] + [place.flipped(dims) for dims in LINKED] + ctx_peers(place)
        greet_signal(place, peers)
        columns = jnp.concatenate(
            [pos_ref[0].astype(f32), pos_ref[1].astype(f32), jnp.zeros((6, 128), f32)], 0
        ).T
        sign = jnp.where(lax.rem(lanes(128), 64) < 32, -1.0, 1.0)
        for m in range(2):
            angle = columns[:, m : m + 1] * freq_ref[...]
            cos_ref[pl.ds(128 * m, 128), :] = jnp.cos(angle)
            sin_ref[pl.ds(128 * m, 128), :] = jnp.sin(angle) * sign
        x_load.wait()
        inputs = x_ref[...].astype(f32)
        scale = lax.rsqrt(jnp.mean(inputs * inputs, axis=-1, keepdims=True) + norm_eps)
        na[...] = (inputs * scale * gain_ref[...]).astype(bf16)
        to_na = push(place, na, na_other_hbm, x_send.at[4], x_recv.at[4], partner)
        na_copy.start()
        w_loads[0].wait()

        def turned(tile, gain):
            u = tile * lax.rsqrt(head_mean(tile * tile) + norm_eps) * gain
            return u * cos_ref[...] + turn_heads(u) * sin_ref[...]

        def store(at, j, tile):
            for m in range(2):
                rows = tile[128 * m : 128 * m + 128].astype(bf16)
                a_first[m, pl.ds(8 * j, 8), :, pl.ds(at, 128)] = rows.reshape(8, 16, 128)

        for i in range(2):
            key_pair = dot(na[...], w_qkv[:, pl.ds(1024 + 256 * i, 256)])
            value_pair = dot(na[...], w_qkv[:, pl.ds(1536 + 256 * i, 256)])
            proj_ref[:, pl.ds(1024 + 256 * i, 256)] = key_pair
            for j in range(2):
                key = turned(key_pair[:, 128 * j : 128 * j + 128], gain_k)
                value = value_pair[:, 128 * j : 128 * j + 128]
                store(128, 4 * i + 2 * j, jnp.where(low, key, pltpu.roll(value, 64, 1)))
                store(128, 4 * i + 2 * j + 1, jnp.where(low, pltpu.roll(key, 64, 1), value))
        greet_wait(place, peers)
        to_dy.start()

        w_loads[1].wait()
        for i in range(4):
            p = lax.rem(lax.div(place.ctx, 2) + 1 + i, 4)
            at = pl.ds(pl.multiple_of(256 * p, 256), 256)
            pair = dot(na[...], w_qkv[:, at])
            proj_ref[:, at] = pair
            for j in range(2):
                store(0, 2 * p + j, turned(pair[:, 128 * j : 128 * j + 128], gain_q) * 0.125)
            for j in range(2):
                off = lax.rem(2 * p + j + 8 - place.ctx, 8)

                @pl.when(off > 0)
                def _(off=off):
                    heads_out.copy(0, off).start()

        heads_out.keep(0)
        heads_out.send(1)
        to_na.start()
        proj_copy.start()

        def heads(m, carry):
            heads_out.arrived(m)
            ends = document_edges(bounds_ref, m)[1]
            for b in range(4):
                query = b_first[m, pl.ds(16 * b, 16), :, pl.ds(0, 128)].reshape(256, 128)
                pair = b_first[m, pl.ds(16 * b, 16), :, pl.ds(128, 128)].reshape(256, 128)
                pair = pair.astype(f32)
                swapped = pltpu.roll(pair, 64, 1)
                q2[b] = head_rows(query)
                kk[b] = jnp.where(low, pair, swapped).astype(bf16)
                vo[b] = jnp.where(low, swapped, 1.0).astype(bf16)
            for qb in range(4):
                acc = jnp.zeros((512, 128), f32)
                for kb in range(qb + 1):
                    scores = dot_cols(q2[qb], kk[kb])
                    t = 256 * qb + lax.rem(lax.broadcasted_iota(jnp.int32, (512, 256), 0), 256)
                    keep = t < ends[:, 256 * kb : 256 * kb + 256]
                    if kb == qb:
                        s = 256 * kb + lax.broadcasted_iota(jnp.int32, (512, 256), 1)
                        keep = keep & (s <= t)
                    weights = jnp.where(keep, jnp.exp(scores), 0.0).astype(bf16)
                    acc = acc + dot(weights, vo[kb])
                total = pltpu.roll(acc, 64, 1)
                head0 = acc[:256]
                head1 = pltpu.roll(acc[256:], 64, 1)
                denominator = jnp.where(low, total[:256], acc[256:])
                out = jnp.where(low, head0, head1) / denominator
                log_total = jnp.log(denominator).T
                l_ref[m, pl.ds(0, 1), pl.ds(256 * qb, 256)] = log_total[0:1]
                l_ref[m, pl.ds(1, 1), pl.ds(256 * qb, 256)] = log_total[64:65]
                b_first[4 + m, pl.ds(16 * qb, 16), :, pl.ds(0, 128)] = out.astype(bf16).reshape(
                    16, 16, 128
                )
            heads_back.send(m)
            return carry

        lax.fori_loop(0, 2, heads, 0)
        qkv_copy.start()
        o_copy.start()
        na_copy.wait()
        proj_copy.wait()
        to_na.wait()

    pl.run_scoped(
        attend,
        pltpu.VMEM((1024, 2048), bf16),
        pltpu.VMEM((256, 1024), bf16),
        pltpu.VMEM((256, 1024), bf16),
        pltpu.VMEM((256, 1536), f32),
        pltpu.VMEM((4, 512, 128), bf16),
        pltpu.VMEM((4, 256, 128), bf16),
        pltpu.VMEM((4, 256, 128), bf16),
    )

    to_dm = push(place, dm_own.at[1 - core], dmin, x_send.at[6], x_recv.at[6], partner)
    out_copy = pltpu.make_async_copy(sum_send, out_hbm, l_sems.at[0])

    def feed_forward(wgu, wd, nft, h, ht, dgu, sum_own):
        def unit_loads(i):
            at = pl.multiple_of(core * FF_HALF + 768 * i, 256)
            up_at = pl.multiple_of(4608 + core * FF_HALF + 768 * i, 256)
            here = pl.ds(pl.multiple_of(768 * i, 256), 768)
            up_here = pl.ds(pl.multiple_of(FF_HALF + 768 * i, 256), 768)
            return [
                pltpu.make_async_copy(
                    wgu_hbm.at[:, pl.ds(at, 768)], wgu.at[:, here], w_sems.at[3 * i]
                ),
                pltpu.make_async_copy(
                    wgu_hbm.at[:, pl.ds(up_at, 768)], wgu.at[:, up_here], w_sems.at[3 * i + 1]
                ),
                pltpu.make_async_copy(
                    wd_hbm.at[pl.ds(at, 768)], wd.at[here], w_sems.at[3 * i + 2]
                ),
            ]

        w_out_loads = [
            pltpu.make_async_copy(
                w_out_hbm.at[pl.ds(512 * i, 512)], dgu.at[:, pl.ds(1024 * i, 1024)], l_sems.at[2 + i]
            )
            for i in range(2)
        ]
        x_load = pltpu.make_async_copy(x_hbm, sum_send, l_sems.at[4])
        for load in (x_load, *w_out_loads):
            load.start()
        for i in range(3):
            for copy in unit_loads(i):
                copy.start()
        for m in range(2):
            heads_back.arrived(m)
            for j in range(8):
                tile = b_first[2 + m, pl.ds(8 * j, 8), :, pl.ds(0, 128)].reshape(128, 128)
                dm_own[j // 4, pl.ds(128 * m, 128), pl.ds(128 * (j % 4), 128)] = tile
        to_att.start()
        att_copy.start()
        for load in (x_load, *w_out_loads):
            load.wait()
        mid = sum_send[...].astype(f32) + (
            dot(dm_own[0], dgu[:, pl.ds(0, 1024)]) + dot(dm_own[1], dgu[:, pl.ds(1024, 1024)])
        )
        mid_ref[...] = mid
        scale = lax.rsqrt(jnp.mean(mid * mid, axis=-1, keepdims=True) + norm_eps)
        nf[own_rows, :] = (mid * scale * gain_ffn_ref[...]).astype(bf16)
        to_nf.start()
        nft[:, own_rows] = nf[own_rows, :].T
        heads_out.sent()
        heads_back.sent()
        qkv_copy.wait()
        o_copy.wait()
        cot_load.wait()

        def token_half(half, carry):
            rows = pl.ds(pl.multiple_of(256 * half, 256), 256)

            @pl.when(half == 1)
            def _():
                to_dy.wait_recv()
                to_nf.wait_recv()

            def units(i, inner):
                @pl.when(half == 0)
                def _():
                    for copy in unit_loads(i):
                        copy.wait()

                cols = pl.ds(pl.multiple_of(768 * i, 256), 768)
                up_cols = pl.ds(pl.multiple_of(FF_HALF + 768 * i, 256), 768)
                gated = dot(nf[rows, :], wgu[:, cols])
                upward = dot(nf[rows, :], wgu[:, up_cols])
                grad_hidden = dot_cols(dyb[rows, :], wd[cols, :])
                sigma = 1.0 / (1.0 + jnp.exp(-gated))
                silu = gated * sigma
                h[rows, cols] = (silu * upward).astype(bf16)
                dgu[rows, cols] = (grad_hidden * upward * (sigma + silu * (1.0 - sigma))).astype(
                    bf16
                )
                dgu[rows, up_cols] = (grad_hidden * silu).astype(bf16)
                return inner

            return lax.fori_loop(0, 3, units, carry)

        lax.fori_loop(0, 2, token_half, 0)
        nft[:, other_rows] = nf[other_rows, :].T

        def down_grads():
            for block in range(3):
                ht[...] = h[:, pl.ds(768 * block, 768)].T
                for z in range(4):
                    part = dot(ht[...], dyb[:, pl.ds(256 * z, 256)])
                    for i in range(16):
                        q = 16 * block + i
                        y, core_to, x_lo, rg = q // 12, (q // 6) % 2, (q // 3) % 2, q % 3
                        for ch in range(2):
                            s = 2 * rg + ch
                            slot = slot_of(chip_number(core_to, x_lo, y, z), DOWN_ORDERS[s])
                            d_first[s, slot] = part[
                                48 * i : 48 * i + 48, 128 * ch : 128 * ch + 128
                            ].astype(bf16)
            for s in range(6):
                down.send(s, 0)

        def back_to_norm():
            for j in range(4):
                at = pl.ds(256 * j, 256)
                part = dot_cols(dgu[...], wgu[at, :])
                dmid[:, at] = part[:256]
                sum_send[:, at] = part[256:].astype(bf16)
            to_back.start()

        def wide_grads(scatter, first, base, orders, p):
            for x_hi in range(2):
                rows = nft[pl.ds(512 * x_hi, 512), :]
                for j in range(3):
                    part = dot(rows, dgu[:, pl.ds(base + 768 * p + 256 * j, 256)])
                    for k in range(2):
                        tile = 2 * j + k
                        s = 2 * p + tile // 3
                        reorder_store(
                            part[:, 128 * k : 128 * k + 128],
                            first,
                            s,
                            orders[s],
                            x_hi,
                            pl.ds(128 * (tile % 3), 128),
                            128,
                        )
            for s in (2 * p, 2 * p + 1):
                scatter.send(s, 0)

        w_out_load = pltpu.make_async_copy(w_out_hbm, wd.at[pl.ds(0, 1024)], l_sems.at[4])

        def output():
            to_back.wait_send()

            def pair(i, carry):
                for j in range(2):
                    at = pl.ds(pl.multiple_of(512 * i + 256 * j, 256), 256)
                    part = dot(h[...], wd[:, at])
                    sum_own[:, at] = part[:256]
                    sum_send[:, at] = part[256:].astype(bf16)
                return carry

            lax.fori_loop(0, 2, pair, 0)
            to_out.start()
            w_out_load.start()

        def output_sum():
            to_out.wait()
            sum_send[...] = (mid_ref[...] + sum_own[...] + sum_recv[0].astype(f32)).astype(bf16)
            out_copy.start()

        def norm_back():
            to_back.wait_recv()
            mid = mid_ref[...]
            scale = lax.rsqrt(jnp.mean(mid * mid, axis=-1, keepdims=True) + norm_eps)
            normed = mid * scale
            grad_nffn = dmid[...] + sum_recv[1].astype(f32)
            gain_grad = jnp.sum(grad_nffn * normed, axis=0, keepdims=True)
            for i in range(8):
                vec[0, pl.ds(8 + i, 1), :] = gain_grad[:, 128 * i : 128 * i + 128]
            grad_e = grad_nffn * gain_ffn_ref[...]
            dmid[...] = dyb[own_rows, :].astype(f32) + scale * (
                grad_e - normed * jnp.mean(grad_e * normed, axis=-1, keepdims=True)
            )
            to_att.wait_send()
            att_copy.wait()
            for half in range(2):
                dm_own[half] = dmid[:, pl.ds(512 * half, 512)].astype(bf16)
            to_dm.start()

            to_nf.wait_send()
            w_out_load.wait()
            for i in range(4):
                pair = dot_cols(dm_own[0], wd[pl.ds(256 * i, 256), pl.ds(0, 512)]) + dot_cols(
                    dm_own[1], wd[pl.ds(256 * i, 256), pl.ds(512, 512)]
                )
                for j in range(2):
                    for m in range(2):
                        do_out[m, 2 * i + j] = pair[
                            128 * m : 128 * m + 128, 128 * j : 128 * j + 128
                        ].astype(bf16)
            for m in range(2):
                grads_out.send(m)

        ops = {
            "down": down_grads,
            "dn": back_to_norm,
            "lo": output,
            "datt": norm_back,
            "out": output_sum,
        }
        for p in range(3):
            ops[f"Amm{p}"] = functools.partial(wide_grads, gate, a_first, 0, GATE_ORDERS, p)
            ops[f"Bmm{p}"] = functools.partial(wide_grads, up, b_first, FF_HALF, UP_ORDERS, p)
        run(ops, "split")

    pl.run_scoped(
        feed_forward,
        pltpu.VMEM((1024, 4608), bf16),
        pltpu.VMEM((FF_HALF, 1024), bf16),
        pltpu.VMEM((1024, 512), bf16),
        pltpu.VMEM((512, FF_HALF), bf16),
        pltpu.VMEM((768, 512), bf16),
        pltpu.VMEM((512, 4608), bf16),
        pltpu.VMEM((256, 1024), f32),
    )

    def vec_move(step):
        device = place.neighbour(step) if step < 6 else partner
        return push(place, vec.at[step], vec_in.at[step], v_send, v_recv.at[step], device)

    def vec_take(step):
        vec_move(step).wait_recv()
        vec[step + 1] = vec[step] + vec_in[step]
        vec_move(step + 1).start()

    down_out = DownOwners(place, d_stage, d_in, f_send, f_recv)

    def down_end():
        down_out.send(down, d_acc)

    swap = push(place, g_fin.at[1 - core], g_in, x_send.at[8], x_recv.at[8], partner)
    swap_q = push(place, q_fin.at[1 - core], q_in, x_send.at[9], x_recv.at[9], partner)

    def wide_end():
        for s in range(12):
            total = (gate if s < 6 else up).last(s % 6)
            g_fin[0, s] = total[:8]
            g_fin[1, s] = total[8:]
        swap.start()

    def quad_end():
        for s in range(6):
            total = quad.last(s)
            q_fin[0, s] = total[:8]
            q_fin[1, s] = total[8:]
        swap_q.start()

    def attention_back(
        w_qkv, x_ref, gtok, proj_ref, qkv_ref, o_ref, q2, do2, kk, vv, kt, delta, dq, dp,
        na_own, na_other, att_own, att_other, nat, attt, cols, t_out,
    ):
        sources = [qkv_hbm, o_hbm, proj_hbm, x_hbm, w_qkv_hbm]
        loads = [
            pltpu.make_async_copy(source, target, w_sems.at[i])
            for i, (source, target) in enumerate(
                zip(sources, [qkv_ref, o_ref, proj_ref, x_ref, w_qkv], strict=True)
            )
        ]
        for load in loads:
            load.start()
        grads_back = Exchange(
            place,
            lambda m, j: t_out.at[m, j],
            t_at,
            lambda m: t_out.at[m, pl.ds(0, 7)],
            t_send,
            t_recv,
        )

        def heads_grad(m, carry):
            grads_out.arrived(m)
            starts = document_edges(bounds_ref, m)[0]
            for b in range(4):
                query = qkv_ref[m, pl.ds(16 * b, 16), :, pl.ds(0, 128)].reshape(256, 128)
                pair = qkv_ref[m, pl.ds(16 * b, 16), :, pl.ds(128, 128)].reshape(256, 128)
                pair = pair.astype(f32)
                grad = do_in[m, pl.ds(2 * b, 2)].reshape(256, 128)
                swapped = pltpu.roll(pair, 64, 1)
                key_pair = jnp.where(low, pair, swapped)
                q2[b] = head_rows(query)
                do2[b] = head_rows(grad)
                kk[b] = key_pair.astype(bf16)
                vv[b] = jnp.where(low, swapped, pair).astype(bf16)
                kt[b] = key_pair.T.astype(bf16)
                out = o_ref[m, pl.ds(16 * b, 16)].reshape(256, 128).astype(f32)
                inner = (grad.astype(f32) * out).T
                delta[b, :, pl.ds(0, 256)] = jnp.sum(inner[:64], axis=0, keepdims=True)
                delta[b, :, pl.ds(256, 256)] = jnp.sum(inner[64:], axis=0, keepdims=True)
            for kb in range(4):
                grad_key = jnp.zeros((256, 128), f32)
                grad_value = jnp.zeros((256, 128), f32)
                for qb in range(kb, 4):
                    scores = dot_cols(kk[kb], q2[qb])
                    log_total = jnp.concatenate(
                        [l_ref[m, pl.ds(i, 1), pl.ds(256 * qb, 256)] for i in range(2)], 1
                    )
                    start = starts[:, 256 * qb : 256 * qb + 256]
                    s = 256 * kb + lax.broadcasted_iota(jnp.int32, (256, 512), 0)
                    keep = s >= jnp.concatenate([start, start], 1)
                    if kb == qb:
                        t = lax.broadcasted_iota(jnp.int32, (256, 512), 1)
                        keep = keep & (s <= 256 * qb + lax.rem(t, 256))
                    probs = jnp.where(keep, jnp.exp(scores - log_total), 0.0)
                    grad_probs = dot_cols(vv[kb], do2[qb])
                    grad_scores = (probs * (grad_probs - delta[qb])).astype(bf16)
                    grad_value = grad_value + dot(probs.astype(bf16), do2[qb])
                    grad_key = grad_key + dot(grad_scores, q2[qb])
                    grad_query = dot(kt[kb], grad_scores)
                    if kb == 0:
                        dq[qb] = grad_query[:64]
                    else:
                        dq[qb] = dq[qb] + grad_query[:64]
                grad_key = grad_key + pltpu.roll(grad_key, 64, 1)
                grad_value = grad_value + pltpu.roll(grad_value, 64, 1)
                tile = jnp.where(low, grad_key, grad_value).astype(bf16)
                for half in range(2):
                    rows = slice(128 * half, 128 * half + 128)
                    t_out[m, 2 * kb + half, :, pl.ds(128, 128)] = tile[rows]
            for qb in range(4):
                stacked = jnp.concatenate([dq[qb, :, pl.ds(0, 256)], dq[qb, :, pl.ds(256, 256)]], 0)
                tile = (stacked * 0.125).T.astype(bf16)
                for half in range(2):
                    rows = slice(128 * half, 128 * half + 128)
                    t_out[m, 2 * qb + half, :, pl.ds(0, 128)] = tile[rows]
            grads_back.send(m)
            return carry

        def heads_grads():
            for load in loads[:2]:
                load.wait()
            lax.fori_loop(0, 2, heads_grad, 0)

        def sums_free():
            gate.sent(0)
            up.sent(0)
            for dim in range(6):
                pl.semaphore_signal(
                    free_sem, inc=1, device_id=place.neighbour(dim), device_id_type=MESH
                )

        sides = [
            pltpu.make_async_copy(source, target, l_sems.at[2 + i])
            for i, (source, target) in enumerate(
                zip(
                    [na_hbm, att_hbm, na_other_hbm, att_other_hbm],
                    [na_own, att_own, na_other, att_other],
                    strict=True,
                )
            )
        ]
        for load in sides[:3]:
            load.start()

        def token_sides():
            to_att.wait_recv()
            sides[3].start()
            for load in sides[:3]:
                load.wait()
            nat[:, own_rows] = na_own[...].T
            nat[:, other_rows] = na_other[...].T
            sides[3].wait()
            for i in range(2):
                attt[pl.ds(512 * i, 512), own_rows] = att_own[i].T
                attt[pl.ds(512 * i, 512), other_rows] = att_other[i].T
            to_dm.wait_recv()
            cols[own_rows, pl.ds(1024, 512)] = dm_own[core]
            cols[other_rows, pl.ds(1024, 512)] = dmin[...]

        def projection_grads(s):
            left = nat if s < 4 else attt
            if s == 0:
                to_dp.wait_recv()
                cols[other_rows, pl.ds(0, 1024)] = dpin[...]
            for x_hi in range(2):
                part = dot(left[pl.ds(512 * x_hi, 512), :], cols[:, pl.ds(256 * s, 256)])
                reorder_store(part, a_first, s, QUAD_ORDERS[s], x_hi, narrow, 256)
            if s == 4:
                pl.semaphore_wait(free_sem, 6)
            quad.send(s, 0)

        def both_rows(j, at):
            return jnp.concatenate([t_at(m, j)[:, pl.ds(at, 128)] for m in range(2)], 0).astype(f32)

        def head_back(grad, value, gain):
            grad = grad * cos_ref[...] + turn_heads(grad * sin_ref[...])
            scale = lax.rsqrt(head_mean(value * value) + norm_eps)
            normed = value * scale
            grad_e = grad * gain
            gain_grad = jnp.sum(grad * normed, axis=0, keepdims=True)
            return scale * (grad_e - normed * head_mean(grad_e * normed)), gain_grad

        to_dp = push(place, dp.at[1 - core], dpin, x_send.at[7], x_recv.at[7], partner)
        gtok_copy = pltpu.make_async_copy(gtok, gtok_hbm, l_sems.at[1])

        def turn_back():
            loads[2].wait()
            for m in range(2):
                grads_back.arrived(m)
            sum_k = jnp.zeros((1, 128), f32)

            def query_pair(i, total):
                for j in range(2):
                    at = pl.ds(pl.multiple_of(256 * i + 128 * j, 128), 128)
                    back, part = head_back(both_rows(2 * i + j, 0), proj_ref[:, at], gain_q)
                    dp[0, :, at] = back.astype(bf16)
                    total = total + part
                return total

            sum_q = lax.fori_loop(0, 4, query_pair, jnp.zeros((1, 128), f32))
            for i in range(4):
                first = both_rows(2 * i, 128)
                second = both_rows(2 * i + 1, 128)
                grad_key = jnp.where(low, first, pltpu.roll(second, 64, 1))
                grad_value = jnp.where(low, pltpu.roll(first, 64, 1), second)
                back, part = head_back(grad_key, proj_ref[:, pl.ds(1024 + 128 * i, 128)], gain_k)
                dp[1, :, pl.ds(128 * i, 128)] = back.astype(bf16)
                dp[1, :, pl.ds(512 + 128 * i, 128)] = grad_value.astype(bf16)
                sum_k = sum_k + part
            to_dp.start()
            sum_q = sum_q + pltpu.roll(sum_q, 64, 1)
            sum_k = sum_k + pltpu.roll(sum_k, 64, 1)
            vec[0, pl.ds(16, 8), :] = jnp.zeros((8, 128), f32)
            vec[0, pl.ds(16, 1), :] = jnp.where(
                lax.broadcasted_iota(jnp.int32, (1, 128), 1) < 64, sum_q, sum_k
            )
            cols[own_rows, pl.ds(0, 1024)] = dp[core]

        def last_norm():
            loads[3].wait()
            loads[4].wait()
            inputs = x_ref[...].astype(f32)
            scale = lax.rsqrt(jnp.mean(inputs * inputs, axis=-1, keepdims=True) + norm_eps)
            normed = inputs * scale
            grad_n = dot_cols(dp[0], w_qkv[:, pl.ds(0, 1024)]) + dot_cols(
                dp[1], w_qkv[:, pl.ds(1024, 1024)]
            )
            gain_grad = jnp.sum(grad_n * normed, axis=0, keepdims=True)
            grad_e = grad_n * gain_ref[...]
            gtok[...] = dmid[...] + scale * (
                grad_e - normed * jnp.mean(grad_e * normed, axis=-1, keepdims=True)
            )
            gtok_copy.start()
            for i in range(8):
                vec[0, pl.ds(i, 1), :] = gain_grad[:, 128 * i : 128 * i + 128]
            vec_move(0).start()

        ops = {
            "heads": heads_grads,
            "free": sums_free,
            "nat": token_sides,
            "headb": turn_back,
            "lastnorm": last_norm,
            "Dfin": down_end,
            "Afin": wide_end,
            "Qfin": quad_end,
        }
        for s in range(6):
            ops[f"Qmm{s}"] = functools.partial(projection_grads, s)
            ops[f"v{s}"] = functools.partial(vec_take, s)
        run(ops, "end")
        gtok_copy.wait()
        to_dp.wait_send()
        grads_back.sent()

    pl.run_scoped(
        attention_back,
        pltpu.VMEM((1024, 2048), bf16),
        pltpu.VMEM((256, 1024), bf16),
        pltpu.VMEM((256, 1024), f32),
        pltpu.VMEM((256, 1536), f32),
        pltpu.VMEM((2, 64, 16, 256), bf16),
        pltpu.VMEM((2, 64, 16, 128), bf16),
        pltpu.VMEM((4, 512, 128), bf16),
        pltpu.VMEM((4, 512, 128), bf16),
        pltpu.VMEM((4, 256, 128), bf16),
        pltpu.VMEM((4, 256, 128), bf16),
        pltpu.VMEM((4, 128, 256), bf16),
        pltpu.VMEM((4, 1, 512), f32),
        pltpu.VMEM((4, 64, 512), f32),
        pltpu.VMEM((2, 256, 1024), bf16),
        pltpu.VMEM((256, 1024), bf16),
        pltpu.VMEM((256, 1024), bf16),
        pltpu.VMEM((2, 256, 512), bf16),
        pltpu.VMEM((2, 256, 512), bf16),
        pltpu.VMEM((1024, 512), bf16),
        pltpu.VMEM((1024, 512), bf16),
        pltpu.VMEM((512, 1536), bf16),
        pltpu.VMEM((2, 8, 128, 256), bf16),
    )

    def wide_cols(of, s):
        return pl.ds(pl.multiple_of((s // 6) * 4608 + of * FF_HALF + (s % 6) * 384, 128), 384)

    def quad_cols(of, s):
        if s < 4:
            return gqkv_ref, pl.ds(pl.multiple_of(of * 1024 + 256 * s, 256), 256)
        return gout_ref, pl.ds(pl.multiple_of(of * 512 + 256 * (s - 4), 256), 256)

    results = [
        pltpu.make_async_copy(source, target, r_sems.at[i])
        for i, (source, target) in enumerate(
            (
                (gdn_ref, gdn_hbm),
                (ggu_ref, ggu_hbm),
                (gqkv_ref, gqkv_hbm),
                (gout_ref, gout_hbm),
                (vec.at[7], vec_hbm),
            )
        )
    ]
    for s in range(12):
        ggu_ref[:, wide_cols(core, s)] = g_fin[core, s]
    down_out.arrived(gdn_ref)
    results[0].start()
    swap.wait_recv()
    for s in range(12):
        ggu_ref[:, wide_cols(1 - core, s)] = g_in[s]
    results[1].start()
    vec_move(6).wait_recv()
    vec[7] = vec[6] + vec_in[6]
    results[4].start()
    for s in range(6):
        ref, at = quad_cols(core, s)
        ref[:, at] = q_fin[core, s]
    swap_q.wait_recv()
    for s in range(6):
        ref, at = quad_cols(1 - core, s)
        ref[:, at] = q_in[s]
    results[2].start()
    results[3].start()

    for move in (to_dy, to_dm, swap, swap_q):
        move.wait_send()
    out_copy.wait()
    push(place, vec_in, vec_in, v_send, v_recv.at[0], partner).wait_send()
    for scatter, parts in ((down, (0, 1)), (gate, (1,)), (up, (1,)), (quad, (0, 1))):
        for part in parts:
            scatter.sent(part)
    grads_out.sent()
    down_out.sent()
    for copy in results:
        copy.wait()


def block(bounds, *arrays):
    vmem = pl.BlockSpec(memory_space=pltpu.VMEM)
    hbm = pl.BlockSpec(memory_space=pl.ANY)
    smem = pl.BlockSpec(memory_space=pltpu.SMEM)
    dma = pltpu.SemaphoreType.DMA
    return pl.pallas_call(
        block_kernel,
        out_shape=(
            jax.ShapeDtypeStruct((256, 1024), bf16),
            jax.ShapeDtypeStruct((256, 1024), f32),
            jax.ShapeDtypeStruct((8, 9216), f32),
            jax.ShapeDtypeStruct((36, 1024), f32),
            jax.ShapeDtypeStruct((8, 2048), f32),
            jax.ShapeDtypeStruct((8, 1024), f32),
            jax.ShapeDtypeStruct((24, 128), f32),
            jax.ShapeDtypeStruct((256, 1024), bf16),
            jax.ShapeDtypeStruct((256, 1024), bf16),
            jax.ShapeDtypeStruct((2, 256, 512), bf16),
            jax.ShapeDtypeStruct((2, 256, 512), bf16),
            jax.ShapeDtypeStruct((256, 1536), f32),
            jax.ShapeDtypeStruct((2, 64, 16, 256), bf16),
            jax.ShapeDtypeStruct((2, 64, 16, 128), bf16),
        ),
        in_specs=[smem] + [vmem] * 5 + [hbm] * 6,
        out_specs=(hbm,) * 14,
        scratch_shapes=[
            pltpu.VMEM((6, 64, 16, 384), bf16),
            pltpu.VMEM((6, 63, 16, 384), bf16),
            pltpu.VMEM((6, 64, 16, 384), bf16),
            pltpu.VMEM((6, 63, 16, 384), bf16),
            pltpu.VMEM((6, 64, 48, 128), bf16),
            pltpu.VMEM((6, 63, 48, 128), bf16),
            pltpu.VMEM((512, 1024), bf16),
            pltpu.VMEM((512, 1024), bf16),
            pltpu.VMEM((256, 1024), bf16),
            pltpu.VMEM((2, 256, 1024), bf16),
            pltpu.VMEM((256, 1024), f32),
            pltpu.VMEM((256, 1024), f32),
            pltpu.VMEM((256, 128), f32),
            pltpu.VMEM((256, 128), f32),
            pltpu.VMEM((2, 2, 1024), f32),
            pltpu.VMEM((2, 8, 128, 128), bf16),
            pltpu.VMEM((2, 8, 128, 128), bf16),
            pltpu.VMEM((256, 1024), bf16),
            pltpu.VMEM((256, 512), bf16),
            pltpu.VMEM((2, 256, 512), bf16),
            pltpu.VMEM((2, 12, 8, 384), f32),
            pltpu.VMEM((12, 8, 384), f32),
            pltpu.VMEM((144, 256), f32),
            pltpu.VMEM((4, 40, 256), f32),
            pltpu.VMEM((4, 40, 256), f32),
            pltpu.VMEM((2, 6, 8, 256), f32),
            pltpu.VMEM((6, 8, 256), f32),
            pltpu.VMEM((8, 24, 128), f32),
            pltpu.VMEM((7, 24, 128), f32),
            pltpu.VMEM((8, 9216), f32),
            pltpu.VMEM((36, 1024), f32),
            pltpu.VMEM((8, 2048), f32),
            pltpu.VMEM((8, 1024), f32),
            dma((9,)),
            dma((10,)),
            dma((5,)),
            dma((10,)),
            dma((10,)),
            dma((2,)),
            dma((6, 6)),
            dma((2,)),
            dma((6, 6)),
            dma((2,)),
            dma((6, 6)),
            dma((2,)),
            dma((6, 4)),
            dma((2,)),
            dma((2,)),
            dma((2,)),
            dma((2,)),
            dma((2,)),
            dma((2,)),
            dma((2,)),
            dma((2,)),
            dma((2,)),
            dma((2,)),
            dma,
            dma((7,)),
            pltpu.SemaphoreType.REGULAR,
        ],
        compiler_params=pltpu.CompilerParams(
            collective_id=0, has_side_effects=True, vmem_limit_bytes=VMEM_LIMIT
        ),
        name="transformer_block",
    )(bounds, *arrays)


def finish_kernel(*refs):
    arrays, vec = refs[:6], refs[6]
    targets, (gain_a, gain_f, gain_qk) = refs[7:13], refs[13:16]
    passing, (in_sems, out_sems) = refs[16:22], refs[22:]
    pieces = [
        (source, held, target, pl.ds(first, min(64, source.shape[0])))
        for source, held, target in zip(arrays, passing, targets, strict=True)
        for first in range(0, source.shape[0], 64)
    ]
    reads = [
        pltpu.make_async_copy(source.at[rows], held.at[rows], in_sems.at[i])
        for i, (source, held, _, rows) in enumerate(pieces)
    ]
    writes = [
        pltpu.make_async_copy(held.at[rows], target.at[rows], out_sems.at[i])
        for i, (_, held, target, rows) in enumerate(pieces)
    ]
    for read in reads:
        read.start()
    own = lax.axis_index("rows") * 8 + lax.axis_index("ctx")
    row = lax.div(own, 16)
    at = lax.rem(own, 16)
    lane = lax.broadcasted_iota(jnp.int32, (8, 128), 1)
    tile = lax.broadcasted_iota(jnp.int32, (8, 128), 0)

    def pick(values, of_row, of_lane, count):
        kept = jnp.sum(jnp.where(tile == of_row, values, 0.0), axis=0, keepdims=True)
        place = lax.broadcasted_iota(jnp.int32, (128, count), 0)
        order = lax.broadcasted_iota(jnp.int32, (128, count), 1)
        rows = jnp.broadcast_to(kept, (8, 128)).T[:, :count]
        return jnp.sum(jnp.where(place == of_lane + order, rows, 0.0), axis=0, keepdims=True)

    gain_a[...] = pick(vec[pl.ds(0, 8), :], row, 8 * at, 8)
    gain_f[...] = pick(vec[pl.ds(8, 8), :], row, 8 * at, 8)
    gain_qk[...] = pick(vec[pl.ds(16, 8), :], 0, own, 1)
    for read, write in zip(reads, writes, strict=True):
        read.wait()
        write.start()
    for write in writes:
        write.wait()


def finish(out, gtok, ggu, gdn, gqkv, gout, vec):
    vmem = pl.BlockSpec(memory_space=pltpu.VMEM)
    hbm = pl.BlockSpec(memory_space=pl.ANY)
    same = [jax.ShapeDtypeStruct(a.shape, a.dtype) for a in (out, gtok, ggu, gdn, gqkv, gout)]
    return pl.pallas_call(
        finish_kernel,
        out_shape=(
            *same,
            jax.ShapeDtypeStruct((1, 8), f32),
            jax.ShapeDtypeStruct((1, 8), f32),
            jax.ShapeDtypeStruct((1, 1), f32),
        ),
        in_specs=[hbm] * 6 + [vmem],
        out_specs=(hbm,) * 6 + (vmem,) * 3,
        scratch_shapes=[pltpu.VMEM(a.shape, a.dtype) for a in same]
        + [pltpu.SemaphoreType.DMA((12,)), pltpu.SemaphoreType.DMA((12,))],
        name="results",
    )(out, gtok, ggu, gdn, gqkv, gout, vec)


def local(
    tokens,
    cotangent,
    bounds,
    positions,
    norm_gain_attn,
    w_qkv,
    qk_gain,
    w_out,
    norm_gain_ffn,
    w_gate_up,
    w_down,
):
    lane = np.arange(128) % 32
    freqs = (rope_theta ** (-2.0 * lane / 64)).astype(np.float32)[None]
    results = block(
        bounds,
        positions,
        freqs,
        norm_gain_attn[None],
        norm_gain_ffn[None],
        qk_gain[None],
        tokens.reshape(256, 1024),
        cotangent.reshape(256, 1024),
        w_gate_up,
        w_down,
        w_qkv,
        w_out,
    )
    layer_out, grad_tokens, sum_gate_up, sum_down, sum_qkv, sum_out, gain_a, gain_f, gain_qk = (
        finish(*results[:7])
    )
    return (
        layer_out.reshape(tokens.shape),
        grad_tokens.reshape(tokens.shape),
        gain_a.reshape(8),
        sum_qkv,
        gain_qk.reshape(1),
        sum_out,
        gain_f.reshape(8),
        sum_gate_up,
        sum_down,
    )


def solution(mesh):
    placed = (
        P(None, "rows", "ctx", None),
        P(None, "rows", "ctx", None),
        P(None, "rows", None),
        P(None, "rows", "ctx"),
        P(),
        P(),
        P(),
        P(),
        P(),
        P(),
        P(),
    )
    return jax.shard_map(
        local,
        mesh=mesh,
        in_specs=placed,
        out_specs=(
            P(None, "rows", "ctx", None),
            P(None, "rows", "ctx", None),
            P(("rows", "ctx")),
            P(("rows", "ctx"), None),
            P(("rows", "ctx")),
            P(("rows", "ctx"), None),
            P(("rows", "ctx")),
            P(("rows", "ctx"), None),
            P(("rows", "ctx"), None),
        ),
        check_vma=False,
    )
```

```python
import functools

import jax
import jax.numpy as jnp
import numpy as np
from jax import lax
from jax.experimental import pallas as pl
from jax.experimental.pallas import tpu as pltpu
from jax.sharding import PartitionSpec as P

MESH = pl.DeviceIdType.MESH
norm_eps = 1e-05
rope_theta = 1000000.0
f32 = jnp.float32
bf16 = jnp.bfloat16
VMEM_LIMIT = 64 * 2**20 - 2**18


class Place:
    def __init__(self):
        r = lax.axis_index("rows")
        k = lax.axis_index("ctx")
        self.x_hi = lax.div(r, 8)
        self.y = lax.rem(lax.div(r, 2), 4)
        self.core = lax.rem(r, 2)
        self.x_lo = lax.div(k, 4)
        self.z = lax.rem(k, 4)
        self.rows = r
        self.ctx = k
        self.bits = [
            self.x_hi,
            lax.rem(self.x_hi + self.x_lo, 2),
            lax.div(self.y, 2),
            lax.rem(lax.div(self.y, 2) + lax.rem(self.y, 2), 2),
            lax.div(self.z, 2),
            lax.rem(lax.div(self.z, 2) + lax.rem(self.z, 2), 2),
        ]

    def at(self, x_hi=None, x_lo=None, y=None, z=None, core=None):
        x_hi = self.x_hi if x_hi is None else x_hi
        x_lo = self.x_lo if x_lo is None else x_lo
        y = self.y if y is None else y
        z = self.z if z is None else z
        core = self.core if core is None else core
        return (x_hi * 8 + y * 2 + core, x_lo * 4 + z)

    def partner(self):
        return self.at(core=1 - self.core)

    def neighbour(self, dim):
        if dim == 0:
            return self.at(x_hi=1 - self.x_hi, x_lo=1 - self.x_lo)
        if dim == 1:
            return self.at(x_lo=1 - self.x_lo)
        if dim == 2:
            return self.at(y=3 - self.y)
        if dim == 3:
            return self.at(y=self.y + 1 - 2 * lax.rem(self.y, 2))
        if dim == 4:
            return self.at(z=3 - self.z)
        return self.at(z=self.z + 1 - 2 * lax.rem(self.z, 2))


    def flipped(self, dims):
        if len(dims) == 1:
            return self.neighbour(dims[0])
        if 0 in dims:
            return self.at(x_hi=1 - self.x_hi)
        if 2 in dims:
            return self.at(y=lax.rem(self.y + 2, 4))
        return self.at(z=lax.rem(self.z + 2, 4))


def gray(v):
    return v ^ (v >> 1)


def chip_number(x_hi, x_lo, y, z):
    return gray(2 * x_hi + x_lo) * 16 + gray(y) * 4 + gray(z)


def slot_of(number, order):
    return sum(((number >> (5 - dim)) & 1) << (5 - t) for t, dim in enumerate(order))


ONES = (1, 1, 1, 1, 1, 1)
FLIPS = {1: ((1,),), 2: ((0, 1), (1, 0), (1, 1))}


class Scatter:
    def __init__(self, place, orders, shape, first, held, send_sems, recv_sems):
        self.place = place
        self.orders = orders
        self.first, self.first_cols = first
        self.held, self.held_cols = held
        self.send_sems = send_sems
        self.recv_sems = recv_sems
        self.stages = []
        at, slots, base = 0, 64, 0
        for width in shape:
            size = slots >> width
            self.stages.append((at, width, size, base))
            base += size * len(FLIPS[width])
            at += width
            slots = size

    def source(self, k):
        if k == 0:
            return self.first, 0, self.first_cols
        return self.held, self.stages[k - 1][3], self.held_cols

    def part(self, s, k, flips):
        at, width, size, _ = self.stages[k]
        which = 0
        for dim, flip in zip(self.orders[s][at : at + width], flips, strict=True):
            bit = self.place.bits[dim]
            which = 2 * which + (1 - bit if flip else bit)
        return which * size

    def copies(self, s, k):
        at, width, size, base = self.stages[k]
        ref, start, cols = self.source(k)
        dims = self.orders[s][at : at + width]
        return [
            pltpu.make_async_remote_copy(
                src_ref=ref.at[s, pl.ds(start + self.part(s, k, flips), size), :, cols],
                dst_ref=self.held.at[s, pl.ds(base + i * size, size), :, self.held_cols],
                send_sem=self.send_sems.at[min(k, 1)],
                recv_sem=self.recv_sems.at[s, k],
                device_id=self.place.flipped([d for d, f in zip(dims, flips, strict=True) if f]),
                device_id_type=MESH,
            )
            for i, flips in enumerate(FLIPS[width])
        ]

    def send(self, s, k):
        for copy in self.copies(s, k):
            copy.start()

    def arrived(self, s, k):
        _, width, size, base = self.stages[k]
        place = self.held.at[s, pl.ds(base, size * len(FLIPS[width])), :, self.held_cols]
        self.wait(place, 0, self.recv_sems.at[s, k]).wait_recv()
        ref, start, cols = self.source(k)
        own = start + self.part(s, k, (0,) * width)

        def total(at):
            value = ref[s, own + at, :, cols].astype(f32)
            for i in range(len(FLIPS[width])):
                value = value + self.held[s, base + i * size + at, :, self.held_cols].astype(f32)
            return value

        return total, size, base

    def take(self, s, k):
        total, size, base = self.arrived(s, k)
        ref, start, cols = self.source(k)
        own = start + self.part(s, k, (0,) * self.stages[k][1])
        per = min(16, size)

        def body(i, carry):
            for j in range(per):
                at = i * per + j
                if self.stages[k][1] == 1:
                    value = ref[s, own + at, :, cols] + self.held[s, base + at, :, self.held_cols]
                else:
                    value = total(at).astype(bf16)
                self.held[s, base + at, :, self.held_cols] = value
            return carry

        lax.fori_loop(0, size // per, body, 0)
        self.send(s, k + 1)

    def last(self, s):
        return self.arrived(s, len(self.stages) - 1)[0](0)

    def wait(self, ref, part, recv_sem):
        return push(
            self.place, ref, ref, self.send_sems.at[part], recv_sem, self.place.partner()
        )

    def sent(self, part):
        slots = pl.ds(0, 32) if part == 0 else pl.ds(32, 31)
        self.wait(
            self.held.at[:, slots, :, self.held_cols], part, self.recv_sems.at[0, 0]
        ).wait_send()


def greet_signal(place, devices):
    barrier = pltpu.get_barrier_semaphore()
    targets = down_targets(place)
    for device in devices + targets[1:]:
        pl.semaphore_signal(barrier, inc=1, device_id=device, device_id_type=MESH)

    @pl.when(place.x_hi != place.core)
    def _():
        pl.semaphore_signal(barrier, inc=1, device_id=targets[0], device_id_type=MESH)


def greet_wait(place, devices):
    barrier = pltpu.get_barrier_semaphore()
    count = len(devices) + 3

    @pl.when(place.x_hi != place.core)
    def _():
        pl.semaphore_wait(barrier, count + 1)

    @pl.when(place.x_hi == place.core)
    def _():
        pl.semaphore_wait(barrier, count)


def push(place, src, dst, send_sem, recv_sem, device):
    return pltpu.make_async_remote_copy(
        src_ref=src,
        dst_ref=dst,
        send_sem=send_sem,
        recv_sem=recv_sem,
        device_id=device,
        device_id_type=MESH,
    )


def down_targets(place):
    return [
        place.at(x_hi=place.core, core=place.x_hi, z=lax.rem(place.z + off, 4)) for off in range(4)
    ]


def dot(left, right):
    return jnp.dot(left, right, preferred_element_type=f32)


def dot_cols(left, right):
    return lax.dot_general(left, right, (((1,), (1,)), ((), ())), preferred_element_type=f32)


FF_HALF = 2304
DOWN_ORDERS = (
    (0, 3, 5, 2, 1, 4),
    (3, 5, 4, 2, 0, 1),
    (2, 3, 0, 4, 1, 5),
    (4, 2, 0, 1, 3, 5),
    (5, 2, 3, 4, 0, 1),
    (0, 3, 4, 1, 5, 2),
)
GATE_ORDERS = (
    (5, 2, 1, 3, 4, 0),
    (4, 0, 3, 5, 1, 2),
    (2, 1, 4, 3, 0, 5),
    (0, 3, 2, 5, 4, 1),
    (4, 0, 2, 3, 5, 1),
    (5, 3, 0, 2, 1, 4),
)
UP_ORDERS = (
    (2, 3, 1, 4, 0, 5),
    (3, 4, 5, 0, 2, 1),
    (0, 2, 5, 4, 3, 1),
    (1, 0, 2, 3, 5, 4),
    (1, 2, 5, 0, 4, 3),
    (3, 1, 2, 0, 4, 5),
)
QUAD_ORDERS = (
    (2, 3, 1, 0, 4, 5),
    (1, 0, 5, 4, 2, 3),
    (3, 2, 1, 0, 5, 4),
    (5, 4, 3, 2, 1, 0),
    (4, 5, 2, 3, 0, 1),
    (1, 0, 5, 4, 2, 3),
)
QUAD_STAGES = (1, 1, 2, 2)
LINKED = ((0,), (1,), (2,), (3,), (4,), (5,), (0, 1), (2, 3), (4, 5))
STEPS = (
    "Bmm0", "Amm0", "Bmm1", "Bmm2", "Amm2", "Amm1", "dn", "B00", "down", "lo",
    "B20", "A20", "A00", "A10", "B30", "datt", "B50", "A40", "B10", "B40",
    "A30", "D40", "D10", "out", "A21", "B01", "A50", "split", "D20", "B21",
    "heads", "A31", "nat", "D00", "B51", "B11", "free", "D11", "A11", "D21",
    "D30", "A01", "A22", "D50", "B41", "D41", "B02", "B22", "A51", "B31",
    "Qmm4", "B52", "Qmm5", "A12", "D01", "A32", "headb", "A41", "lastnorm", "A02",
    "D12", "B03", "B12", "D31", "D51", "B23", "B32", "Qmm0", "Qmm1", "Qmm3",
    "Qmm2", "D42", "B53", "A13", "v0", "D13", "B24", "A42", "A23", "A52",
    "B42", "Q50", "A33", "B13", "A03", "D02", "B04", "D22", "D32", "D14",
    "Q40", "A24", "D52", "B33", "B43", "D43", "Q00", "B54", "Q10", "Q30",
    "v1", "Q20", "A53", "A34", "Q51", "B14", "A04", "D23", "D33", "D03",
    "A43", "D53", "v2", "Q41", "B44", "A54", "Q01", "B34", "Q11", "A14",
    "Q31", "Q21", "D04", "D34", "v3", "Q52", "D54", "D24", "A44", "D44",
    "Q42", "Q02", "Q12", "Q32", "Q22", "v4", "Afin", "Dfin", "Qfin", "v5",
    "end",
)


class DownOwners:
    def __init__(self, place, stage, into, send_sems, recv_sems):
        self.swapped = place.x_hi != place.core
        self.place = place
        self.stage = stage
        self.into = into
        targets = down_targets(place)
        self.moves = [
            push(
                place,
                stage.at[lax.rem(place.z + off, 4)],
                into.at[place.z],
                send_sems.at[min(off, 1)],
                recv_sems.at[min(off, 1)],
                targets[off],
            )
            for off in range(4)
        ]
        three = into.at[pl.ds(0, 3)]
        self.others = push(place, three, three, send_sems.at[1], recv_sems.at[1], targets[1])

    def send(self, down, acc):
        for s in range(6):
            acc[pl.ds(48 * (s // 2), 48), pl.ds(128 * (s % 2), 128)] = down.last(s)
        for z in range(4):
            self.stage[z, pl.ds(0, 36), :] = acc[pl.ds(36 * z, 36), :]
            self.stage[z, pl.ds(36, 4), :] = jnp.zeros((4, 256), f32)
        for move in self.moves[1:]:
            move.start()

        @pl.when(self.swapped)
        def _():
            self.moves[0].start()

        @pl.when(jnp.logical_not(self.swapped))
        def _():
            self.into[self.place.z] = self.stage[self.place.z]

    def arrived(self, out):
        @pl.when(self.swapped)
        def _():
            self.moves[0].wait_recv()

        self.others.wait_recv()
        for z in range(4):
            out[:, pl.ds(256 * z, 256)] = self.into[z, pl.ds(0, 36), :]

    def sent(self):
        self.others.wait_send()

        @pl.when(self.swapped)
        def _():
            self.moves[0].wait_send()


def lanes(rows):
    return lax.broadcasted_iota(jnp.int32, (rows, 128), 1)


def turn_heads(values):
    low = lax.rem(lanes(values.shape[0]), 64) < 32
    return jnp.where(low, pltpu.roll(values, 96, 1), pltpu.roll(values, 32, 1))


def head_mean(values):
    i = lax.broadcasted_iota(jnp.int32, (128, 128), 0)
    j = lax.broadcasted_iota(jnp.int32, (128, 128), 1)
    ones = jnp.where(lax.div(i, 64) == lax.div(j, 64), 1.0 / 64, 0.0).astype(bf16)
    high = values.astype(bf16)
    rest = (values - high.astype(f32)).astype(bf16)
    return dot(high, ones) + dot(rest, ones)


def gain_tiles(qk_gain):
    swapped = pltpu.roll(qk_gain, 64, 1)
    low = lax.broadcasted_iota(jnp.int32, (1, 128), 1) < 64
    return jnp.where(low, qk_gain, swapped), jnp.where(low, swapped, qk_gain)


def head_rows(values):
    low = lanes(values.shape[0]) < 64
    zero = jnp.zeros_like(values)
    return jnp.concatenate([jnp.where(low, values, zero), jnp.where(low, zero, values)], 0)


class Exchange:
    def __init__(self, place, out_at, into_at, seven, send_sems, recv_sems):
        self.place = place
        self.seven = seven
        self.out_at = out_at
        self.into_at = into_at
        self.send_sems = send_sems
        self.recv_sems = recv_sems

    def copy(self, m, off):
        j = lax.rem(self.place.ctx + off, 8)
        return push(
            self.place,
            self.out_at(m, j),
            self.into_at(m, self.place.ctx),
            self.send_sems.at[m],
            self.recv_sems.at[m],
            (self.place.rows, j),
        )

    def send(self, m):
        for off in range(1, 8):
            self.copy(m, off).start()
        self.keep(m)

    def keep(self, m):
        self.into_at(m, self.place.ctx)[...] = self.out_at(m, self.place.ctx)[...]

    def all_seven(self, m):
        ref = self.seven(m)
        return push(
            self.place, ref, ref, self.send_sems.at[m], self.recv_sems.at[m], self.place.partner()
        )

    def arrived(self, m):
        self.all_seven(m).wait_recv()

    def sent(self):
        for m in range(2):
            self.all_seven(m).wait_send()


def ctx_peers(place):
    return [(place.rows, lax.rem(place.ctx + off, 8)) for off in range(1, 8)]


def document_edges(bounds_ref, m):
    index = lax.broadcasted_iota(jnp.int32, (1, 1024), 1)
    start = jnp.zeros((1, 1024), jnp.int32)
    end = jnp.full((1, 1024), 1024, jnp.int32)
    for k in range(1, 4):
        cut = bounds_ref[m, 0, k]
        start = jnp.where(index >= cut, cut, start)
        end = jnp.where(index < bounds_ref[m, 0, 4 - k], bounds_ref[m, 0, 4 - k], end)
    return start, end


def reorder_store(part, first, s, order, x_hi, at, width):
    part = part.reshape(4, 2, 8, 8, width)
    for y in range(4):
        for x_lo in range(2):
            for z in range(4):
                slot = slot_of(chip_number(x_hi, x_lo, y, z), order)
                first[s, slot, :, at] = part[y, :, 4 * x_lo + z].reshape(16, width).astype(bf16)


def block_kernel(
    bounds_ref,
    pos_ref,
    freq_ref,
    gain_ref,
    gain_ffn_ref,
    qk_gain_ref,
    x_hbm,
    cot_hbm,
    wgu_hbm,
    wd_hbm,
    w_qkv_hbm,
    w_out_hbm,
    out_hbm,
    gtok_hbm,
    ggu_hbm,
    gdn_hbm,
    gqkv_hbm,
    gout_hbm,
    vec_hbm,
    na_hbm,
    na_other_hbm,
    att_hbm,
    att_other_hbm,
    proj_hbm,
    qkv_hbm,
    o_hbm,
    a_first,
    a_held,
    b_first,
    b_held,
    d_first,
    d_held,
    nf,
    dyb,
    sum_send,
    sum_recv,
    mid_ref,
    dmid,
    cos_ref,
    sin_ref,
    l_ref,
    do_out,
    do_in,
    dpin,
    dmin,
    dm_own,
    g_fin,
    g_in,
    d_acc,
    d_stage,
    d_in,
    q_fin,
    q_in,
    vec,
    vec_in,
    ggu_ref,
    gdn_ref,
    gqkv_ref,
    gout_ref,
    w_sems,
    l_sems,
    r_sems,
    x_send,
    x_recv,
    a_send,
    a_recv,
    b_send,
    b_recv,
    d_send,
    d_recv,
    q_send,
    q_recv,
    f_send,
    f_recv,
    k_send,
    k_recv,
    e_send,
    e_recv,
    do_send,
    do_recv,
    t_send,
    t_recv,
    v_send,
    v_recv,
    free_sem,
):
    place = Place()
    core = place.core
    partner = place.partner()
    every = slice(None)
    down = Scatter(place, DOWN_ORDERS, ONES, (d_first, every), (d_held, every), d_send, d_recv)
    gate = Scatter(place, GATE_ORDERS, ONES, (a_first, every), (a_held, every), a_send, a_recv)
    up = Scatter(place, UP_ORDERS, ONES, (b_first, every), (b_held, every), b_send, b_recv)
    narrow = pl.ds(0, 256)
    quad = Scatter(
        place, QUAD_ORDERS, QUAD_STAGES, (a_first, narrow), (b_first, narrow), q_send, q_recv
    )
    sums = {"D": down, "A": gate, "B": up, "Q": quad}
    steps = iter(STEPS)

    def run(ops, until):
        for name in steps:
            if name == until:
                return
            if name in ops:
                ops[name]()
            else:
                sums[name[0]].take(int(name[1]), int(name[2]))
    def t_at(m, j):
        return nf.at[
            pl.ds(pl.multiple_of(256 * m + 128 * lax.div(j, 4), 128), 128),
            pl.ds(pl.multiple_of(256 * lax.rem(j, 4), 256), 256),
        ]

    def tiles(ref, s, j, width):
        return ref.at[s, pl.ds(pl.multiple_of(8 * j, 8), 8), :, pl.ds(0, width)]

    heads_out = Exchange(
        place,
        lambda m, j: tiles(a_first, m, j, 256),
        lambda m, j: tiles(b_first, m, j, 256),
        lambda m: b_first.at[m, pl.ds(0, 56), :, pl.ds(0, 256)],
        k_send,
        k_recv,
    )
    heads_back = Exchange(
        place,
        lambda m, j: tiles(b_first, 4 + m, j, 128),
        lambda m, j: tiles(b_first, 2 + m, j, 128),
        lambda m: b_first.at[2 + m, pl.ds(0, 56), :, pl.ds(0, 128)],
        e_send,
        e_recv,
    )
    grads_out = Exchange(
        place,
        lambda m, j: do_out.at[m, j],
        lambda m, j: do_in.at[m, j],
        lambda m: do_in.at[m, pl.ds(0, 7)],
        do_send,
        do_recv,
    )
    own_rows = pl.ds(0, 256)
    other_rows = pl.ds(256, 256)
    to_dy = push(place, cot_hbm, dyb.at[other_rows], x_send.at[0], x_recv.at[0], partner)
    to_nf = push(place, nf.at[own_rows], nf.at[other_rows], x_send.at[1], x_recv.at[1], partner)
    to_out = push(place, sum_send, sum_recv.at[0], x_send.at[2], x_recv.at[2], partner)
    to_back = push(place, sum_send, sum_recv.at[1], x_send.at[3], x_recv.at[3], partner)
    to_att = push(place, dm_own, att_other_hbm, x_send.at[5], x_recv.at[5], partner)
    att_copy = pltpu.make_async_copy(dm_own, att_hbm, l_sems.at[7])
    qkv_copy = pltpu.make_async_copy(
        b_first.at[pl.ds(0, 2), :, :, pl.ds(0, 256)], qkv_hbm, l_sems.at[8]
    )
    o_copy = pltpu.make_async_copy(
        b_first.at[pl.ds(4, 2), :, :, pl.ds(0, 128)], o_hbm, l_sems.at[9]
    )
    cot_load = pltpu.make_async_copy(cot_hbm, dyb.at[own_rows], l_sems.at[1])
    low = lanes(256) < 64
    gain_q, gain_k = gain_tiles(qk_gain_ref[...])

    def attend(w_qkv, x_ref, na, proj_ref, q2, kk, vo):
        x_load = pltpu.make_async_copy(x_hbm, x_ref, l_sems.at[2])
        w_loads = [
            pltpu.make_async_copy(w_qkv_hbm.at[:, cols], w_qkv.at[:, cols], sem)
            for cols, sem in (
                (pl.ds(1024, 1024), l_sems.at[3]),
                (pl.ds(0, 1024), l_sems.at[6]),
            )
        ]
        na_copy = pltpu.make_async_copy(na, na_hbm, l_sems.at[4])
        proj_copy = pltpu.make_async_copy(proj_ref, proj_hbm, l_sems.at[5])
        for load in (x_load, *w_loads, cot_load):
            load.start()
        peers = [partner] + [place.flipped(dims) for dims in LINKED] + ctx_peers(place)
        greet_signal(place, peers)
        columns = jnp.concatenate(
            [pos_ref[0].astype(f32), pos_ref[1].astype(f32), jnp.zeros((6, 128), f32)], 0
        ).T
        sign = jnp.where(lax.rem(lanes(128), 64) < 32, -1.0, 1.0)
        for m in range(2):
            angle = columns[:, m : m + 1] * freq_ref[...]
            cos_ref[pl.ds(128 * m, 128), :] = jnp.cos(angle)
            sin_ref[pl.ds(128 * m, 128), :] = jnp.sin(angle) * sign
        x_load.wait()
        inputs = x_ref[...].astype(f32)
        scale = lax.rsqrt(jnp.mean(inputs * inputs, axis=-1, keepdims=True) + norm_eps)
        na[...] = (inputs * scale * gain_ref[...]).astype(bf16)
        to_na = push(place, na, na_other_hbm, x_send.at[4], x_recv.at[4], partner)
        na_copy.start()
        w_loads[0].wait()

        def turned(tile, gain):
            u = tile * lax.rsqrt(head_mean(tile * tile) + norm_eps) * gain
            return u * cos_ref[...] + turn_heads(u) * sin_ref[...]

        def store(at, j, tile):
            for m in range(2):
                rows = tile[128 * m : 128 * m + 128].astype(bf16)
                a_first[m, pl.ds(8 * j, 8), :, pl.ds(at, 128)] = rows.reshape(8, 16, 128)

        for i in range(2):
            key_pair = dot(na[...], w_qkv[:, pl.ds(1024 + 256 * i, 256)])
            value_pair = dot(na[...], w_qkv[:, pl.ds(1536 + 256 * i, 256)])
            proj_ref[:, pl.ds(1024 + 256 * i, 256)] = key_pair
            for j in range(2):
                key = turned(key_pair[:, 128 * j : 128 * j + 128], gain_k)
                value = value_pair[:, 128 * j : 128 * j + 128]
                store(128, 4 * i + 2 * j, jnp.where(low, key, pltpu.roll(value, 64, 1)))
                store(128, 4 * i + 2 * j + 1, jnp.where(low, pltpu.roll(key, 64, 1), value))
        greet_wait(place, peers)
        to_dy.start()

        w_loads[1].wait()
        for i in range(4):
            p = lax.rem(lax.div(place.ctx, 2) + 1 + i, 4)
            at = pl.ds(pl.multiple_of(256 * p, 256), 256)
            pair = dot(na[...], w_qkv[:, at])
            proj_ref[:, at] = pair
            for j in range(2):
                store(0, 2 * p + j, turned(pair[:, 128 * j : 128 * j + 128], gain_q) * 0.125)
            for j in range(2):
                off = lax.rem(2 * p + j + 8 - place.ctx, 8)

                @pl.when(off > 0)
                def _(off=off):
                    heads_out.copy(0, off).start()

        heads_out.keep(0)
        heads_out.send(1)
        to_na.start()
        proj_copy.start()

        def heads(m, carry):
            heads_out.arrived(m)
            ends = document_edges(bounds_ref, m)[1]
            for b in range(4):
                query = b_first[m, pl.ds(16 * b, 16), :, pl.ds(0, 128)].reshape(256, 128)
                pair = b_first[m, pl.ds(16 * b, 16), :, pl.ds(128, 128)].reshape(256, 128)
                pair = pair.astype(f32)
                swapped = pltpu.roll(pair, 64, 1)
                q2[b] = head_rows(query)
                kk[b] = jnp.where(low, pair, swapped).astype(bf16)
                vo[b] = jnp.where(low, swapped, 1.0).astype(bf16)
            for qb in range(4):
                acc = jnp.zeros((512, 128), f32)
                for kb in range(qb + 1):
                    scores = dot_cols(q2[qb], kk[kb])
                    t = 256 * qb + lax.rem(lax.broadcasted_iota(jnp.int32, (512, 256), 0), 256)
                    keep = t < ends[:, 256 * kb : 256 * kb + 256]
                    if kb == qb:
                        s = 256 * kb + lax.broadcasted_iota(jnp.int32, (512, 256), 1)
                        keep = keep & (s <= t)
                    weights = jnp.where(keep, jnp.exp(scores), 0.0).astype(bf16)
                    acc = acc + dot(weights, vo[kb])
                total = pltpu.roll(acc, 64, 1)
                head0 = acc[:256]
                head1 = pltpu.roll(acc[256:], 64, 1)
                denominator = jnp.where(low, total[:256], acc[256:])
                out = jnp.where(low, head0, head1) / denominator
                log_total = jnp.log(denominator).T
                l_ref[m, pl.ds(0, 1), pl.ds(256 * qb, 256)] = log_total[0:1]
                l_ref[m, pl.ds(1, 1), pl.ds(256 * qb, 256)] = log_total[64:65]
                b_first[4 + m, pl.ds(16 * qb, 16), :, pl.ds(0, 128)] = out.astype(bf16).reshape(
                    16, 16, 128
                )
            heads_back.send(m)
            return carry

        lax.fori_loop(0, 2, heads, 0)
        qkv_copy.start()
        o_copy.start()
        na_copy.wait()
        proj_copy.wait()
        to_na.wait()

    pl.run_scoped(
        attend,
        pltpu.VMEM((1024, 2048), bf16),
        pltpu.VMEM((256, 1024), bf16),
        pltpu.VMEM((256, 1024), bf16),
        pltpu.VMEM((256, 1536), f32),
        pltpu.VMEM((4, 512, 128), bf16),
        pltpu.VMEM((4, 256, 128), bf16),
        pltpu.VMEM((4, 256, 128), bf16),
    )

    to_dm = push(place, dm_own.at[1 - core], dmin, x_send.at[6], x_recv.at[6], partner)
    out_copy = pltpu.make_async_copy(sum_send, out_hbm, l_sems.at[0])

    def feed_forward(wgu, wd, nft, h, ht, dgu, sum_own):
        def unit_loads(i):
            at = pl.multiple_of(core * FF_HALF + 768 * i, 256)
            up_at = pl.multiple_of(4608 + core * FF_HALF + 768 * i, 256)
            here = pl.ds(pl.multiple_of(768 * i, 256), 768)
            up_here = pl.ds(pl.multiple_of(FF_HALF + 768 * i, 256), 768)
            return [
                pltpu.make_async_copy(
                    wgu_hbm.at[:, pl.ds(at, 768)], wgu.at[:, here], w_sems.at[3 * i]
                ),
                pltpu.make_async_copy(
                    wgu_hbm.at[:, pl.ds(up_at, 768)], wgu.at[:, up_here], w_sems.at[3 * i + 1]
                ),
                pltpu.make_async_copy(
                    wd_hbm.at[pl.ds(at, 768)], wd.at[here], w_sems.at[3 * i + 2]
                ),
            ]

        w_out_loads = [
            pltpu.make_async_copy(
                w_out_hbm.at[pl.ds(512 * i, 512)], dgu.at[:, pl.ds(1024 * i, 1024)], l_sems.at[2 + i]
            )
            for i in range(2)
        ]
        x_load = pltpu.make_async_copy(x_hbm, sum_send, l_sems.at[4])
        for load in (x_load, *w_out_loads):
            load.start()
        for i in range(3):
            for copy in unit_loads(i):
                copy.start()
        for m in range(2):
            heads_back.arrived(m)
            for j in range(8):
                tile = b_first[2 + m, pl.ds(8 * j, 8), :, pl.ds(0, 128)].reshape(128, 128)
                dm_own[j // 4, pl.ds(128 * m, 128), pl.ds(128 * (j % 4), 128)] = tile
        to_att.start()
        att_copy.start()
        for load in (x_load, *w_out_loads):
            load.wait()
        mid = sum_send[...].astype(f32) + (
            dot(dm_own[0], dgu[:, pl.ds(0, 1024)]) + dot(dm_own[1], dgu[:, pl.ds(1024, 1024)])
        )
        mid_ref[...] = mid
        scale = lax.rsqrt(jnp.mean(mid * mid, axis=-1, keepdims=True) + norm_eps)
        nf[own_rows, :] = (mid * scale * gain_ffn_ref[...]).astype(bf16)
        to_nf.start()
        nft[:, own_rows] = nf[own_rows, :].T
        heads_out.sent()
        heads_back.sent()
        qkv_copy.wait()
        o_copy.wait()
        cot_load.wait()

        def token_half(half, carry):
            rows = pl.ds(pl.multiple_of(256 * half, 256), 256)

            @pl.when(half == 1)
            def _():
                to_dy.wait_recv()
                to_nf.wait_recv()

            def units(i, inner):
                @pl.when(half == 0)
                def _():
                    for copy in unit_loads(i):
                        copy.wait()

                cols = pl.ds(pl.multiple_of(768 * i, 256), 768)
                up_cols = pl.ds(pl.multiple_of(FF_HALF + 768 * i, 256), 768)
                gated = dot(nf[rows, :], wgu[:, cols])
                upward = dot(nf[rows, :], wgu[:, up_cols])
                grad_hidden = dot_cols(dyb[rows, :], wd[cols, :])
                sigma = 1.0 / (1.0 + jnp.exp(-gated))
                silu = gated * sigma
                h[rows, cols] = (silu * upward).astype(bf16)
                dgu[rows, cols] = (grad_hidden * upward * (sigma + silu * (1.0 - sigma))).astype(
                    bf16
                )
                dgu[rows, up_cols] = (grad_hidden * silu).astype(bf16)
                return inner

            return lax.fori_loop(0, 3, units, carry)

        lax.fori_loop(0, 2, token_half, 0)
        nft[:, other_rows] = nf[other_rows, :].T

        def down_grads():
            for block in range(3):
                ht[...] = h[:, pl.ds(768 * block, 768)].T
                for z in range(4):
                    part = dot(ht[...], dyb[:, pl.ds(256 * z, 256)])
                    for i in range(16):
                        q = 16 * block + i
                        y, core_to, x_lo, rg = q // 12, (q // 6) % 2, (q // 3) % 2, q % 3
                        for ch in range(2):
                            s = 2 * rg + ch
                            slot = slot_of(chip_number(core_to, x_lo, y, z), DOWN_ORDERS[s])
                            d_first[s, slot] = part[
                                48 * i : 48 * i + 48, 128 * ch : 128 * ch + 128
                            ].astype(bf16)
            for s in range(6):
                down.send(s, 0)

        def back_to_norm():
            for j in range(4):
                at = pl.ds(256 * j, 256)
                part = dot_cols(dgu[...], wgu[at, :])
                dmid[:, at] = part[:256]
                sum_send[:, at] = part[256:].astype(bf16)
            to_back.start()

        def wide_grads(scatter, first, base, orders, p):
            for x_hi in range(2):
                rows = nft[pl.ds(512 * x_hi, 512), :]
                for j in range(3):
                    part = dot(rows, dgu[:, pl.ds(base + 768 * p + 256 * j, 256)])
                    for k in range(2):
                        tile = 2 * j + k
                        s = 2 * p + tile // 3
                        reorder_store(
                            part[:, 128 * k : 128 * k + 128],
                            first,
                            s,
                            orders[s],
                            x_hi,
                            pl.ds(128 * (tile % 3), 128),
                            128,
                        )
            for s in (2 * p, 2 * p + 1):
                scatter.send(s, 0)

        w_out_load = pltpu.make_async_copy(w_out_hbm, wd.at[pl.ds(0, 1024)], l_sems.at[4])

        def output():
            to_back.wait_send()

            def pair(i, carry):
                for j in range(2):
                    at = pl.ds(pl.multiple_of(512 * i + 256 * j, 256), 256)
                    part = dot(h[...], wd[:, at])
                    sum_own[:, at] = part[:256]
                    sum_send[:, at] = part[256:].astype(bf16)
                return carry

            lax.fori_loop(0, 2, pair, 0)
            to_out.start()
            w_out_load.start()

        def output_sum():
            to_out.wait()
            sum_send[...] = (mid_ref[...] + sum_own[...] + sum_recv[0].astype(f32)).astype(bf16)
            out_copy.start()

        def norm_back():
            to_back.wait_recv()
            mid = mid_ref[...]
            scale = lax.rsqrt(jnp.mean(mid * mid, axis=-1, keepdims=True) + norm_eps)
            normed = mid * scale
            grad_nffn = dmid[...] + sum_recv[1].astype(f32)
            gain_grad = jnp.sum(grad_nffn * normed, axis=0, keepdims=True)
            for i in range(8):
                vec[0, pl.ds(8 + i, 1), :] = gain_grad[:, 128 * i : 128 * i + 128]
            grad_e = grad_nffn * gain_ffn_ref[...]
            dmid[...] = dyb[own_rows, :].astype(f32) + scale * (
                grad_e - normed * jnp.mean(grad_e * normed, axis=-1, keepdims=True)
            )
            to_att.wait_send()
            att_copy.wait()
            for half in range(2):
                dm_own[half] = dmid[:, pl.ds(512 * half, 512)].astype(bf16)
            to_dm.start()

            to_nf.wait_send()
            w_out_load.wait()
            for i in range(4):
                pair = dot_cols(dm_own[0], wd[pl.ds(256 * i, 256), pl.ds(0, 512)]) + dot_cols(
                    dm_own[1], wd[pl.ds(256 * i, 256), pl.ds(512, 512)]
                )
                for j in range(2):
                    for m in range(2):
                        do_out[m, 2 * i + j] = pair[
                            128 * m : 128 * m + 128, 128 * j : 128 * j + 128
                        ].astype(bf16)
            for m in range(2):
                grads_out.send(m)

        ops = {
            "down": down_grads,
            "dn": back_to_norm,
            "lo": output,
            "datt": norm_back,
            "out": output_sum,
        }
        for p in range(3):
            ops[f"Amm{p}"] = functools.partial(wide_grads, gate, a_first, 0, GATE_ORDERS, p)
            ops[f"Bmm{p}"] = functools.partial(wide_grads, up, b_first, FF_HALF, UP_ORDERS, p)
        run(ops, "split")

    pl.run_scoped(
        feed_forward,
        pltpu.VMEM((1024, 4608), bf16),
        pltpu.VMEM((FF_HALF, 1024), bf16),
        pltpu.VMEM((1024, 512), bf16),
        pltpu.VMEM((512, FF_HALF), bf16),
        pltpu.VMEM((768, 512), bf16),
        pltpu.VMEM((512, 4608), bf16),
        pltpu.VMEM((256, 1024), f32),
    )

    def vec_move(step):
        device = place.neighbour(step) if step < 6 else partner
        return push(place, vec.at[step], vec_in.at[step], v_send, v_recv.at[step], device)

    def vec_take(step):
        vec_move(step).wait_recv()
        vec[step + 1] = vec[step] + vec_in[step]
        vec_move(step + 1).start()

    down_out = DownOwners(place, d_stage, d_in, f_send, f_recv)

    def down_end():
        down_out.send(down, d_acc)

    swap = push(place, g_fin.at[1 - core], g_in, x_send.at[8], x_recv.at[8], partner)
    swap_q = push(place, q_fin.at[1 - core], q_in, x_send.at[9], x_recv.at[9], partner)

    def wide_end():
        for s in range(12):
            total = (gate if s < 6 else up).last(s % 6)
            g_fin[0, s] = total[:8]
            g_fin[1, s] = total[8:]
        swap.start()

    def quad_end():
        for s in range(6):
            total = quad.last(s)
            q_fin[0, s] = total[:8]
            q_fin[1, s] = total[8:]
        swap_q.start()

    def attention_back(
        w_qkv, x_ref, gtok, proj_ref, qkv_ref, o_ref, q2, do2, kk, vv, kt, delta, dq, dp,
        na_own, na_other, att_own, att_other, nat, attt, cols, t_out,
    ):
        sources = [qkv_hbm, o_hbm, proj_hbm, x_hbm, w_qkv_hbm]
        loads = [
            pltpu.make_async_copy(source, target, w_sems.at[i])
            for i, (source, target) in enumerate(
                zip(sources, [qkv_ref, o_ref, proj_ref, x_ref, w_qkv], strict=True)
            )
        ]
        for load in loads:
            load.start()
        grads_back = Exchange(
            place,
            lambda m, j: t_out.at[m, j],
            t_at,
            lambda m: t_out.at[m, pl.ds(0, 7)],
            t_send,
            t_recv,
        )

        def heads_grad(m, carry):
            grads_out.arrived(m)
            starts = document_edges(bounds_ref, m)[0]
            for b in range(4):
                query = qkv_ref[m, pl.ds(16 * b, 16), :, pl.ds(0, 128)].reshape(256, 128)
                pair = qkv_ref[m, pl.ds(16 * b, 16), :, pl.ds(128, 128)].reshape(256, 128)
                pair = pair.astype(f32)
                grad = do_in[m, pl.ds(2 * b, 2)].reshape(256, 128)
                swapped = pltpu.roll(pair, 64, 1)
                key_pair = jnp.where(low, pair, swapped)
                q2[b] = head_rows(query)
                do2[b] = head_rows(grad)
                kk[b] = key_pair.astype(bf16)
                vv[b] = jnp.where(low, swapped, pair).astype(bf16)
                kt[b] = key_pair.T.astype(bf16)
                out = o_ref[m, pl.ds(16 * b, 16)].reshape(256, 128).astype(f32)
                inner = (grad.astype(f32) * out).T
                delta[b, :, pl.ds(0, 256)] = jnp.sum(inner[:64], axis=0, keepdims=True)
                delta[b, :, pl.ds(256, 256)] = jnp.sum(inner[64:], axis=0, keepdims=True)
            for kb in range(4):
                grad_key = jnp.zeros((256, 128), f32)
                grad_value = jnp.zeros((256, 128), f32)
                for qb in range(kb, 4):
                    scores = dot_cols(kk[kb], q2[qb])
                    log_total = jnp.concatenate(
                        [l_ref[m, pl.ds(i, 1), pl.ds(256 * qb, 256)] for i in range(2)], 1
                    )
                    start = starts[:, 256 * qb : 256 * qb + 256]
                    s = 256 * kb + lax.broadcasted_iota(jnp.int32, (256, 512), 0)
                    keep = s >= jnp.concatenate([start, start], 1)
                    if kb == qb:
                        t = lax.broadcasted_iota(jnp.int32, (256, 512), 1)
                        keep = keep & (s <= 256 * qb + lax.rem(t, 256))
                    probs = jnp.where(keep, jnp.exp(scores - log_total), 0.0)
                    grad_probs = dot_cols(vv[kb], do2[qb])
                    grad_scores = (probs * (grad_probs - delta[qb])).astype(bf16)
                    grad_value = grad_value + dot(probs.astype(bf16), do2[qb])
                    grad_key = grad_key + dot(grad_scores, q2[qb])
                    grad_query = dot(kt[kb], grad_scores)
                    if kb == 0:
                        dq[qb] = grad_query[:64]
                    else:
                        dq[qb] = dq[qb] + grad_query[:64]
                grad_key = grad_key + pltpu.roll(grad_key, 64, 1)
                grad_value = grad_value + pltpu.roll(grad_value, 64, 1)
                tile = jnp.where(low, grad_key, grad_value).astype(bf16)
                for half in range(2):
                    rows = slice(128 * half, 128 * half + 128)
                    t_out[m, 2 * kb + half, :, pl.ds(128, 128)] = tile[rows]
            for qb in range(4):
                stacked = jnp.concatenate([dq[qb, :, pl.ds(0, 256)], dq[qb, :, pl.ds(256, 256)]], 0)
                tile = (stacked * 0.125).T.astype(bf16)
                for half in range(2):
                    rows = slice(128 * half, 128 * half + 128)
                    t_out[m, 2 * qb + half, :, pl.ds(0, 128)] = tile[rows]
            grads_back.send(m)
            return carry

        def heads_grads():
            for load in loads[:2]:
                load.wait()
            lax.fori_loop(0, 2, heads_grad, 0)

        def sums_free():
            gate.sent(0)
            up.sent(0)
            for dim in range(6):
                pl.semaphore_signal(
                    free_sem, inc=1, device_id=place.neighbour(dim), device_id_type=MESH
                )

        sides = [
            pltpu.make_async_copy(source, target, l_sems.at[2 + i])
            for i, (source, target) in enumerate(
                zip(
                    [na_hbm, att_hbm, na_other_hbm, att_other_hbm],
                    [na_own, att_own, na_other, att_other],
                    strict=True,
                )
            )
        ]
        for load in sides[:3]:
            load.start()

        def token_sides():
            to_att.wait_recv()
            sides[3].start()
            for load in sides[:3]:
                load.wait()
            nat[:, own_rows] = na_own[...].T
            nat[:, other_rows] = na_other[...].T
            sides[3].wait()
            for i in range(2):
                attt[pl.ds(512 * i, 512), own_rows] = att_own[i].T
                attt[pl.ds(512 * i, 512), other_rows] = att_other[i].T
            to_dm.wait_recv()
            cols[own_rows, pl.ds(1024, 512)] = dm_own[core]
            cols[other_rows, pl.ds(1024, 512)] = dmin[...]

        def projection_grads(s):
            left = nat if s < 4 else attt
            if s == 0:
                to_dp.wait_recv()
                cols[other_rows, pl.ds(0, 1024)] = dpin[...]
            for x_hi in range(2):
                part = dot(left[pl.ds(512 * x_hi, 512), :], cols[:, pl.ds(256 * s, 256)])
                reorder_store(part, a_first, s, QUAD_ORDERS[s], x_hi, narrow, 256)
            if s == 4:
                pl.semaphore_wait(free_sem, 6)
            quad.send(s, 0)

        def both_rows(j, at):
            return jnp.concatenate([t_at(m, j)[:, pl.ds(at, 128)] for m in range(2)], 0).astype(f32)

        def head_back(grad, value, gain):
            grad = grad * cos_ref[...] + turn_heads(grad * sin_ref[...])
            scale = lax.rsqrt(head_mean(value * value) + norm_eps)
            normed = value * scale
            grad_e = grad * gain
            gain_grad = jnp.sum(grad * normed, axis=0, keepdims=True)
            return scale * (grad_e - normed * head_mean(grad_e * normed)), gain_grad

        to_dp = push(place, dp.at[1 - core], dpin, x_send.at[7], x_recv.at[7], partner)
        gtok_copy = pltpu.make_async_copy(gtok, gtok_hbm, l_sems.at[1])

        def turn_back():
            loads[2].wait()
            for m in range(2):
                grads_back.arrived(m)
            sum_k = jnp.zeros((1, 128), f32)

            def query_pair(i, total):
                for j in range(2):
                    at = pl.ds(pl.multiple_of(256 * i + 128 * j, 128), 128)
                    back, part = head_back(both_rows(2 * i + j, 0), proj_ref[:, at], gain_q)
                    dp[0, :, at] = back.astype(bf16)
                    total = total + part
                return total

            sum_q = lax.fori_loop(0, 4, query_pair, jnp.zeros((1, 128), f32))
            for i in range(4):
                first = both_rows(2 * i, 128)
                second = both_rows(2 * i + 1, 128)
                grad_key = jnp.where(low, first, pltpu.roll(second, 64, 1))
                grad_value = jnp.where(low, pltpu.roll(first, 64, 1), second)
                back, part = head_back(grad_key, proj_ref[:, pl.ds(1024 + 128 * i, 128)], gain_k)
                dp[1, :, pl.ds(128 * i, 128)] = back.astype(bf16)
                dp[1, :, pl.ds(512 + 128 * i, 128)] = grad_value.astype(bf16)
                sum_k = sum_k + part
            to_dp.start()
            sum_q = sum_q + pltpu.roll(sum_q, 64, 1)
            sum_k = sum_k + pltpu.roll(sum_k, 64, 1)
            vec[0, pl.ds(16, 8), :] = jnp.zeros((8, 128), f32)
            vec[0, pl.ds(16, 1), :] = jnp.where(
                lax.broadcasted_iota(jnp.int32, (1, 128), 1) < 64, sum_q, sum_k
            )
            cols[own_rows, pl.ds(0, 1024)] = dp[core]

        def last_norm():
            loads[3].wait()
            loads[4].wait()
            inputs = x_ref[...].astype(f32)
            scale = lax.rsqrt(jnp.mean(inputs * inputs, axis=-1, keepdims=True) + norm_eps)
            normed = inputs * scale
            grad_n = dot_cols(dp[0], w_qkv[:, pl.ds(0, 1024)]) + dot_cols(
                dp[1], w_qkv[:, pl.ds(1024, 1024)]
            )
            gain_grad = jnp.sum(grad_n * normed, axis=0, keepdims=True)
            grad_e = grad_n * gain_ref[...]
            gtok[...] = dmid[...] + scale * (
                grad_e - normed * jnp.mean(grad_e * normed, axis=-1, keepdims=True)
            )
            gtok_copy.start()
            for i in range(8):
                vec[0, pl.ds(i, 1), :] = gain_grad[:, 128 * i : 128 * i + 128]
            vec_move(0).start()

        ops = {
            "heads": heads_grads,
            "free": sums_free,
            "nat": token_sides,
            "headb": turn_back,
            "lastnorm": last_norm,
            "Dfin": down_end,
            "Afin": wide_end,
            "Qfin": quad_end,
        }
        for s in range(6):
            ops[f"Qmm{s}"] = functools.partial(projection_grads, s)
            ops[f"v{s}"] = functools.partial(vec_take, s)
        run(ops, "end")
        gtok_copy.wait()
        to_dp.wait_send()
        grads_back.sent()

    pl.run_scoped(
        attention_back,
        pltpu.VMEM((1024, 2048), bf16),
        pltpu.VMEM((256, 1024), bf16),
        pltpu.VMEM((256, 1024), f32),
        pltpu.VMEM((256, 1536), f32),
        pltpu.VMEM((2, 64, 16, 256), bf16),
        pltpu.VMEM((2, 64, 16, 128), bf16),
        pltpu.VMEM((4, 512, 128), bf16),
        pltpu.VMEM((4, 512, 128), bf16),
        pltpu.VMEM((4, 256, 128), bf16),
        pltpu.VMEM((4, 256, 128), bf16),
        pltpu.VMEM((4, 128, 256), bf16),
        pltpu.VMEM((4, 1, 512), f32),
        pltpu.VMEM((4, 64, 512), f32),
        pltpu.VMEM((2, 256, 1024), bf16),
        pltpu.VMEM((256, 1024), bf16),
        pltpu.VMEM((256, 1024), bf16),
        pltpu.VMEM((2, 256, 512), bf16),
        pltpu.VMEM((2, 256, 512), bf16),
        pltpu.VMEM((1024, 512), bf16),
        pltpu.VMEM((1024, 512), bf16),
        pltpu.VMEM((512, 1536), bf16),
        pltpu.VMEM((2, 8, 128, 256), bf16),
    )

    def wide_cols(of, s):
        return pl.ds(pl.multiple_of((s // 6) * 4608 + of * FF_HALF + (s % 6) * 384, 128), 384)

    def quad_cols(of, s):
        if s < 4:
            return gqkv_ref, pl.ds(pl.multiple_of(of * 1024 + 256 * s, 256), 256)
        return gout_ref, pl.ds(pl.multiple_of(of * 512 + 256 * (s - 4), 256), 256)

    results = [
        pltpu.make_async_copy(source, target, r_sems.at[i])
        for i, (source, target) in enumerate(
            (
                (gdn_ref, gdn_hbm),
                (ggu_ref, ggu_hbm),
                (gqkv_ref, gqkv_hbm),
                (gout_ref, gout_hbm),
                (vec.at[7], vec_hbm),
            )
        )
    ]
    for s in range(12):
        ggu_ref[:, wide_cols(core, s)] = g_fin[core, s]
    down_out.arrived(gdn_ref)
    results[0].start()
    swap.wait_recv()
    for s in range(12):
        ggu_ref[:, wide_cols(1 - core, s)] = g_in[s]
    results[1].start()
    vec_move(6).wait_recv()
    vec[7] = vec[6] + vec_in[6]
    results[4].start()
    for s in range(6):
        ref, at = quad_cols(core, s)
        ref[:, at] = q_fin[core, s]
    swap_q.wait_recv()
    for s in range(6):
        ref, at = quad_cols(1 - core, s)
        ref[:, at] = q_in[s]
    results[2].start()
    results[3].start()

    for move in (to_dy, to_dm, swap, swap_q):
        move.wait_send()
    out_copy.wait()
    push(place, vec_in, vec_in, v_send, v_recv.at[0], partner).wait_send()
    for scatter, parts in ((down, (0, 1)), (gate, (1,)), (up, (1,)), (quad, (0, 1))):
        for part in parts:
            scatter.sent(part)
    grads_out.sent()
    down_out.sent()
    for copy in results:
        copy.wait()


def block(bounds, *arrays):
    vmem = pl.BlockSpec(memory_space=pltpu.VMEM)
    hbm = pl.BlockSpec(memory_space=pl.ANY)
    smem = pl.BlockSpec(memory_space=pltpu.SMEM)
    dma = pltpu.SemaphoreType.DMA
    return pl.pallas_call(
        block_kernel,
        out_shape=(
            jax.ShapeDtypeStruct((256, 1024), bf16),
            jax.ShapeDtypeStruct((256, 1024), f32),
            jax.ShapeDtypeStruct((8, 9216), f32),
            jax.ShapeDtypeStruct((36, 1024), f32),
            jax.ShapeDtypeStruct((8, 2048), f32),
            jax.ShapeDtypeStruct((8, 1024), f32),
            jax.ShapeDtypeStruct((24, 128), f32),
            jax.ShapeDtypeStruct((256, 1024), bf16),
            jax.ShapeDtypeStruct((256, 1024), bf16),
            jax.ShapeDtypeStruct((2, 256, 512), bf16),
            jax.ShapeDtypeStruct((2, 256, 512), bf16),
            jax.ShapeDtypeStruct((256, 1536), f32),
            jax.ShapeDtypeStruct((2, 64, 16, 256), bf16),
            jax.ShapeDtypeStruct((2, 64, 16, 128), bf16),
        ),
        in_specs=[smem] + [vmem] * 5 + [hbm] * 6,
        out_specs=(hbm,) * 14,
        scratch_shapes=[
            pltpu.VMEM((6, 64, 16, 384), bf16),
            pltpu.VMEM((6, 63, 16, 384), bf16),
            pltpu.VMEM((6, 64, 16, 384), bf16),
            pltpu.VMEM((6, 63, 16, 384), bf16),
            pltpu.VMEM((6, 64, 48, 128), bf16),
            pltpu.VMEM((6, 63, 48, 128), bf16),
            pltpu.VMEM((512, 1024), bf16),
            pltpu.VMEM((512, 1024), bf16),
            pltpu.VMEM((256, 1024), bf16),
            pltpu.VMEM((2, 256, 1024), bf16),
            pltpu.VMEM((256, 1024), f32),
            pltpu.VMEM((256, 1024), f32),
            pltpu.VMEM((256, 128), f32),
            pltpu.VMEM((256, 128), f32),
            pltpu.VMEM((2, 2, 1024), f32),
            pltpu.VMEM((2, 8, 128, 128), bf16),
            pltpu.VMEM((2, 8, 128, 128), bf16),
            pltpu.VMEM((256, 1024), bf16),
            pltpu.VMEM((256, 512), bf16),
            pltpu.VMEM((2, 256, 512), bf16),
            pltpu.VMEM((2, 12, 8, 384), f32),
            pltpu.VMEM((12, 8, 384), f32),
            pltpu.VMEM((144, 256), f32),
            pltpu.VMEM((4, 40, 256), f32),
            pltpu.VMEM((4, 40, 256), f32),
            pltpu.VMEM((2, 6, 8, 256), f32),
            pltpu.VMEM((6, 8, 256), f32),
            pltpu.VMEM((8, 24, 128), f32),
            pltpu.VMEM((7, 24, 128), f32),
            pltpu.VMEM((8, 9216), f32),
            pltpu.VMEM((36, 1024), f32),
            pltpu.VMEM((8, 2048), f32),
            pltpu.VMEM((8, 1024), f32),
            dma((9,)),
            dma((10,)),
            dma((5,)),
            dma((10,)),
            dma((10,)),
            dma((2,)),
            dma((6, 6)),
            dma((2,)),
            dma((6, 6)),
            dma((2,)),
            dma((6, 6)),
            dma((2,)),
            dma((6, 4)),
            dma((2,)),
            dma((2,)),
            dma((2,)),
            dma((2,)),
            dma((2,)),
            dma((2,)),
            dma((2,)),
            dma((2,)),
            dma((2,)),
            dma((2,)),
            dma,
            dma((7,)),
            pltpu.SemaphoreType.REGULAR,
        ],
        compiler_params=pltpu.CompilerParams(
            collective_id=0, has_side_effects=True, vmem_limit_bytes=VMEM_LIMIT
        ),
        name="transformer_block",
    )(bounds, *arrays)


def finish_kernel(*refs):
    arrays, vec = refs[:6], refs[6]
    targets, (gain_a, gain_f, gain_qk) = refs[7:13], refs[13:16]
    passing, (in_sems, out_sems) = refs[16:22], refs[22:]
    pieces = [
        (source, held, target, pl.ds(first, min(64, source.shape[0])))
        for source, held, target in zip(arrays, passing, targets, strict=True)
        for first in range(0, source.shape[0], 64)
    ]
    reads = [
        pltpu.make_async_copy(source.at[rows], held.at[rows], in_sems.at[i])
        for i, (source, held, _, rows) in enumerate(pieces)
    ]
    writes = [
        pltpu.make_async_copy(held.at[rows], target.at[rows], out_sems.at[i])
        for i, (_, held, target, rows) in enumerate(pieces)
    ]
    for read in reads:
        read.start()
    own = lax.axis_index("rows") * 8 + lax.axis_index("ctx")
    row = lax.div(own, 16)
    at = lax.rem(own, 16)
    lane = lax.broadcasted_iota(jnp.int32, (8, 128), 1)
    tile = lax.broadcasted_iota(jnp.int32, (8, 128), 0)

    def pick(values, of_row, of_lane, count):
        kept = jnp.sum(jnp.where(tile == of_row, values, 0.0), axis=0, keepdims=True)
        place = lax.broadcasted_iota(jnp.int32, (128, count), 0)
        order = lax.broadcasted_iota(jnp.int32, (128, count), 1)
        rows = jnp.broadcast_to(kept, (8, 128)).T[:, :count]
        return jnp.sum(jnp.where(place == of_lane + order, rows, 0.0), axis=0, keepdims=True)

    gain_a[...] = pick(vec[pl.ds(0, 8), :], row, 8 * at, 8)
    gain_f[...] = pick(vec[pl.ds(8, 8), :], row, 8 * at, 8)
    gain_qk[...] = pick(vec[pl.ds(16, 8), :], 0, own, 1)
    for read, write in zip(reads, writes, strict=True):
        read.wait()
        write.start()
    for write in writes:
        write.wait()


def finish(out, gtok, ggu, gdn, gqkv, gout, vec):
    vmem = pl.BlockSpec(memory_space=pltpu.VMEM)
    hbm = pl.BlockSpec(memory_space=pl.ANY)
    same = [jax.ShapeDtypeStruct(a.shape, a.dtype) for a in (out, gtok, ggu, gdn, gqkv, gout)]
    return pl.pallas_call(
        finish_kernel,
        out_shape=(
            *same,
            jax.ShapeDtypeStruct((1, 8), f32),
            jax.ShapeDtypeStruct((1, 8), f32),
            jax.ShapeDtypeStruct((1, 1), f32),
        ),
        in_specs=[hbm] * 6 + [vmem],
        out_specs=(hbm,) * 6 + (vmem,) * 3,
        scratch_shapes=[pltpu.VMEM(a.shape, a.dtype) for a in same]
        + [pltpu.SemaphoreType.DMA((12,)), pltpu.SemaphoreType.DMA((12,))],
        name="results",
    )(out, gtok, ggu, gdn, gqkv, gout, vec)


def local(
    tokens,
    cotangent,
    bounds,
    positions,
    norm_gain_attn,
    w_qkv,
    qk_gain,
    w_out,
    norm_gain_ffn,
    w_gate_up,
    w_down,
):
    lane = np.arange(128) % 32
    freqs = (rope_theta ** (-2.0 * lane / 64)).astype(np.float32)[None]
    results = block(
        bounds,
        positions,
        freqs,
        norm_gain_attn[None],
        norm_gain_ffn[None],
        qk_gain[None],
        tokens.reshape(256, 1024),
        cotangent.reshape(256, 1024),
        w_gate_up,
        w_down,
        w_qkv,
        w_out,
    )
    layer_out, grad_tokens, sum_gate_up, sum_down, sum_qkv, sum_out, gain_a, gain_f, gain_qk = (
        finish(*results[:7])
    )
    return (
        layer_out.reshape(tokens.shape),
        grad_tokens.reshape(tokens.shape),
        gain_a.reshape(8),
        sum_qkv,
        gain_qk.reshape(1),
        sum_out,
        gain_f.reshape(8),
        sum_gate_up,
        sum_down,
    )


def solution(mesh):
    placed = (
        P(None, "rows", "ctx", None),
        P(None, "rows", "ctx", None),
        P(None, "rows", None),
        P(None, "rows", "ctx"),
        P(),
        P(),
        P(),
        P(),
        P(),
        P(),
        P(),
    )
    return jax.shard_map(
        local,
        mesh=mesh,
        in_specs=placed,
        out_specs=(
            P(None, "rows", "ctx", None),
            P(None, "rows", "ctx", None),
            P(("rows", "ctx")),
            P(("rows", "ctx"), None),
            P(("rows", "ctx")),
            P(("rows", "ctx"), None),
            P(("rows", "ctx")),
            P(("rows", "ctx"), None),
            P(("rows", "ctx"), None),
        ),
        check_vma=False,
    )
```

```python
import functools

import jax
import jax.numpy as jnp
import numpy as np
from jax import lax
from jax.experimental import pallas as pl
from jax.experimental.pallas import tpu as pltpu
from jax.sharding import PartitionSpec as P

MESH = pl.DeviceIdType.MESH
norm_eps = 1e-05
rope_theta = 1000000.0
f32 = jnp.float32
bf16 = jnp.bfloat16
VMEM_LIMIT = 64 * 2**20 - 2**18


class Place:
    def __init__(self):
        r = lax.axis_index("rows")
        k = lax.axis_index("ctx")
        self.x_hi = lax.div(r, 8)
        self.y = lax.rem(lax.div(r, 2), 4)
        self.core = lax.rem(r, 2)
        self.x_lo = lax.div(k, 4)
        self.z = lax.rem(k, 4)
        self.rows = r
        self.ctx = k
        self.bits = [
            self.x_hi,
            lax.rem(self.x_hi + self.x_lo, 2),
            lax.div(self.y, 2),
            lax.rem(lax.div(self.y, 2) + lax.rem(self.y, 2), 2),
            lax.div(self.z, 2),
            lax.rem(lax.div(self.z, 2) + lax.rem(self.z, 2), 2),
        ]

    def at(self, x_hi=None, x_lo=None, y=None, z=None, core=None):
        x_hi = self.x_hi if x_hi is None else x_hi
        x_lo = self.x_lo if x_lo is None else x_lo
        y = self.y if y is None else y
        z = self.z if z is None else z
        core = self.core if core is None else core
        return (x_hi * 8 + y * 2 + core, x_lo * 4 + z)

    def partner(self):
        return self.at(core=1 - self.core)

    def neighbour(self, dim):
        if dim == 0:
            return self.at(x_hi=1 - self.x_hi, x_lo=1 - self.x_lo)
        if dim == 1:
            return self.at(x_lo=1 - self.x_lo)
        if dim == 2:
            return self.at(y=3 - self.y)
        if dim == 3:
            return self.at(y=self.y + 1 - 2 * lax.rem(self.y, 2))
        if dim == 4:
            return self.at(z=3 - self.z)
        return self.at(z=self.z + 1 - 2 * lax.rem(self.z, 2))


    def flipped(self, dims):
        if len(dims) == 1:
            return self.neighbour(dims[0])
        if 0 in dims:
            return self.at(x_hi=1 - self.x_hi)
        if 2 in dims:
            return self.at(y=lax.rem(self.y + 2, 4))
        return self.at(z=lax.rem(self.z + 2, 4))


def gray(v):
    return v ^ (v >> 1)


def chip_number(x_hi, x_lo, y, z):
    return gray(2 * x_hi + x_lo) * 16 + gray(y) * 4 + gray(z)


def slot_of(number, order):
    return sum(((number >> (5 - dim)) & 1) << (5 - t) for t, dim in enumerate(order))


ONES = (1, 1, 1, 1, 1, 1)
FLIPS = {1: ((1,),), 2: ((0, 1), (1, 0), (1, 1))}


class Scatter:
    def __init__(self, place, orders, shape, first, held, send_sems, recv_sems):
        self.place = place
        self.orders = orders
        self.first, self.first_cols = first
        self.held, self.held_cols = held
        self.send_sems = send_sems
        self.recv_sems = recv_sems
        self.stages = []
        at, slots, base = 0, 64, 0
        for width in shape:
            size = slots >> width
            self.stages.append((at, width, size, base))
            base += size * len(FLIPS[width])
            at += width
            slots = size

    def source(self, k):
        if k == 0:
            return self.first, 0, self.first_cols
        return self.held, self.stages[k - 1][3], self.held_cols

    def part(self, s, k, flips):
        at, width, size, _ = self.stages[k]
        which = 0
        for dim, flip in zip(self.orders[s][at : at + width], flips, strict=True):
            bit = self.place.bits[dim]
            which = 2 * which + (1 - bit if flip else bit)
        return which * size

    def copies(self, s, k):
        at, width, size, base = self.stages[k]
        ref, start, cols = self.source(k)
        dims = self.orders[s][at : at + width]
        return [
            pltpu.make_async_remote_copy(
                src_ref=ref.at[s, pl.ds(start + self.part(s, k, flips), size), :, cols],
                dst_ref=self.held.at[s, pl.ds(base + i * size, size), :, self.held_cols],
                send_sem=self.send_sems.at[min(k, 1)],
                recv_sem=self.recv_sems.at[s, k],
                device_id=self.place.flipped([d for d, f in zip(dims, flips, strict=True) if f]),
                device_id_type=MESH,
            )
            for i, flips in enumerate(FLIPS[width])
        ]

    def send(self, s, k):
        for copy in self.copies(s, k):
            copy.start()

    def arrived(self, s, k):
        _, width, size, base = self.stages[k]
        place = self.held.at[s, pl.ds(base, size * len(FLIPS[width])), :, self.held_cols]
        self.wait(place, 0, self.recv_sems.at[s, k]).wait_recv()
        ref, start, cols = self.source(k)
        own = start + self.part(s, k, (0,) * width)

        def total(at):
            value = ref[s, own + at, :, cols].astype(f32)
            for i in range(len(FLIPS[width])):
                value = value + self.held[s, base + i * size + at, :, self.held_cols].astype(f32)
            return value

        return total, size, base

    def take(self, s, k):
        total, size, base = self.arrived(s, k)
        ref, start, cols = self.source(k)
        own = start + self.part(s, k, (0,) * self.stages[k][1])
        per = min(16, size)

        def body(i, carry):
            for j in range(per):
                at = i * per + j
                if self.stages[k][1] == 1:
                    value = ref[s, own + at, :, cols] + self.held[s, base + at, :, self.held_cols]
                else:
                    value = total(at).astype(bf16)
                self.held[s, base + at, :, self.held_cols] = value
            return carry

        lax.fori_loop(0, size // per, body, 0)
        self.send(s, k + 1)

    def last(self, s):
        return self.arrived(s, len(self.stages) - 1)[0](0)

    def wait(self, ref, part, recv_sem):
        return push(
            self.place, ref, ref, self.send_sems.at[part], recv_sem, self.place.partner()
        )

    def sent(self, part):
        slots = pl.ds(0, 32) if part == 0 else pl.ds(32, 31)
        self.wait(
            self.held.at[:, slots, :, self.held_cols], part, self.recv_sems.at[0, 0]
        ).wait_send()


def greet_signal(place, devices):
    barrier = pltpu.get_barrier_semaphore()
    targets = down_targets(place)
    for device in devices + targets[1:]:
        pl.semaphore_signal(barrier, inc=1, device_id=device, device_id_type=MESH)

    @pl.when(place.x_hi != place.core)
    def _():
        pl.semaphore_signal(barrier, inc=1, device_id=targets[0], device_id_type=MESH)


def greet_wait(place, devices):
    barrier = pltpu.get_barrier_semaphore()
    count = len(devices) + 3

    @pl.when(place.x_hi != place.core)
    def _():
        pl.semaphore_wait(barrier, count + 1)

    @pl.when(place.x_hi == place.core)
    def _():
        pl.semaphore_wait(barrier, count)


def push(place, src, dst, send_sem, recv_sem, device):
    return pltpu.make_async_remote_copy(
        src_ref=src,
        dst_ref=dst,
        send_sem=send_sem,
        recv_sem=recv_sem,
        device_id=device,
        device_id_type=MESH,
    )


def down_targets(place):
    return [
        place.at(x_hi=place.core, core=place.x_hi, z=lax.rem(place.z + off, 4)) for off in range(4)
    ]


def dot(left, right):
    return jnp.dot(left, right, preferred_element_type=f32)


def dot_cols(left, right):
    return lax.dot_general(left, right, (((1,), (1,)), ((), ())), preferred_element_type=f32)


FF_HALF = 2304
DOWN_ORDERS = (
    (0, 3, 5, 2, 1, 4),
    (3, 5, 4, 2, 0, 1),
    (2, 3, 0, 4, 1, 5),
    (4, 2, 0, 1, 3, 5),
    (5, 2, 3, 4, 0, 1),
    (0, 3, 4, 1, 5, 2),
)
GATE_ORDERS = (
    (5, 2, 1, 3, 4, 0),
    (4, 0, 3, 5, 1, 2),
    (2, 1, 4, 3, 0, 5),
    (0, 3, 2, 5, 4, 1),
    (4, 0, 2, 3, 5, 1),
    (5, 3, 0, 2, 1, 4),
)
UP_ORDERS = (
    (2, 3, 1, 4, 0, 5),
    (3, 4, 5, 0, 2, 1),
    (0, 2, 5, 4, 3, 1),
    (1, 0, 2, 3, 5, 4),
    (1, 2, 5, 0, 4, 3),
    (3, 1, 2, 0, 4, 5),
)
QUAD_ORDERS = (
    (2, 3, 1, 0, 4, 5),
    (1, 0, 5, 4, 2, 3),
    (3, 2, 1, 0, 5, 4),
    (5, 4, 3, 2, 1, 0),
    (4, 5, 2, 3, 0, 1),
    (1, 0, 5, 4, 2, 3),
)
QUAD_STAGES = (1, 1, 2, 2)
LINKED = ((0,), (1,), (2,), (3,), (4,), (5,), (0, 1), (2, 3), (4, 5))
STEPS = (
    "Bmm0", "Amm0", "Bmm1", "Bmm2", "Amm2", "Amm1", "dn", "B00", "down", "lo",
    "B20", "A20", "A00", "A10", "B30", "datt", "B50", "A40", "B10", "B40",
    "A30", "D40", "D10", "out", "A21", "B01", "A50", "split", "D20", "B21",
    "heads", "A31", "nat", "D00", "B51", "B11", "free", "D11", "A11", "D21",
    "D30", "A01", "A22", "D50", "B41", "D41", "B02", "B22", "A51", "B31",
    "Qmm4", "B52", "Qmm5", "A12", "D01", "A32", "headb", "A41", "lastnorm", "A02",
    "D12", "B03", "B12", "D31", "D51", "B23", "B32", "Qmm0", "Qmm1", "Qmm3",
    "Qmm2", "D42", "B53", "A13", "v0", "D13", "B24", "A42", "A23", "A52",
    "B42", "Q50", "A33", "B13", "A03", "D02", "B04", "D22", "D32", "D14",
    "Q40", "A24", "D52", "B33", "B43", "D43", "Q00", "B54", "Q10", "Q30",
    "v1", "Q20", "A53", "A34", "Q51", "B14", "A04", "D23", "D33", "D03",
    "A43", "D53", "v2", "Q41", "B44", "A54", "Q01", "B34", "Q11", "A14",
    "Q31", "Q21", "D04", "D34", "v3", "Q52", "D54", "D24", "A44", "D44",
    "Q42", "Q02", "Q12", "Q32", "Q22", "v4", "Afin", "Dfin", "Qfin", "v5",
    "end",
)


class DownOwners:
    def __init__(self, place, stage, into, send_sems, recv_sems):
        self.swapped = place.x_hi != place.core
        self.place = place
        self.stage = stage
        self.into = into
        targets = down_targets(place)
        self.moves = [
            push(
                place,
                stage.at[lax.rem(place.z + off, 4)],
                into.at[place.z],
                send_sems.at[min(off, 1)],
                recv_sems.at[min(off, 1)],
                targets[off],
            )
            for off in range(4)
        ]
        three = into.at[pl.ds(0, 3)]
        self.others = push(place, three, three, send_sems.at[1], recv_sems.at[1], targets[1])

    def send(self, down, acc):
        for s in range(6):
            acc[pl.ds(48 * (s // 2), 48), pl.ds(128 * (s % 2), 128)] = down.last(s)
        for z in range(4):
            self.stage[z, pl.ds(0, 36), :] = acc[pl.ds(36 * z, 36), :]
            self.stage[z, pl.ds(36, 4), :] = jnp.zeros((4, 256), f32)
        for move in self.moves[1:]:
            move.start()

        @pl.when(self.swapped)
        def _():
            self.moves[0].start()

        @pl.when(jnp.logical_not(self.swapped))
        def _():
            self.into[self.place.z] = self.stage[self.place.z]

    def arrived(self, out):
        @pl.when(self.swapped)
        def _():
            self.moves[0].wait_recv()

        self.others.wait_recv()
        for z in range(4):
            out[:, pl.ds(256 * z, 256)] = self.into[z, pl.ds(0, 36), :]

    def sent(self):
        self.others.wait_send()

        @pl.when(self.swapped)
        def _():
            self.moves[0].wait_send()


def lanes(rows):
    return lax.broadcasted_iota(jnp.int32, (rows, 128), 1)


def turn_heads(values):
    low = lax.rem(lanes(values.shape[0]), 64) < 32
    return jnp.where(low, pltpu.roll(values, 96, 1), pltpu.roll(values, 32, 1))


def head_mean(values):
    i = lax.broadcasted_iota(jnp.int32, (128, 128), 0)
    j = lax.broadcasted_iota(jnp.int32, (128, 128), 1)
    ones = jnp.where(lax.div(i, 64) == lax.div(j, 64), 1.0 / 64, 0.0).astype(bf16)
    high = values.astype(bf16)
    rest = (values - high.astype(f32)).astype(bf16)
    return dot(high, ones) + dot(rest, ones)


def gain_tiles(qk_gain):
    swapped = pltpu.roll(qk_gain, 64, 1)
    low = lax.broadcasted_iota(jnp.int32, (1, 128), 1) < 64
    return jnp.where(low, qk_gain, swapped), jnp.where(low, swapped, qk_gain)


def head_rows(values):
    low = lanes(values.shape[0]) < 64
    zero = jnp.zeros_like(values)
    return jnp.concatenate([jnp.where(low, values, zero), jnp.where(low, zero, values)], 0)


class Exchange:
    def __init__(self, place, out_at, into_at, seven, send_sems, recv_sems):
        self.place = place
        self.seven = seven
        self.out_at = out_at
        self.into_at = into_at
        self.send_sems = send_sems
        self.recv_sems = recv_sems

    def copy(self, m, off):
        j = lax.rem(self.place.ctx + off, 8)
        return push(
            self.place,
            self.out_at(m, j),
            self.into_at(m, self.place.ctx),
            self.send_sems.at[m],
            self.recv_sems.at[m],
            (self.place.rows, j),
        )

    def send(self, m):
        for off in range(1, 8):
            self.copy(m, off).start()
        self.keep(m)

    def keep(self, m):
        self.into_at(m, self.place.ctx)[...] = self.out_at(m, self.place.ctx)[...]

    def all_seven(self, m):
        ref = self.seven(m)
        return push(
            self.place, ref, ref, self.send_sems.at[m], self.recv_sems.at[m], self.place.partner()
        )

    def arrived(self, m):
        self.all_seven(m).wait_recv()

    def sent(self):
        for m in range(2):
            self.all_seven(m).wait_send()


def ctx_peers(place):
    return [(place.rows, lax.rem(place.ctx + off, 8)) for off in range(1, 8)]


def document_edges(bounds_ref, m):
    index = lax.broadcasted_iota(jnp.int32, (1, 1024), 1)
    start = jnp.zeros((1, 1024), jnp.int32)
    end = jnp.full((1, 1024), 1024, jnp.int32)
    for k in range(1, 4):
        cut = bounds_ref[m, 0, k]
        start = jnp.where(index >= cut, cut, start)
        end = jnp.where(index < bounds_ref[m, 0, 4 - k], bounds_ref[m, 0, 4 - k], end)
    return start, end


def reorder_store(part, first, s, order, x_hi, at, width):
    part = part.reshape(4, 2, 8, 8, width)
    for y in range(4):
        for x_lo in range(2):
            for z in range(4):
                slot = slot_of(chip_number(x_hi, x_lo, y, z), order)
                first[s, slot, :, at] = part[y, :, 4 * x_lo + z].reshape(16, width).astype(bf16)


def block_kernel(
    bounds_ref,
    pos_ref,
    freq_ref,
    gain_ref,
    gain_ffn_ref,
    qk_gain_ref,
    x_hbm,
    cot_hbm,
    wgu_hbm,
    wd_hbm,
    w_qkv_hbm,
    w_out_hbm,
    out_hbm,
    gtok_hbm,
    ggu_hbm,
    gdn_hbm,
    gqkv_hbm,
    gout_hbm,
    vec_hbm,
    na_hbm,
    na_other_hbm,
    att_hbm,
    att_other_hbm,
    proj_hbm,
    qkv_hbm,
    o_hbm,
    a_first,
    a_held,
    b_first,
    b_held,
    d_first,
    d_held,
    nf,
    dyb,
    sum_send,
    sum_recv,
    mid_ref,
    dmid,
    cos_ref,
    sin_ref,
    l_ref,
    do_out,
    do_in,
    dpin,
    dmin,
    dm_own,
    g_fin,
    g_in,
    d_acc,
    d_stage,
    d_in,
    q_fin,
    q_in,
    vec,
    vec_in,
    ggu_ref,
    gdn_ref,
    gqkv_ref,
    gout_ref,
    w_sems,
    l_sems,
    r_sems,
    x_send,
    x_recv,
    a_send,
    a_recv,
    b_send,
    b_recv,
    d_send,
    d_recv,
    q_send,
    q_recv,
    f_send,
    f_recv,
    k_send,
    k_recv,
    e_send,
    e_recv,
    do_send,
    do_recv,
    t_send,
    t_recv,
    v_send,
    v_recv,
    free_sem,
):
    place = Place()
    core = place.core
    partner = place.partner()
    every = slice(None)
    down = Scatter(place, DOWN_ORDERS, ONES, (d_first, every), (d_held, every), d_send, d_recv)
    gate = Scatter(place, GATE_ORDERS, ONES, (a_first, every), (a_held, every), a_send, a_recv)
    up = Scatter(place, UP_ORDERS, ONES, (b_first, every), (b_held, every), b_send, b_recv)
    narrow = pl.ds(0, 256)
    quad = Scatter(
        place, QUAD_ORDERS, QUAD_STAGES, (a_first, narrow), (b_first, narrow), q_send, q_recv
    )
    sums = {"D": down, "A": gate, "B": up, "Q": quad}
    steps = iter(STEPS)

    def run(ops, until):
        for name in steps:
            if name == until:
                return
            if name in ops:
                ops[name]()
            else:
                sums[name[0]].take(int(name[1]), int(name[2]))
    def t_at(m, j):
        return nf.at[
            pl.ds(pl.multiple_of(256 * m + 128 * lax.div(j, 4), 128), 128),
            pl.ds(pl.multiple_of(256 * lax.rem(j, 4), 256), 256),
        ]

    def tiles(ref, s, j, width):
        return ref.at[s, pl.ds(pl.multiple_of(8 * j, 8), 8), :, pl.ds(0, width)]

    heads_out = Exchange(
        place,
        lambda m, j: tiles(a_first, m, j, 256),
        lambda m, j: tiles(b_first, m, j, 256),
        lambda m: b_first.at[m, pl.ds(0, 56), :, pl.ds(0, 256)],
        k_send,
        k_recv,
    )
    heads_back = Exchange(
        place,
        lambda m, j: tiles(b_first, 4 + m, j, 128),
        lambda m, j: tiles(b_first, 2 + m, j, 128),
        lambda m: b_first.at[2 + m, pl.ds(0, 56), :, pl.ds(0, 128)],
        e_send,
        e_recv,
    )
    grads_out = Exchange(
        place,
        lambda m, j: do_out.at[m, j],
        lambda m, j: do_in.at[m, j],
        lambda m: do_in.at[m, pl.ds(0, 7)],
        do_send,
        do_recv,
    )
    own_rows = pl.ds(0, 256)
    other_rows = pl.ds(256, 256)
    to_dy = push(place, cot_hbm, dyb.at[other_rows], x_send.at[0], x_recv.at[0], partner)
    to_nf = push(place, nf.at[own_rows], nf.at[other_rows], x_send.at[1], x_recv.at[1], partner)
    to_out = push(place, sum_send, sum_recv.at[0], x_send.at[2], x_recv.at[2], partner)
    to_back = push(place, sum_send, sum_recv.at[1], x_send.at[3], x_recv.at[3], partner)
    to_att = push(place, dm_own, att_other_hbm, x_send.at[5], x_recv.at[5], partner)
    att_copy = pltpu.make_async_copy(dm_own, att_hbm, l_sems.at[7])
    qkv_copy = pltpu.make_async_copy(
        b_first.at[pl.ds(0, 2), :, :, pl.ds(0, 256)], qkv_hbm, l_sems.at[8]
    )
    o_copy = pltpu.make_async_copy(
        b_first.at[pl.ds(4, 2), :, :, pl.ds(0, 128)], o_hbm, l_sems.at[9]
    )
    cot_load = pltpu.make_async_copy(cot_hbm, dyb.at[own_rows], l_sems.at[1])
    low = lanes(256) < 64
    gain_q, gain_k = gain_tiles(qk_gain_ref[...])

    def attend(w_qkv, x_ref, na, proj_ref, q2, kk, vo):
        x_load = pltpu.make_async_copy(x_hbm, x_ref, l_sems.at[2])
        w_loads = [
            pltpu.make_async_copy(w_qkv_hbm.at[:, cols], w_qkv.at[:, cols], sem)
            for cols, sem in (
                (pl.ds(1024, 1024), l_sems.at[3]),
                (pl.ds(0, 1024), l_sems.at[6]),
            )
        ]
        na_copy = pltpu.make_async_copy(na, na_hbm, l_sems.at[4])
        proj_copy = pltpu.make_async_copy(proj_ref, proj_hbm, l_sems.at[5])
        for load in (x_load, *w_loads, cot_load):
            load.start()
        peers = [partner] + [place.flipped(dims) for dims in LINKED] + ctx_peers(place)
        greet_signal(place, peers)
        columns = jnp.concatenate(
            [pos_ref[0].astype(f32), pos_ref[1].astype(f32), jnp.zeros((6, 128), f32)], 0
        ).T
        sign = jnp.where(lax.rem(lanes(128), 64) < 32, -1.0, 1.0)
        for m in range(2):
            angle = columns[:, m : m + 1] * freq_ref[...]
            cos_ref[pl.ds(128 * m, 128), :] = jnp.cos(angle)
            sin_ref[pl.ds(128 * m, 128), :] = jnp.sin(angle) * sign
        x_load.wait()
        inputs = x_ref[...].astype(f32)
        scale = lax.rsqrt(jnp.mean(inputs * inputs, axis=-1, keepdims=True) + norm_eps)
        na[...] = (inputs * scale * gain_ref[...]).astype(bf16)
        to_na = push(place, na, na_other_hbm, x_send.at[4], x_recv.at[4], partner)
        na_copy.start()
        w_loads[0].wait()

        def turned(tile, gain):
            u = tile * lax.rsqrt(head_mean(tile * tile) + norm_eps) * gain
            return u * cos_ref[...] + turn_heads(u) * sin_ref[...]

        def store(at, j, tile):
            for m in range(2):
                rows = tile[128 * m : 128 * m + 128].astype(bf16)
                a_first[m, pl.ds(8 * j, 8), :, pl.ds(at, 128)] = rows.reshape(8, 16, 128)

        for i in range(2):
            key_pair = dot(na[...], w_qkv[:, pl.ds(1024 + 256 * i, 256)])
            value_pair = dot(na[...], w_qkv[:, pl.ds(1536 + 256 * i, 256)])
            proj_ref[:, pl.ds(1024 + 256 * i, 256)] = key_pair
            for j in range(2):
                key = turned(key_pair[:, 128 * j : 128 * j + 128], gain_k)
                value = value_pair[:, 128 * j : 128 * j + 128]
                store(128, 4 * i + 2 * j, jnp.where(low, key, pltpu.roll(value, 64, 1)))
                store(128, 4 * i + 2 * j + 1, jnp.where(low, pltpu.roll(key, 64, 1), value))
        greet_wait(place, peers)
        to_dy.start()

        w_loads[1].wait()
        for i in range(4):
            p = lax.rem(lax.div(place.ctx, 2) + 1 + i, 4)
            at = pl.ds(pl.multiple_of(256 * p, 256), 256)
            pair = dot(na[...], w_qkv[:, at])
            proj_ref[:, at] = pair
            for j in range(2):
                store(0, 2 * p + j, turned(pair[:, 128 * j : 128 * j + 128], gain_q) * 0.125)
            for j in range(2):
                off = lax.rem(2 * p + j + 8 - place.ctx, 8)

                @pl.when(off > 0)
                def _(off=off):
                    heads_out.copy(0, off).start()

        heads_out.keep(0)
        heads_out.send(1)
        to_na.start()
        proj_copy.start()

        def heads(m, carry):
            heads_out.arrived(m)
            ends = document_edges(bounds_ref, m)[1]
            for b in range(4):
                query = b_first[m, pl.ds(16 * b, 16), :, pl.ds(0, 128)].reshape(256, 128)
                pair = b_first[m, pl.ds(16 * b, 16), :, pl.ds(128, 128)].reshape(256, 128)
                pair = pair.astype(f32)
                swapped = pltpu.roll(pair, 64, 1)
                q2[b] = head_rows(query)
                kk[b] = jnp.where(low, pair, swapped).astype(bf16)
                vo[b] = jnp.where(low, swapped, 1.0).astype(bf16)
            for qb in range(4):
                acc = jnp.zeros((512, 128), f32)
                for kb in range(qb + 1):
                    scores = dot_cols(q2[qb], kk[kb])
                    t = 256 * qb + lax.rem(lax.broadcasted_iota(jnp.int32, (512, 256), 0), 256)
                    keep = t < ends[:, 256 * kb : 256 * kb + 256]
                    if kb == qb:
                        s = 256 * kb + lax.broadcasted_iota(jnp.int32, (512, 256), 1)
                        keep = keep & (s <= t)
                    weights = jnp.where(keep, jnp.exp(scores), 0.0).astype(bf16)
                    acc = acc + dot(weights, vo[kb])
                total = pltpu.roll(acc, 64, 1)
                head0 = acc[:256]
                head1 = pltpu.roll(acc[256:], 64, 1)
                denominator = jnp.where(low, total[:256], acc[256:])
                out = jnp.where(low, head0, head1) / denominator
                log_total = jnp.log(denominator).T
                l_ref[m, pl.ds(0, 1), pl.ds(256 * qb, 256)] = log_total[0:1]
                l_ref[m, pl.ds(1, 1), pl.ds(256 * qb, 256)] = log_total[64:65]
                b_first[4 + m, pl.ds(16 * qb, 16), :, pl.ds(0, 128)] = out.astype(bf16).reshape(
                    16, 16, 128
                )
            heads_back.send(m)
            return carry

        lax.fori_loop(0, 2, heads, 0)
        qkv_copy.start()
        o_copy.start()
        na_copy.wait()
        proj_copy.wait()
        to_na.wait()

    pl.run_scoped(
        attend,
        pltpu.VMEM((1024, 2048), bf16),
        pltpu.VMEM((256, 1024), bf16),
        pltpu.VMEM((256, 1024), bf16),
        pltpu.VMEM((256, 1536), f32),
        pltpu.VMEM((4, 512, 128), bf16),
        pltpu.VMEM((4, 256, 128), bf16),
        pltpu.VMEM((4, 256, 128), bf16),
    )

    to_dm = push(place, dm_own.at[1 - core], dmin, x_send.at[6], x_recv.at[6], partner)
    out_copy = pltpu.make_async_copy(sum_send, out_hbm, l_sems.at[0])

    def feed_forward(wgu, wd, nft, h, ht, dgu, sum_own):
        def unit_loads(i):
            at = pl.multiple_of(core * FF_HALF + 768 * i, 256)
            up_at = pl.multiple_of(4608 + core * FF_HALF + 768 * i, 256)
            here = pl.ds(pl.multiple_of(768 * i, 256), 768)
            up_here = pl.ds(pl.multiple_of(FF_HALF + 768 * i, 256), 768)
            return [
                pltpu.make_async_copy(
                    wgu_hbm.at[:, pl.ds(at, 768)], wgu.at[:, here], w_sems.at[3 * i]
                ),
                pltpu.make_async_copy(
                    wgu_hbm.at[:, pl.ds(up_at, 768)], wgu.at[:, up_here], w_sems.at[3 * i + 1]
                ),
                pltpu.make_async_copy(
                    wd_hbm.at[pl.ds(at, 768)], wd.at[here], w_sems.at[3 * i + 2]
                ),
            ]

        w_out_loads = [
            pltpu.make_async_copy(
                w_out_hbm.at[pl.ds(512 * i, 512)], dgu.at[:, pl.ds(1024 * i, 1024)], l_sems.at[2 + i]
            )
            for i in range(2)
        ]
        x_load = pltpu.make_async_copy(x_hbm, sum_send, l_sems.at[4])
        for load in (x_load, *w_out_loads):
            load.start()
        for i in range(3):
            for copy in unit_loads(i):
                copy.start()
        for m in range(2):
            heads_back.arrived(m)
            for j in range(8):
                tile = b_first[2 + m, pl.ds(8 * j, 8), :, pl.ds(0, 128)].reshape(128, 128)
                dm_own[j // 4, pl.ds(128 * m, 128), pl.ds(128 * (j % 4), 128)] = tile
        to_att.start()
        att_copy.start()
        for load in (x_load, *w_out_loads):
            load.wait()
        mid = sum_send[...].astype(f32) + (
            dot(dm_own[0], dgu[:, pl.ds(0, 1024)]) + dot(dm_own[1], dgu[:, pl.ds(1024, 1024)])
        )
        mid_ref[...] = mid
        scale = lax.rsqrt(jnp.mean(mid * mid, axis=-1, keepdims=True) + norm_eps)
        nf[own_rows, :] = (mid * scale * gain_ffn_ref[...]).astype(bf16)
        to_nf.start()
        nft[:, own_rows] = nf[own_rows, :].T
        heads_out.sent()
        heads_back.sent()
        qkv_copy.wait()
        o_copy.wait()
        cot_load.wait()

        def token_half(half, carry):
            rows = pl.ds(pl.multiple_of(256 * half, 256), 256)

            @pl.when(half == 1)
            def _():
                to_dy.wait_recv()
                to_nf.wait_recv()

            def units(i, inner):
                @pl.when(half == 0)
                def _():
                    for copy in unit_loads(i):
                        copy.wait()

                cols = pl.ds(pl.multiple_of(768 * i, 256), 768)
                up_cols = pl.ds(pl.multiple_of(FF_HALF + 768 * i, 256), 768)
                gated = dot(nf[rows, :], wgu[:, cols])
                upward = dot(nf[rows, :], wgu[:, up_cols])
                grad_hidden = dot_cols(dyb[rows, :], wd[cols, :])
                sigma = 1.0 / (1.0 + jnp.exp(-gated))
                silu = gated * sigma
                h[rows, cols] = (silu * upward).astype(bf16)
                dgu[rows, cols] = (grad_hidden * upward * (sigma + silu * (1.0 - sigma))).astype(
                    bf16
                )
                dgu[rows, up_cols] = (grad_hidden * silu).astype(bf16)
                return inner

            return lax.fori_loop(0, 3, units, carry)

        lax.fori_loop(0, 2, token_half, 0)
        nft[:, other_rows] = nf[other_rows, :].T

        def down_grads():
            for block in range(3):
                ht[...] = h[:, pl.ds(768 * block, 768)].T
                for z in range(4):
                    part = dot(ht[...], dyb[:, pl.ds(256 * z, 256)])
                    for i in range(16):
                        q = 16 * block + i
                        y, core_to, x_lo, rg = q // 12, (q // 6) % 2, (q // 3) % 2, q % 3
                        for ch in range(2):
                            s = 2 * rg + ch
                            slot = slot_of(chip_number(core_to, x_lo, y, z), DOWN_ORDERS[s])
                            d_first[s, slot] = part[
                                48 * i : 48 * i + 48, 128 * ch : 128 * ch + 128
                            ].astype(bf16)
            for s in range(6):
                down.send(s, 0)

        def back_to_norm():
            for j in range(4):
                at = pl.ds(256 * j, 256)
                part = dot_cols(dgu[...], wgu[at, :])
                dmid[:, at] = part[:256]
                sum_send[:, at] = part[256:].astype(bf16)
            to_back.start()

        def wide_grads(scatter, first, base, orders, p):
            for x_hi in range(2):
                rows = nft[pl.ds(512 * x_hi, 512), :]
                for j in range(3):
                    part = dot(rows, dgu[:, pl.ds(base + 768 * p + 256 * j, 256)])
                    for k in range(2):
                        tile = 2 * j + k
                        s = 2 * p + tile // 3
                        reorder_store(
                            part[:, 128 * k : 128 * k + 128],
                            first,
                            s,
                            orders[s],
                            x_hi,
                            pl.ds(128 * (tile % 3), 128),
                            128,
                        )
            for s in (2 * p, 2 * p + 1):
                scatter.send(s, 0)

        w_out_load = pltpu.make_async_copy(w_out_hbm, wd.at[pl.ds(0, 1024)], l_sems.at[4])

        def output():
            to_back.wait_send()
            for j in range(4):
                at = pl.ds(256 * j, 256)
                part = dot(h[...], wd[:, at])
                sum_own[:, at] = part[:256]
                sum_send[:, at] = part[256:].astype(bf16)
            to_out.start()
            w_out_load.start()

        def output_sum():
            to_out.wait()
            sum_send[...] = (mid_ref[...] + sum_own[...] + sum_recv[0].astype(f32)).astype(bf16)
            out_copy.start()

        def norm_back():
            to_back.wait_recv()
            mid = mid_ref[...]
            scale = lax.rsqrt(jnp.mean(mid * mid, axis=-1, keepdims=True) + norm_eps)
            normed = mid * scale
            grad_nffn = dmid[...] + sum_recv[1].astype(f32)
            gain_grad = jnp.sum(grad_nffn * normed, axis=0, keepdims=True)
            for i in range(8):
                vec[0, pl.ds(8 + i, 1), :] = gain_grad[:, 128 * i : 128 * i + 128]
            grad_e = grad_nffn * gain_ffn_ref[...]
            dmid[...] = dyb[own_rows, :].astype(f32) + scale * (
                grad_e - normed * jnp.mean(grad_e * normed, axis=-1, keepdims=True)
            )
            to_att.wait_send()
            att_copy.wait()
            for half in range(2):
                dm_own[half] = dmid[:, pl.ds(512 * half, 512)].astype(bf16)
            to_dm.start()

            to_nf.wait_send()
            w_out_load.wait()
            for i in range(4):
                pair = dot_cols(dm_own[0], wd[pl.ds(256 * i, 256), pl.ds(0, 512)]) + dot_cols(
                    dm_own[1], wd[pl.ds(256 * i, 256), pl.ds(512, 512)]
                )
                for j in range(2):
                    for m in range(2):
                        do_out[m, 2 * i + j] = pair[
                            128 * m : 128 * m + 128, 128 * j : 128 * j + 128
                        ].astype(bf16)
            for m in range(2):
                grads_out.send(m)

        ops = {
            "down": down_grads,
            "dn": back_to_norm,
            "lo": output,
            "datt": norm_back,
            "out": output_sum,
        }
        for p in range(3):
            ops[f"Amm{p}"] = functools.partial(wide_grads, gate, a_first, 0, GATE_ORDERS, p)
            ops[f"Bmm{p}"] = functools.partial(wide_grads, up, b_first, FF_HALF, UP_ORDERS, p)
        run(ops, "split")

    pl.run_scoped(
        feed_forward,
        pltpu.VMEM((1024, 4608), bf16),
        pltpu.VMEM((FF_HALF, 1024), bf16),
        pltpu.VMEM((1024, 512), bf16),
        pltpu.VMEM((512, FF_HALF), bf16),
        pltpu.VMEM((768, 512), bf16),
        pltpu.VMEM((512, 4608), bf16),
        pltpu.VMEM((256, 1024), f32),
    )

    def vec_move(step):
        device = place.neighbour(step) if step < 6 else partner
        return push(place, vec.at[step], vec_in.at[step], v_send, v_recv.at[step], device)

    def vec_take(step):
        vec_move(step).wait_recv()
        vec[step + 1] = vec[step] + vec_in[step]
        vec_move(step + 1).start()

    down_out = DownOwners(place, d_stage, d_in, f_send, f_recv)

    def down_end():
        down_out.send(down, d_acc)

    swap = push(place, g_fin.at[1 - core], g_in, x_send.at[8], x_recv.at[8], partner)
    swap_q = push(place, q_fin.at[1 - core], q_in, x_send.at[9], x_recv.at[9], partner)

    def wide_end():
        for s in range(12):
            total = (gate if s < 6 else up).last(s % 6)
            g_fin[0, s] = total[:8]
            g_fin[1, s] = total[8:]
        swap.start()

    def quad_end():
        for s in range(6):
            total = quad.last(s)
            q_fin[0, s] = total[:8]
            q_fin[1, s] = total[8:]
        swap_q.start()

    def attention_back(
        w_qkv, x_ref, gtok, proj_ref, qkv_ref, o_ref, q2, do2, kk, vv, kt, delta, dq, dp,
        na_own, na_other, att_own, att_other, nat, attt, cols, t_out,
    ):
        sources = [qkv_hbm, o_hbm, proj_hbm, x_hbm, w_qkv_hbm]
        loads = [
            pltpu.make_async_copy(source, target, w_sems.at[i])
            for i, (source, target) in enumerate(
                zip(sources, [qkv_ref, o_ref, proj_ref, x_ref, w_qkv], strict=True)
            )
        ]
        for load in loads:
            load.start()
        grads_back = Exchange(
            place,
            lambda m, j: t_out.at[m, j],
            t_at,
            lambda m: t_out.at[m, pl.ds(0, 7)],
            t_send,
            t_recv,
        )

        def heads_grad(m, carry):
            grads_out.arrived(m)
            starts = document_edges(bounds_ref, m)[0]
            for b in range(4):
                query = qkv_ref[m, pl.ds(16 * b, 16), :, pl.ds(0, 128)].reshape(256, 128)
                pair = qkv_ref[m, pl.ds(16 * b, 16), :, pl.ds(128, 128)].reshape(256, 128)
                pair = pair.astype(f32)
                grad = do_in[m, pl.ds(2 * b, 2)].reshape(256, 128)
                swapped = pltpu.roll(pair, 64, 1)
                key_pair = jnp.where(low, pair, swapped)
                q2[b] = head_rows(query)
                do2[b] = head_rows(grad)
                kk[b] = key_pair.astype(bf16)
                vv[b] = jnp.where(low, swapped, pair).astype(bf16)
                kt[b] = key_pair.T.astype(bf16)
                out = o_ref[m, pl.ds(16 * b, 16)].reshape(256, 128).astype(f32)
                inner = (grad.astype(f32) * out).T
                delta[b, :, pl.ds(0, 256)] = jnp.sum(inner[:64], axis=0, keepdims=True)
                delta[b, :, pl.ds(256, 256)] = jnp.sum(inner[64:], axis=0, keepdims=True)
            for kb in range(4):
                grad_key = jnp.zeros((256, 128), f32)
                grad_value = jnp.zeros((256, 128), f32)
                for qb in range(kb, 4):
                    scores = dot_cols(kk[kb], q2[qb])
                    log_total = jnp.concatenate(
                        [l_ref[m, pl.ds(i, 1), pl.ds(256 * qb, 256)] for i in range(2)], 1
                    )
                    start = starts[:, 256 * qb : 256 * qb + 256]
                    s = 256 * kb + lax.broadcasted_iota(jnp.int32, (256, 512), 0)
                    keep = s >= jnp.concatenate([start, start], 1)
                    if kb == qb:
                        t = lax.broadcasted_iota(jnp.int32, (256, 512), 1)
                        keep = keep & (s <= 256 * qb + lax.rem(t, 256))
                    probs = jnp.where(keep, jnp.exp(scores - log_total), 0.0)
                    grad_probs = dot_cols(vv[kb], do2[qb])
                    grad_scores = (probs * (grad_probs - delta[qb])).astype(bf16)
                    grad_value = grad_value + dot(probs.astype(bf16), do2[qb])
                    grad_key = grad_key + dot(grad_scores, q2[qb])
                    grad_query = dot(kt[kb], grad_scores)
                    if kb == 0:
                        dq[qb] = grad_query[:64]
                    else:
                        dq[qb] = dq[qb] + grad_query[:64]
                grad_key = grad_key + pltpu.roll(grad_key, 64, 1)
                grad_value = grad_value + pltpu.roll(grad_value, 64, 1)
                tile = jnp.where(low, grad_key, grad_value).astype(bf16)
                for half in range(2):
                    rows = slice(128 * half, 128 * half + 128)
                    t_out[m, 2 * kb + half, :, pl.ds(128, 128)] = tile[rows]
            for qb in range(4):
                stacked = jnp.concatenate([dq[qb, :, pl.ds(0, 256)], dq[qb, :, pl.ds(256, 256)]], 0)
                tile = (stacked * 0.125).T.astype(bf16)
                for half in range(2):
                    rows = slice(128 * half, 128 * half + 128)
                    t_out[m, 2 * qb + half, :, pl.ds(0, 128)] = tile[rows]
            grads_back.send(m)
            return carry

        def heads_grads():
            for load in loads[:2]:
                load.wait()
            lax.fori_loop(0, 2, heads_grad, 0)

        def sums_free():
            gate.sent(0)
            up.sent(0)
            for dim in range(6):
                pl.semaphore_signal(
                    free_sem, inc=1, device_id=place.neighbour(dim), device_id_type=MESH
                )

        sides = [
            pltpu.make_async_copy(source, target, l_sems.at[2 + i])
            for i, (source, target) in enumerate(
                zip(
                    [na_hbm, att_hbm, na_other_hbm, att_other_hbm],
                    [na_own, att_own, na_other, att_other],
                    strict=True,
                )
            )
        ]
        for load in sides[:3]:
            load.start()

        def token_sides():
            to_att.wait_recv()
            sides[3].start()
            for load in sides[:3]:
                load.wait()
            nat[:, own_rows] = na_own[...].T
            nat[:, other_rows] = na_other[...].T
            sides[3].wait()
            for i in range(2):
                attt[pl.ds(512 * i, 512), own_rows] = att_own[i].T
                attt[pl.ds(512 * i, 512), other_rows] = att_other[i].T
            to_dm.wait_recv()
            cols[own_rows, pl.ds(1024, 512)] = dm_own[core]
            cols[other_rows, pl.ds(1024, 512)] = dmin[...]

        def projection_grads(s):
            left = nat if s < 4 else attt
            if s == 0:
                to_dp.wait_recv()
                cols[other_rows, pl.ds(0, 1024)] = dpin[...]
            for x_hi in range(2):
                part = dot(left[pl.ds(512 * x_hi, 512), :], cols[:, pl.ds(256 * s, 256)])
                reorder_store(part, a_first, s, QUAD_ORDERS[s], x_hi, narrow, 256)
            if s == 4:
                pl.semaphore_wait(free_sem, 6)
            quad.send(s, 0)

        def both_rows(j, at):
            return jnp.concatenate([t_at(m, j)[:, pl.ds(at, 128)] for m in range(2)], 0).astype(f32)

        def head_back(grad, value, gain):
            grad = grad * cos_ref[...] + turn_heads(grad * sin_ref[...])
            scale = lax.rsqrt(head_mean(value * value) + norm_eps)
            normed = value * scale
            grad_e = grad * gain
            gain_grad = jnp.sum(grad * normed, axis=0, keepdims=True)
            return scale * (grad_e - normed * head_mean(grad_e * normed)), gain_grad

        to_dp = push(place, dp.at[1 - core], dpin, x_send.at[7], x_recv.at[7], partner)
        gtok_copy = pltpu.make_async_copy(gtok, gtok_hbm, l_sems.at[1])

        def turn_back():
            loads[2].wait()
            for m in range(2):
                grads_back.arrived(m)
            sum_k = jnp.zeros((1, 128), f32)
            sum_q = jnp.zeros((1, 128), f32)
            for j in range(8):
                at = pl.ds(128 * j, 128)
                back, part = head_back(both_rows(j, 0), proj_ref[:, at], gain_q)
                dp[0, :, at] = back.astype(bf16)
                sum_q = sum_q + part
            for i in range(4):
                first = both_rows(2 * i, 128)
                second = both_rows(2 * i + 1, 128)
                grad_key = jnp.where(low, first, pltpu.roll(second, 64, 1))
                grad_value = jnp.where(low, pltpu.roll(first, 64, 1), second)
                back, part = head_back(grad_key, proj_ref[:, pl.ds(1024 + 128 * i, 128)], gain_k)
                dp[1, :, pl.ds(128 * i, 128)] = back.astype(bf16)
                dp[1, :, pl.ds(512 + 128 * i, 128)] = grad_value.astype(bf16)
                sum_k = sum_k + part
            to_dp.start()
            sum_q = sum_q + pltpu.roll(sum_q, 64, 1)
            sum_k = sum_k + pltpu.roll(sum_k, 64, 1)
            vec[0, pl.ds(16, 8), :] = jnp.zeros((8, 128), f32)
            vec[0, pl.ds(16, 1), :] = jnp.where(
                lax.broadcasted_iota(jnp.int32, (1, 128), 1) < 64, sum_q, sum_k
            )
            cols[own_rows, pl.ds(0, 1024)] = dp[core]

        def last_norm():
            loads[3].wait()
            loads[4].wait()
            inputs = x_ref[...].astype(f32)
            scale = lax.rsqrt(jnp.mean(inputs * inputs, axis=-1, keepdims=True) + norm_eps)
            normed = inputs * scale
            grad_n = dot_cols(dp[0], w_qkv[:, pl.ds(0, 1024)]) + dot_cols(
                dp[1], w_qkv[:, pl.ds(1024, 1024)]
            )
            gain_grad = jnp.sum(grad_n * normed, axis=0, keepdims=True)
            grad_e = grad_n * gain_ref[...]
            gtok[...] = dmid[...] + scale * (
                grad_e - normed * jnp.mean(grad_e * normed, axis=-1, keepdims=True)
            )
            gtok_copy.start()
            for i in range(8):
                vec[0, pl.ds(i, 1), :] = gain_grad[:, 128 * i : 128 * i + 128]
            vec_move(0).start()

        ops = {
            "heads": heads_grads,
            "free": sums_free,
            "nat": token_sides,
            "headb": turn_back,
            "lastnorm": last_norm,
            "Dfin": down_end,
            "Afin": wide_end,
            "Qfin": quad_end,
        }
        for s in range(6):
            ops[f"Qmm{s}"] = functools.partial(projection_grads, s)
            ops[f"v{s}"] = functools.partial(vec_take, s)
        run(ops, "end")
        gtok_copy.wait()
        to_dp.wait_send()
        grads_back.sent()

    pl.run_scoped(
        attention_back,
        pltpu.VMEM((1024, 2048), bf16),
        pltpu.VMEM((256, 1024), bf16),
        pltpu.VMEM((256, 1024), f32),
        pltpu.VMEM((256, 1536), f32),
        pltpu.VMEM((2, 64, 16, 256), bf16),
        pltpu.VMEM((2, 64, 16, 128), bf16),
        pltpu.VMEM((4, 512, 128), bf16),
        pltpu.VMEM((4, 512, 128), bf16),
        pltpu.VMEM((4, 256, 128), bf16),
        pltpu.VMEM((4, 256, 128), bf16),
        pltpu.VMEM((4, 128, 256), bf16),
        pltpu.VMEM((4, 1, 512), f32),
        pltpu.VMEM((4, 64, 512), f32),
        pltpu.VMEM((2, 256, 1024), bf16),
        pltpu.VMEM((256, 1024), bf16),
        pltpu.VMEM((256, 1024), bf16),
        pltpu.VMEM((2, 256, 512), bf16),
        pltpu.VMEM((2, 256, 512), bf16),
        pltpu.VMEM((1024, 512), bf16),
        pltpu.VMEM((1024, 512), bf16),
        pltpu.VMEM((512, 1536), bf16),
        pltpu.VMEM((2, 8, 128, 256), bf16),
    )

    def wide_cols(of, s):
        return pl.ds(pl.multiple_of((s // 6) * 4608 + of * FF_HALF + (s % 6) * 384, 128), 384)

    def quad_cols(of, s):
        if s < 4:
            return gqkv_ref, pl.ds(pl.multiple_of(of * 1024 + 256 * s, 256), 256)
        return gout_ref, pl.ds(pl.multiple_of(of * 512 + 256 * (s - 4), 256), 256)

    results = [
        pltpu.make_async_copy(source, target, r_sems.at[i])
        for i, (source, target) in enumerate(
            (
                (gdn_ref, gdn_hbm),
                (ggu_ref, ggu_hbm),
                (gqkv_ref, gqkv_hbm),
                (gout_ref, gout_hbm),
                (vec.at[7], vec_hbm),
            )
        )
    ]
    for s in range(12):
        ggu_ref[:, wide_cols(core, s)] = g_fin[core, s]
    down_out.arrived(gdn_ref)
    results[0].start()
    swap.wait_recv()
    for s in range(12):
        ggu_ref[:, wide_cols(1 - core, s)] = g_in[s]
    results[1].start()
    vec_move(6).wait_recv()
    vec[7] = vec[6] + vec_in[6]
    results[4].start()
    for s in range(6):
        ref, at = quad_cols(core, s)
        ref[:, at] = q_fin[core, s]
    swap_q.wait_recv()
    for s in range(6):
        ref, at = quad_cols(1 - core, s)
        ref[:, at] = q_in[s]
    results[2].start()
    results[3].start()

    for move in (to_dy, to_dm, swap, swap_q):
        move.wait_send()
    out_copy.wait()
    push(place, vec_in, vec_in, v_send, v_recv.at[0], partner).wait_send()
    for scatter, parts in ((down, (0, 1)), (gate, (1,)), (up, (1,)), (quad, (0, 1))):
        for part in parts:
            scatter.sent(part)
    grads_out.sent()
    down_out.sent()
    for copy in results:
        copy.wait()


def block(bounds, *arrays):
    vmem = pl.BlockSpec(memory_space=pltpu.VMEM)
    hbm = pl.BlockSpec(memory_space=pl.ANY)
    smem = pl.BlockSpec(memory_space=pltpu.SMEM)
    dma = pltpu.SemaphoreType.DMA
    return pl.pallas_call(
        block_kernel,
        out_shape=(
            jax.ShapeDtypeStruct((256, 1024), bf16),
            jax.ShapeDtypeStruct((256, 1024), f32),
            jax.ShapeDtypeStruct((8, 9216), f32),
            jax.ShapeDtypeStruct((36, 1024), f32),
            jax.ShapeDtypeStruct((8, 2048), f32),
            jax.ShapeDtypeStruct((8, 1024), f32),
            jax.ShapeDtypeStruct((24, 128), f32),
            jax.ShapeDtypeStruct((256, 1024), bf16),
            jax.ShapeDtypeStruct((256, 1024), bf16),
            jax.ShapeDtypeStruct((2, 256, 512), bf16),
            jax.ShapeDtypeStruct((2, 256, 512), bf16),
            jax.ShapeDtypeStruct((256, 1536), f32),
            jax.ShapeDtypeStruct((2, 64, 16, 256), bf16),
            jax.ShapeDtypeStruct((2, 64, 16, 128), bf16),
        ),
        in_specs=[smem] + [vmem] * 5 + [hbm] * 6,
        out_specs=(hbm,) * 14,
        scratch_shapes=[
            pltpu.VMEM((6, 64, 16, 384), bf16),
            pltpu.VMEM((6, 63, 16, 384), bf16),
            pltpu.VMEM((6, 64, 16, 384), bf16),
            pltpu.VMEM((6, 63, 16, 384), bf16),
            pltpu.VMEM((6, 64, 48, 128), bf16),
            pltpu.VMEM((6, 63, 48, 128), bf16),
            pltpu.VMEM((512, 1024), bf16),
            pltpu.VMEM((512, 1024), bf16),
            pltpu.VMEM((256, 1024), bf16),
            pltpu.VMEM((2, 256, 1024), bf16),
            pltpu.VMEM((256, 1024), f32),
            pltpu.VMEM((256, 1024), f32),
            pltpu.VMEM((256, 128), f32),
            pltpu.VMEM((256, 128), f32),
            pltpu.VMEM((2, 2, 1024), f32),
            pltpu.VMEM((2, 8, 128, 128), bf16),
            pltpu.VMEM((2, 8, 128, 128), bf16),
            pltpu.VMEM((256, 1024), bf16),
            pltpu.VMEM((256, 512), bf16),
            pltpu.VMEM((2, 256, 512), bf16),
            pltpu.VMEM((2, 12, 8, 384), f32),
            pltpu.VMEM((12, 8, 384), f32),
            pltpu.VMEM((144, 256), f32),
            pltpu.VMEM((4, 40, 256), f32),
            pltpu.VMEM((4, 40, 256), f32),
            pltpu.VMEM((2, 6, 8, 256), f32),
            pltpu.VMEM((6, 8, 256), f32),
            pltpu.VMEM((8, 24, 128), f32),
            pltpu.VMEM((7, 24, 128), f32),
            pltpu.VMEM((8, 9216), f32),
            pltpu.VMEM((36, 1024), f32),
            pltpu.VMEM((8, 2048), f32),
            pltpu.VMEM((8, 1024), f32),
            dma((9,)),
            dma((10,)),
            dma((5,)),
            dma((10,)),
            dma((10,)),
            dma((2,)),
            dma((6, 6)),
            dma((2,)),
            dma((6, 6)),
            dma((2,)),
            dma((6, 6)),
            dma((2,)),
            dma((6, 4)),
            dma((2,)),
            dma((2,)),
            dma((2,)),
            dma((2,)),
            dma((2,)),
            dma((2,)),
            dma((2,)),
            dma((2,)),
            dma((2,)),
            dma((2,)),
            dma,
            dma((7,)),
            pltpu.SemaphoreType.REGULAR,
        ],
        compiler_params=pltpu.CompilerParams(
            collective_id=0, has_side_effects=True, vmem_limit_bytes=VMEM_LIMIT
        ),
        name="transformer_block",
    )(bounds, *arrays)


def finish_kernel(*refs):
    arrays, vec = refs[:6], refs[6]
    targets, (gain_a, gain_f, gain_qk) = refs[7:13], refs[13:16]
    passing, (in_sems, out_sems) = refs[16:22], refs[22:]
    pieces = [
        (source, held, target, pl.ds(first, min(64, source.shape[0])))
        for source, held, target in zip(arrays, passing, targets, strict=True)
        for first in range(0, source.shape[0], 64)
    ]
    reads = [
        pltpu.make_async_copy(source.at[rows], held.at[rows], in_sems.at[i])
        for i, (source, held, _, rows) in enumerate(pieces)
    ]
    writes = [
        pltpu.make_async_copy(held.at[rows], target.at[rows], out_sems.at[i])
        for i, (_, held, target, rows) in enumerate(pieces)
    ]
    for read in reads:
        read.start()
    own = lax.axis_index("rows") * 8 + lax.axis_index("ctx")
    row = lax.div(own, 16)
    at = lax.rem(own, 16)
    lane = lax.broadcasted_iota(jnp.int32, (8, 128), 1)
    tile = lax.broadcasted_iota(jnp.int32, (8, 128), 0)

    def pick(values, of_row, of_lane, count):
        kept = jnp.sum(jnp.where(tile == of_row, values, 0.0), axis=0, keepdims=True)
        place = lax.broadcasted_iota(jnp.int32, (128, count), 0)
        order = lax.broadcasted_iota(jnp.int32, (128, count), 1)
        rows = jnp.broadcast_to(kept, (8, 128)).T[:, :count]
        return jnp.sum(jnp.where(place == of_lane + order, rows, 0.0), axis=0, keepdims=True)

    gain_a[...] = pick(vec[pl.ds(0, 8), :], row, 8 * at, 8)
    gain_f[...] = pick(vec[pl.ds(8, 8), :], row, 8 * at, 8)
    gain_qk[...] = pick(vec[pl.ds(16, 8), :], 0, own, 1)
    for read, write in zip(reads, writes, strict=True):
        read.wait()
        write.start()
    for write in writes:
        write.wait()


def finish(out, gtok, ggu, gdn, gqkv, gout, vec):
    vmem = pl.BlockSpec(memory_space=pltpu.VMEM)
    hbm = pl.BlockSpec(memory_space=pl.ANY)
    same = [jax.ShapeDtypeStruct(a.shape, a.dtype) for a in (out, gtok, ggu, gdn, gqkv, gout)]
    return pl.pallas_call(
        finish_kernel,
        out_shape=(
            *same,
            jax.ShapeDtypeStruct((1, 8), f32),
            jax.ShapeDtypeStruct((1, 8), f32),
            jax.ShapeDtypeStruct((1, 1), f32),
        ),
        in_specs=[hbm] * 6 + [vmem],
        out_specs=(hbm,) * 6 + (vmem,) * 3,
        scratch_shapes=[pltpu.VMEM(a.shape, a.dtype) for a in same]
        + [pltpu.SemaphoreType.DMA((12,)), pltpu.SemaphoreType.DMA((12,))],
        name="results",
    )(out, gtok, ggu, gdn, gqkv, gout, vec)


def local(
    tokens,
    cotangent,
    bounds,
    positions,
    norm_gain_attn,
    w_qkv,
    qk_gain,
    w_out,
    norm_gain_ffn,
    w_gate_up,
    w_down,
):
    lane = np.arange(128) % 32
    freqs = (rope_theta ** (-2.0 * lane / 64)).astype(np.float32)[None]
    results = block(
        bounds,
        positions,
        freqs,
        norm_gain_attn[None],
        norm_gain_ffn[None],
        qk_gain[None],
        tokens.reshape(256, 1024),
        cotangent.reshape(256, 1024),
        w_gate_up,
        w_down,
        w_qkv,
        w_out,
    )
    layer_out, grad_tokens, sum_gate_up, sum_down, sum_qkv, sum_out, gain_a, gain_f, gain_qk = (
        finish(*results[:7])
    )
    return (
        layer_out.reshape(tokens.shape),
        grad_tokens.reshape(tokens.shape),
        gain_a.reshape(8),
        sum_qkv,
        gain_qk.reshape(1),
        sum_out,
        gain_f.reshape(8),
        sum_gate_up,
        sum_down,
    )


def solution(mesh):
    placed = (
        P(None, "rows", "ctx", None),
        P(None, "rows", "ctx", None),
        P(None, "rows", None),
        P(None, "rows", "ctx"),
        P(),
        P(),
        P(),
        P(),
        P(),
        P(),
        P(),
    )
    return jax.shard_map(
        local,
        mesh=mesh,
        in_specs=placed,
        out_specs=(
            P(None, "rows", "ctx", None),
            P(None, "rows", "ctx", None),
            P(("rows", "ctx")),
            P(("rows", "ctx"), None),
            P(("rows", "ctx")),
            P(("rows", "ctx"), None),
            P(("rows", "ctx")),
            P(("rows", "ctx"), None),
            P(("rows", "ctx"), None),
        ),
        check_vma=False,
    )
```
